32 devices in a mesh: groups: 2 (over y), ex: 4 (over z), ey: 4 (over x, core).
Axes of the slice: x: 2, y: 2, z: 4, core: 2. Of those that a mesh axis runs over, the one named last changes fastest.
Arguments:
- inputs: bfloat16 [2048, 4096], P(('groups', 'ex'), 'ey'), parts along dimension 0, may hold values from -6 to 6
- grad_output: bfloat16 [2048, 4096], P(('groups', 'ex'), 'ey'), parts along dimension 0, may hold values from -6 to 6
- routes: int32 [2048, 8], P(('groups', 'ex')), parts along dimension 0, may hold values from 0 to 127, as said below
- gate_probs: bfloat16 [2048, 8], P(('groups', 'ex')), parts along dimension 0, may hold values from 0.19921875 to 1
- gate_up: bfloat16 [4, 2, 1536, 4096], P('ex', None, None, 'ey'), may hold values from -0.09375 to 0.09375
- down_proj: bfloat16 [4, 1536, 4096], P('ex', None, 'ey'), may hold values from -0.15625 to 0.15625
Outputs:
- grad_inputs: bfloat16 [2048, 4096], P(('groups', 'ex'), 'ey'), parts along dimension 0
- grad_gate_up: bfloat16 [4, 4, 1536, 4096], P('ex', 'groups', None, 'ey'), parts along dimension 1
- grad_down: bfloat16 [4, 3072, 4096], P('ex', 'groups', 'ey'), parts along dimension 1
The draws below stay inside these ranges and needn't reach their ends.
There are 2 independent parts, one for each index of `groups`. The reference program is written for one: setup_inputs(seed, part) draws one part's arguments, and reference() takes and returns one part's arrays. A program takes and returns all parts, laid end to end along the dimension named above; an argument that names none is the same for every part. Nothing has to cross between parts.
Inputs may be any that keep to these rules, and one draw needn't show every extreme that they name: `routes`: each row names 8 different experts. Within the 256 rows of one index of ex (aligned blocks), every expert is named by either no row or exactly 40 rows, except at most one expert of the block, which is named by fewer.
All inputs are finite; a program needn't handle non-finite values.
Results may differ from the reference program's by a relative error of at most 0.017.
Values may be sent and summed in bfloat16 or wider, within the bound.
No kernel may reach another device: no remote copies, remote signals or barrier semaphores. Data moves between devices by JAX's collectives and lax.ppermute only.
A program may use at most 64 MiB of HBM per device.

```python
import jax
import jax.numpy as jnp
from jax import lax

D = 4096
FF = 1536
EXPERTS = 128
TOPK = 8
TOK_EX = 256
TOKENS = 1024
EXP_WIN = 4
CAP = 80
MOST = 40
N_EY = 4


def draw_routes(key, part):
    key = jax.random.fold_in(key, 11)
    block_count = TOKENS // TOK_EX
    pool_size = (TOK_EX * TOPK + MOST - 1) // MOST
    pair_index = jnp.arange(TOPK, dtype=jnp.int32)[None, :] * TOK_EX + jnp.arange(TOK_EX, dtype=jnp.int32)[:, None]

    def one_block(block_key):
        pool_key, order_key = jax.random.split(block_key)
        pool = jax.random.permutation(pool_key, EXPERTS)[:pool_size].astype(jnp.int32)
        order = jax.random.permutation(order_key, TOK_EX).astype(jnp.int32)
        chosen = jnp.take(pool, pair_index // MOST)
        return jnp.take(chosen, order, axis=0)
    block_keys = jax.random.split(key, block_count)
    return jax.vmap(one_block)(block_keys).reshape(TOKENS, TOPK).astype(jnp.int32)


def block_levels(key, extent, shards, smallest, top_value):
    def one(axis_at, shards_of):
        heights = jax.random.uniform(jax.random.fold_in(jax.random.fold_in(key, 6), axis_at), (shards_of,), jnp.float32, smallest / len(shards), top_value / len(shards))
        return jnp.repeat(jnp.exp(heights), extent[axis_at] // shards_of).reshape((-1,) + (1,) * (len(extent) - axis_at - 1))

    factor_of = one(*shards[0])
    for cut in shards[1:]:
        factor_of = factor_of * one(*cut)
    return factor_of


def gaussian(own_key, shape, spread, most, cuts=(), kind=jnp.bfloat16):
    values = jax.random.normal(own_key, shape, jnp.float32) * spread
    if len(cuts) > 0:
        values = block_levels(own_key, shape, cuts, -0.22, 0.18) * values
    return jnp.clip(values, min=-most, max=most).astype(kind)


def setup_inputs(seed: int = 0, part: int = 0) -> dict:
    key_of = jax.random.split(jax.random.key(seed), 7)
    part_splits = jax.random.split(jax.random.fold_in(key_of[6], part), 7)
    return {
        "inputs": gaussian(part_splits[0], (TOKENS, D), 1.0, 6.0, ((0, 4), (1, 4))),
        "grad_output": gaussian(part_splits[1], (TOKENS, D), 1.0, 6.0, ((0, 4), (1, 4))),
        "routes": draw_routes(jax.random.fold_in(jax.random.fold_in(key_of[6], part), 71), part),
        "gate_probs": jnp.clip(0.19921875 + 0.80078125 * jax.random.uniform(part_splits[3], (TOKENS, TOPK), jnp.float32) ** block_levels(part_splits[3], (TOKENS, TOPK), ((0, 4),), -0.2, 0.2), 0.19921875, 1.0).astype(jnp.bfloat16),
        "gate_up": gaussian(key_of[4], (EXP_WIN, 2, FF, D), D ** -0.5, 0.09375, ((0, 4), (3, 4))),
        "down_proj": gaussian(key_of[5], (EXP_WIN, FF, D), FF ** -0.5, 0.15625, ((0, 4), (2, 4))),
    }


def block_sum(left, weight):
    width = left.shape[1] // N_EY
    left_blocks = left.reshape(left.shape[0], N_EY, width)
    weight_blocks = weight.reshape(weight.shape[0], N_EY, width)
    partial_sums = jnp.einsum("cbd,fbd->bcf", left_blocks, weight_blocks, precision=lax.Precision.HIGHEST)
    rounded = lax.optimization_barrier(partial_sums.astype(jnp.bfloat16))
    return jnp.sum(rounded.astype(jnp.float32), axis=0)


def swiglu_backward(gate_sum, up_sum, grad_act):
    sigmoid_gate = jax.nn.sigmoid(gate_sum)
    silu_gate = gate_sum * sigmoid_gate
    activation = (silu_gate * up_sum).astype(jnp.bfloat16)
    grad_gate = (grad_act * up_sum * sigmoid_gate * (1.0 + gate_sum * (1.0 - sigmoid_gate))).astype(jnp.bfloat16)
    grad_up = (grad_act * silu_gate).astype(jnp.bfloat16)
    return activation, grad_gate, grad_up


def reference(inputs, grad_output, routes, gate_probs, gate_up, down_proj):
    token_count = inputs.shape[0]
    token_iota = jnp.arange(token_count, dtype=jnp.int32)
    probs_wide = gate_probs.astype(jnp.float32)

    def per_expert(accumulated, expert):
        matches = routes == expert
        routed = jnp.any(matches, axis=1).astype(jnp.int32)
        position = (jnp.cumsum(routed) - routed).astype(jnp.int32)
        weight_prob = jnp.sum(jnp.where(matches, probs_wide, 0.0), axis=1)
        kept = (routed == 1) & (position < CAP)
        target = jnp.where(kept, position, CAP).astype(jnp.int32)
        slot_token = jnp.full((CAP + 1,), -1, jnp.int32).at[target].set(token_iota)[:CAP]
        valid = slot_token >= 0
        safe_token = jnp.maximum(slot_token, 0).astype(jnp.int32)
        rows_in = jnp.where(valid[:, None], inputs[safe_token].astype(jnp.float32), 0.0)
        scaled = grad_output[safe_token].astype(jnp.float32) * weight_prob[safe_token][:, None]
        scaled = lax.optimization_barrier(scaled.astype(jnp.bfloat16)).astype(jnp.float32)
        rows_grad = jnp.where(valid[:, None], scaled, 0.0)
        gate_weight = gate_up[expert, 0].astype(jnp.float32)
        up_weight = gate_up[expert, 1].astype(jnp.float32)
        down_weight = down_proj[expert].astype(jnp.float32)
        gate_sum = block_sum(rows_in, gate_weight)
        up_sum = block_sum(rows_in, up_weight)
        grad_act = block_sum(rows_grad, down_weight)
        activation, grad_gate, grad_up = swiglu_backward(gate_sum, up_sum, grad_act)
        grad_gate_wide = grad_gate.astype(jnp.float32)
        grad_up_wide = grad_up.astype(jnp.float32)
        down_grad = jnp.dot(activation.astype(jnp.float32).T, rows_grad).astype(jnp.bfloat16)
        gate_grad = jnp.dot(grad_gate_wide.T, rows_in)
        up_grad = jnp.dot(grad_up_wide.T, rows_in)
        pair_grad = jnp.stack([gate_grad, up_grad]).astype(jnp.bfloat16)
        grad_rows = jnp.dot(grad_gate_wide, gate_weight) + jnp.dot(grad_up_wide, up_weight)
        accumulated = accumulated.at[safe_token].add(jnp.where(valid[:, None], grad_rows, 0.0))
        return accumulated, (pair_grad, down_grad)

    start_grad = jnp.zeros((token_count, D), jnp.float32)
    total_grad, outputs = lax.scan(per_expert, start_grad, jnp.arange(EXP_WIN, dtype=jnp.int32))
    return total_grad.astype(jnp.bfloat16), outputs[0], outputs[1]
```

```python
import jax
import jax.numpy as jnp
from jax import lax
from jax.sharding import PartitionSpec as P

MOST = 40
EXPERTS = 128
EMPTY = 64.0


def swap(value, axis, bit):
    count = lax.axis_size(axis)
    return lax.ppermute(value, axis, [(i, i ^ bit) for i in range(count)])


def exchange(pieces, axis):
    return [pieces[0]] + [swap(pieces[k], axis, k) for k in range(1, len(pieces))]


def local(inputs, grad_output, routes, gate_probs, gate_up, down_proj):
    experts = lax.axis_size("ex")
    me = lax.axis_index("ex")
    tokens, width = inputs.shape
    capacity = 5 * tokens * experts * routes.shape[1] // (4 * EXPERTS)
    order = me ^ jnp.arange(experts, dtype=jnp.int32)
    matches = routes[:, :, None] == order[None, None, :]
    routed = jnp.any(matches, axis=1)
    prob = jnp.sum(jnp.where(matches, gate_probs.astype(jnp.float32)[:, :, None], 0.0), axis=1)
    token = jnp.arange(tokens, dtype=jnp.int32)
    before = (token[:, None] > token[None, :]).astype(jnp.bfloat16)
    rank = jnp.dot(before, routed.astype(jnp.bfloat16), preferred_element_type=jnp.float32)
    rank = rank.astype(jnp.int32)
    picks = (rank[:, :, None] == jnp.arange(MOST, dtype=jnp.int32)) & routed[:, :, None]
    pick = picks.reshape(tokens, experts * MOST).astype(jnp.bfloat16)
    slot_prob = jnp.sum(jnp.where(picks, prob[:, :, None], 0.0), axis=0).reshape(-1)
    filled = jnp.any(picks, axis=0).reshape(-1)
    contract_rows = (((0,), (0,)), ((), ()))
    send_in = lax.dot_general(pick, inputs, contract_rows, preferred_element_type=jnp.float32)
    send_in = jnp.where(filled[:, None], send_in, EMPTY).astype(jnp.bfloat16)
    send_grad = lax.dot_general(pick, grad_output, contract_rows, preferred_element_type=jnp.float32)
    send_grad = (send_grad * slot_prob[:, None]).astype(jnp.bfloat16)
    got_in = exchange([send_in[k * MOST : (k + 1) * MOST] for k in range(experts)], "ex")
    got_grad = exchange([send_grad[k * MOST : (k + 1) * MOST] for k in range(experts)], "ex")
    got_in = jnp.concatenate(got_in, axis=0)
    got_grad = jnp.concatenate(got_grad, axis=0)

    row = jnp.arange(experts * MOST, dtype=jnp.int32)
    key = (me ^ (row // MOST)) * MOST + row % MOST
    full = got_in[:, :1] < EMPTY / 2
    earlier = (key[None, :] < key[:, None]).astype(jnp.bfloat16)
    slot = jnp.dot(earlier, full.astype(jnp.bfloat16), preferred_element_type=jnp.float32)
    place = (slot.astype(jnp.int32) == jnp.arange(capacity, dtype=jnp.int32)[None, :]) & full
    place = place.astype(jnp.bfloat16)
    rows_in = lax.dot_general(place, got_in, contract_rows, preferred_element_type=jnp.float32)
    rows_in = rows_in.astype(jnp.bfloat16)
    rows_grad = lax.dot_general(place, got_grad, contract_rows, preferred_element_type=jnp.float32)
    rows_grad = rows_grad.astype(jnp.bfloat16)

    gate_weight = gate_up[0, 0]
    up_weight = gate_up[0, 1]
    down_weight = down_proj[0]
    contract_width = (((1,), (1,)), ((), ()))

    def product(left, right):
        return lax.dot_general(left, right, contract_width, preferred_element_type=jnp.float32).astype(
            jnp.bfloat16
        )

    core = lax.axis_index("ey") & 1
    ways = lax.axis_size("ey")
    hidden = gate_weight.shape[0]
    half = hidden // 2

    def total(part):
        mine = lax.dynamic_slice_in_dim(part, core * half, half, 1)
        other = lax.dynamic_slice_in_dim(part, (1 - core) * half, half, 1)
        held = mine.astype(jnp.float32) + swap(other, "ey", 1).astype(jnp.float32)
        bit = 2
        while bit < ways:
            held = held + swap(held.astype(jnp.bfloat16), "ey", bit).astype(jnp.float32)
            bit *= 2
        return held

    gate_sum = total(product(rows_in, gate_weight))
    up_sum = total(product(rows_in, up_weight))
    grad_act = total(product(rows_grad, down_weight))
    sigmoid_gate = jax.nn.sigmoid(gate_sum)
    silu_gate = gate_sum * sigmoid_gate
    activation = (silu_gate * up_sum).astype(jnp.bfloat16)
    grad_gate = (
        grad_act * up_sum * sigmoid_gate * (1.0 + gate_sum * (1.0 - sigmoid_gate))
    ).astype(jnp.bfloat16)
    grad_up = (grad_act * silu_gate).astype(jnp.bfloat16)
    mine = jnp.stack([activation, grad_gate, grad_up])
    other = swap(mine, "ey", 1)
    low = jnp.where(core == 0, mine, other)
    high = jnp.where(core == 0, other, mine)
    whole = jnp.concatenate([low, high], axis=2)
    activation, grad_gate, grad_up = whole[0], whole[1], whole[2]

    grad_rows = jnp.dot(grad_gate, gate_weight, preferred_element_type=jnp.float32) + jnp.dot(
        grad_up, up_weight, preferred_element_type=jnp.float32
    )
    back = jnp.dot(place, grad_rows.astype(jnp.bfloat16), preferred_element_type=jnp.float32)
    back = back.astype(jnp.bfloat16)
    home = exchange([back[k * MOST : (k + 1) * MOST] for k in range(experts)], "ex")
    home = jnp.concatenate(home, axis=0)
    grad_inputs = jnp.dot(pick, home, preferred_element_type=jnp.float32).astype(jnp.bfloat16)

    def weight_grad(left, right):
        return lax.dot_general(left, right, contract_rows, preferred_element_type=jnp.float32).astype(
            jnp.bfloat16
        )

    down_grad = weight_grad(activation, rows_grad)
    pair_grad = jnp.stack([weight_grad(grad_gate, rows_in), weight_grad(grad_up, rows_in)])
    return (grad_inputs, pair_grad[None], down_grad[None])


def solution(mesh):
    return jax.shard_map(
        local,
        mesh=mesh,
        in_specs=(
            P(("groups", "ex"), "ey"),
            P(("groups", "ex"), "ey"),
            P(("groups", "ex"), None),
            P(("groups", "ex"), None),
            P("ex", None, None, "ey"),
            P("ex", None, "ey"),
        ),
        out_specs=(
            P(("groups", "ex"), "ey"),
            P("ex", "groups", None, "ey"),
            P("ex", "groups", "ey"),
        ),
        check_vma=False,
    )
```

```python
import jax
import jax.numpy as jnp
from jax import lax
from jax.sharding import PartitionSpec as P

MOST = 40
EXPERTS = 128
EMPTY = 64.0


def swap(value, axis, bit):
    count = lax.axis_size(axis)
    return lax.ppermute(value, axis, [(i, i ^ bit) for i in range(count)])


def exchange(value, axis):
    pieces = value.reshape(lax.axis_size(axis), MOST, value.shape[1])
    return lax.all_to_all(pieces, axis, 0, 0, tiled=True).reshape(value.shape)


def local(inputs, grad_output, routes, gate_probs, gate_up, down_proj):
    experts = lax.axis_size("ex")
    tokens, width = inputs.shape
    capacity = 5 * tokens * experts * routes.shape[1] // (4 * EXPERTS)
    order = jnp.arange(experts, dtype=jnp.int32)
    matches = routes[:, :, None] == order[None, None, :]
    routed = jnp.any(matches, axis=1)
    prob = jnp.sum(jnp.where(matches, gate_probs.astype(jnp.float32)[:, :, None], 0.0), axis=1)
    token = jnp.arange(tokens, dtype=jnp.int32)
    before = (token[:, None] > token[None, :]).astype(jnp.bfloat16)
    rank = jnp.dot(before, routed.astype(jnp.bfloat16), preferred_element_type=jnp.float32)
    rank = rank.astype(jnp.int32)
    picks = (rank[:, :, None] == jnp.arange(MOST, dtype=jnp.int32)) & routed[:, :, None]
    pick = picks.reshape(tokens, experts * MOST).astype(jnp.bfloat16)
    slot_prob = jnp.sum(jnp.where(picks, prob[:, :, None], 0.0), axis=0).reshape(-1)
    filled = jnp.any(picks, axis=0).reshape(-1)
    contract_rows = (((0,), (0,)), ((), ()))
    send_in = lax.dot_general(pick, inputs, contract_rows, preferred_element_type=jnp.float32)
    send_in = jnp.where(filled[:, None], send_in, EMPTY).astype(jnp.bfloat16)
    send_grad = lax.dot_general(pick, grad_output, contract_rows, preferred_element_type=jnp.float32)
    send_grad = (send_grad * slot_prob[:, None]).astype(jnp.bfloat16)
    got_in = exchange(send_in, "ex")
    got_grad = exchange(send_grad, "ex")

    row = jnp.arange(experts * MOST, dtype=jnp.int32)
    full = got_in[:, :1] < EMPTY / 2
    earlier = (row[None, :] < row[:, None]).astype(jnp.bfloat16)
    slot = jnp.dot(earlier, full.astype(jnp.bfloat16), preferred_element_type=jnp.float32)
    place = (slot.astype(jnp.int32) == jnp.arange(capacity, dtype=jnp.int32)[None, :]) & full
    place = place.astype(jnp.bfloat16)
    rows_in = lax.dot_general(place, got_in, contract_rows, preferred_element_type=jnp.float32)
    rows_in = rows_in.astype(jnp.bfloat16)
    rows_grad = lax.dot_general(place, got_grad, contract_rows, preferred_element_type=jnp.float32)
    rows_grad = rows_grad.astype(jnp.bfloat16)

    gate_weight = gate_up[0, 0]
    up_weight = gate_up[0, 1]
    down_weight = down_proj[0]
    contract_width = (((1,), (1,)), ((), ()))

    def product(left, right):
        return lax.dot_general(left, right, contract_width, preferred_element_type=jnp.float32).astype(
            jnp.bfloat16
        )

    core = lax.axis_index("ey") & 1
    ways = lax.axis_size("ey")
    hidden = gate_weight.shape[0]
    half = hidden // 2

    def total(part):
        mine = lax.dynamic_slice_in_dim(part, core * half, half, 1)
        other = lax.dynamic_slice_in_dim(part, (1 - core) * half, half, 1)
        held = mine.astype(jnp.float32) + swap(other, "ey", 1).astype(jnp.float32)
        bit = 2
        while bit < ways:
            held = held + swap(held.astype(jnp.bfloat16), "ey", bit).astype(jnp.float32)
            bit *= 2
        return held

    gate_sum = total(product(rows_in, gate_weight))
    up_sum = total(product(rows_in, up_weight))
    grad_act = total(product(rows_grad, down_weight))
    sigmoid_gate = jax.nn.sigmoid(gate_sum)
    silu_gate = gate_sum * sigmoid_gate
    activation = (silu_gate * up_sum).astype(jnp.bfloat16)
    grad_gate = (
        grad_act * up_sum * sigmoid_gate * (1.0 + gate_sum * (1.0 - sigmoid_gate))
    ).astype(jnp.bfloat16)
    grad_up = (grad_act * silu_gate).astype(jnp.bfloat16)
    mine = jnp.stack([activation, grad_gate, grad_up])
    other = swap(mine, "ey", 1)
    low = jnp.where(core == 0, mine, other)
    high = jnp.where(core == 0, other, mine)
    whole = jnp.concatenate([low, high], axis=2)
    activation, grad_gate, grad_up = whole[0], whole[1], whole[2]

    grad_rows = jnp.dot(grad_gate, gate_weight, preferred_element_type=jnp.float32) + jnp.dot(
        grad_up, up_weight, preferred_element_type=jnp.float32
    )
    back = jnp.dot(place, grad_rows.astype(jnp.bfloat16), preferred_element_type=jnp.float32)
    back = back.astype(jnp.bfloat16)
    home = exchange(back, "ex")
    grad_inputs = jnp.dot(pick, home, preferred_element_type=jnp.float32).astype(jnp.bfloat16)

    def weight_grad(left, right):
        return lax.dot_general(left, right, contract_rows, preferred_element_type=jnp.float32).astype(
            jnp.bfloat16
        )

    down_grad = weight_grad(activation, rows_grad)
    pair_grad = jnp.stack([weight_grad(grad_gate, rows_in), weight_grad(grad_up, rows_in)])
    return (grad_inputs, pair_grad[None], down_grad[None])


def solution(mesh):
    return jax.shard_map(
        local,
        mesh=mesh,
        in_specs=(
            P(("groups", "ex"), "ey"),
            P(("groups", "ex"), "ey"),
            P(("groups", "ex"), None),
            P(("groups", "ex"), None),
            P("ex", None, None, "ey"),
            P("ex", None, "ey"),
        ),
        out_specs=(
            P(("groups", "ex"), "ey"),
            P("ex", "groups", None, "ey"),
            P("ex", "groups", "ey"),
        ),
        check_vma=False,
    )
```

```python
import functools

import jax
import jax.numpy as jnp
from jax import lax
from jax.experimental import pallas as pl
from jax.experimental.pallas import tpu as pltpu
from jax.sharding import PartitionSpec as P

MOST = 40
EXPERTS = 128
EMPTY = 64.0
BF = jnp.bfloat16
F32 = jnp.float32
MIB = 1 << 20
VMEM = pl.BlockSpec(memory_space=pltpu.VMEM)
ANY = pl.BlockSpec(memory_space=pl.ANY)
ROWS = (((0,), (0,)), ((), ()))
LANES = (((1,), (1,)), ((), ()))
PLAIN = (((1,), (0,)), ((), ()))


def mm(left, right, dims=PLAIN):
    return lax.dot_general(left, right, dims, preferred_element_type=F32)


def iota(shape, dim):
    return lax.broadcasted_iota(jnp.int32, shape, dim)


def block_of(position, blocks):
    found = jnp.zeros_like(position)
    for k in range(1, blocks):
        found = found + (position >= k * MOST).astype(jnp.int32)
    return found


def call(body, outs, operands, specs, scratch=(), limit=16, flops=0, traffic=0, out_specs=None):
    return pl.pallas_call(
        body,
        out_shape=outs,
        in_specs=specs,
        out_specs=out_specs if out_specs is not None else jax.tree.map(lambda _: VMEM, outs),
        scratch_shapes=list(scratch),
        compiler_params=pltpu.CompilerParams(vmem_limit_bytes=limit * MIB),
        cost_estimate=pl.CostEstimate(flops=flops, bytes_accessed=traffic, transcendentals=0),
    )(*operands)


def pick_inputs(experts, routes, probs, inputs, pick_out, prob_out, *pieces):
    me = lax.axis_index("ex")
    tokens = inputs.shape[0]
    rows = experts * MOST
    owner = block_of(iota((rows, routes.shape[1]), 0), experts)
    named = jnp.zeros((rows, tokens), F32)
    weight = jnp.zeros((rows, tokens), F32)
    chosen = routes[...]
    wide = probs[...].astype(F32)
    for k in range(experts):
        spread = jnp.where(owner == k, 1.0, 0.0).astype(BF)
        hit = chosen == (me ^ k)
        named = named + mm(spread, jnp.where(hit, 1.0, 0.0).astype(BF), LANES)
        weight = weight + mm(spread, jnp.where(hit, wide, 0.0).astype(BF), LANES)
    earlier = iota((tokens, tokens), 0) < iota((tokens, tokens), 1)
    rank = mm(named.astype(BF), jnp.where(earlier, 1.0, 0.0).astype(BF)).astype(jnp.int32)
    row = iota((rows, tokens), 0)
    slot = row - block_of(row, experts) * MOST
    picks = (rank == slot) & (named > 0.5)
    pick = jnp.where(picks, 1.0, 0.0)
    prob_out[...] = jnp.sum(jnp.where(picks, weight, 0.0), axis=1, keepdims=True)
    filled = jnp.max(pick, axis=1, keepdims=True) > 0.5
    pick = pick.astype(BF)
    pick_out[...] = pick
    sent = jnp.where(filled, mm(pick, inputs[...]), EMPTY)
    for k in range(experts):
        pieces[k][...] = sent[k * MOST : (k + 1) * MOST].astype(BF)


def pick_grads(experts, pick, prob, grads, *pieces):
    sent = mm(pick[...], grads[...]) * prob[...]
    for k in range(experts):
        pieces[k][...] = sent[k * MOST : (k + 1) * MOST].astype(BF)


def stacked(pieces):
    return jnp.concatenate([piece[...].astype(F32) for piece in pieces], axis=0)


def copies(weight, index, held, sems, core, slots):
    half = held.shape[-2]
    out = []
    for slot, (matrix, own) in enumerate(slots):
        start = (core if own else 1 - core) * half
        source = weight.at[(0,) + ((matrix,) if index else ()) + (pl.ds(start, half),)]
        out.append(pltpu.make_async_copy(source, held.at[slot], sems.at[slot]))
    return out


def gate_up_parts(experts, capacity, *refs):
    pieces = refs[:experts]
    weight, place_out, rows_out, other, mine, held, sems = refs[experts:]
    core = lax.axis_index("ey") & 1
    me = lax.axis_index("ex")
    slots = [(0, False), (1, False), (0, True), (1, True)]
    loads = copies(weight, True, held, sems, core, slots)
    for load in loads:
        load.start()
    rows = experts * MOST
    got = stacked(pieces)
    full = got[:, :1] < EMPTY / 2
    key = []
    for dim in (0, 1):
        row = iota((rows, rows), dim)
        block = block_of(row, experts)
        key.append((me ^ block) * MOST + row - block * MOST)
    earlier = jnp.where(key[1] < key[0], 1.0, 0.0).astype(BF)
    wide = jnp.broadcast_to(full, (rows, capacity))
    slot = mm(earlier, jnp.where(wide, 1.0, 0.0).astype(BF)).astype(jnp.int32)
    place = jnp.where((slot == iota((rows, capacity), 1)) & wide, 1.0, 0.0).astype(BF)
    place_out[...] = place
    rows_in = mm(place, got.astype(BF), ROWS).astype(BF)
    rows_out[...] = rows_in
    for at, (matrix, own) in enumerate(slots):
        loads[at].wait()
        (mine if own else other)[matrix] = mm(rows_in, held[at], LANES).astype(BF)


def act_parts(experts, *refs):
    pieces = refs[:experts]
    place, weight, rows_out, other, mine, held, sems = refs[experts:]
    core = lax.axis_index("ey") & 1
    slots = [(0, False), (0, True)]
    loads = copies(weight, False, held, sems, core, slots)
    for load in loads:
        load.start()
    rows_grad = mm(place[...], stacked(pieces).astype(BF), ROWS).astype(BF)
    rows_out[...] = rows_grad
    for at, (_, own) in enumerate(slots):
        loads[at].wait()
        (mine if own else other)[...] = mm(rows_grad, held[at], LANES).astype(BF)


def middle(pair, pair_far, act, act_far, out):
    gate_sum = pair[0] + pair_far[0].astype(F32)
    up_sum = pair[1] + pair_far[1].astype(F32)
    grad_act = act[...] + act_far[...].astype(F32)
    sigmoid_gate = jax.nn.sigmoid(gate_sum)
    silu_gate = gate_sum * sigmoid_gate
    out[0] = (silu_gate * up_sum).astype(BF)
    out[1] = (grad_act * up_sum * sigmoid_gate * (1.0 + gate_sum * (1.0 - sigmoid_gate))).astype(BF)
    out[2] = (grad_act * silu_gate).astype(BF)


def own_rows(mine, weight, out, held, sems):
    core = lax.axis_index("ey") & 1
    loads = copies(weight, True, held, sems, core, [(0, True), (1, True)])
    for load in loads:
        load.start()
    loads[0].wait()
    total = mm(mine[1], held[0])
    loads[1].wait()
    out[...] = total + mm(mine[2], held[1])


def other_rows(experts, total_in, other, place, weight, *refs):
    pieces = refs[:experts]
    held, sems = refs[experts:]
    core = lax.axis_index("ey") & 1
    loads = copies(weight, True, held, sems, core, [(0, False), (1, False)])
    for load in loads:
        load.start()
    loads[0].wait()
    total = total_in[...] + mm(other[1], held[0])
    loads[1].wait()
    total = total + mm(other[2], held[1])
    back = mm(place[...], total.astype(BF))
    for k in range(experts):
        pieces[k][...] = back[k * MOST : (k + 1) * MOST].astype(BF)


def weight_grads(mine, other, rows_in, rows_grad, pair_out, down_out, held, sems):
    core = lax.axis_index("ey") & 1
    half = mine.shape[2]
    step = half // 2
    stores = []
    for matrix in range(3):
        right = rows_grad[...] if matrix == 0 else rows_in[...]
        for own in range(2):
            start = (core if own else 1 - core) * half
            for part in range(2):
                left = (mine if own else other)[matrix, :, part * step : (part + 1) * step]
                at = len(stores)
                held[at] = mm(left, right, ROWS).astype(BF)
                rows = pl.ds(start + part * step, step)
                target = down_out.at[0, rows] if matrix == 0 else pair_out.at[0, matrix - 1, rows]
                store = pltpu.make_async_copy(held.at[at], target, sems.at[at])
                store.start()
                stores.append(store)
    for store in stores:
        store.wait()


def combine(experts, pick, *refs):
    home = stacked(refs[:experts]).astype(BF)
    refs[experts][...] = mm(pick[...], home, ROWS).astype(BF)


def swap(value, axis, bit):
    count = lax.axis_size(axis)
    return lax.ppermute(value, axis, [(i, i ^ bit) for i in range(count)])


def exchange(pieces, axis):
    return [pieces[0]] + [swap(pieces[k], axis, k) for k in range(1, len(pieces))]


def local(inputs, grad_output, routes, gate_probs, gate_up, down_proj):
    experts = lax.axis_size("ex")
    ways = lax.axis_size("ey")
    tokens, width = inputs.shape
    hidden = gate_up.shape[2]
    half = hidden // 2
    capacity = 5 * tokens * experts * routes.shape[1] // (4 * EXPERTS)
    rows = experts * MOST
    weight_bytes = hidden * width * 2
    weight_flops = 2 * capacity * hidden * width
    sds = jax.ShapeDtypeStruct
    piece = [sds((MOST, width), BF)] * experts
    dma = lambda count: pltpu.SemaphoreType.DMA((count,))

    pick, prob, *send_in = call(
        functools.partial(pick_inputs, experts),
        [sds((rows, tokens), BF), sds((rows, 1), F32)] + piece,
        (routes, gate_probs, inputs),
        [VMEM] * 3,
        flops=2 * rows * tokens * width,
        traffic=4 * tokens * width,
    )
    got_in = exchange(send_in, "ex")
    send_grad = call(
        functools.partial(pick_grads, experts),
        piece,
        (pick, prob, grad_output),
        [VMEM] * 3,
        flops=2 * rows * tokens * width,
        traffic=4 * tokens * width,
    )
    got_grad = exchange(send_grad, "ex")

    place, rows_in, pair_other, pair_mine = call(
        functools.partial(gate_up_parts, experts, capacity),
        [
            sds((rows, capacity), BF),
            sds((capacity, width), BF),
            sds((2, capacity, half), BF),
            sds((2, capacity, half), BF),
        ],
        (*got_in, gate_up),
        [VMEM] * experts + [ANY],
        [pltpu.VMEM((4, half, width), BF), dma(4)],
        limit=20,
        flops=2 * weight_flops,
        traffic=2 * weight_bytes,
    )

    def total(mine, other):
        held = mine.astype(F32) + swap(other, "ey", 1).astype(F32)
        bit = 2
        while bit * 2 < ways:
            held = held + swap(held.astype(BF), "ey", bit).astype(F32)
            bit *= 2
        return held, swap(held.astype(BF), "ey", bit)

    pair, pair_far = total(pair_mine, pair_other)
    rows_grad, act_other, act_mine = call(
        functools.partial(act_parts, experts),
        [sds((capacity, width), BF), sds((capacity, half), BF), sds((capacity, half), BF)],
        (*got_grad, place, down_proj),
        [VMEM] * (experts + 1) + [ANY],
        [pltpu.VMEM((2, half, width), BF), dma(2)],
        flops=weight_flops,
        traffic=weight_bytes,
    )
    act, act_far = total(act_mine, act_other)
    mine = call(
        middle,
        sds((3, capacity, half), BF),
        (pair, pair_far, act, act_far),
        [VMEM] * 4,
        traffic=24 * capacity * half,
    )
    other = swap(mine, "ey", 1)
    own = call(
        own_rows,
        sds((capacity, width), F32),
        (mine, gate_up),
        [VMEM, ANY],
        [pltpu.VMEM((2, half, width), BF), dma(2)],
        flops=weight_flops,
        traffic=weight_bytes,
    )
    back = call(
        functools.partial(other_rows, experts),
        piece,
        (own, other, place, gate_up),
        [VMEM] * 3 + [ANY],
        [pltpu.VMEM((2, half, width), BF), dma(2)],
        flops=weight_flops,
        traffic=weight_bytes,
    )
    home = exchange(back, "ex")
    pair_grad, down_grad = call(
        weight_grads,
        [sds((1, 2, hidden, width), BF), sds((1, hidden, width), BF)],
        (mine, other, rows_in, rows_grad),
        [VMEM] * 4,
        [pltpu.VMEM((12, half // 2, width), BF), dma(12)],
        limit=24,
        flops=3 * weight_flops,
        traffic=3 * weight_bytes,
        out_specs=[ANY, ANY],
    )
    grad_inputs = call(
        functools.partial(combine, experts),
        sds((tokens, width), BF),
        (pick, *home),
        [VMEM] * (experts + 1),
        flops=2 * rows * tokens * width,
        traffic=4 * tokens * width,
    )
    return (grad_inputs, pair_grad, down_grad)


def solution(mesh):
    return jax.shard_map(
        local,
        mesh=mesh,
        in_specs=(
            P(("groups", "ex"), "ey"),
            P(("groups", "ex"), "ey"),
            P(("groups", "ex"), None),
            P(("groups", "ex"), None),
            P("ex", None, None, "ey"),
            P("ex", None, "ey"),
        ),
        out_specs=(
            P(("groups", "ex"), "ey"),
            P("ex", "groups", None, "ey"),
            P("ex", "groups", "ey"),
        ),
        check_vma=False,
    )
```

```python
import functools

import jax
import jax.numpy as jnp
from jax import lax
from jax.experimental import pallas as pl
from jax.experimental.pallas import tpu as pltpu
from jax.sharding import PartitionSpec as P

MOST = 40
EXPERTS = 128
EMPTY = 64.0
BF = jnp.bfloat16
F32 = jnp.float32
MIB = 1 << 20
GATE_COST = 18
C2COST = 100
VMEM = pl.BlockSpec(memory_space=pltpu.VMEM)
ANY = pl.BlockSpec(memory_space=pl.ANY)
HBM = pl.BlockSpec(memory_space=pltpu.HBM)
ROWS = (((0,), (0,)), ((), ()))
LANES = (((1,), (1,)), ((), ()))
PLAIN = (((1,), (0,)), ((), ()))


def mm(left, right, dims=PLAIN):
    return lax.dot_general(left, right, dims, preferred_element_type=F32)


def iota(shape, dim):
    return lax.broadcasted_iota(jnp.int32, shape, dim)


def block_of(position, blocks):
    found = jnp.zeros_like(position)
    for k in range(1, blocks):
        found = found + (position >= k * MOST).astype(jnp.int32)
    return found


def call(body, outs, operands, specs, scratch=(), limit=16, flops=0, traffic=0, out_specs=None):
    return pl.pallas_call(
        body,
        out_shape=outs,
        in_specs=specs,
        out_specs=out_specs if out_specs is not None else jax.tree.map(lambda _: VMEM, outs),
        scratch_shapes=list(scratch),
        compiler_params=pltpu.CompilerParams(vmem_limit_bytes=limit * MIB),
        cost_estimate=pl.CostEstimate(flops=flops, bytes_accessed=traffic, transcendentals=0),
    )(*operands)


def pick_rows(experts, routes_in, probs_in, inputs, grads, pick_out, *refs):
    *pieces, routes, probs, held, sems = refs
    loads = [
        pltpu.make_async_copy(source, target, sems.at[at])
        for at, (source, target) in enumerate(
            [(routes_in, routes), (probs_in, probs), (inputs, held.at[0]), (grads, held.at[1])]
        )
    ]
    for load in loads:
        load.start()
    me = lax.axis_index("ex")
    tokens = inputs.shape[0]
    rows = experts * MOST
    owner = block_of(iota((rows, routes.shape[0]), 0), experts)
    named = jnp.zeros((rows, tokens), F32)
    weight = jnp.zeros((rows, tokens), F32)
    loads[0].wait()
    loads[1].wait()
    chosen = routes[...]
    wide = probs[...].astype(F32)
    for k in range(experts):
        spread = jnp.where(owner == k, 1.0, 0.0).astype(BF)
        hit = chosen == (me ^ k)
        named = named + mm(spread, jnp.where(hit, 1.0, 0.0).astype(BF))
        weight = weight + mm(spread, jnp.where(hit, wide, 0.0).astype(BF))
    earlier = iota((tokens, tokens), 0) < iota((tokens, tokens), 1)
    rank = mm(named.astype(BF), jnp.where(earlier, 1.0, 0.0).astype(BF)).astype(jnp.int32)
    row = iota((rows, tokens), 0)
    slot = row - block_of(row, experts) * MOST
    picks = (rank == slot) & (named > 0.5)
    pick = jnp.where(picks, 1.0, 0.0)
    prob = jnp.sum(jnp.where(picks, weight, 0.0), axis=1, keepdims=True)
    filled = jnp.max(pick, axis=1, keepdims=True) > 0.5
    pick = pick.astype(BF)
    pick_out[...] = pick
    loads[2].wait()
    sent = jnp.where(filled, mm(pick, held[0]), EMPTY)
    for k in range(experts):
        pieces[k][...] = sent[k * MOST : (k + 1) * MOST].astype(BF)
    loads[3].wait()
    sent = mm(pick, held[1]) * prob
    for k in range(experts):
        pieces[experts + k][...] = sent[k * MOST : (k + 1) * MOST].astype(BF)


def stacked(pieces):
    return jnp.concatenate([piece[...].astype(F32) for piece in pieces], axis=0)


def rows_of(half, own):
    core = lax.axis_index("ey") & 1
    return pl.ds(pl.multiple_of((core if own else 1 - core) * half, 128), half)


def place_rows(experts, capacity, pieces):
    me = lax.axis_index("ex")
    rows = experts * MOST
    got = stacked(pieces)
    full = got[:, :1] < EMPTY / 2
    key = []
    for dim in (0, 1):
        row = iota((rows, rows), dim)
        block = block_of(row, experts)
        key.append((me ^ block) * MOST + row - block * MOST)
    earlier = jnp.where(key[1] < key[0], 1.0, 0.0).astype(BF)
    wide = jnp.broadcast_to(full, (rows, capacity))
    slot = mm(earlier, jnp.where(wide, 1.0, 0.0).astype(BF)).astype(jnp.int32)
    place = jnp.where((slot == iota((rows, capacity), 1)) & wide, 1.0, 0.0).astype(BF)
    return place, mm(place, got.astype(BF), ROWS).astype(BF)


def gate_up_parts(experts, capacity, own, *refs):
    pieces = refs[:experts]
    weight, held, out, *extra, sems = refs[experts:]
    half = weight.shape[2] // 2
    loads = []
    for matrix in range(2):
        source = weight.at[0, matrix, rows_of(half, own)]
        loads.append(pltpu.make_async_copy(source, held.at[matrix], sems.at[matrix]))
        loads[matrix].start()
    place, rows_in = place_rows(experts, capacity, pieces)
    if extra:
        extra[0][...] = place
        extra[1][...] = rows_in
    for matrix in range(2):
        loads[matrix].wait()
        out[matrix] = mm(rows_in, held[matrix], LANES).astype(BF)


def act_parts(experts, *refs):
    pieces = refs[:experts]
    place, weight, _, rows_out, other, mine, held, sems = refs[experts:]
    half = weight.shape[1] // 2
    loads = []
    for own in range(2):
        source = weight.at[0, rows_of(half, own == 1)]
        loads.append(pltpu.make_async_copy(source, held.at[own], sems.at[own]))
        loads[own].start()
    rows_grad = mm(place[...], stacked(pieces).astype(BF), ROWS).astype(BF)
    rows_out[...] = rows_grad
    for own, out in enumerate((other, mine)):
        loads[own].wait()
        out[...] = mm(rows_grad, held[own], LANES).astype(BF)


def gates(pair, pair_far, act_out, by_gate, by_up):
    gate_sum = pair[0] + pair_far[0].astype(F32)
    up_sum = pair[1] + pair_far[1].astype(F32)
    sigmoid_gate = jax.nn.sigmoid(gate_sum)
    silu_gate = gate_sum * sigmoid_gate
    act_out[...] = (silu_gate * up_sum).astype(BF)
    by_gate[...] = up_sum * sigmoid_gate * (1.0 + gate_sum * (1.0 - sigmoid_gate))
    by_up[...] = silu_gate


def grads_of(act, act_far, by_gate, by_up, out):
    grad_act = act[...] + act_far[...].astype(F32)
    out[0] = (grad_act * by_gate[...]).astype(BF)
    out[1] = (grad_act * by_up[...]).astype(BF)


def own_rows(mine, held, out):
    out[...] = mm(mine[0], held[0]) + mm(mine[1], held[1])


def other_rows(experts, total, other, place, held, *pieces):
    rows = total[...] + mm(other[0], held[0]) + mm(other[1], held[1])
    back = mm(place[...], rows.astype(BF))
    for k in range(experts):
        pieces[k][...] = back[k * MOST : (k + 1) * MOST].astype(BF)


def weight_grads(mine_act, other_act, mine, other, rows_in, rows_grad, pair_out, down_out, held, sems):
    core = lax.axis_index("ey") & 1
    half = mine_act.shape[1]
    step = half // 2
    stores = []
    for matrix in range(3):
        right = rows_grad[...] if matrix == 0 else rows_in[...]
        for own in range(2):
            start = (core if own else 1 - core) * half
            for part in range(2):
                columns = slice(part * step, (part + 1) * step)
                if matrix == 0:
                    left = (mine_act if own else other_act)[:, columns]
                else:
                    left = (mine if own else other)[matrix - 1, :, columns]
                at = len(stores)
                held[at] = mm(left, right, ROWS).astype(BF)
                rows = pl.ds(start + part * step, step)
                target = down_out.at[0, rows] if matrix == 0 else pair_out.at[0, matrix - 1, rows]
                store = pltpu.make_async_copy(held.at[at], target, sems.at[at])
                store.start()
                stores.append(store)
    for store in stores:
        store.wait()


def combine(experts, pick, *refs):
    home = stacked(refs[:experts]).astype(BF)
    refs[experts][...] = mm(pick[...], home, ROWS).astype(BF)


def far(value):
    return pltpu.with_memory_space_constraint(value, pltpu.HBM)


def swap(value, axis, bit):
    count = lax.axis_size(axis)
    return lax.ppermute(value, axis, [(i, i ^ bit) for i in range(count)])


def exchange(pieces, axis):
    got = list(pieces)
    for k in list(range(2, len(pieces))) + [1]:
        got[k] = swap(pieces[k], axis, k)
    return got


def local(inputs, grad_output, routes, gate_probs, gate_up, down_proj):
    experts = lax.axis_size("ex")
    ways = lax.axis_size("ey")
    tokens, width = inputs.shape
    hidden = gate_up.shape[2]
    half = hidden // 2
    capacity = 5 * tokens * experts * routes.shape[1] // (4 * EXPERTS)
    rows = experts * MOST
    weight_bytes = hidden * width * 2
    weight_flops = 2 * capacity * hidden * width
    sds = jax.ShapeDtypeStruct
    piece = [sds((MOST, width), BF)] * experts
    dma = lambda count: pltpu.SemaphoreType.DMA((count,))

    pick, *sent = call(
        functools.partial(pick_rows, experts),
        [sds((rows, tokens), BF)] + piece * 2,
        (far(routes.T), far(gate_probs.T), far(inputs), far(grad_output)),
        [HBM] * 4,
        [
            pltpu.VMEM(routes.shape[::-1], jnp.int32),
            pltpu.VMEM(routes.shape[::-1], BF),
            pltpu.VMEM((2, tokens, width), BF),
            dma(4),
        ],
        flops=4 * rows * tokens * width,
        traffic=4 * tokens * width,
    )
    got_in = exchange(sent[:experts], "ex")
    got_grad = exchange(sent[experts:], "ex")
    def pair_part(own, extra, cost):
        return call(
            functools.partial(gate_up_parts, experts, capacity, own),
            [pltpu.VMEM((2, half, width), BF), sds((2, capacity, half), BF)] + extra,
            (*got_in, far(gate_up)),
            [VMEM] * experts + [HBM],
            [dma(2)],
            flops=cost * weight_flops,
            traffic=cost * weight_bytes,
        )

    held_other, pair_other = pair_part(False, [], 1)
    held_mine, pair_mine, place, rows_in = pair_part(
        True, [sds((rows, capacity), BF), sds((capacity, width), BF)], C2COST
    )
    def total(mine, other):
        held = mine.astype(F32) + other.astype(F32)
        bit = 2
        while bit * 2 < ways:
            held = held + swap(held.astype(BF), "ey", bit).astype(F32)
            bit *= 2
        sent = held.astype(BF)
        return held, sent, swap(sent, "ey", bit)

    pair, pair_sent, pair_far = total(pair_mine, swap(pair_other, "ey", 1))
    rows_grad, act_other, act_mine = call(
        functools.partial(act_parts, experts),
        [sds((capacity, width), BF), sds((capacity, half), BF), sds((capacity, half), BF)],
        (*got_grad, place, far(down_proj), pair_sent),
        [VMEM] * (experts + 1) + [HBM, ANY],
        [pltpu.VMEM((2, half, width), BF), dma(2)],
        flops=weight_flops,
        traffic=weight_bytes,
    )
    act, _, act_far = total(act_mine, swap(act_other, "ey", 1))
    mine_act, by_gate, by_up = call(
        gates,
        [sds((capacity, half), BF)] + [sds((capacity, half), F32)] * 2,
        (pair, pair_far),
        [VMEM] * 2,
        traffic=GATE_COST * capacity * half,
    )
    other_act = swap(mine_act, "ey", 1)
    mine = call(
        grads_of,
        sds((2, capacity, half), BF),
        (act, act_far, by_gate, by_up),
        [VMEM] * 4,
        traffic=18 * capacity * half,
    )
    other = swap(mine, "ey", 1)
    own = call(
        own_rows,
        sds((capacity, width), F32),
        (mine, held_mine),
        [VMEM] * 2,
        flops=weight_flops,
        traffic=weight_bytes,
    )
    back = call(
        functools.partial(other_rows, experts),
        piece,
        (own, other, place, held_other),
        [VMEM] * 4,
        flops=weight_flops,
        traffic=weight_bytes,
    )
    home = exchange(back, "ex")
    pair_grad, down_grad = call(
        weight_grads,
        [sds((1, 2, hidden, width), BF), sds((1, hidden, width), BF)],
        (mine_act, other_act, mine, other, rows_in, rows_grad),
        [VMEM] * 6,
        [pltpu.VMEM((12, half // 2, width), BF), dma(12)],
        limit=24,
        flops=3 * weight_flops,
        traffic=3 * weight_bytes,
        out_specs=[ANY, ANY],
    )
    grad_inputs = call(
        functools.partial(combine, experts),
        sds((tokens, width), BF),
        (pick, *home),
        [VMEM] * (experts + 1),
        flops=2 * rows * tokens * width,
        traffic=4 * tokens * width,
    )
    return (grad_inputs, pair_grad, down_grad)


def solution(mesh):
    return jax.shard_map(
        local,
        mesh=mesh,
        in_specs=(
            P(("groups", "ex"), "ey"),
            P(("groups", "ex"), "ey"),
            P(("groups", "ex"), None),
            P(("groups", "ex"), None),
            P("ex", None, None, "ey"),
            P("ex", None, "ey"),
        ),
        out_specs=(
            P(("groups", "ex"), "ey"),
            P("ex", "groups", None, "ey"),
            P("ex", "groups", "ey"),
        ),
        check_vma=False,
    )
```

```python
import functools

import jax
import jax.numpy as jnp
from jax import lax
from jax.experimental import pallas as pl
from jax.experimental.pallas import tpu as pltpu
from jax.sharding import PartitionSpec as P

MOST = 40
EXPERTS = 128
EMPTY = 64.0
BF = jnp.bfloat16
F32 = jnp.float32
MIB = 1 << 20
GATE_COST = 18
C2COST = 100
D0COST = 100
WCOST = 3
VMEM = pl.BlockSpec(memory_space=pltpu.VMEM)
ANY = pl.BlockSpec(memory_space=pl.ANY)
HBM = pl.BlockSpec(memory_space=pltpu.HBM)
ROWS = (((0,), (0,)), ((), ()))
LANES = (((1,), (1,)), ((), ()))
PLAIN = (((1,), (0,)), ((), ()))


def mm(left, right, dims=PLAIN):
    return lax.dot_general(left, right, dims, preferred_element_type=F32)


def iota(shape, dim):
    return lax.broadcasted_iota(jnp.int32, shape, dim)


def far_first(count):
    return sorted(range(count), key=lambda k: (-k.bit_length(), k))


def block_of(position, names):
    found = jnp.full_like(position, names[0])
    for at in range(1, len(names)):
        found = found + (position >= at * MOST).astype(jnp.int32) * (names[at] - names[at - 1])
    return found


def call(body, outs, operands, specs, scratch=(), limit=16, flops=0, traffic=0, out_specs=None):
    return pl.pallas_call(
        body,
        out_shape=outs,
        in_specs=specs,
        out_specs=out_specs if out_specs is not None else jax.tree.map(lambda _: VMEM, outs),
        scratch_shapes=list(scratch),
        compiler_params=pltpu.CompilerParams(vmem_limit_bytes=limit * MIB),
        cost_estimate=pl.CostEstimate(flops=flops, bytes_accessed=traffic, transcendentals=0),
    )(*operands)


def pick_rows(experts, routes_in, probs_in, inputs, grads, pick_out, *refs):
    *pieces, routes, probs, held, sems = refs
    loads = [
        pltpu.make_async_copy(source, target, sems.at[at])
        for at, (source, target) in enumerate(
            [(routes_in, routes), (probs_in, probs), (inputs, held.at[0]), (grads, held.at[1])]
        )
    ]
    for load in loads:
        load.start()
    me = lax.axis_index("ex")
    tokens = inputs.shape[0]
    rows = experts * MOST
    order = far_first(experts)
    owner = block_of(iota((rows, routes.shape[0]), 0), order)
    named = jnp.zeros((rows, tokens), F32)
    weight = jnp.zeros((rows, tokens), F32)
    loads[0].wait()
    loads[1].wait()
    chosen = routes[...]
    wide = probs[...].astype(F32)
    for k in range(experts):
        spread = jnp.where(owner == k, 1.0, 0.0).astype(BF)
        hit = chosen == (me ^ k)
        named = named + mm(spread, jnp.where(hit, 1.0, 0.0).astype(BF))
        weight = weight + mm(spread, jnp.where(hit, wide, 0.0).astype(BF))
    earlier = iota((tokens, tokens), 0) < iota((tokens, tokens), 1)
    rank = mm(named.astype(BF), jnp.where(earlier, 1.0, 0.0).astype(BF)).astype(jnp.int32)
    row = iota((rows, tokens), 0)
    slot = row - block_of(row, range(experts)) * MOST
    picks = (rank == slot) & (named > 0.5)
    pick = jnp.where(picks, 1.0, 0.0)
    prob = jnp.sum(jnp.where(picks, weight, 0.0), axis=1, keepdims=True)
    filled = jnp.max(pick, axis=1, keepdims=True) > 0.5
    pick = pick.astype(BF)
    pick_out[...] = pick
    loads[2].wait()
    sent = jnp.where(filled, mm(pick, held[0]), EMPTY)
    for k in range(experts):
        pieces[k][...] = sent[k * MOST : (k + 1) * MOST].astype(BF)
    loads[3].wait()
    sent = mm(pick, held[1]) * prob
    for k in range(experts):
        pieces[experts + k][...] = sent[k * MOST : (k + 1) * MOST].astype(BF)


def stacked(pieces):
    return jnp.concatenate([piece[...].astype(F32) for piece in pieces], axis=0)


def rows_of(half, own):
    core = lax.axis_index("ey") & 1
    return pl.ds(pl.multiple_of((core if own else 1 - core) * half, 128), half)


def place_rows(experts, capacity, pieces):
    me = lax.axis_index("ex")
    rows = experts * MOST
    got = stacked(pieces)
    full = got[:, :1] < EMPTY / 2
    key = []
    for dim in (0, 1):
        row = iota((rows, rows), dim)
        local_row = row - block_of(row, range(experts)) * MOST
        key.append((me ^ block_of(row, far_first(experts))) * MOST + local_row)
    earlier = jnp.where(key[1] < key[0], 1.0, 0.0).astype(BF)
    wide = jnp.broadcast_to(full, (rows, capacity))
    slot = mm(earlier, jnp.where(wide, 1.0, 0.0).astype(BF)).astype(jnp.int32)
    place = jnp.where((slot == iota((rows, capacity), 1)) & wide, 1.0, 0.0).astype(BF)
    return place, mm(place, got.astype(BF), ROWS).astype(BF)


def stage(gate_up, down, _, *refs):
    (*held, sems) = refs
    half = down.shape[1] // 2
    loads = []
    for own, out in enumerate(held):
        rows = rows_of(half, own == 1)
        for matrix in range(3):
            source = down.at[0, rows] if matrix == 2 else gate_up.at[0, matrix, rows]
            loads.append(pltpu.make_async_copy(source, out.at[matrix], sems.at[len(loads)]))
            loads[-1].start()
    for load in loads:
        load.wait()


def gate_up_parts(experts, capacity, *refs):
    pieces = refs[:experts]
    held, out, *extra = refs[experts:]
    place, rows_in = place_rows(experts, capacity, pieces)
    if extra:
        extra[0][...] = place
        extra[1][...] = rows_in
    for matrix in range(2):
        out[matrix] = mm(rows_in, held[matrix], LANES).astype(BF)


def place_grads(experts, *refs):
    place, rows_out = refs[experts:]
    rows_out[...] = mm(place[...], stacked(refs[:experts]).astype(BF), ROWS).astype(BF)


def act_parts(rows_grad, held_other, held_mine, _, other, mine):
    other[...] = mm(rows_grad[...], held_other[2], LANES).astype(BF)
    mine[...] = mm(rows_grad[...], held_mine[2], LANES).astype(BF)


def gates(gate, gate_far, up, up_far, act_out, by_gate, by_up):
    gate_sum = gate[...] + gate_far[...].astype(F32)
    up_sum = up[...] + up_far[...].astype(F32)
    sigmoid_gate = jax.nn.sigmoid(gate_sum)
    silu_gate = gate_sum * sigmoid_gate
    act_out[...] = (silu_gate * up_sum).astype(BF)
    by_gate[...] = up_sum * sigmoid_gate * (1.0 + gate_sum * (1.0 - sigmoid_gate))
    by_up[...] = silu_gate


def grads_of(act, act_far, by_gate, by_up, out):
    grad_act = act[...] + act_far[...].astype(F32)
    out[0] = (grad_act * by_gate[...]).astype(BF)
    out[1] = (grad_act * by_up[...]).astype(BF)


def own_rows(mine, held, out):
    out[...] = mm(mine[0], held[0]) + mm(mine[1], held[1])


def other_rows(experts, total, other, place, held, *pieces):
    rows = total[...] + mm(other[0], held[0]) + mm(other[1], held[1])
    back = mm(place[...], rows.astype(BF))
    for k in range(experts):
        pieces[k][...] = back[k * MOST : (k + 1) * MOST].astype(BF)


def weight_grads(mine_act, other_act, mine, other, rows_in, rows_grad, pair_out, down_out, held, sems):
    core = lax.axis_index("ey") & 1
    half = mine_act.shape[1]
    step = half // 2
    stores = []
    for matrix in range(3):
        right = rows_grad[...] if matrix == 0 else rows_in[...]
        for own in range(2):
            start = (core if own else 1 - core) * half
            for part in range(2):
                columns = slice(part * step, (part + 1) * step)
                if matrix == 0:
                    left = (mine_act if own else other_act)[:, columns]
                else:
                    left = (mine if own else other)[matrix - 1, :, columns]
                at = len(stores)
                held[at] = mm(left, right, ROWS).astype(BF)
                rows = pl.ds(start + part * step, step)
                target = down_out.at[0, rows] if matrix == 0 else pair_out.at[0, matrix - 1, rows]
                store = pltpu.make_async_copy(held.at[at], target, sems.at[at])
                store.start()
                stores.append(store)
    for store in stores:
        store.wait()


def combine(experts, pick, *refs):
    home = stacked(refs[:experts]).astype(BF)
    refs[experts][...] = mm(pick[...], home, ROWS).astype(BF)


def far(value):
    return pltpu.with_memory_space_constraint(value, pltpu.HBM)


def swap(value, axis, bit):
    count = lax.axis_size(axis)
    return lax.ppermute(value, axis, [(i, i ^ bit) for i in range(count)])


def exchange(pieces, axis):
    order = far_first(len(pieces))
    return [swap(piece, axis, k) if k else piece for piece, k in zip(pieces, order)]


def local(inputs, grad_output, routes, gate_probs, gate_up, down_proj):
    experts = lax.axis_size("ex")
    ways = lax.axis_size("ey")
    tokens, width = inputs.shape
    hidden = gate_up.shape[2]
    half = hidden // 2
    capacity = 5 * tokens * experts * routes.shape[1] // (4 * EXPERTS)
    rows = experts * MOST
    weight_bytes = hidden * width * 2
    weight_flops = 2 * capacity * hidden * width
    sds = jax.ShapeDtypeStruct
    piece = [sds((MOST, width), BF)] * experts
    dma = lambda count: pltpu.SemaphoreType.DMA((count,))

    pick, *sent = call(
        functools.partial(pick_rows, experts),
        [sds((rows, tokens), BF)] + piece * 2,
        (far(routes.T), far(gate_probs.T), far(inputs), far(grad_output)),
        [HBM] * 4,
        [
            pltpu.VMEM(routes.shape[::-1], jnp.int32),
            pltpu.VMEM(routes.shape[::-1], BF),
            pltpu.VMEM((2, tokens, width), BF),
            dma(4),
        ],
        flops=4 * rows * tokens * width,
        traffic=4 * tokens * width,
    )
    got_in = exchange(sent[:experts], "ex")
    got_grad = exchange(sent[experts:], "ex")
    held_other, held_mine = call(
        stage,
        [pltpu.VMEM((3, half, width), BF)] * 2,
        (far(gate_up), far(down_proj), pick),
        [HBM, HBM, ANY],
        [dma(6)],
        flops=WCOST * weight_flops,
        traffic=WCOST * weight_bytes,
    )

    def pair_part(held, extra, cost):
        return call(
            functools.partial(gate_up_parts, experts, capacity),
            [sds((2, capacity, half), BF)] + extra,
            (*got_in, held),
            [VMEM] * (experts + 1),
            flops=cost * weight_flops,
            traffic=cost * weight_bytes,
        )

    (pair_other,) = pair_part(held_other, [], 1)
    pair_mine, place, rows_in = pair_part(
        held_mine, [sds((rows, capacity), BF), sds((capacity, width), BF)], C2COST
    )
    def total(held):
        bit = 2
        while bit * 2 < ways:
            held = held + swap(held.astype(BF), "ey", bit).astype(F32)
            bit *= 2
        return held, swap(held.astype(BF), "ey", bit)

    pair = pair_mine.astype(F32) + swap(pair_other, "ey", 1).astype(F32)
    gate, gate_far = total(pair[0])
    up, up_far = total(pair[1])
    rows_grad = call(
        functools.partial(place_grads, experts),
        sds((capacity, width), BF),
        (*got_grad, place),
        [VMEM] * (experts + 1),
        flops=D0COST * weight_flops,
        traffic=D0COST * weight_bytes,
    )
    act_other, act_mine = call(
        act_parts,
        [sds((capacity, half), BF)] * 2,
        (rows_grad, held_other, held_mine, gate_far),
        [VMEM] * 3 + [ANY],
        flops=weight_flops,
        traffic=weight_bytes,
    )
    act, act_far = total(act_mine.astype(F32) + swap(act_other, "ey", 1).astype(F32))
    mine_act, by_gate, by_up = call(
        gates,
        [sds((capacity, half), BF)] + [sds((capacity, half), F32)] * 2,
        (gate, gate_far, up, up_far),
        [VMEM] * 4,
        traffic=GATE_COST * capacity * half,
    )
    other_act = swap(mine_act, "ey", 1)
    mine = call(
        grads_of,
        sds((2, capacity, half), BF),
        (act, act_far, by_gate, by_up),
        [VMEM] * 4,
        traffic=18 * capacity * half,
    )
    other = swap(mine, "ey", 1)
    own = call(
        own_rows,
        sds((capacity, width), F32),
        (mine, held_mine),
        [VMEM] * 2,
        flops=weight_flops,
        traffic=weight_bytes,
    )
    back = call(
        functools.partial(other_rows, experts),
        piece,
        (own, other, place, held_other),
        [VMEM] * 4,
        flops=weight_flops,
        traffic=weight_bytes,
    )
    home = exchange(back, "ex")
    pair_grad, down_grad = call(
        weight_grads,
        [sds((1, 2, hidden, width), BF), sds((1, hidden, width), BF)],
        (mine_act, other_act, mine, other, rows_in, rows_grad),
        [VMEM] * 6,
        [pltpu.VMEM((12, half // 2, width), BF), dma(12)],
        limit=24,
        flops=3 * weight_flops,
        traffic=3 * weight_bytes,
        out_specs=[ANY, ANY],
    )
    grad_inputs = call(
        functools.partial(combine, experts),
        sds((tokens, width), BF),
        (pick, *home),
        [VMEM] * (experts + 1),
        flops=2 * rows * tokens * width,
        traffic=4 * tokens * width,
    )
    return (grad_inputs, pair_grad, down_grad)


def solution(mesh):
    return jax.shard_map(
        local,
        mesh=mesh,
        in_specs=(
            P(("groups", "ex"), "ey"),
            P(("groups", "ex"), "ey"),
            P(("groups", "ex"), None),
            P(("groups", "ex"), None),
            P("ex", None, None, "ey"),
            P("ex", None, "ey"),
        ),
        out_specs=(
            P(("groups", "ex"), "ey"),
            P("ex", "groups", None, "ey"),
            P("ex", "groups", "ey"),
        ),
        check_vma=False,
    )
```

```python
import functools

import jax
import jax.numpy as jnp
from jax import lax
from jax.experimental import pallas as pl
from jax.experimental.pallas import tpu as pltpu
from jax.sharding import PartitionSpec as P

MOST = 40
EXPERTS = 128
EMPTY = 64.0
BF = jnp.bfloat16
F32 = jnp.float32
MIB = 1 << 20
C2COST = 100
WCOST = 3
GFLOP = 100
D1COST = 1
D2COST = 100
VMEM = pl.BlockSpec(memory_space=pltpu.VMEM)
ANY = pl.BlockSpec(memory_space=pl.ANY)
HBM = pl.BlockSpec(memory_space=pltpu.HBM)
ROWS = (((0,), (0,)), ((), ()))
LANES = (((1,), (1,)), ((), ()))
PLAIN = (((1,), (0,)), ((), ()))


def mm(left, right, dims=PLAIN):
    return lax.dot_general(left, right, dims, preferred_element_type=F32)


def iota(shape, dim):
    return lax.broadcasted_iota(jnp.int32, shape, dim)


def far_first(count):
    return sorted(range(count), key=lambda k: (-k.bit_length(), k))


def block_of(position, names):
    found = jnp.full_like(position, names[0])
    for at in range(1, len(names)):
        found = found + (position >= at * MOST).astype(jnp.int32) * (names[at] - names[at - 1])
    return found


def call(body, outs, operands, specs, scratch=(), limit=16, flops=0, traffic=0, out_specs=None):
    return pl.pallas_call(
        body,
        out_shape=outs,
        in_specs=specs,
        out_specs=out_specs if out_specs is not None else jax.tree.map(lambda _: VMEM, outs),
        scratch_shapes=list(scratch),
        compiler_params=pltpu.CompilerParams(vmem_limit_bytes=limit * MIB),
        cost_estimate=pl.CostEstimate(flops=flops, bytes_accessed=traffic, transcendentals=0),
    )(*operands)


def pick_inputs(experts, routes_in, probs_in, inputs, pick_out, prob_out, *refs):
    *pieces, routes, probs, held, sems = refs
    loads = [
        pltpu.make_async_copy(source, target, sems.at[at])
        for at, (source, target) in enumerate(
            [(routes_in, routes), (probs_in, probs), (inputs, held)]
        )
    ]
    for load in loads:
        load.start()
    me = lax.axis_index("ex")
    tokens = inputs.shape[0]
    rows = experts * MOST
    order = far_first(experts)
    owner = block_of(iota((rows, routes.shape[0]), 0), order)
    named = jnp.zeros((rows, tokens), F32)
    weight = jnp.zeros((rows, tokens), F32)
    earlier = iota((tokens, tokens), 0) < iota((tokens, tokens), 1)
    earlier = jnp.where(earlier, 1.0, 0.0).astype(BF)
    row = iota((rows, tokens), 0)
    slot = row - block_of(row, range(experts)) * MOST
    loads[0].wait()
    loads[1].wait()
    chosen = routes[...]
    wide = probs[...].astype(F32)
    for k in range(experts):
        spread = jnp.where(owner == k, 1.0, 0.0).astype(BF)
        hit = chosen == (me ^ k)
        named = named + mm(spread, jnp.where(hit, 1.0, 0.0).astype(BF))
        weight = weight + mm(spread, jnp.where(hit, wide, 0.0).astype(BF))
    rank = mm(named.astype(BF), earlier).astype(jnp.int32)
    picks = (rank == slot) & (named > 0.5)
    pick = jnp.where(picks, 1.0, 0.0)
    filled = jnp.max(pick, axis=1, keepdims=True) > 0.5
    pick = pick.astype(BF)
    pick_out[...] = pick
    prob_out[...] = jnp.sum(jnp.where(picks, weight, 0.0), axis=1, keepdims=True)
    loads[2].wait()
    sent = jnp.where(filled, mm(pick, held[...]), EMPTY)
    for k in range(experts):
        pieces[k][...] = sent[k * MOST : (k + 1) * MOST].astype(BF)


def pick_grads(experts, pick, prob, grads, _, *pieces):
    sent = mm(pick[...], grads[...]) * prob[...]
    for k in range(experts):
        pieces[k][...] = sent[k * MOST : (k + 1) * MOST].astype(BF)


def stacked(pieces):
    return jnp.concatenate([piece[...].astype(F32) for piece in pieces], axis=0)


def rows_of(half, own):
    core = lax.axis_index("ey") & 1
    return pl.ds(pl.multiple_of((core if own else 1 - core) * half, 128), half)


def place_rows(experts, capacity, pieces):
    me = lax.axis_index("ex")
    rows = experts * MOST
    got = stacked(pieces)
    full = got[:, :1] < EMPTY / 2
    key = []
    for dim in (0, 1):
        row = iota((rows, rows), dim)
        local_row = row - block_of(row, range(experts)) * MOST
        key.append((me ^ block_of(row, far_first(experts))) * MOST + local_row)
    earlier = jnp.where(key[1] < key[0], 1.0, 0.0).astype(BF)
    wide = jnp.broadcast_to(full, (rows, capacity))
    slot = mm(earlier, jnp.where(wide, 1.0, 0.0).astype(BF)).astype(jnp.int32)
    place = jnp.where((slot == iota((rows, capacity), 1)) & wide, 1.0, 0.0).astype(BF)
    return place, mm(place, got.astype(BF), ROWS).astype(BF)


def stage(gate_up, down, grads, _, *refs):
    *held, grads_out, sems = refs
    half = down.shape[1] // 2
    loads = []
    for own, out in enumerate(held):
        rows = rows_of(half, own == 1)
        for matrix in range(3):
            source = down.at[0, rows] if matrix == 2 else gate_up.at[0, matrix, rows]
            loads.append(pltpu.make_async_copy(source, out.at[matrix], sems.at[len(loads)]))
            loads[-1].start()
    loads.append(pltpu.make_async_copy(grads, grads_out, sems.at[len(loads)]))
    loads[-1].start()
    for load in loads:
        load.wait()


def gate_up_parts(experts, capacity, *refs):
    pieces = refs[:experts]
    held, out, *extra = refs[experts:]
    place, rows_in = place_rows(experts, capacity, pieces)
    if extra:
        extra[0][...] = place
        extra[1][...] = rows_in
    for matrix in range(2):
        out[matrix] = mm(rows_in, held[matrix], LANES).astype(BF)


def act_part(experts, own, *refs):
    place, held = refs[experts : experts + 2]
    rows_grad = mm(place[...], stacked(refs[:experts]).astype(BF), ROWS).astype(BF)
    if own:
        refs[-2][...] = rows_grad
    refs[-1][...] = mm(rows_grad, held[2], LANES).astype(BF)


def gates(pair, pair_far, act_out, by_gate, by_up):
    gate_sum = pair[0] + pair_far[0].astype(F32)
    up_sum = pair[1] + pair_far[1].astype(F32)
    sigmoid_gate = jax.nn.sigmoid(gate_sum)
    silu_gate = gate_sum * sigmoid_gate
    act_out[...] = (silu_gate * up_sum).astype(BF)
    by_gate[...] = up_sum * sigmoid_gate * (1.0 + gate_sum * (1.0 - sigmoid_gate))
    by_up[...] = silu_gate


def grads_of(act, act_far, by_gate, by_up, out):
    grad_act = act[...] + act_far[...].astype(F32)
    out[0] = (grad_act * by_gate[...]).astype(BF)
    out[1] = (grad_act * by_up[...]).astype(BF)


def own_rows(mine, held, out):
    out[...] = mm(mine[0], held[0]) + mm(mine[1], held[1])


def other_rows(experts, total, other, place, held, *pieces):
    rows = total[...] + mm(other[0], held[0]) + mm(other[1], held[1])
    back = mm(place[...], rows.astype(BF))
    for k in range(experts):
        pieces[k][...] = back[k * MOST : (k + 1) * MOST].astype(BF)


def weight_grads(mine_act, other_act, mine, other, rows_in, rows_grad, pair_out, down_out, held, sems):
    core = lax.axis_index("ey") & 1
    half = mine_act.shape[1]
    step = half // 2
    stores = []
    for matrix in range(3):
        right = rows_grad[...] if matrix == 0 else rows_in[...]
        for own in range(2):
            start = (core if own else 1 - core) * half
            for part in range(2):
                columns = slice(part * step, (part + 1) * step)
                if matrix == 0:
                    left = (mine_act if own else other_act)[:, columns]
                else:
                    left = (mine if own else other)[matrix - 1, :, columns]
                at = len(stores)
                held[at] = mm(left, right, ROWS).astype(BF)
                rows = pl.ds(start + part * step, step)
                target = down_out.at[0, rows] if matrix == 0 else pair_out.at[0, matrix - 1, rows]
                store = pltpu.make_async_copy(held.at[at], target, sems.at[at])
                store.start()
                stores.append(store)
    for store in stores:
        store.wait()


def combine(experts, pick, *refs):
    home = stacked(refs[:experts]).astype(BF)
    refs[experts][...] = mm(pick[...], home, ROWS).astype(BF)


def far(value):
    return pltpu.with_memory_space_constraint(value, pltpu.HBM)


def swap(value, axis, bit):
    count = lax.axis_size(axis)
    return lax.ppermute(value, axis, [(i, i ^ bit) for i in range(count)])


def exchange(pieces, axis):
    order = far_first(len(pieces))
    return [swap(piece, axis, k) if k else piece for piece, k in zip(pieces, order)]


def local(inputs, grad_output, routes, gate_probs, gate_up, down_proj):
    experts = lax.axis_size("ex")
    ways = lax.axis_size("ey")
    tokens, width = inputs.shape
    hidden = gate_up.shape[2]
    half = hidden // 2
    capacity = 5 * tokens * experts * routes.shape[1] // (4 * EXPERTS)
    rows = experts * MOST
    weight_bytes = hidden * width * 2
    weight_flops = 2 * capacity * hidden * width
    sds = jax.ShapeDtypeStruct
    piece = [sds((MOST, width), BF)] * experts
    dma = lambda count: pltpu.SemaphoreType.DMA((count,))

    pick, prob, *send_in = call(
        functools.partial(pick_inputs, experts),
        [sds((rows, tokens), BF), sds((rows, 1), F32)] + piece,
        (far(routes.T), far(gate_probs.T), far(inputs)),
        [HBM] * 3,
        [
            pltpu.VMEM(routes.shape[::-1], jnp.int32),
            pltpu.VMEM(routes.shape[::-1], BF),
            pltpu.VMEM((tokens, width), BF),
            dma(3),
        ],
        flops=2 * rows * tokens * width,
        traffic=2 * tokens * width,
    )
    got_in = exchange(send_in, "ex")
    held_other, held_mine, grads = call(
        stage,
        [pltpu.VMEM((3, half, width), BF)] * 2 + [pltpu.VMEM((tokens, width), BF)],
        (far(gate_up), far(down_proj), far(grad_output), pick),
        [HBM] * 3 + [ANY],
        [dma(7)],
        flops=WCOST * weight_flops,
        traffic=WCOST * weight_bytes,
    )
    send_grad = call(
        functools.partial(pick_grads, experts),
        piece,
        (pick, prob, grads, held_mine),
        [VMEM] * 3 + [ANY],
        flops=2 * rows * tokens * width,
        traffic=2 * tokens * width,
    )
    got_grad = exchange(send_grad, "ex")
    sent = []

    def pair_part(held, extra, cost):
        return call(
            functools.partial(gate_up_parts, experts, capacity),
            [sds((2, capacity, half), BF)] + extra,
            (*got_in, held),
            [VMEM] * (experts + 1),
            flops=cost * weight_flops,
            traffic=cost * weight_bytes,
        )

    (pair_other,) = pair_part(held_other, [], 1)
    pair_mine, place, rows_in = pair_part(
        held_mine, [sds((rows, capacity), BF), sds((capacity, width), BF)], C2COST
    )
    def total(held):
        bit = 2
        while bit * 2 < ways:
            held = held + swap(held.astype(BF), "ey", bit).astype(F32)
            bit *= 2
        sent.append(held.astype(BF))
        return held, swap(sent[-1], "ey", bit)


    pair = pair_mine.astype(F32) + swap(pair_other, "ey", 1).astype(F32)
    pair, pair_far = total(pair)
    def act_of(own, held, outs, tied, cost):
        return call(
            functools.partial(act_part, experts, own),
            outs + [sds((capacity, half), BF)],
            (*got_grad, place, held, *tied),
            [VMEM] * (experts + 2) + [ANY] * len(tied),
            flops=cost * weight_flops,
            traffic=cost * weight_bytes,
        )

    (act_other,) = act_of(False, held_other, [], sent[-1:], D1COST)
    rows_grad, act_mine = act_of(True, held_mine, [sds((capacity, width), BF)], [], D2COST)
    act, act_far = total(act_mine.astype(F32) + swap(act_other, "ey", 1).astype(F32))
    mine_act, by_gate, by_up = call(
        gates,
        [sds((capacity, half), BF)] + [sds((capacity, half), F32)] * 2,
        (pair, pair_far),
        [VMEM] * 2,
        traffic=18 * capacity * half,
        flops=GFLOP * weight_flops,
    )
    other_act = swap(mine_act, "ey", 1)
    mine = call(
        grads_of,
        sds((2, capacity, half), BF),
        (act, act_far, by_gate, by_up),
        [VMEM] * 4,
        traffic=18 * capacity * half,
    )
    other = swap(mine, "ey", 1)
    own = call(
        own_rows,
        sds((capacity, width), F32),
        (mine, held_mine),
        [VMEM] * 2,
        flops=weight_flops,
        traffic=weight_bytes,
    )
    back = call(
        functools.partial(other_rows, experts),
        piece,
        (own, other, place, held_other),
        [VMEM] * 4,
        flops=weight_flops,
        traffic=weight_bytes,
    )
    home = exchange(back, "ex")
    pair_grad, down_grad = call(
        weight_grads,
        [sds((1, 2, hidden, width), BF), sds((1, hidden, width), BF)],
        (mine_act, other_act, mine, other, rows_in, rows_grad),
        [VMEM] * 6,
        [pltpu.VMEM((12, half // 2, width), BF), dma(12)],
        limit=24,
        flops=3 * weight_flops,
        traffic=3 * weight_bytes,
        out_specs=[ANY, ANY],
    )
    grad_inputs = call(
        functools.partial(combine, experts),
        sds((tokens, width), BF),
        (pick, *home),
        [VMEM] * (experts + 1),
        flops=2 * rows * tokens * width,
        traffic=4 * tokens * width,
    )
    return (grad_inputs, pair_grad, down_grad)


def solution(mesh):
    return jax.shard_map(
        local,
        mesh=mesh,
        in_specs=(
            P(("groups", "ex"), "ey"),
            P(("groups", "ex"), "ey"),
            P(("groups", "ex"), None),
            P(("groups", "ex"), None),
            P("ex", None, None, "ey"),
            P("ex", None, "ey"),
        ),
        out_specs=(
            P(("groups", "ex"), "ey"),
            P("ex", "groups", None, "ey"),
            P("ex", "groups", "ey"),
        ),
        check_vma=False,
    )
```

```python
import functools

import jax
import jax.numpy as jnp
from jax import lax
from jax.experimental import pallas as pl
from jax.experimental.pallas import tpu as pltpu
from jax.sharding import PartitionSpec as P

MOST = 40
EXPERTS = 128
EMPTY = 64.0
BF = jnp.bfloat16
F32 = jnp.float32
MIB = 1 << 20
C2COST = 100
WCOST = 100
GFLOP = 100
D1COST = 1
D2COST = 100
VMEM = pl.BlockSpec(memory_space=pltpu.VMEM)
ANY = pl.BlockSpec(memory_space=pl.ANY)
HBM = pl.BlockSpec(memory_space=pltpu.HBM)
ROWS = (((0,), (0,)), ((), ()))
LANES = (((1,), (1,)), ((), ()))
PLAIN = (((1,), (0,)), ((), ()))


def mm(left, right, dims=PLAIN):
    return lax.dot_general(left, right, dims, preferred_element_type=F32)


def iota(shape, dim):
    return lax.broadcasted_iota(jnp.int32, shape, dim)


def far_first(count):
    return sorted(range(count), key=lambda k: (-k.bit_length(), k))


def block_of(position, names):
    found = jnp.full_like(position, names[0])
    for at in range(1, len(names)):
        found = found + (position >= at * MOST).astype(jnp.int32) * (names[at] - names[at - 1])
    return found


def call(body, outs, operands, specs, scratch=(), limit=16, flops=0, traffic=0, out_specs=None):
    return pl.pallas_call(
        body,
        out_shape=outs,
        in_specs=specs,
        out_specs=out_specs if out_specs is not None else jax.tree.map(lambda _: VMEM, outs),
        scratch_shapes=list(scratch),
        compiler_params=pltpu.CompilerParams(vmem_limit_bytes=limit * MIB),
        cost_estimate=pl.CostEstimate(flops=flops, bytes_accessed=traffic, transcendentals=0),
    )(*operands)


def pick_inputs(experts, routes_in, probs_in, inputs, grads, pick_out, prob_out, grads_out, *refs):
    *pieces, routes, probs, held, sems = refs
    loads = [
        pltpu.make_async_copy(source, target, sems.at[at])
        for at, (source, target) in enumerate(
            [(routes_in, routes), (probs_in, probs), (inputs, held), (grads, grads_out)]
        )
    ]
    for load in loads:
        load.start()
    me = lax.axis_index("ex")
    tokens = inputs.shape[0]
    rows = experts * MOST
    order = far_first(experts)
    owner = block_of(iota((rows, routes.shape[0]), 0), order)
    named = jnp.zeros((rows, tokens), F32)
    weight = jnp.zeros((rows, tokens), F32)
    earlier = iota((tokens, tokens), 0) < iota((tokens, tokens), 1)
    earlier = jnp.where(earlier, 1.0, 0.0).astype(BF)
    row = iota((rows, tokens), 0)
    slot = row - block_of(row, range(experts)) * MOST
    loads[0].wait()
    loads[1].wait()
    chosen = routes[...]
    wide = probs[...].astype(F32)
    for k in range(experts):
        spread = jnp.where(owner == k, 1.0, 0.0).astype(BF)
        hit = chosen == (me ^ k)
        named = named + mm(spread, jnp.where(hit, 1.0, 0.0).astype(BF))
        weight = weight + mm(spread, jnp.where(hit, wide, 0.0).astype(BF))
    rank = mm(named.astype(BF), earlier).astype(jnp.int32)
    picks = (rank == slot) & (named > 0.5)
    pick = jnp.where(picks, 1.0, 0.0)
    filled = jnp.max(pick, axis=1, keepdims=True) > 0.5
    pick = pick.astype(BF)
    pick_out[...] = pick
    prob_out[...] = jnp.sum(jnp.where(picks, weight, 0.0), axis=1, keepdims=True)
    loads[2].wait()
    sent = jnp.where(filled, mm(pick, held[...]), EMPTY)
    for k in range(experts):
        pieces[k][...] = sent[k * MOST : (k + 1) * MOST].astype(BF)
    loads[3].wait()


def pick_grads(experts, pick, prob, grads, near_in, near, *pieces):
    sent = mm(pick[...], grads[...]) * prob[...]
    for at, k in enumerate(far_first(experts)):
        rows = sent[at * MOST : (at + 1) * MOST]
        if k == 1:
            both = jnp.concatenate([near_in[...].astype(F32), rows], axis=0)
            near[...] = both.astype(BF)
        else:
            pieces[at if k else at - 1][...] = rows.astype(BF)


def stacked(pieces, part=0):
    rows = [piece[...].astype(F32) for piece in pieces]
    rows = [row[part * MOST : (part + 1) * MOST] if row.shape[0] > MOST else row for row in rows]
    return jnp.concatenate(rows, axis=0)


def rows_of(half, own):
    core = lax.axis_index("ey") & 1
    return pl.ds(pl.multiple_of((core if own else 1 - core) * half, 128), half)


def place_rows(experts, capacity, pieces):
    me = lax.axis_index("ex")
    rows = experts * MOST
    got = stacked(pieces)
    full = got[:, :1] < EMPTY / 2
    key = []
    for dim in (0, 1):
        row = iota((rows, rows), dim)
        local_row = row - block_of(row, range(experts)) * MOST
        key.append((me ^ block_of(row, far_first(experts))) * MOST + local_row)
    earlier = jnp.where(key[1] < key[0], 1.0, 0.0).astype(BF)
    wide = jnp.broadcast_to(full, (rows, capacity))
    slot = mm(earlier, jnp.where(wide, 1.0, 0.0).astype(BF)).astype(jnp.int32)
    place = jnp.where((slot == iota((rows, capacity), 1)) & wide, 1.0, 0.0).astype(BF)
    return place, mm(place, got.astype(BF), ROWS).astype(BF)


def stage(far_count, gate_up, down, *refs):
    pieces, refs = refs[:far_count], refs[far_count:]
    held, pieces_out, sems = refs[:2], refs[2:-1], refs[-1]
    half = down.shape[1] // 2
    moves = list(zip(pieces, pieces_out))
    for own, out in enumerate(held):
        rows = rows_of(half, own == 1)
        for matrix in range(3):
            source = down.at[0, rows] if matrix == 2 else gate_up.at[0, matrix, rows]
            moves.append((source, out.at[matrix]))
    loads = [
        pltpu.make_async_copy(source, target, sems.at[at]) for at, (source, target) in enumerate(moves)
    ]
    for load in loads:
        load.start()
    for load in loads:
        load.wait()


def other_pair(experts, capacity, *refs):
    held, out, place_out, rows_out = refs[experts:]
    place, rows_in = place_rows(experts, capacity, refs[:experts])
    place_out[...] = place
    rows_out[...] = rows_in
    for matrix in range(2):
        out[matrix] = mm(rows_in, held[matrix], LANES).astype(BF)


def mine_pair(rows_in, held, out):
    for matrix in range(2):
        out[matrix] = mm(rows_in[...], held[matrix], LANES).astype(BF)


def act_part(experts, own, *refs):
    place, held = refs[experts : experts + 2]
    rows_grad = mm(place[...], stacked(refs[:experts], 1).astype(BF), ROWS).astype(BF)
    if own:
        refs[-2][...] = rows_grad
    refs[-1][...] = mm(rows_grad, held[2], LANES).astype(BF)


def gates(pair, pair_far, act_out, by_gate, by_up):
    gate_sum = pair[0] + pair_far[0].astype(F32)
    up_sum = pair[1] + pair_far[1].astype(F32)
    sigmoid_gate = jax.nn.sigmoid(gate_sum)
    silu_gate = gate_sum * sigmoid_gate
    act_out[...] = (silu_gate * up_sum).astype(BF)
    by_gate[...] = up_sum * sigmoid_gate * (1.0 + gate_sum * (1.0 - sigmoid_gate))
    by_up[...] = silu_gate


def grads_of(act, act_far, by_gate, by_up, _, out):
    grad_act = act[...] + act_far[...].astype(F32)
    out[0] = (grad_act * by_gate[...]).astype(BF)
    out[1] = (grad_act * by_up[...]).astype(BF)


def own_rows(mine, held, out):
    out[...] = mm(mine[0], held[0]) + mm(mine[1], held[1])


def other_rows(experts, total, other, place, held, *pieces):
    rows = total[...] + mm(other[0], held[0]) + mm(other[1], held[1])
    back = mm(place[...], rows.astype(BF))
    for k in range(experts):
        pieces[k][...] = back[k * MOST : (k + 1) * MOST].astype(BF)


def weight_grads(mine_act, other_act, mine, other, rows_in, rows_grad, pair_out, down_out, held, sems):
    core = lax.axis_index("ey") & 1
    half = mine_act.shape[1]
    step = half // 2
    stores = []
    for matrix in range(3):
        right = rows_grad[...] if matrix == 0 else rows_in[...]
        for own in range(2):
            start = (core if own else 1 - core) * half
            for part in range(2):
                columns = slice(part * step, (part + 1) * step)
                if matrix == 0:
                    left = (mine_act if own else other_act)[:, columns]
                else:
                    left = (mine if own else other)[matrix - 1, :, columns]
                at = len(stores)
                held[at] = mm(left, right, ROWS).astype(BF)
                rows = pl.ds(start + part * step, step)
                target = down_out.at[0, rows] if matrix == 0 else pair_out.at[0, matrix - 1, rows]
                store = pltpu.make_async_copy(held.at[at], target, sems.at[at])
                store.start()
                stores.append(store)
    for store in stores:
        store.wait()


def combine(experts, pick, *refs):
    home = stacked(refs[:experts]).astype(BF)
    refs[experts][...] = mm(pick[...], home, ROWS).astype(BF)


def far(value):
    return pltpu.with_memory_space_constraint(value, pltpu.HBM)


def swap(value, axis, bit):
    count = lax.axis_size(axis)
    return lax.ppermute(value, axis, [(i, i ^ bit) for i in range(count)])


def exchange(pieces, axis):
    order = far_first(len(pieces))
    return [swap(piece, axis, k) if k else piece for piece, k in zip(pieces, order)]


def local(inputs, grad_output, routes, gate_probs, gate_up, down_proj):
    experts = lax.axis_size("ex")
    ways = lax.axis_size("ey")
    tokens, width = inputs.shape
    hidden = gate_up.shape[2]
    half = hidden // 2
    capacity = 5 * tokens * experts * routes.shape[1] // (4 * EXPERTS)
    rows = experts * MOST
    weight_bytes = hidden * width * 2
    weight_flops = 2 * capacity * hidden * width
    sds = jax.ShapeDtypeStruct
    piece = [sds((MOST, width), BF)] * experts
    dma = lambda count: pltpu.SemaphoreType.DMA((count,))

    order = far_first(experts)
    far_count = experts - 2
    pick, prob, grads, *send_in = call(
        functools.partial(pick_inputs, experts),
        [
            sds((rows, tokens), BF),
            sds((rows, 1), F32),
            pltpu.VMEM((tokens, width), BF),
        ]
        + piece,
        (far(routes.T), far(gate_probs.T), far(inputs), far(grad_output)),
        [HBM] * 4,
        [
            pltpu.VMEM(routes.shape[::-1], jnp.int32),
            pltpu.VMEM(routes.shape[::-1], BF),
            pltpu.VMEM((tokens, width), BF),
            dma(4),
        ],
        flops=2 * rows * tokens * width,
        traffic=4 * tokens * width,
    )
    near, *send_grad = call(
        functools.partial(pick_grads, experts),
        [sds((2 * MOST, width), BF)] + piece[1:],
        (pick, prob, grads, send_in[-2]),
        [VMEM] * 4,
        flops=2 * rows * tokens * width,
        traffic=2 * tokens * width,
    )
    got_in = [swap(send_in[at], "ex", order[at]) for at in range(far_count)]
    near = swap(near, "ex", 1)
    got_in = got_in + [near, send_in[-1]]
    held_other, held_mine, *far_grad = call(
        functools.partial(stage, far_count),
        [pltpu.VMEM((3, half, width), BF)] * 2 + piece[2:],
        (far(gate_up), far(down_proj), *send_grad[:-1]),
        [HBM] * 2 + [VMEM] * far_count,
        [dma(far_count + 6)],
        flops=WCOST * weight_flops,
        traffic=WCOST * weight_bytes,
    )
    got_grad = [swap(far_grad[at], "ex", order[at]) for at in range(far_count)]
    got_grad = got_grad + [near, send_grad[-1]]
    sent = []

    pair_other, place, rows_in = call(
        functools.partial(other_pair, experts, capacity),
        [sds((2, capacity, half), BF), sds((rows, capacity), BF), sds((capacity, width), BF)],
        (*got_in, held_other),
        [VMEM] * (experts + 1),
        flops=2 * weight_flops,
        traffic=weight_bytes,
    )
    pair_mine = call(
        mine_pair,
        sds((2, capacity, half), BF),
        (rows_in, held_mine),
        [VMEM] * 2,
        flops=C2COST * weight_flops,
        traffic=C2COST * weight_bytes,
    )

    def total(held):
        bit = 2
        while bit * 2 < ways:
            held = held + swap(held.astype(BF), "ey", bit).astype(F32)
            bit *= 2
        sent.append(held.astype(BF))
        return held, swap(sent[-1], "ey", bit)


    pair = pair_mine.astype(F32) + swap(pair_other, "ey", 1).astype(F32)
    pair, pair_far = total(pair)
    def act_of(own, held, outs, tied, cost):
        return call(
            functools.partial(act_part, experts, own),
            outs + [sds((capacity, half), BF)],
            (*got_grad, place, held, *tied),
            [VMEM] * (experts + 2) + [ANY] * len(tied),
            flops=cost * weight_flops,
            traffic=cost * weight_bytes,
        )

    (act_other,) = act_of(False, held_other, [], sent[-1:], D1COST)
    rows_grad, act_mine = act_of(True, held_mine, [sds((capacity, width), BF)], [], D2COST)
    act, act_far = total(act_mine.astype(F32) + swap(act_other, "ey", 1).astype(F32))
    mine_act, by_gate, by_up = call(
        gates,
        [sds((capacity, half), BF)] + [sds((capacity, half), F32)] * 2,
        (pair, pair_far),
        [VMEM] * 2,
        traffic=18 * capacity * half,
        flops=GFLOP * weight_flops,
    )
    other_act = swap(mine_act, "ey", 1)
    mine = call(
        grads_of,
        sds((2, capacity, half), BF),
        (act, act_far, by_gate, by_up, other_act),
        [VMEM] * 4 + [ANY],
        traffic=18 * capacity * half,
    )
    other = swap(mine, "ey", 1)
    own = call(
        own_rows,
        sds((capacity, width), F32),
        (mine, held_mine),
        [VMEM] * 2,
        flops=weight_flops,
        traffic=weight_bytes,
    )
    back = call(
        functools.partial(other_rows, experts),
        piece,
        (own, other, place, held_other),
        [VMEM] * 4,
        flops=weight_flops,
        traffic=weight_bytes,
    )
    home = exchange(back, "ex")
    pair_grad, down_grad = call(
        weight_grads,
        [sds((1, 2, hidden, width), BF), sds((1, hidden, width), BF)],
        (mine_act, other_act, mine, other, rows_in, rows_grad),
        [VMEM] * 6,
        [pltpu.VMEM((12, half // 2, width), BF), dma(12)],
        limit=24,
        flops=3 * weight_flops,
        traffic=3 * weight_bytes,
        out_specs=[ANY, ANY],
    )
    grad_inputs = call(
        functools.partial(combine, experts),
        sds((tokens, width), BF),
        (pick, *home),
        [VMEM] * (experts + 1),
        flops=2 * rows * tokens * width,
        traffic=4 * tokens * width,
    )
    return (grad_inputs, pair_grad, down_grad)


def solution(mesh):
    return jax.shard_map(
        local,
        mesh=mesh,
        in_specs=(
            P(("groups", "ex"), "ey"),
            P(("groups", "ex"), "ey"),
            P(("groups", "ex"), None),
            P(("groups", "ex"), None),
            P("ex", None, None, "ey"),
            P("ex", None, "ey"),
        ),
        out_specs=(
            P(("groups", "ex"), "ey"),
            P("ex", "groups", None, "ey"),
            P("ex", "groups", "ey"),
        ),
        check_vma=False,
    )
```

```python
import functools

import jax
import jax.numpy as jnp
from jax import lax
from jax.experimental import pallas as pl
from jax.experimental.pallas import tpu as pltpu
from jax.sharding import PartitionSpec as P

MOST = 40
EXPERTS = 128
EMPTY = 64.0
BF = jnp.bfloat16
F32 = jnp.float32
MIB = 1 << 20
C2COST = 100
WCOST = 100
GFLOP = 100
D1COST = 1
D2COST = 100
VMEM = pl.BlockSpec(memory_space=pltpu.VMEM)
ANY = pl.BlockSpec(memory_space=pl.ANY)
HBM = pl.BlockSpec(memory_space=pltpu.HBM)
ROWS = (((0,), (0,)), ((), ()))
LANES = (((1,), (1,)), ((), ()))
PLAIN = (((1,), (0,)), ((), ()))


def mm(left, right, dims=PLAIN):
    return lax.dot_general(left, right, dims, preferred_element_type=F32)


def iota(shape, dim):
    return lax.broadcasted_iota(jnp.int32, shape, dim)


def far_first(count):
    return list(reversed(range(count)))


def block_of(position, names):
    found = jnp.full_like(position, names[0])
    for at in range(1, len(names)):
        found = found + (position >= at * MOST).astype(jnp.int32) * (names[at] - names[at - 1])
    return found


def call(body, outs, operands, specs, scratch=(), limit=16, flops=0, traffic=0, out_specs=None):
    return pl.pallas_call(
        body,
        out_shape=outs,
        in_specs=specs,
        out_specs=out_specs if out_specs is not None else jax.tree.map(lambda _: VMEM, outs),
        scratch_shapes=list(scratch),
        compiler_params=pltpu.CompilerParams(vmem_limit_bytes=limit * MIB),
        cost_estimate=pl.CostEstimate(flops=flops, bytes_accessed=traffic, transcendentals=0),
    )(*operands)


def pick_inputs(experts, routes_in, probs_in, inputs, grads, pick_out, prob_out, grads_out, *refs):
    *pieces, routes, probs, held, sems = refs
    loads = [
        pltpu.make_async_copy(source, target, sems.at[at])
        for at, (source, target) in enumerate(
            [(routes_in, routes), (probs_in, probs), (inputs, held), (grads, grads_out)]
        )
    ]
    for load in loads:
        load.start()
    me = lax.axis_index("ex")
    tokens = inputs.shape[0]
    rows = experts * MOST
    order = far_first(experts)
    owner = block_of(iota((rows, routes.shape[0]), 0), order)
    named = jnp.zeros((rows, tokens), F32)
    weight = jnp.zeros((rows, tokens), F32)
    earlier = iota((tokens, tokens), 0) < iota((tokens, tokens), 1)
    earlier = jnp.where(earlier, 1.0, 0.0).astype(BF)
    row = iota((rows, tokens), 0)
    slot = row - block_of(row, range(experts)) * MOST
    loads[0].wait()
    loads[1].wait()
    chosen = routes[...]
    wide = probs[...].astype(F32)
    for k in range(experts):
        spread = jnp.where(owner == k, 1.0, 0.0).astype(BF)
        hit = chosen == (me ^ k)
        named = named + mm(spread, jnp.where(hit, 1.0, 0.0).astype(BF))
        weight = weight + mm(spread, jnp.where(hit, wide, 0.0).astype(BF))
    rank = mm(named.astype(BF), earlier).astype(jnp.int32)
    picks = (rank == slot) & (named > 0.5)
    pick = jnp.where(picks, 1.0, 0.0)
    filled = jnp.max(pick, axis=1, keepdims=True) > 0.5
    pick = pick.astype(BF)
    pick_out[...] = pick
    prob_out[...] = jnp.sum(jnp.where(picks, weight, 0.0), axis=1, keepdims=True)
    loads[2].wait()
    sent = jnp.where(filled, mm(pick, held[...]), EMPTY)
    for k in range(experts):
        pieces[k][...] = sent[k * MOST : (k + 1) * MOST].astype(BF)
    loads[3].wait()


def pick_grads(experts, pick, prob, grads, *pieces):
    sent = mm(pick[...], grads[...]) * prob[...]
    for k in range(experts):
        pieces[k][...] = sent[k * MOST : (k + 1) * MOST].astype(BF)


def stacked(pieces):
    return jnp.concatenate([piece[...].astype(F32) for piece in pieces], axis=0)


def rows_of(half, own):
    core = lax.axis_index("ey") & 1
    return pl.ds(pl.multiple_of((core if own else 1 - core) * half, 128), half)


def place_rows(experts, capacity, pieces):
    me = lax.axis_index("ex")
    rows = experts * MOST
    got = stacked(pieces)
    full = got[:, :1] < EMPTY / 2
    key = []
    for dim in (0, 1):
        row = iota((rows, rows), dim)
        local_row = row - block_of(row, range(experts)) * MOST
        key.append((me ^ block_of(row, far_first(experts))) * MOST + local_row)
    earlier = jnp.where(key[1] < key[0], 1.0, 0.0).astype(BF)
    wide = jnp.broadcast_to(full, (rows, capacity))
    slot = mm(earlier, jnp.where(wide, 1.0, 0.0).astype(BF)).astype(jnp.int32)
    place = jnp.where((slot == iota((rows, capacity), 1)) & wide, 1.0, 0.0).astype(BF)
    return place, mm(place, got.astype(BF), ROWS).astype(BF)


def stage(far_count, gate_up, *refs):
    pieces, refs = refs[:far_count], refs[far_count:]
    held, pieces_out, sems = refs[:2], refs[2:-1], refs[-1]
    half = gate_up.shape[2] // 2
    moves = list(zip(pieces, pieces_out))
    for own, out in enumerate(held):
        for matrix in range(2):
            moves.append((gate_up.at[0, matrix, rows_of(half, own == 1)], out.at[matrix]))
    loads = [
        pltpu.make_async_copy(source, target, sems.at[at]) for at, (source, target) in enumerate(moves)
    ]
    for load in loads:
        load.start()
    for load in loads:
        load.wait()


def load_down(down, own, out, sem):
    half = down.shape[1] // 2
    return pltpu.make_async_copy(down.at[0, rows_of(half, own)], out, sem)


def other_pair(experts, capacity, *refs):
    held, down, near, out, place_out, rows_out, down_out, near_out, sem = refs[experts:]
    near_out[...] = near[...]
    load = load_down(down, False, down_out, sem)
    load.start()
    place, rows_in = place_rows(experts, capacity, refs[:experts])
    place_out[...] = place
    rows_out[...] = rows_in
    for matrix in range(2):
        out[matrix] = mm(rows_in, held[matrix], LANES).astype(BF)
    load.wait()


def mine_pair(rows_in, held, down, out, down_out, sem):
    load = load_down(down, True, down_out, sem)
    load.start()
    for matrix in range(2):
        out[matrix] = mm(rows_in[...], held[matrix], LANES).astype(BF)
    load.wait()


def pair_sum(mine, other, held_out, sent_out):
    held = mine[...].astype(F32) + other[...].astype(F32)
    held_out[...] = held
    sent_out[...] = held.astype(BF)


def act_part(experts, own, *refs):
    place, held = refs[experts : experts + 2]
    rows_grad = mm(place[...], stacked(refs[:experts]).astype(BF), ROWS).astype(BF)
    if own:
        refs[-2][...] = rows_grad
    refs[-1][...] = mm(rows_grad, held[...], LANES).astype(BF)


def gates(pair, pair_far, act_out, by_gate, by_up):
    gate_sum = pair[0] + pair_far[0].astype(F32)
    up_sum = pair[1] + pair_far[1].astype(F32)
    sigmoid_gate = jax.nn.sigmoid(gate_sum)
    silu_gate = gate_sum * sigmoid_gate
    act_out[...] = (silu_gate * up_sum).astype(BF)
    by_gate[...] = up_sum * sigmoid_gate * (1.0 + gate_sum * (1.0 - sigmoid_gate))
    by_up[...] = silu_gate


def grads_of(act, act_far, by_gate, by_up, _, out):
    grad_act = act[...] + act_far[...].astype(F32)
    out[0] = (grad_act * by_gate[...]).astype(BF)
    out[1] = (grad_act * by_up[...]).astype(BF)


def own_rows(mine, held, out):
    out[...] = mm(mine[0], held[0]) + mm(mine[1], held[1])


def other_rows(experts, total, other, place, held, *pieces):
    rows = total[...] + mm(other[0], held[0]) + mm(other[1], held[1])
    back = mm(place[...], rows.astype(BF))
    for k in range(experts):
        pieces[k][...] = back[k * MOST : (k + 1) * MOST].astype(BF)


def weight_grads(mine_act, other_act, mine, other, rows_in, rows_grad, pair_out, down_out, held, sems):
    core = lax.axis_index("ey") & 1
    half = mine_act.shape[1]
    step = half // 2
    stores = []
    for matrix in range(3):
        right = rows_grad[...] if matrix == 0 else rows_in[...]
        for own in range(2):
            start = (core if own else 1 - core) * half
            for part in range(2):
                columns = slice(part * step, (part + 1) * step)
                if matrix == 0:
                    left = (mine_act if own else other_act)[:, columns]
                else:
                    left = (mine if own else other)[matrix - 1, :, columns]
                at = len(stores)
                held[at] = mm(left, right, ROWS).astype(BF)
                rows = pl.ds(start + part * step, step)
                target = down_out.at[0, rows] if matrix == 0 else pair_out.at[0, matrix - 1, rows]
                store = pltpu.make_async_copy(held.at[at], target, sems.at[at])
                store.start()
                stores.append(store)
    for store in stores:
        store.wait()


def combine(experts, pick, *refs):
    home = stacked(refs[:experts]).astype(BF)
    refs[experts][...] = mm(pick[...], home, ROWS).astype(BF)


def far(value):
    return pltpu.with_memory_space_constraint(value, pltpu.HBM)


def swap(value, axis, bit):
    count = lax.axis_size(axis)
    return lax.ppermute(value, axis, [(i, i ^ bit) for i in range(count)])


def exchange(pieces, axis):
    order = far_first(len(pieces))
    return [swap(piece, axis, k) if k else piece for piece, k in zip(pieces, order)]


def local(inputs, grad_output, routes, gate_probs, gate_up, down_proj):
    experts = lax.axis_size("ex")
    ways = lax.axis_size("ey")
    tokens, width = inputs.shape
    hidden = gate_up.shape[2]
    half = hidden // 2
    capacity = 5 * tokens * experts * routes.shape[1] // (4 * EXPERTS)
    rows = experts * MOST
    weight_bytes = hidden * width * 2
    weight_flops = 2 * capacity * hidden * width
    sds = jax.ShapeDtypeStruct
    piece = [sds((MOST, width), BF)] * experts
    dma = lambda count: pltpu.SemaphoreType.DMA((count,))

    order = far_first(experts)
    far_count = experts - 2
    pick, prob, grads, *send_in = call(
        functools.partial(pick_inputs, experts),
        [
            sds((rows, tokens), BF),
            sds((rows, 1), F32),
            pltpu.VMEM((tokens, width), BF),
        ]
        + piece,
        (far(routes.T), far(gate_probs.T), far(inputs), far(grad_output)),
        [HBM] * 4,
        [
            pltpu.VMEM(routes.shape[::-1], jnp.int32),
            pltpu.VMEM(routes.shape[::-1], BF),
            pltpu.VMEM((tokens, width), BF),
            dma(4),
        ],
        flops=2 * rows * tokens * width,
        traffic=4 * tokens * width,
    )
    send_grad = call(
        functools.partial(pick_grads, experts),
        piece,
        (pick, prob, grads),
        [VMEM] * 3,
        flops=2 * rows * tokens * width,
        traffic=2 * tokens * width,
    )
    got_in = exchange(send_in, "ex")
    held_other, held_mine, *far_grad = call(
        functools.partial(stage, far_count),
        [pltpu.VMEM((2, half, width), BF)] * 2 + piece[2:],
        (far(gate_up), *send_grad[:far_count]),
        [HBM] + [VMEM] * far_count,
        [dma(far_count + 4)],
        flops=WCOST * weight_flops,
        traffic=WCOST * weight_bytes,
    )
    got_grad = [swap(far_grad[at], "ex", order[at]) for at in range(far_count)]

    one_dma = pltpu.SemaphoreType.DMA
    down_half = pltpu.VMEM((half, width), BF)
    pair_other, place, rows_in, down_other, near_grad = call(
        functools.partial(other_pair, experts, capacity),
        [sds((2, capacity, half), BF), sds((rows, capacity), BF), sds((capacity, width), BF)]
        + [down_half, piece[0]],
        (*got_in, held_other, far(down_proj), send_grad[-2]),
        [VMEM] * (experts + 1) + [HBM, VMEM],
        [one_dma],
        flops=2 * weight_flops,
        traffic=weight_bytes,
    )
    pair_mine, down_mine = call(
        mine_pair,
        [sds((2, capacity, half), BF), down_half],
        (rows_in, held_mine, far(down_proj)),
        [VMEM] * 2 + [HBM],
        [one_dma],
        flops=C2COST * weight_flops,
        traffic=C2COST * weight_bytes,
    )

    def total(held, sent):
        bit = 2
        while bit * 2 < ways:
            held = held + swap(sent, "ey", bit).astype(F32)
            sent = held.astype(BF)
            bit *= 2
        return held, swap(sent, "ey", bit)

    pair, pair_sent = call(
        pair_sum,
        [sds((2, capacity, half), F32), sds((2, capacity, half), BF)],
        (pair_mine, swap(pair_other, "ey", 1)),
        [VMEM] * 2,
        traffic=10 * capacity * hidden,
    )
    pair, pair_far = total(pair, pair_sent)
    got_grad = got_grad + [swap(near_grad, "ex", 1), send_grad[-1]]

    def act_of(own, held, outs, tied, cost):
        return call(
            functools.partial(act_part, experts, own),
            outs + [sds((capacity, half), BF)],
            (*got_grad, place, held, *tied),
            [VMEM] * (experts + 2) + [ANY] * len(tied),
            flops=cost * weight_flops,
            traffic=cost * weight_bytes,
        )

    (act_other,) = act_of(False, down_other, [], [pair_sent], D1COST)
    rows_grad, act_mine = act_of(True, down_mine, [sds((capacity, width), BF)], [], D2COST)
    act = act_mine.astype(F32) + swap(act_other, "ey", 1).astype(F32)
    act, act_far = total(act, act.astype(BF))
    mine_act, by_gate, by_up = call(
        gates,
        [sds((capacity, half), BF)] + [sds((capacity, half), F32)] * 2,
        (pair, pair_far),
        [VMEM] * 2,
        traffic=18 * capacity * half,
        flops=GFLOP * weight_flops,
    )
    other_act = swap(mine_act, "ey", 1)
    mine = call(
        grads_of,
        sds((2, capacity, half), BF),
        (act, act_far, by_gate, by_up, other_act),
        [VMEM] * 4 + [ANY],
        traffic=18 * capacity * half,
    )
    other = swap(mine, "ey", 1)
    own = call(
        own_rows,
        sds((capacity, width), F32),
        (mine, held_mine),
        [VMEM] * 2,
        flops=weight_flops,
        traffic=weight_bytes,
    )
    back = call(
        functools.partial(other_rows, experts),
        piece,
        (own, other, place, held_other),
        [VMEM] * 4,
        flops=weight_flops,
        traffic=weight_bytes,
    )
    home = exchange(back, "ex")
    pair_grad, down_grad = call(
        weight_grads,
        [sds((1, 2, hidden, width), BF), sds((1, hidden, width), BF)],
        (mine_act, other_act, mine, other, rows_in, rows_grad),
        [VMEM] * 6,
        [pltpu.VMEM((12, half // 2, width), BF), dma(12)],
        limit=24,
        flops=3 * weight_flops,
        traffic=3 * weight_bytes,
        out_specs=[ANY, ANY],
    )
    grad_inputs = call(
        functools.partial(combine, experts),
        sds((tokens, width), BF),
        (pick, *home),
        [VMEM] * (experts + 1),
        flops=2 * rows * tokens * width,
        traffic=4 * tokens * width,
    )
    return (grad_inputs, pair_grad, down_grad)


def solution(mesh):
    return jax.shard_map(
        local,
        mesh=mesh,
        in_specs=(
            P(("groups", "ex"), "ey"),
            P(("groups", "ex"), "ey"),
            P(("groups", "ex"), None),
            P(("groups", "ex"), None),
            P("ex", None, None, "ey"),
            P("ex", None, "ey"),
        ),
        out_specs=(
            P(("groups", "ex"), "ey"),
            P("ex", "groups", None, "ey"),
            P("ex", "groups", "ey"),
        ),
        check_vma=False,
    )
```

```python
import functools

import jax
import jax.numpy as jnp
from jax import lax
from jax.experimental import pallas as pl
from jax.experimental.pallas import tpu as pltpu
from jax.sharding import PartitionSpec as P

MOST = 40
EXPERTS = 128
EMPTY = 64.0
BF = jnp.bfloat16
F32 = jnp.float32
MIB = 1 << 20
C2COST = 100
WCOST = 100
CUTS = 6
GFLOP = 100
D1COST = 1
D2COST = 100
VMEM = pl.BlockSpec(memory_space=pltpu.VMEM)
ANY = pl.BlockSpec(memory_space=pl.ANY)
HBM = pl.BlockSpec(memory_space=pltpu.HBM)
ROWS = (((0,), (0,)), ((), ()))
LANES = (((1,), (1,)), ((), ()))
PLAIN = (((1,), (0,)), ((), ()))


def mm(left, right, dims=PLAIN):
    return lax.dot_general(left, right, dims, preferred_element_type=F32)


def iota(shape, dim):
    return lax.broadcasted_iota(jnp.int32, shape, dim)


def far_first(count):
    return sorted(range(count), key=lambda k: (-k.bit_length(), k))


def cut(source, target, sems, first, pieces):
    rows = target.shape[-2] // pieces
    out = []
    for at in range(pieces):
        part = pl.ds(at * rows, rows)
        out.append(pltpu.make_async_copy(source.at[part], target.at[part], sems.at[first + at]))
    return out


def run(loads):
    for load in loads:
        load.start()
    return loads


def wait(loads):
    for load in loads:
        load.wait()


def block_of(position, names):
    found = jnp.full_like(position, names[0])
    for at in range(1, len(names)):
        found = found + (position >= at * MOST).astype(jnp.int32) * (names[at] - names[at - 1])
    return found


def call(body, outs, operands, specs, scratch=(), limit=16, flops=0, traffic=0, out_specs=None):
    return pl.pallas_call(
        body,
        out_shape=outs,
        in_specs=specs,
        out_specs=out_specs if out_specs is not None else jax.tree.map(lambda _: VMEM, outs),
        scratch_shapes=list(scratch),
        compiler_params=pltpu.CompilerParams(vmem_limit_bytes=limit * MIB),
        cost_estimate=pl.CostEstimate(flops=flops, bytes_accessed=traffic, transcendentals=0),
    )(*operands)


def pick_inputs(experts, routes_in, probs_in, inputs, grads, pick_out, prob_out, grads_out, *refs):
    *pieces, routes, probs, held, sems = refs
    loads = run(
        [
            pltpu.make_async_copy(routes_in, routes, sems.at[0]),
            pltpu.make_async_copy(probs_in, probs, sems.at[1]),
        ]
    )
    input_loads = run(cut(inputs, held, sems, 2, 4))
    grad_loads = run(cut(grads, grads_out, sems, 6, 4))
    me = lax.axis_index("ex")
    tokens = inputs.shape[0]
    rows = experts * MOST
    order = far_first(experts)
    owner = block_of(iota((rows, routes.shape[0]), 0), order)
    named = jnp.zeros((rows, tokens), F32)
    weight = jnp.zeros((rows, tokens), F32)
    earlier = iota((tokens, tokens), 0) < iota((tokens, tokens), 1)
    earlier = jnp.where(earlier, 1.0, 0.0).astype(BF)
    row = iota((rows, tokens), 0)
    slot = row - block_of(row, range(experts)) * MOST
    wait(loads)
    chosen = routes[...]
    wide = probs[...].astype(F32)
    for k in range(experts):
        spread = jnp.where(owner == k, 1.0, 0.0).astype(BF)
        hit = chosen == (me ^ k)
        named = named + mm(spread, jnp.where(hit, 1.0, 0.0).astype(BF))
        weight = weight + mm(spread, jnp.where(hit, wide, 0.0).astype(BF))
    rank = mm(named.astype(BF), earlier).astype(jnp.int32)
    picks = (rank == slot) & (named > 0.5)
    pick = jnp.where(picks, 1.0, 0.0)
    filled = jnp.max(pick, axis=1, keepdims=True) > 0.5
    pick = pick.astype(BF)
    pick_out[...] = pick
    prob_out[...] = jnp.sum(jnp.where(picks, weight, 0.0), axis=1, keepdims=True)
    wait(input_loads)
    sent = jnp.where(filled, mm(pick, held[...]), EMPTY)
    for k in range(experts):
        pieces[k][...] = sent[k * MOST : (k + 1) * MOST].astype(BF)
    wait(grad_loads)


def pick_grads(experts, pick, prob, grads, *pieces):
    sent = mm(pick[...], grads[...]) * prob[...]
    for k in range(experts):
        pieces[k][...] = sent[k * MOST : (k + 1) * MOST].astype(BF)


def stacked(pieces):
    return jnp.concatenate([piece[...].astype(F32) for piece in pieces], axis=0)


def rows_of(half, own):
    core = lax.axis_index("ey") & 1
    return pl.ds(pl.multiple_of((core if own else 1 - core) * half, 128), half)


def place_rows(experts, capacity, pieces):
    me = lax.axis_index("ex")
    rows = experts * MOST
    got = stacked(pieces)
    full = got[:, :1] < EMPTY / 2
    key = []
    for dim in (0, 1):
        row = iota((rows, rows), dim)
        local_row = row - block_of(row, range(experts)) * MOST
        key.append((me ^ block_of(row, far_first(experts))) * MOST + local_row)
    earlier = jnp.where(key[1] < key[0], 1.0, 0.0).astype(BF)
    wide = jnp.broadcast_to(full, (rows, capacity))
    slot = mm(earlier, jnp.where(wide, 1.0, 0.0).astype(BF)).astype(jnp.int32)
    place = jnp.where((slot == iota((rows, capacity), 1)) & wide, 1.0, 0.0).astype(BF)
    return place, mm(place, got.astype(BF), ROWS).astype(BF)


def stage(far_count, gate_up, *refs):
    pieces, refs = refs[:far_count], refs[far_count:]
    held, pieces_out, sems = refs[:2], refs[2:-1], refs[-1]
    half = gate_up.shape[2] // 2
    loads = []
    for own, out in enumerate(held):
        for matrix in range(2):
            source = gate_up.at[0, matrix, rows_of(half, own == 1)]
            loads += cut(source, out.at[matrix], sems, len(loads), CUTS)
    run(loads)
    for source, target in zip(pieces, pieces_out):
        target[...] = source[...]
    wait(loads)


def load_down(down, own, out, sems):
    half = down.shape[1] // 2
    return run(cut(down.at[0, rows_of(half, own)], out, sems, 0, CUTS))


def other_pair(experts, capacity, *refs):
    held, down, near, out, place_out, rows_out, down_out, near_out, sems = refs[experts:]
    near_out[...] = near[...]
    loads = load_down(down, False, down_out, sems)
    place, rows_in = place_rows(experts, capacity, refs[:experts])
    place_out[...] = place
    rows_out[...] = rows_in
    for matrix in range(2):
        out[matrix] = mm(rows_in, held[matrix], LANES).astype(BF)
    wait(loads)


def mine_pair(rows_in, held, down, out, down_out, sems):
    loads = load_down(down, True, down_out, sems)
    for matrix in range(2):
        out[matrix] = mm(rows_in[...], held[matrix], LANES).astype(BF)
    wait(loads)


def pair_sum(mine, other, held_out, sent_out):
    held = mine[...].astype(F32) + other[...].astype(F32)
    held_out[...] = held
    sent_out[...] = held.astype(BF)


def act_part(experts, own, *refs):
    place, held = refs[experts : experts + 2]
    rows_grad = mm(place[...], stacked(refs[:experts]).astype(BF), ROWS).astype(BF)
    if own:
        refs[-2][...] = rows_grad
    refs[-1][...] = mm(rows_grad, held[...], LANES).astype(BF)


def gates(pair, pair_far, act_out, by_gate, by_up):
    gate_sum = pair[0] + pair_far[0].astype(F32)
    up_sum = pair[1] + pair_far[1].astype(F32)
    sigmoid_gate = jax.nn.sigmoid(gate_sum)
    silu_gate = gate_sum * sigmoid_gate
    act_out[...] = (silu_gate * up_sum).astype(BF)
    by_gate[...] = up_sum * sigmoid_gate * (1.0 + gate_sum * (1.0 - sigmoid_gate))
    by_up[...] = silu_gate


def grads_of(act, act_far, by_gate, by_up, _, out):
    grad_act = act[...] + act_far[...].astype(F32)
    out[0] = (grad_act * by_gate[...]).astype(BF)
    out[1] = (grad_act * by_up[...]).astype(BF)


def own_rows(mine, held, out):
    out[...] = mm(mine[0], held[0]) + mm(mine[1], held[1])


def other_rows(experts, total, other, place, held, *pieces):
    rows = total[...] + mm(other[0], held[0]) + mm(other[1], held[1])
    back = mm(place[...], rows.astype(BF))
    for k in range(experts):
        pieces[k][...] = back[k * MOST : (k + 1) * MOST].astype(BF)


def weight_grads(mine_act, other_act, mine, other, rows_in, rows_grad, pair_out, down_out, held, sems):
    core = lax.axis_index("ey") & 1
    half = mine_act.shape[1]
    step = half // 2
    stores = []
    for matrix in range(3):
        right = rows_grad[...] if matrix == 0 else rows_in[...]
        for own in range(2):
            start = (core if own else 1 - core) * half
            for part in range(2):
                columns = slice(part * step, (part + 1) * step)
                if matrix == 0:
                    left = (mine_act if own else other_act)[:, columns]
                else:
                    left = (mine if own else other)[matrix - 1, :, columns]
                at = len(stores)
                held[at] = mm(left, right, ROWS).astype(BF)
                rows = pl.ds(start + part * step, step)
                target = down_out.at[0, rows] if matrix == 0 else pair_out.at[0, matrix - 1, rows]
                store = pltpu.make_async_copy(held.at[at], target, sems.at[at])
                store.start()
                stores.append(store)
    for store in stores:
        store.wait()


def combine(experts, pick, *refs):
    out, held, sems = refs[experts:]
    home = stacked(refs[:experts]).astype(BF)
    rows = out.shape[0] // held.shape[0]
    stores = []
    for at in range(held.shape[0]):
        part = pick[:, at * rows : (at + 1) * rows]
        held[at] = mm(part, home, ROWS).astype(BF)
        target = out.at[pl.ds(at * rows, rows)]
        stores += run([pltpu.make_async_copy(held.at[at], target, sems.at[at])])
    wait(stores)


def far(value):
    return pltpu.with_memory_space_constraint(value, pltpu.HBM)


def swap(value, axis, bit):
    count = lax.axis_size(axis)
    return lax.ppermute(value, axis, [(i, i ^ bit) for i in range(count)])


def exchange(pieces, axis):
    order = far_first(len(pieces))
    return [swap(piece, axis, k) if k else piece for piece, k in zip(pieces, order)]


def local(inputs, grad_output, routes, gate_probs, gate_up, down_proj):
    experts = lax.axis_size("ex")
    ways = lax.axis_size("ey")
    tokens, width = inputs.shape
    hidden = gate_up.shape[2]
    half = hidden // 2
    capacity = 5 * tokens * experts * routes.shape[1] // (4 * EXPERTS)
    rows = experts * MOST
    weight_bytes = hidden * width * 2
    weight_flops = 2 * capacity * hidden * width
    sds = jax.ShapeDtypeStruct
    piece = [sds((MOST, width), BF)] * experts
    dma = lambda count: pltpu.SemaphoreType.DMA((count,))

    order = far_first(experts)
    far_count = experts - 2
    pick, prob, grads, *send_in = call(
        functools.partial(pick_inputs, experts),
        [
            sds((rows, tokens), BF),
            sds((rows, 1), F32),
            pltpu.VMEM((tokens, width), BF),
        ]
        + piece,
        (far(routes.T), far(gate_probs.T), far(inputs), far(grad_output)),
        [HBM] * 4,
        [
            pltpu.VMEM(routes.shape[::-1], jnp.int32),
            pltpu.VMEM(routes.shape[::-1], BF),
            pltpu.VMEM((tokens, width), BF),
            dma(10),
        ],
        flops=2 * rows * tokens * width,
        traffic=4 * tokens * width,
    )
    send_grad = call(
        functools.partial(pick_grads, experts),
        piece,
        (pick, prob, grads),
        [VMEM] * 3,
        flops=2 * rows * tokens * width,
        traffic=2 * tokens * width,
    )
    got_in = exchange(send_in, "ex")
    held_other, held_mine, *far_grad = call(
        functools.partial(stage, far_count),
        [pltpu.VMEM((2, half, width), BF)] * 2 + piece[2:],
        (far(gate_up), *send_grad[:far_count]),
        [HBM] + [VMEM] * far_count,
        [dma(4 * CUTS)],
        flops=WCOST * weight_flops,
        traffic=WCOST * weight_bytes,
    )
    got_grad = [swap(far_grad[at], "ex", order[at]) for at in range(far_count)]

    down_half = pltpu.VMEM((half, width), BF)
    pair_other, place, rows_in, down_other, near_grad = call(
        functools.partial(other_pair, experts, capacity),
        [sds((2, capacity, half), BF), sds((rows, capacity), BF), sds((capacity, width), BF)]
        + [down_half, piece[0]],
        (*got_in, held_other, far(down_proj), send_grad[-2]),
        [VMEM] * (experts + 1) + [HBM, VMEM],
        [dma(CUTS)],
        flops=2 * weight_flops,
        traffic=weight_bytes,
    )
    pair_mine, down_mine = call(
        mine_pair,
        [sds((2, capacity, half), BF), down_half],
        (rows_in, held_mine, far(down_proj)),
        [VMEM] * 2 + [HBM],
        [dma(CUTS)],
        flops=C2COST * weight_flops,
        traffic=C2COST * weight_bytes,
    )

    def total(held, sent):
        bit = 2
        while bit * 2 < ways:
            held = held + swap(sent, "ey", bit).astype(F32)
            sent = held.astype(BF)
            bit *= 2
        return held, swap(sent, "ey", bit)

    pair, pair_sent = call(
        pair_sum,
        [sds((2, capacity, half), F32), sds((2, capacity, half), BF)],
        (pair_mine, swap(pair_other, "ey", 1)),
        [VMEM] * 2,
        traffic=10 * capacity * hidden,
    )
    pair, pair_far = total(pair, pair_sent)
    got_grad = got_grad + [swap(near_grad, "ex", 1), send_grad[-1]]

    def act_of(own, held, outs, tied, cost):
        return call(
            functools.partial(act_part, experts, own),
            outs + [sds((capacity, half), BF)],
            (*got_grad, place, held, *tied),
            [VMEM] * (experts + 2) + [ANY] * len(tied),
            flops=cost * weight_flops,
            traffic=cost * weight_bytes,
        )

    (act_other,) = act_of(False, down_other, [], [pair_sent], D1COST)
    rows_grad, act_mine = act_of(True, down_mine, [sds((capacity, width), BF)], [], D2COST)
    act = act_mine.astype(F32) + swap(act_other, "ey", 1).astype(F32)
    act, act_far = total(act, act.astype(BF))
    mine_act, by_gate, by_up = call(
        gates,
        [sds((capacity, half), BF)] + [sds((capacity, half), F32)] * 2,
        (pair, pair_far),
        [VMEM] * 2,
        traffic=18 * capacity * half,
        flops=GFLOP * weight_flops,
    )
    other_act = swap(mine_act, "ey", 1)
    mine = call(
        grads_of,
        sds((2, capacity, half), BF),
        (act, act_far, by_gate, by_up, other_act),
        [VMEM] * 4 + [ANY],
        traffic=18 * capacity * half,
    )
    other = swap(mine, "ey", 1)
    own = call(
        own_rows,
        sds((capacity, width), F32),
        (mine, held_mine),
        [VMEM] * 2,
        flops=weight_flops,
        traffic=weight_bytes,
    )
    back = call(
        functools.partial(other_rows, experts),
        piece,
        (own, other, place, held_other),
        [VMEM] * 4,
        flops=weight_flops,
        traffic=weight_bytes,
    )
    home = exchange(back, "ex")
    pair_grad, down_grad = call(
        weight_grads,
        [sds((1, 2, hidden, width), BF), sds((1, hidden, width), BF)],
        (mine_act, other_act, mine, other, rows_in, rows_grad),
        [VMEM] * 6,
        [pltpu.VMEM((12, half // 2, width), BF), dma(12)],
        limit=24,
        flops=3 * weight_flops,
        traffic=3 * weight_bytes,
        out_specs=[ANY, ANY],
    )
    grad_inputs = call(
        functools.partial(combine, experts),
        sds((tokens, width), BF),
        (pick, *home),
        [VMEM] * (experts + 1),
        [pltpu.VMEM((2, tokens // 2, width), BF), dma(2)],
        flops=2 * rows * tokens * width,
        traffic=4 * tokens * width,
        out_specs=ANY,
    )
    return (grad_inputs, pair_grad, down_grad)


def solution(mesh):
    return jax.shard_map(
        local,
        mesh=mesh,
        in_specs=(
            P(("groups", "ex"), "ey"),
            P(("groups", "ex"), "ey"),
            P(("groups", "ex"), None),
            P(("groups", "ex"), None),
            P("ex", None, None, "ey"),
            P("ex", None, "ey"),
        ),
        out_specs=(
            P(("groups", "ex"), "ey"),
            P("ex", "groups", None, "ey"),
            P("ex", "groups", "ey"),
        ),
        check_vma=False,
    )
```

```python
import functools

import jax
import jax.numpy as jnp
from jax import lax
from jax.experimental import pallas as pl
from jax.experimental.pallas import tpu as pltpu
from jax.sharding import PartitionSpec as P

MOST = 40
EXPERTS = 128
EMPTY = 64.0
BF = jnp.bfloat16
F32 = jnp.float32
MIB = 1 << 20
C2COST = 100
WCOST = 100
GFLOP = 100
D1COST = 1
D2COST = 100
VMEM = pl.BlockSpec(memory_space=pltpu.VMEM)
ANY = pl.BlockSpec(memory_space=pl.ANY)
HBM = pl.BlockSpec(memory_space=pltpu.HBM)
ROWS = (((0,), (0,)), ((), ()))
LANES = (((1,), (1,)), ((), ()))
PLAIN = (((1,), (0,)), ((), ()))


def mm(left, right, dims=PLAIN):
    return lax.dot_general(left, right, dims, preferred_element_type=F32)


def iota(shape, dim):
    return lax.broadcasted_iota(jnp.int32, shape, dim)


def far_first(count):
    return sorted(range(count), key=lambda k: (-k.bit_length(), k))


def farthest_first(count):
    return list(reversed(range(count)))


def cut(source, target, sems, first, pieces):
    rows = target.shape[-2] // pieces
    out = []
    for at in range(pieces):
        part = pl.ds(at * rows, rows)
        out.append(pltpu.make_async_copy(source.at[part], target.at[part], sems.at[first + at]))
    return out


def run(loads):
    for load in loads:
        load.start()
    return loads


def wait(loads):
    for load in loads:
        load.wait()


def block_of(position, names):
    found = jnp.full_like(position, names[0])
    for at in range(1, len(names)):
        found = found + (position >= at * MOST).astype(jnp.int32) * (names[at] - names[at - 1])
    return found


def call(body, outs, operands, specs, scratch=(), limit=16, flops=0, traffic=0, out_specs=None):
    return pl.pallas_call(
        body,
        out_shape=outs,
        in_specs=specs,
        out_specs=out_specs if out_specs is not None else jax.tree.map(lambda _: VMEM, outs),
        scratch_shapes=list(scratch),
        compiler_params=pltpu.CompilerParams(vmem_limit_bytes=limit * MIB),
        cost_estimate=pl.CostEstimate(flops=flops, bytes_accessed=traffic, transcendentals=0),
    )(*operands)


def pick_inputs(experts, routes_in, probs_in, inputs, grads, pick_out, prob_out, grads_out, *refs):
    *pieces, routes, probs, held, sems = refs
    loads = run(
        [
            pltpu.make_async_copy(routes_in, routes, sems.at[0]),
            pltpu.make_async_copy(probs_in, probs, sems.at[1]),
        ]
    )
    input_loads = run(cut(inputs, held, sems, 2, 1))
    grad_loads = run(cut(grads, grads_out, sems, 3, 1))
    me = lax.axis_index("ex")
    tokens = inputs.shape[0]
    rows = experts * MOST
    order = far_first(experts)
    owner = block_of(iota((rows, routes.shape[0]), 0), order)
    named = jnp.zeros((rows, tokens), F32)
    weight = jnp.zeros((rows, tokens), F32)
    earlier = iota((tokens, tokens), 0) < iota((tokens, tokens), 1)
    earlier = jnp.where(earlier, 1.0, 0.0).astype(BF)
    row = iota((rows, tokens), 0)
    slot = row - block_of(row, range(experts)) * MOST
    wait(loads)
    chosen = routes[...]
    wide = probs[...].astype(F32)
    for k in range(experts):
        spread = jnp.where(owner == k, 1.0, 0.0).astype(BF)
        hit = chosen == (me ^ k)
        named = named + mm(spread, jnp.where(hit, 1.0, 0.0).astype(BF))
        weight = weight + mm(spread, jnp.where(hit, wide, 0.0).astype(BF))
    rank = mm(named.astype(BF), earlier).astype(jnp.int32)
    picks = (rank == slot) & (named > 0.5)
    pick = jnp.where(picks, 1.0, 0.0)
    filled = jnp.max(pick, axis=1, keepdims=True) > 0.5
    pick = pick.astype(BF)
    pick_out[...] = pick
    prob_out[...] = jnp.sum(jnp.where(picks, weight, 0.0), axis=1, keepdims=True)
    wait(input_loads)
    sent = jnp.where(filled, mm(pick, held[...]), EMPTY)
    for k in range(experts):
        pieces[k][...] = sent[k * MOST : (k + 1) * MOST].astype(BF)
    wait(grad_loads)


def pick_grads(experts, pick, prob, grads, *pieces):
    sent = mm(pick[...], grads[...]) * prob[...]
    for k in range(experts):
        pieces[k][...] = sent[k * MOST : (k + 1) * MOST].astype(BF)


def stacked(pieces):
    return jnp.concatenate([piece[...].astype(F32) for piece in pieces], axis=0)


def rows_of(half, own):
    core = lax.axis_index("ey") & 1
    return pl.ds(pl.multiple_of((core if own else 1 - core) * half, 128), half)


def place_rows(experts, capacity, pieces):
    me = lax.axis_index("ex")
    rows = experts * MOST
    got = stacked(pieces)
    full = got[:, :1] < EMPTY / 2
    key = []
    for dim in (0, 1):
        row = iota((rows, rows), dim)
        local_row = row - block_of(row, range(experts)) * MOST
        key.append((me ^ block_of(row, far_first(experts))) * MOST + local_row)
    earlier = jnp.where(key[1] < key[0], 1.0, 0.0).astype(BF)
    wide = jnp.broadcast_to(full, (rows, capacity))
    slot = mm(earlier, jnp.where(wide, 1.0, 0.0).astype(BF)).astype(jnp.int32)
    place = jnp.where((slot == iota((rows, capacity), 1)) & wide, 1.0, 0.0).astype(BF)
    return place, mm(place, got.astype(BF), ROWS).astype(BF)


def stage(count, gate_up, down, *refs):
    pieces, refs = refs[:count], refs[count:]
    held, pieces_out, sems = refs[:2], refs[2:-1], refs[-1]
    half = down.shape[1] // 2
    loads = []
    for own, out in enumerate(held):
        rows = rows_of(half, own == 1)
        for matrix in range(3):
            source = down.at[0, rows] if matrix == 2 else gate_up.at[0, matrix, rows]
            loads.append(pltpu.make_async_copy(source, out.at[matrix], sems.at[len(loads)]))
    run(loads)
    for source, target in zip(pieces, pieces_out):
        target[...] = source[...]
    wait(loads)


def other_pair(experts, capacity, *refs):
    held, out, place_out, rows_out = refs[experts:]
    place, rows_in = place_rows(experts, capacity, refs[:experts])
    place_out[...] = place
    rows_out[...] = rows_in
    for matrix in range(2):
        out[matrix] = mm(rows_in, held[matrix], LANES).astype(BF)


def mine_pair(rows_in, held, out):
    for matrix in range(2):
        out[matrix] = mm(rows_in[...], held[matrix], LANES).astype(BF)


def pair_sum(mine, other, held_out, sent_out):
    held = mine[...].astype(F32) + other[...].astype(F32)
    held_out[...] = held
    sent_out[...] = held.astype(BF)


def act_part(experts, own, *refs):
    place, held = refs[experts : experts + 2]
    order = far_first(experts)
    pieces = [refs[:experts][farthest_first(experts).index(k)] for k in order]
    rows_grad = mm(place[...], stacked(pieces).astype(BF), ROWS).astype(BF)
    if own:
        refs[-2][...] = rows_grad
    refs[-1][...] = mm(rows_grad, held[2], LANES).astype(BF)


def gates(pair, pair_far, act_out, by_gate, by_up):
    gate_sum = pair[0] + pair_far[0].astype(F32)
    up_sum = pair[1] + pair_far[1].astype(F32)
    sigmoid_gate = jax.nn.sigmoid(gate_sum)
    silu_gate = gate_sum * sigmoid_gate
    act_out[...] = (silu_gate * up_sum).astype(BF)
    by_gate[...] = up_sum * sigmoid_gate * (1.0 + gate_sum * (1.0 - sigmoid_gate))
    by_up[...] = silu_gate


def grads_of(act, act_far, by_gate, by_up, _, out):
    grad_act = act[...] + act_far[...].astype(F32)
    out[0] = (grad_act * by_gate[...]).astype(BF)
    out[1] = (grad_act * by_up[...]).astype(BF)


def own_rows(mine, held, out):
    out[...] = mm(mine[0], held[0]) + mm(mine[1], held[1])


def other_rows(experts, total, other, place, held, *pieces):
    rows = total[...] + mm(other[0], held[0]) + mm(other[1], held[1])
    back = mm(place[...], rows.astype(BF))
    for k in range(experts):
        pieces[k][...] = back[k * MOST : (k + 1) * MOST].astype(BF)


def weight_grads(mine_act, other_act, mine, other, rows_in, rows_grad, pair_out, down_out, held, sems):
    core = lax.axis_index("ey") & 1
    half = mine_act.shape[1]
    step = half // 2
    stores = []
    for matrix in range(3):
        right = rows_grad[...] if matrix == 0 else rows_in[...]
        for own in range(2):
            start = (core if own else 1 - core) * half
            for part in range(2):
                columns = slice(part * step, (part + 1) * step)
                if matrix == 0:
                    left = (mine_act if own else other_act)[:, columns]
                else:
                    left = (mine if own else other)[matrix - 1, :, columns]
                at = len(stores)
                held[at] = mm(left, right, ROWS).astype(BF)
                rows = pl.ds(start + part * step, step)
                target = down_out.at[0, rows] if matrix == 0 else pair_out.at[0, matrix - 1, rows]
                store = pltpu.make_async_copy(held.at[at], target, sems.at[at])
                store.start()
                stores.append(store)
    for store in stores:
        store.wait()


def combine(experts, pick, *refs):
    out, held, sems = refs[experts:]
    home = stacked(refs[:experts]).astype(BF)
    rows = out.shape[0] // held.shape[0]
    stores = []
    for at in range(held.shape[0]):
        part = pick[:, at * rows : (at + 1) * rows]
        held[at] = mm(part, home, ROWS).astype(BF)
        target = out.at[pl.ds(at * rows, rows)]
        stores += run([pltpu.make_async_copy(held.at[at], target, sems.at[at])])
    wait(stores)


def far(value):
    return pltpu.with_memory_space_constraint(value, pltpu.HBM)


def swap(value, axis, bit):
    count = lax.axis_size(axis)
    return lax.ppermute(value, axis, [(i, i ^ bit) for i in range(count)])


def exchange(pieces, axis):
    order = far_first(len(pieces))
    return [swap(piece, axis, k) if k else piece for piece, k in zip(pieces, order)]


def local(inputs, grad_output, routes, gate_probs, gate_up, down_proj):
    experts = lax.axis_size("ex")
    ways = lax.axis_size("ey")
    tokens, width = inputs.shape
    hidden = gate_up.shape[2]
    half = hidden // 2
    capacity = 5 * tokens * experts * routes.shape[1] // (4 * EXPERTS)
    rows = experts * MOST
    weight_bytes = hidden * width * 2
    weight_flops = 2 * capacity * hidden * width
    sds = jax.ShapeDtypeStruct
    piece = [sds((MOST, width), BF)] * experts
    dma = lambda count: pltpu.SemaphoreType.DMA((count,))

    order = far_first(experts)
    pick, prob, grads, *send_in = call(
        functools.partial(pick_inputs, experts),
        [
            sds((rows, tokens), BF),
            sds((rows, 1), F32),
            pltpu.VMEM((tokens, width), BF),
        ]
        + piece,
        (far(routes.T), far(gate_probs.T), far(inputs), far(grad_output)),
        [HBM] * 4,
        [
            pltpu.VMEM(routes.shape[::-1], jnp.int32),
            pltpu.VMEM(routes.shape[::-1], BF),
            pltpu.VMEM((tokens, width), BF),
            dma(4),
        ],
        flops=2 * rows * tokens * width,
        traffic=4 * tokens * width,
    )
    send_grad = call(
        functools.partial(pick_grads, experts),
        piece,
        (pick, prob, grads),
        [VMEM] * 3,
        flops=2 * rows * tokens * width,
        traffic=2 * tokens * width,
    )
    got_in = exchange(send_in, "ex")
    held_other, held_mine, *send_grad = call(
        functools.partial(stage, experts),
        [pltpu.VMEM((3, half, width), BF)] * 2 + piece,
        (far(gate_up), far(down_proj), *send_grad),
        [HBM] * 2 + [VMEM] * experts,
        [dma(6)],
        flops=WCOST * weight_flops,
        traffic=WCOST * weight_bytes,
    )
    got_grad = [
        swap(send_grad[order.index(k)], "ex", k) if k else send_grad[-1]
        for k in farthest_first(experts)
    ]
    pair_other, place, rows_in = call(
        functools.partial(other_pair, experts, capacity),
        [sds((2, capacity, half), BF), sds((rows, capacity), BF), sds((capacity, width), BF)],
        (*got_in, held_other),
        [VMEM] * (experts + 1),
        flops=2 * weight_flops,
        traffic=weight_bytes,
    )
    pair_mine = call(
        mine_pair,
        sds((2, capacity, half), BF),
        (rows_in, held_mine),
        [VMEM] * 2,
        flops=C2COST * weight_flops,
        traffic=C2COST * weight_bytes,
    )

    def total(held, sent):
        bit = 2
        while bit * 2 < ways:
            held = held + swap(sent, "ey", bit).astype(F32)
            sent = held.astype(BF)
            bit *= 2
        return held, swap(sent, "ey", bit)

    pair, pair_sent = call(
        pair_sum,
        [sds((2, capacity, half), F32), sds((2, capacity, half), BF)],
        (pair_mine, swap(pair_other, "ey", 1)),
        [VMEM] * 2,
        traffic=10 * capacity * hidden,
    )
    pair, pair_far = total(pair, pair_sent)
    def act_of(own, held, outs, tied, cost):
        return call(
            functools.partial(act_part, experts, own),
            outs + [sds((capacity, half), BF)],
            (*got_grad, place, held, *tied),
            [VMEM] * (experts + 2) + [ANY] * len(tied),
            flops=cost * weight_flops,
            traffic=cost * weight_bytes,
        )

    (act_other,) = act_of(False, held_other, [], [pair_sent], D1COST)
    rows_grad, act_mine = act_of(True, held_mine, [sds((capacity, width), BF)], [], D2COST)
    act = act_mine.astype(F32) + swap(act_other, "ey", 1).astype(F32)
    act, act_far = total(act, act.astype(BF))
    mine_act, by_gate, by_up = call(
        gates,
        [sds((capacity, half), BF)] + [sds((capacity, half), F32)] * 2,
        (pair, pair_far),
        [VMEM] * 2,
        traffic=18 * capacity * half,
        flops=GFLOP * weight_flops,
    )
    other_act = swap(mine_act, "ey", 1)
    mine = call(
        grads_of,
        sds((2, capacity, half), BF),
        (act, act_far, by_gate, by_up, other_act),
        [VMEM] * 4 + [ANY],
        traffic=18 * capacity * half,
    )
    other = swap(mine, "ey", 1)
    own = call(
        own_rows,
        sds((capacity, width), F32),
        (mine, held_mine),
        [VMEM] * 2,
        flops=weight_flops,
        traffic=weight_bytes,
    )
    back = call(
        functools.partial(other_rows, experts),
        piece,
        (own, other, place, held_other),
        [VMEM] * 4,
        flops=weight_flops,
        traffic=weight_bytes,
    )
    home = exchange(back, "ex")
    pair_grad, down_grad = call(
        weight_grads,
        [sds((1, 2, hidden, width), BF), sds((1, hidden, width), BF)],
        (mine_act, other_act, mine, other, rows_in, rows_grad),
        [VMEM] * 6,
        [pltpu.VMEM((12, half // 2, width), BF), dma(12)],
        limit=24,
        flops=3 * weight_flops,
        traffic=3 * weight_bytes,
        out_specs=[ANY, ANY],
    )
    grad_inputs = call(
        functools.partial(combine, experts),
        sds((tokens, width), BF),
        (pick, *home),
        [VMEM] * (experts + 1),
        [pltpu.VMEM((2, tokens // 2, width), BF), dma(2)],
        flops=2 * rows * tokens * width,
        traffic=4 * tokens * width,
        out_specs=ANY,
    )
    return (grad_inputs, pair_grad, down_grad)


def solution(mesh):
    return jax.shard_map(
        local,
        mesh=mesh,
        in_specs=(
            P(("groups", "ex"), "ey"),
            P(("groups", "ex"), "ey"),
            P(("groups", "ex"), None),
            P(("groups", "ex"), None),
            P("ex", None, None, "ey"),
            P("ex", None, "ey"),
        ),
        out_specs=(
            P(("groups", "ex"), "ey"),
            P("ex", "groups", None, "ey"),
            P("ex", "groups", "ey"),
        ),
        check_vma=False,
    )
```

```python
import functools

import jax
import jax.numpy as jnp
from jax import lax
from jax.experimental import pallas as pl
from jax.experimental.pallas import tpu as pltpu
from jax.sharding import PartitionSpec as P

MOST = 40
EXPERTS = 128
EMPTY = 64.0
BF = jnp.bfloat16
F32 = jnp.float32
MIB = 1 << 20
C2COST = 100
WCOST = 100
GFLOP = 100
D1COST = 1
D2COST = 100
VMEM = pl.BlockSpec(memory_space=pltpu.VMEM)
ANY = pl.BlockSpec(memory_space=pl.ANY)
HBM = pl.BlockSpec(memory_space=pltpu.HBM)
ROWS = (((0,), (0,)), ((), ()))
LANES = (((1,), (1,)), ((), ()))
PLAIN = (((1,), (0,)), ((), ()))


def mm(left, right, dims=PLAIN):
    return lax.dot_general(left, right, dims, preferred_element_type=F32)


def iota(shape, dim):
    return lax.broadcasted_iota(jnp.int32, shape, dim)


def far_first(count):
    return sorted(range(count), key=lambda k: (-k.bit_length(), k))


def farthest_first(count):
    return list(reversed(range(count)))


def cut(source, target, sems, first, pieces):
    rows = target.shape[-2] // pieces
    out = []
    for at in range(pieces):
        part = pl.ds(at * rows, rows)
        out.append(pltpu.make_async_copy(source.at[part], target.at[part], sems.at[first + at]))
    return out


def run(loads):
    for load in loads:
        load.start()
    return loads


def wait(loads):
    for load in loads:
        load.wait()


def block_of(position, names):
    found = jnp.full_like(position, names[0])
    for at in range(1, len(names)):
        found = found + (position >= at * MOST).astype(jnp.int32) * (names[at] - names[at - 1])
    return found


def call(body, outs, operands, specs, scratch=(), limit=16, flops=0, traffic=0, out_specs=None):
    return pl.pallas_call(
        body,
        out_shape=outs,
        in_specs=specs,
        out_specs=out_specs if out_specs is not None else jax.tree.map(lambda _: VMEM, outs),
        scratch_shapes=list(scratch),
        compiler_params=pltpu.CompilerParams(vmem_limit_bytes=limit * MIB),
        cost_estimate=pl.CostEstimate(flops=flops, bytes_accessed=traffic, transcendentals=0),
    )(*operands)


def pick_inputs(experts, routes_in, probs_in, inputs, grads, pick_out, prob_out, grads_out, *refs):
    *pieces, routes, probs, held, sems = refs
    loads = run(
        [
            pltpu.make_async_copy(routes_in, routes, sems.at[0]),
            pltpu.make_async_copy(probs_in, probs, sems.at[1]),
        ]
    )
    input_loads = run(cut(inputs, held, sems, 2, 1))
    grad_loads = run(cut(grads, grads_out, sems, 3, 1))
    me = lax.axis_index("ex")
    tokens = inputs.shape[0]
    rows = experts * MOST
    order = far_first(experts)
    owner = block_of(iota((rows, routes.shape[0]), 0), order)
    named = jnp.zeros((rows, tokens), F32)
    weight = jnp.zeros((rows, tokens), F32)
    earlier = iota((tokens, tokens), 0) < iota((tokens, tokens), 1)
    earlier = jnp.where(earlier, 1.0, 0.0).astype(BF)
    row = iota((rows, tokens), 0)
    slot = row - block_of(row, range(experts)) * MOST
    wait(loads)
    chosen = routes[...]
    wide = probs[...].astype(F32)
    for k in range(experts):
        spread = jnp.where(owner == k, 1.0, 0.0).astype(BF)
        hit = chosen == (me ^ k)
        named = named + mm(spread, jnp.where(hit, 1.0, 0.0).astype(BF))
        weight = weight + mm(spread, jnp.where(hit, wide, 0.0).astype(BF))
    rank = mm(named.astype(BF), earlier).astype(jnp.int32)
    picks = (rank == slot) & (named > 0.5)
    pick = jnp.where(picks, 1.0, 0.0)
    filled = jnp.max(pick, axis=1, keepdims=True) > 0.5
    pick = pick.astype(BF)
    pick_out[...] = pick
    prob_out[...] = jnp.sum(jnp.where(picks, weight, 0.0), axis=1, keepdims=True)
    wait(input_loads)
    sent = jnp.where(filled, mm(pick, held[...]), EMPTY)
    for k in range(experts):
        pieces[k][...] = sent[k * MOST : (k + 1) * MOST].astype(BF)
    wait(grad_loads)


def pick_grads(experts, pick, prob, grads, *pieces):
    sent = mm(pick[...], grads[...]) * prob[...]
    for k in range(experts):
        pieces[k][...] = sent[k * MOST : (k + 1) * MOST].astype(BF)


def stacked(pieces):
    return jnp.concatenate([piece[...].astype(F32) for piece in pieces], axis=0)


def rows_of(half, own):
    core = lax.axis_index("ey") & 1
    return pl.ds(pl.multiple_of((core if own else 1 - core) * half, 128), half)


def place_rows(experts, capacity, pieces):
    me = lax.axis_index("ex")
    rows = experts * MOST
    got = stacked(pieces)
    full = got[:, :1] < EMPTY / 2
    key = []
    for dim in (0, 1):
        row = iota((rows, rows), dim)
        local_row = row - block_of(row, range(experts)) * MOST
        key.append((me ^ block_of(row, far_first(experts))) * MOST + local_row)
    earlier = jnp.where(key[1] < key[0], 1.0, 0.0).astype(BF)
    wide = jnp.broadcast_to(full, (rows, capacity))
    slot = mm(earlier, jnp.where(wide, 1.0, 0.0).astype(BF)).astype(jnp.int32)
    place = jnp.where((slot == iota((rows, capacity), 1)) & wide, 1.0, 0.0).astype(BF)
    return place, mm(place, got.astype(BF), ROWS).astype(BF)


def stage(count, gate_up, down, *refs):
    pieces, refs = refs[:count], refs[count:]
    held, pieces_out, sems = refs[:2], refs[2:-1], refs[-1]
    half = down.shape[1] // 2
    loads = []
    for own, out in enumerate(held):
        rows = rows_of(half, own == 1)
        for matrix in range(3):
            source = down.at[0, rows] if matrix == 2 else gate_up.at[0, matrix, rows]
            loads.append(pltpu.make_async_copy(source, out.at[matrix], sems.at[len(loads)]))
    run(loads)
    for source, target in zip(pieces, pieces_out):
        target[...] = source[...]
    wait(loads)


def other_pair(experts, capacity, *refs):
    held, out, place_out, rows_out = refs[experts:]
    place, rows_in = place_rows(experts, capacity, refs[:experts])
    place_out[...] = place
    rows_out[...] = rows_in
    for matrix in range(2):
        out[matrix] = mm(rows_in, held[matrix], LANES).astype(BF)


def mine_pair(rows_in, held, out):
    for matrix in range(2):
        out[matrix] = mm(rows_in[...], held[matrix], LANES).astype(BF)


def pair_sum(mine, other, held_out, sent_out):
    held = mine[...].astype(F32) + other[...].astype(F32)
    held_out[...] = held
    sent_out[...] = held.astype(BF)


def act_part(experts, own, *refs):
    place, held = refs[experts : experts + 2]
    order = far_first(experts)
    pieces = [refs[:experts][farthest_first(experts).index(k)] for k in order]
    rows_grad = mm(place[...], stacked(pieces).astype(BF), ROWS).astype(BF)
    if own:
        refs[-2][...] = rows_grad
    refs[-1][...] = mm(rows_grad, held[2], LANES).astype(BF)


def gates(pair, pair_far, act_out, by_gate, by_up):
    gate_sum = pair[0] + pair_far[0].astype(F32)
    up_sum = pair[1] + pair_far[1].astype(F32)
    sigmoid_gate = jax.nn.sigmoid(gate_sum)
    silu_gate = gate_sum * sigmoid_gate
    act_out[...] = (silu_gate * up_sum).astype(BF)
    by_gate[...] = up_sum * sigmoid_gate * (1.0 + gate_sum * (1.0 - sigmoid_gate))
    by_up[...] = silu_gate


def grads_of(act, act_far, by_gate, by_up, _, out):
    grad_act = act[...] + act_far[...].astype(F32)
    out[0] = (grad_act * by_gate[...]).astype(BF)
    out[1] = (grad_act * by_up[...]).astype(BF)


def own_rows(mine, held, out):
    out[...] = mm(mine[0], held[0]) + mm(mine[1], held[1])


def other_rows(experts, total, other, place, held, *refs):
    pieces, whole = refs[:experts], refs[experts]
    rows = total[...] + mm(other[0], held[0]) + mm(other[1], held[1])
    whole[...] = mm(place[...], rows.astype(BF))
    me = lax.axis_index("ex")
    for piece, step in zip(pieces, shifts(experts)):
        piece[...] = whole[place_of(lax.rem(me + step, experts), experts)].astype(BF)


def weight_grads(mine_act, other_act, mine, other, rows_in, rows_grad, pair_out, down_out, held, sems):
    core = lax.axis_index("ey") & 1
    half = mine_act.shape[1]
    step = half // 2
    stores = []
    for matrix in range(3):
        right = rows_grad[...] if matrix == 0 else rows_in[...]
        for own in range(2):
            start = (core if own else 1 - core) * half
            for part in range(2):
                columns = slice(part * step, (part + 1) * step)
                if matrix == 0:
                    left = (mine_act if own else other_act)[:, columns]
                else:
                    left = (mine if own else other)[matrix - 1, :, columns]
                at = len(stores)
                held[at] = mm(left, right, ROWS).astype(BF)
                rows = pl.ds(start + part * step, step)
                target = down_out.at[0, rows] if matrix == 0 else pair_out.at[0, matrix - 1, rows]
                store = pltpu.make_async_copy(held.at[at], target, sems.at[at])
                store.start()
                stores.append(store)
    for store in stores:
        store.wait()


def combine(experts, pick, *refs):
    out, whole, held, sems = refs[experts:]
    me = lax.axis_index("ex")
    for piece, step in zip(refs[:experts], shifts(experts)):
        whole[place_of(lax.rem(me + experts - step, experts), experts)] = piece[...].astype(F32)
    home = whole[...].astype(BF)
    rows = out.shape[0] // held.shape[0]
    stores = []
    for at in range(held.shape[0]):
        part = pick[:, at * rows : (at + 1) * rows]
        held[at] = mm(part, home, ROWS).astype(BF)
        target = out.at[pl.ds(at * rows, rows)]
        stores += run([pltpu.make_async_copy(held.at[at], target, sems.at[at])])
    wait(stores)


def far(value):
    return pltpu.with_memory_space_constraint(value, pltpu.HBM)


def place_of(partner, experts):
    k = lax.axis_index("ex") ^ partner
    spot = jnp.int32(0)
    for at, name in enumerate(far_first(experts)):
        spot = spot + jnp.where(k == name, at * MOST, 0)
    return pl.ds(pl.multiple_of(spot, 8), MOST)


def shifts(experts):
    return list(range(1, experts)) + [0]


def shift(value, axis, step):
    count = lax.axis_size(axis)
    return lax.ppermute(value, axis, [(i, (i + step) % count) for i in range(count)])


def swap(value, axis, bit):
    count = lax.axis_size(axis)
    return lax.ppermute(value, axis, [(i, i ^ bit) for i in range(count)])


def exchange(pieces, axis):
    order = far_first(len(pieces))
    return [swap(piece, axis, k) if k else piece for piece, k in zip(pieces, order)]


def local(inputs, grad_output, routes, gate_probs, gate_up, down_proj):
    experts = lax.axis_size("ex")
    ways = lax.axis_size("ey")
    tokens, width = inputs.shape
    hidden = gate_up.shape[2]
    half = hidden // 2
    capacity = 5 * tokens * experts * routes.shape[1] // (4 * EXPERTS)
    rows = experts * MOST
    weight_bytes = hidden * width * 2
    weight_flops = 2 * capacity * hidden * width
    sds = jax.ShapeDtypeStruct
    piece = [sds((MOST, width), BF)] * experts
    dma = lambda count: pltpu.SemaphoreType.DMA((count,))

    order = far_first(experts)
    pick, prob, grads, *send_in = call(
        functools.partial(pick_inputs, experts),
        [
            sds((rows, tokens), BF),
            sds((rows, 1), F32),
            pltpu.VMEM((tokens, width), BF),
        ]
        + piece,
        (far(routes.T), far(gate_probs.T), far(inputs), far(grad_output)),
        [HBM] * 4,
        [
            pltpu.VMEM(routes.shape[::-1], jnp.int32),
            pltpu.VMEM(routes.shape[::-1], BF),
            pltpu.VMEM((tokens, width), BF),
            dma(4),
        ],
        flops=2 * rows * tokens * width,
        traffic=4 * tokens * width,
    )
    send_grad = call(
        functools.partial(pick_grads, experts),
        piece,
        (pick, prob, grads),
        [VMEM] * 3,
        flops=2 * rows * tokens * width,
        traffic=2 * tokens * width,
    )
    got_in = exchange(send_in, "ex")
    held_other, held_mine, *send_grad = call(
        functools.partial(stage, experts),
        [pltpu.VMEM((3, half, width), BF)] * 2 + piece,
        (far(gate_up), far(down_proj), *send_grad),
        [HBM] * 2 + [VMEM] * experts,
        [dma(6)],
        flops=WCOST * weight_flops,
        traffic=WCOST * weight_bytes,
    )
    got_grad = [
        swap(send_grad[order.index(k)], "ex", k) if k else send_grad[-1]
        for k in farthest_first(experts)
    ]
    pair_other, place, rows_in = call(
        functools.partial(other_pair, experts, capacity),
        [sds((2, capacity, half), BF), sds((rows, capacity), BF), sds((capacity, width), BF)],
        (*got_in, held_other),
        [VMEM] * (experts + 1),
        flops=2 * weight_flops,
        traffic=weight_bytes,
    )
    pair_mine = call(
        mine_pair,
        sds((2, capacity, half), BF),
        (rows_in, held_mine),
        [VMEM] * 2,
        flops=C2COST * weight_flops,
        traffic=C2COST * weight_bytes,
    )

    def total(held, sent):
        bit = 2
        while bit * 2 < ways:
            held = held + swap(sent, "ey", bit).astype(F32)
            sent = held.astype(BF)
            bit *= 2
        return held, swap(sent, "ey", bit)

    pair, pair_sent = call(
        pair_sum,
        [sds((2, capacity, half), F32), sds((2, capacity, half), BF)],
        (pair_mine, swap(pair_other, "ey", 1)),
        [VMEM] * 2,
        traffic=10 * capacity * hidden,
    )
    pair, pair_far = total(pair, pair_sent)
    def act_of(own, held, outs, tied, cost):
        return call(
            functools.partial(act_part, experts, own),
            outs + [sds((capacity, half), BF)],
            (*got_grad, place, held, *tied),
            [VMEM] * (experts + 2) + [ANY] * len(tied),
            flops=cost * weight_flops,
            traffic=cost * weight_bytes,
        )

    (act_other,) = act_of(False, held_other, [], [pair_sent], D1COST)
    rows_grad, act_mine = act_of(True, held_mine, [sds((capacity, width), BF)], [], D2COST)
    act = act_mine.astype(F32) + swap(act_other, "ey", 1).astype(F32)
    act, act_far = total(act, act.astype(BF))
    mine_act, by_gate, by_up = call(
        gates,
        [sds((capacity, half), BF)] + [sds((capacity, half), F32)] * 2,
        (pair, pair_far),
        [VMEM] * 2,
        traffic=18 * capacity * half,
        flops=GFLOP * weight_flops,
    )
    other_act = swap(mine_act, "ey", 1)
    mine = call(
        grads_of,
        sds((2, capacity, half), BF),
        (act, act_far, by_gate, by_up, other_act),
        [VMEM] * 4 + [ANY],
        traffic=18 * capacity * half,
    )
    other = swap(mine, "ey", 1)
    own = call(
        own_rows,
        sds((capacity, width), F32),
        (mine, held_mine),
        [VMEM] * 2,
        flops=weight_flops,
        traffic=weight_bytes,
    )
    back = call(
        functools.partial(other_rows, experts),
        piece,
        (own, other, place, held_other),
        [VMEM] * 4,
        [pltpu.VMEM((rows, width), F32)],
        flops=weight_flops,
        traffic=weight_bytes,
    )
    home = [shift(part, "ex", step) if step else part for part, step in zip(back, shifts(experts))]
    pair_grad, down_grad = call(
        weight_grads,
        [sds((1, 2, hidden, width), BF), sds((1, hidden, width), BF)],
        (mine_act, other_act, mine, other, rows_in, rows_grad),
        [VMEM] * 6,
        [pltpu.VMEM((12, half // 2, width), BF), dma(12)],
        limit=24,
        flops=3 * weight_flops,
        traffic=3 * weight_bytes,
        out_specs=[ANY, ANY],
    )
    grad_inputs = call(
        functools.partial(combine, experts),
        sds((tokens, width), BF),
        (pick, *home),
        [VMEM] * (experts + 1),
        [pltpu.VMEM((rows, width), F32), pltpu.VMEM((2, tokens // 2, width), BF), dma(2)],
        flops=2 * rows * tokens * width,
        traffic=4 * tokens * width,
        out_specs=ANY,
    )
    return (grad_inputs, pair_grad, down_grad)


def solution(mesh):
    return jax.shard_map(
        local,
        mesh=mesh,
        in_specs=(
            P(("groups", "ex"), "ey"),
            P(("groups", "ex"), "ey"),
            P(("groups", "ex"), None),
            P(("groups", "ex"), None),
            P("ex", None, None, "ey"),
            P("ex", None, "ey"),
        ),
        out_specs=(
            P(("groups", "ex"), "ey"),
            P("ex", "groups", None, "ey"),
            P("ex", "groups", "ey"),
        ),
        check_vma=False,
    )
```

```python
import functools

import jax
import jax.numpy as jnp
from jax import lax
from jax.experimental import pallas as pl
from jax.experimental.pallas import tpu as pltpu
from jax.sharding import PartitionSpec as P

MOST = 40
EXPERTS = 128
EMPTY = 64.0
BF = jnp.bfloat16
F32 = jnp.float32
MIB = 1 << 20
C2COST = 100
WCOST = 100
GFLOP = 100
D1COST = 1
D2COST = 100
VMEM = pl.BlockSpec(memory_space=pltpu.VMEM)
ANY = pl.BlockSpec(memory_space=pl.ANY)
HBM = pl.BlockSpec(memory_space=pltpu.HBM)
ROWS = (((0,), (0,)), ((), ()))
LANES = (((1,), (1,)), ((), ()))
PLAIN = (((1,), (0,)), ((), ()))


def mm(left, right, dims=PLAIN):
    return lax.dot_general(left, right, dims, preferred_element_type=F32)


def iota(shape, dim):
    return lax.broadcasted_iota(jnp.int32, shape, dim)


def far_first(count):
    return sorted(range(count), key=lambda k: (-k.bit_length(), k))


def cut(source, target, sems, first, pieces):
    rows = target.shape[-2] // pieces
    out = []
    for at in range(pieces):
        part = pl.ds(at * rows, rows)
        out.append(pltpu.make_async_copy(source.at[part], target.at[part], sems.at[first + at]))
    return out


def run(loads):
    for load in loads:
        load.start()
    return loads


def wait(loads):
    for load in loads:
        load.wait()


def block_of(position, names):
    found = jnp.full_like(position, names[0])
    for at in range(1, len(names)):
        found = found + (position >= at * MOST).astype(jnp.int32) * (names[at] - names[at - 1])
    return found


def call(body, outs, operands, specs, scratch=(), limit=16, flops=0, traffic=0, out_specs=None):
    return pl.pallas_call(
        body,
        out_shape=outs,
        in_specs=specs,
        out_specs=out_specs if out_specs is not None else jax.tree.map(lambda _: VMEM, outs),
        scratch_shapes=list(scratch),
        compiler_params=pltpu.CompilerParams(vmem_limit_bytes=limit * MIB),
        cost_estimate=pl.CostEstimate(flops=flops, bytes_accessed=traffic, transcendentals=0),
    )(*operands)


def pick_inputs(experts, routes_in, probs_in, inputs, grads, pick_out, prob_out, grads_out, *refs):
    *pieces, routes, probs, held, sems = refs
    loads = run(
        [
            pltpu.make_async_copy(routes_in, routes, sems.at[0]),
            pltpu.make_async_copy(probs_in, probs, sems.at[1]),
        ]
    )
    input_loads = run(cut(inputs, held, sems, 2, 1))
    grad_loads = run(cut(grads, grads_out, sems, 3, 1))
    me = lax.axis_index("ex")
    tokens = inputs.shape[0]
    rows = experts * MOST
    order = far_first(experts)
    owner = block_of(iota((rows, routes.shape[0]), 0), order)
    named = jnp.zeros((rows, tokens), F32)
    weight = jnp.zeros((rows, tokens), F32)
    earlier = iota((tokens, tokens), 0) < iota((tokens, tokens), 1)
    earlier = jnp.where(earlier, 1.0, 0.0).astype(BF)
    row = iota((rows, tokens), 0)
    slot = row - block_of(row, range(experts)) * MOST
    wait(loads)
    chosen = routes[...]
    wide = probs[...].astype(F32)
    for k in range(experts):
        spread = jnp.where(owner == k, 1.0, 0.0).astype(BF)
        hit = chosen == (me ^ k)
        named = named + mm(spread, jnp.where(hit, 1.0, 0.0).astype(BF))
        weight = weight + mm(spread, jnp.where(hit, wide, 0.0).astype(BF))
    rank = mm(named.astype(BF), earlier).astype(jnp.int32)
    picks = (rank == slot) & (named > 0.5)
    pick = jnp.where(picks, 1.0, 0.0)
    filled = jnp.max(pick, axis=1, keepdims=True) > 0.5
    pick = pick.astype(BF)
    pick_out[...] = pick
    prob_out[...] = jnp.sum(jnp.where(picks, weight, 0.0), axis=1, keepdims=True)
    wait(input_loads)
    sent = jnp.where(filled, mm(pick, held[...]), EMPTY)
    for k in range(experts):
        pieces[k][...] = sent[k * MOST : (k + 1) * MOST].astype(BF)
    wait(grad_loads)


def pick_grads(experts, pick, prob, grads, *refs):
    near_in, near, *pieces = refs
    sent = mm(pick[...], grads[...]) * prob[...]
    parts = [sent[at * MOST : (at + 1) * MOST] for at in range(experts)]
    near[...] = jnp.concatenate([near_in[...].astype(F32), parts[-2]], axis=0).astype(BF)
    for target, part in zip(pieces, parts[:-2] + parts[-1:]):
        target[...] = part.astype(BF)


def stacked(pieces, part=0):
    rows = [piece[...].astype(F32) for piece in pieces]
    rows = [row[part * MOST : (part + 1) * MOST] if row.shape[0] > MOST else row for row in rows]
    return jnp.concatenate(rows, axis=0)


def rows_of(half, own):
    core = lax.axis_index("ey") & 1
    return pl.ds(pl.multiple_of((core if own else 1 - core) * half, 128), half)


def place_rows(experts, capacity, pieces):
    me = lax.axis_index("ex")
    rows = experts * MOST
    got = stacked(pieces)
    full = got[:, :1] < EMPTY / 2
    key = []
    for dim in (0, 1):
        row = iota((rows, rows), dim)
        local_row = row - block_of(row, range(experts)) * MOST
        key.append((me ^ block_of(row, far_first(experts))) * MOST + local_row)
    earlier = jnp.where(key[1] < key[0], 1.0, 0.0).astype(BF)
    wide = jnp.broadcast_to(full, (rows, capacity))
    slot = mm(earlier, jnp.where(wide, 1.0, 0.0).astype(BF)).astype(jnp.int32)
    place = jnp.where((slot == iota((rows, capacity), 1)) & wide, 1.0, 0.0).astype(BF)
    return place, mm(place, got.astype(BF), ROWS).astype(BF)


def stage(count, gate_up, down, *refs):
    pieces, refs = refs[:count], refs[count:]
    held, pieces_out, sems = refs[:2], refs[2:-1], refs[-1]
    half = down.shape[1] // 2
    loads = []
    for own, out in enumerate(held):
        rows = rows_of(half, own == 1)
        for matrix in range(3):
            source = down.at[0, rows] if matrix == 2 else gate_up.at[0, matrix, rows]
            loads.append(pltpu.make_async_copy(source, out.at[matrix], sems.at[len(loads)]))
    run(loads)
    for source, target in zip(pieces, pieces_out):
        target[...] = source[...]
    wait(loads)


def other_pair(experts, capacity, *refs):
    held, out, place_out, rows_out = refs[experts:]
    place, rows_in = place_rows(experts, capacity, refs[:experts])
    place_out[...] = place
    rows_out[...] = rows_in
    for matrix in range(2):
        out[matrix] = mm(rows_in, held[matrix], LANES).astype(BF)


def mine_pair(rows_in, held, out):
    for matrix in range(2):
        out[matrix] = mm(rows_in[...], held[matrix], LANES).astype(BF)


def pair_sum(mine, other, held_out, sent_out):
    held = mine[...].astype(F32) + other[...].astype(F32)
    held_out[...] = held
    sent_out[...] = held.astype(BF)


def act_part(experts, own, *refs):
    place, held = refs[experts : experts + 2]
    pieces = refs[: experts - 2][::-1] + refs[experts - 2 : experts]
    rows_grad = mm(place[...], stacked(pieces, 1).astype(BF), ROWS).astype(BF)
    if own:
        refs[-2][...] = rows_grad
    refs[-1][...] = mm(rows_grad, held[2], LANES).astype(BF)


def gates(pair, pair_far, act_out, by_gate, by_up):
    gate_sum = pair[0] + pair_far[0].astype(F32)
    up_sum = pair[1] + pair_far[1].astype(F32)
    sigmoid_gate = jax.nn.sigmoid(gate_sum)
    silu_gate = gate_sum * sigmoid_gate
    act_out[...] = (silu_gate * up_sum).astype(BF)
    by_gate[...] = up_sum * sigmoid_gate * (1.0 + gate_sum * (1.0 - sigmoid_gate))
    by_up[...] = silu_gate


def grads_of(act, act_far, by_gate, by_up, _, out):
    grad_act = act[...] + act_far[...].astype(F32)
    out[0] = (grad_act * by_gate[...]).astype(BF)
    out[1] = (grad_act * by_up[...]).astype(BF)


def own_rows(mine, held, out):
    out[...] = mm(mine[0], held[0]) + mm(mine[1], held[1])


def other_rows(experts, total, other, place, held, *refs):
    pieces, whole = refs[:experts], refs[experts]
    rows = total[...] + mm(other[0], held[0]) + mm(other[1], held[1])
    whole[...] = mm(place[...], rows.astype(BF))
    me = lax.axis_index("ex")
    for piece, step in zip(pieces, shifts(experts)):
        piece[...] = whole[place_of(lax.rem(me + step, experts), experts)].astype(BF)


def weight_grads(mine_act, other_act, mine, other, rows_in, rows_grad, pair_out, down_out, held, sems):
    core = lax.axis_index("ey") & 1
    half = mine_act.shape[1]
    step = half // 2
    stores = []
    for matrix in range(3):
        right = rows_grad[...] if matrix == 0 else rows_in[...]
        for own in range(2):
            start = (core if own else 1 - core) * half
            for part in range(2):
                columns = slice(part * step, (part + 1) * step)
                if matrix == 0:
                    left = (mine_act if own else other_act)[:, columns]
                else:
                    left = (mine if own else other)[matrix - 1, :, columns]
                at = len(stores)
                held[at] = mm(left, right, ROWS).astype(BF)
                rows = pl.ds(start + part * step, step)
                target = down_out.at[0, rows] if matrix == 0 else pair_out.at[0, matrix - 1, rows]
                store = pltpu.make_async_copy(held.at[at], target, sems.at[at])
                store.start()
                stores.append(store)
    for store in stores:
        store.wait()


def combine(experts, pick, *refs):
    out, whole, held, sems = refs[experts:]
    me = lax.axis_index("ex")
    for piece, step in zip(refs[:experts], shifts(experts)):
        whole[place_of(lax.rem(me + experts - step, experts), experts)] = piece[...].astype(F32)
    home = whole[...].astype(BF)
    rows = out.shape[0] // held.shape[0]
    stores = []
    for at in range(held.shape[0]):
        part = pick[:, at * rows : (at + 1) * rows]
        held[at] = mm(part, home, ROWS).astype(BF)
        target = out.at[pl.ds(at * rows, rows)]
        stores += run([pltpu.make_async_copy(held.at[at], target, sems.at[at])])
    wait(stores)


def far(value):
    return pltpu.with_memory_space_constraint(value, pltpu.HBM)


def place_of(partner, experts):
    k = lax.axis_index("ex") ^ partner
    spot = jnp.int32(0)
    for at, name in enumerate(far_first(experts)):
        spot = spot + jnp.where(k == name, at * MOST, 0)
    return pl.ds(pl.multiple_of(spot, 8), MOST)


def shifts(experts):
    return list(range(1, experts)) + [0]


def shift(value, axis, step):
    count = lax.axis_size(axis)
    return lax.ppermute(value, axis, [(i, (i + step) % count) for i in range(count)])


def swap(value, axis, bit):
    count = lax.axis_size(axis)
    return lax.ppermute(value, axis, [(i, i ^ bit) for i in range(count)])


def exchange(pieces, axis):
    order = far_first(len(pieces))
    return [swap(piece, axis, k) if k else piece for piece, k in zip(pieces, order)]


def local(inputs, grad_output, routes, gate_probs, gate_up, down_proj):
    experts = lax.axis_size("ex")
    ways = lax.axis_size("ey")
    tokens, width = inputs.shape
    hidden = gate_up.shape[2]
    half = hidden // 2
    capacity = 5 * tokens * experts * routes.shape[1] // (4 * EXPERTS)
    rows = experts * MOST
    weight_bytes = hidden * width * 2
    weight_flops = 2 * capacity * hidden * width
    sds = jax.ShapeDtypeStruct
    piece = [sds((MOST, width), BF)] * experts
    dma = lambda count: pltpu.SemaphoreType.DMA((count,))

    order = far_first(experts)
    pick, prob, grads, *send_in, own_in = call(
        functools.partial(pick_inputs, experts),
        [
            sds((rows, tokens), BF),
            sds((rows, 1), F32),
            pltpu.VMEM((tokens, width), BF),
        ]
        + piece,
        (far(routes.T), far(gate_probs.T), far(inputs), far(grad_output)),
        [HBM] * 4,
        [
            pltpu.VMEM(routes.shape[::-1], jnp.int32),
            pltpu.VMEM(routes.shape[::-1], BF),
            pltpu.VMEM((tokens, width), BF),
            dma(4),
        ],
        flops=2 * rows * tokens * width,
        traffic=4 * tokens * width,
    )
    near, *send_grad = call(
        functools.partial(pick_grads, experts),
        [sds((2 * MOST, width), BF)] + piece[1:],
        (pick, prob, grads, send_in[-1]),
        [VMEM] * 4,
        flops=2 * rows * tokens * width,
        traffic=2 * tokens * width,
    )
    near = swap(near, "ex", 1)
    got_in = [swap(part, "ex", k) for part, k in zip(send_in[:-1], order)] + [near, own_in]
    held_other, held_mine, *send_grad = call(
        functools.partial(stage, experts - 1),
        [pltpu.VMEM((3, half, width), BF)] * 2 + piece[1:],
        (far(gate_up), far(down_proj), *send_grad),
        [HBM] * 2 + [VMEM] * (experts - 1),
        [dma(6)],
        flops=WCOST * weight_flops,
        traffic=WCOST * weight_bytes,
    )
    got_grad = [swap(part, "ex", k) for part, k in zip(send_grad[:-1], order)][::-1]
    got_grad = got_grad + [near, send_grad[-1]]
    pair_other, place, rows_in = call(
        functools.partial(other_pair, experts, capacity),
        [sds((2, capacity, half), BF), sds((rows, capacity), BF), sds((capacity, width), BF)],
        (*got_in, held_other),
        [VMEM] * (experts + 1),
        flops=2 * weight_flops,
        traffic=weight_bytes,
    )
    pair_mine = call(
        mine_pair,
        sds((2, capacity, half), BF),
        (rows_in, held_mine),
        [VMEM] * 2,
        flops=C2COST * weight_flops,
        traffic=C2COST * weight_bytes,
    )

    def total(held, sent):
        bit = 2
        while bit * 2 < ways:
            held = held + swap(sent, "ey", bit).astype(F32)
            sent = held.astype(BF)
            bit *= 2
        return held, swap(sent, "ey", bit)

    pair, pair_sent = call(
        pair_sum,
        [sds((2, capacity, half), F32), sds((2, capacity, half), BF)],
        (pair_mine, swap(pair_other, "ey", 1)),
        [VMEM] * 2,
        traffic=10 * capacity * hidden,
    )
    pair, pair_far = total(pair, pair_sent)
    def act_of(own, held, outs, tied, cost):
        return call(
            functools.partial(act_part, experts, own),
            outs + [sds((capacity, half), BF)],
            (*got_grad, place, held, *tied),
            [VMEM] * (experts + 2) + [ANY] * len(tied),
            flops=cost * weight_flops,
            traffic=cost * weight_bytes,
        )

    (act_other,) = act_of(False, held_other, [], [pair_sent], D1COST)
    rows_grad, act_mine = act_of(True, held_mine, [sds((capacity, width), BF)], [], D2COST)
    act = act_mine.astype(F32) + swap(act_other, "ey", 1).astype(F32)
    act, act_far = total(act, act.astype(BF))
    mine_act, by_gate, by_up = call(
        gates,
        [sds((capacity, half), BF)] + [sds((capacity, half), F32)] * 2,
        (pair, pair_far),
        [VMEM] * 2,
        traffic=18 * capacity * half,
        flops=GFLOP * weight_flops,
    )
    other_act = swap(mine_act, "ey", 1)
    mine = call(
        grads_of,
        sds((2, capacity, half), BF),
        (act, act_far, by_gate, by_up, other_act),
        [VMEM] * 4 + [ANY],
        traffic=18 * capacity * half,
    )
    other = swap(mine, "ey", 1)
    own = call(
        own_rows,
        sds((capacity, width), F32),
        (mine, held_mine),
        [VMEM] * 2,
        flops=weight_flops,
        traffic=weight_bytes,
    )
    back = call(
        functools.partial(other_rows, experts),
        piece,
        (own, other, place, held_other),
        [VMEM] * 4,
        [pltpu.VMEM((rows, width), F32)],
        flops=weight_flops,
        traffic=weight_bytes,
    )
    home = [shift(part, "ex", step) if step else part for part, step in zip(back, shifts(experts))]
    pair_grad, down_grad = call(
        weight_grads,
        [sds((1, 2, hidden, width), BF), sds((1, hidden, width), BF)],
        (mine_act, other_act, mine, other, rows_in, rows_grad),
        [VMEM] * 6,
        [pltpu.VMEM((12, half // 2, width), BF), dma(12)],
        limit=24,
        flops=3 * weight_flops,
        traffic=3 * weight_bytes,
        out_specs=[ANY, ANY],
    )
    grad_inputs = call(
        functools.partial(combine, experts),
        sds((tokens, width), BF),
        (pick, *home),
        [VMEM] * (experts + 1),
        [pltpu.VMEM((rows, width), F32), pltpu.VMEM((2, tokens // 2, width), BF), dma(2)],
        flops=2 * rows * tokens * width,
        traffic=4 * tokens * width,
        out_specs=ANY,
    )
    return (grad_inputs, pair_grad, down_grad)


def solution(mesh):
    return jax.shard_map(
        local,
        mesh=mesh,
        in_specs=(
            P(("groups", "ex"), "ey"),
            P(("groups", "ex"), "ey"),
            P(("groups", "ex"), None),
            P(("groups", "ex"), None),
            P("ex", None, None, "ey"),
            P("ex", None, "ey"),
        ),
        out_specs=(
            P(("groups", "ex"), "ey"),
            P("ex", "groups", None, "ey"),
            P("ex", "groups", "ey"),
        ),
        check_vma=False,
    )
```

```python
import functools

import jax
import jax.numpy as jnp
from jax import lax
from jax.experimental import pallas as pl
from jax.experimental.pallas import tpu as pltpu
from jax.sharding import PartitionSpec as P

MOST = 40
EXPERTS = 128
EMPTY = 64.0
BF = jnp.bfloat16
F32 = jnp.float32
MIB = 1 << 20
C2COST = 100
WCOST = 100
GFLOP = 100
D1COST = 1
D2COST = 100
VMEM = pl.BlockSpec(memory_space=pltpu.VMEM)
ANY = pl.BlockSpec(memory_space=pl.ANY)
HBM = pl.BlockSpec(memory_space=pltpu.HBM)
ROWS = (((0,), (0,)), ((), ()))
LANES = (((1,), (1,)), ((), ()))
PLAIN = (((1,), (0,)), ((), ()))


def mm(left, right, dims=PLAIN):
    return lax.dot_general(left, right, dims, preferred_element_type=F32)


def iota(shape, dim):
    return lax.broadcasted_iota(jnp.int32, shape, dim)


def far_first(count):
    return sorted(range(count), key=lambda k: (-k.bit_length(), k))


def cut(source, target, sems, first, pieces):
    rows = target.shape[-2] // pieces
    out = []
    for at in range(pieces):
        part = pl.ds(at * rows, rows)
        out.append(pltpu.make_async_copy(source.at[part], target.at[part], sems.at[first + at]))
    return out


def run(loads):
    for load in loads:
        load.start()
    return loads


def wait(loads):
    for load in loads:
        load.wait()


def block_of(position, names):
    found = jnp.full_like(position, names[0])
    for at in range(1, len(names)):
        found = found + (position >= at * MOST).astype(jnp.int32) * (names[at] - names[at - 1])
    return found


def call(body, outs, operands, specs, scratch=(), limit=16, flops=0, traffic=0, out_specs=None):
    return pl.pallas_call(
        body,
        out_shape=outs,
        in_specs=specs,
        out_specs=out_specs if out_specs is not None else jax.tree.map(lambda _: VMEM, outs),
        scratch_shapes=list(scratch),
        compiler_params=pltpu.CompilerParams(vmem_limit_bytes=limit * MIB),
        cost_estimate=pl.CostEstimate(flops=flops, bytes_accessed=traffic, transcendentals=0),
    )(*operands)


def pick_inputs(experts, routes_in, probs_in, inputs, grads, pick_out, prob_out, grads_out, *refs):
    *pieces, routes, probs, held, sems = refs
    loads = run(
        [
            pltpu.make_async_copy(routes_in, routes, sems.at[0]),
            pltpu.make_async_copy(probs_in, probs, sems.at[1]),
        ]
    )
    input_loads = run(cut(inputs, held, sems, 2, 1))
    grad_loads = run(cut(grads, grads_out, sems, 3, 1))
    me = lax.axis_index("ex")
    tokens = inputs.shape[0]
    rows = experts * MOST
    order = far_first(experts)
    owner = block_of(iota((rows, routes.shape[0]), 0), order)
    named = jnp.zeros((rows, tokens), F32)
    weight = jnp.zeros((rows, tokens), F32)
    earlier = iota((tokens, tokens), 0) < iota((tokens, tokens), 1)
    earlier = jnp.where(earlier, 1.0, 0.0).astype(BF)
    row = iota((rows, tokens), 0)
    slot = row - block_of(row, range(experts)) * MOST
    wait(loads)
    chosen = routes[...]
    wide = probs[...].astype(F32)
    for k in range(experts):
        spread = jnp.where(owner == k, 1.0, 0.0).astype(BF)
        hit = chosen == (me ^ k)
        named = named + mm(spread, jnp.where(hit, 1.0, 0.0).astype(BF))
        weight = weight + mm(spread, jnp.where(hit, wide, 0.0).astype(BF))
    rank = mm(named.astype(BF), earlier).astype(jnp.int32)
    picks = (rank == slot) & (named > 0.5)
    pick = jnp.where(picks, 1.0, 0.0)
    filled = jnp.max(pick, axis=1, keepdims=True) > 0.5
    pick = pick.astype(BF)
    pick_out[...] = pick
    prob_out[...] = jnp.sum(jnp.where(picks, weight, 0.0), axis=1, keepdims=True)
    wait(input_loads)
    sent = jnp.where(filled, mm(pick, held[...]), EMPTY)
    for k in range(experts):
        pieces[k][...] = sent[k * MOST : (k + 1) * MOST].astype(BF)
    wait(grad_loads)


def pick_grads(experts, pick, prob, grads, *pieces):
    sent = mm(pick[...], grads[...]) * prob[...]
    for k in range(experts):
        pieces[k][...] = sent[k * MOST : (k + 1) * MOST].astype(BF)


def stacked(pieces):
    return jnp.concatenate([piece[...].astype(F32) for piece in pieces], axis=0)


def rows_of(half, own):
    core = lax.axis_index("ey") & 1
    return pl.ds(pl.multiple_of((core if own else 1 - core) * half, 128), half)


def place_rows(experts, capacity, pieces):
    me = lax.axis_index("ex")
    rows = experts * MOST
    got = stacked(pieces)
    full = got[:, :1] < EMPTY / 2
    key = []
    for dim in (0, 1):
        row = iota((rows, rows), dim)
        local_row = row - block_of(row, range(experts)) * MOST
        key.append((me ^ block_of(row, far_first(experts))) * MOST + local_row)
    earlier = jnp.where(key[1] < key[0], 1.0, 0.0).astype(BF)
    wide = jnp.broadcast_to(full, (rows, capacity))
    slot = mm(earlier, jnp.where(wide, 1.0, 0.0).astype(BF)).astype(jnp.int32)
    place = jnp.where((slot == iota((rows, capacity), 1)) & wide, 1.0, 0.0).astype(BF)
    return place, mm(place, got.astype(BF), ROWS).astype(BF)


def stage(count, gate_up, down, *refs):
    pieces, refs = refs[:count], refs[count:]
    held, pieces_out, sems = refs[:2], refs[2:-1], refs[-1]
    half = down.shape[1] // 2
    loads = []
    for own, out in enumerate(held):
        rows = rows_of(half, own == 1)
        for matrix in range(3):
            source = down.at[0, rows] if matrix == 2 else gate_up.at[0, matrix, rows]
            loads.append(pltpu.make_async_copy(source, out.at[matrix], sems.at[len(loads)]))
    run(loads)
    for source, target in zip(pieces, pieces_out):
        target[...] = source[...]
    wait(loads)


def other_pair(experts, capacity, *refs):
    held, out, place_out, rows_out = refs[experts:]
    place, rows_in = place_rows(experts, capacity, refs[:experts])
    place_out[...] = place
    rows_out[...] = rows_in
    for matrix in range(2):
        out[matrix] = mm(rows_in, held[matrix], LANES).astype(BF)


def mine_pair(rows_in, held, near, out, near_out):
    near_out[...] = near[...]
    for matrix in range(2):
        out[matrix] = mm(rows_in[...], held[matrix], LANES).astype(BF)


def pair_sum(mine, other, held_out, sent_out):
    held = mine[...].astype(F32) + other[...].astype(F32)
    held_out[...] = held
    sent_out[...] = held.astype(BF)


def act_part(experts, own, *refs):
    place, held = refs[experts : experts + 2]
    pieces = refs[: experts - 2][::-1] + refs[experts - 2 : experts]
    rows_grad = mm(place[...], stacked(pieces).astype(BF), ROWS).astype(BF)
    if own:
        refs[-2][...] = rows_grad
    refs[-1][...] = mm(rows_grad, held[2], LANES).astype(BF)


def gates(pair, pair_far, act_out, by_gate, by_up):
    gate_sum = pair[0] + pair_far[0].astype(F32)
    up_sum = pair[1] + pair_far[1].astype(F32)
    sigmoid_gate = jax.nn.sigmoid(gate_sum)
    silu_gate = gate_sum * sigmoid_gate
    act_out[...] = (silu_gate * up_sum).astype(BF)
    by_gate[...] = up_sum * sigmoid_gate * (1.0 + gate_sum * (1.0 - sigmoid_gate))
    by_up[...] = silu_gate


def grads_of(act, act_far, by_gate, by_up, _, out):
    grad_act = act[...] + act_far[...].astype(F32)
    out[0] = (grad_act * by_gate[...]).astype(BF)
    out[1] = (grad_act * by_up[...]).astype(BF)


def own_rows(mine, held, out):
    out[...] = mm(mine[0], held[0]) + mm(mine[1], held[1])


def other_rows(experts, total, other, place, held, *refs):
    pieces, whole = refs[:experts], refs[experts]
    rows = total[...] + mm(other[0], held[0]) + mm(other[1], held[1])
    whole[...] = mm(place[...], rows.astype(BF))
    me = lax.axis_index("ex")
    for piece, step in zip(pieces, shifts(experts)):
        piece[...] = whole[place_of(lax.rem(me + step, experts), experts)].astype(BF)


def weight_grads(mine_act, other_act, mine, other, rows_in, rows_grad, pair_out, down_out, held, sems):
    core = lax.axis_index("ey") & 1
    half = mine_act.shape[1]
    step = half // 2
    stores = []
    for matrix in range(3):
        right = rows_grad[...] if matrix == 0 else rows_in[...]
        for own in range(2):
            start = (core if own else 1 - core) * half
            for part in range(2):
                columns = slice(part * step, (part + 1) * step)
                if matrix == 0:
                    left = (mine_act if own else other_act)[:, columns]
                else:
                    left = (mine if own else other)[matrix - 1, :, columns]
                at = len(stores)
                held[at] = mm(left, right, ROWS).astype(BF)
                rows = pl.ds(start + part * step, step)
                target = down_out.at[0, rows] if matrix == 0 else pair_out.at[0, matrix - 1, rows]
                store = pltpu.make_async_copy(held.at[at], target, sems.at[at])
                store.start()
                stores.append(store)
    for store in stores:
        store.wait()


def combine(experts, pick, *refs):
    out, whole, held, sems = refs[experts:]
    me = lax.axis_index("ex")
    for piece, step in zip(refs[:experts], shifts(experts)):
        whole[place_of(lax.rem(me + experts - step, experts), experts)] = piece[...].astype(F32)
    home = whole[...].astype(BF)
    rows = out.shape[0] // held.shape[0]
    stores = []
    for at in range(held.shape[0]):
        part = pick[:, at * rows : (at + 1) * rows]
        held[at] = mm(part, home, ROWS).astype(BF)
        target = out.at[pl.ds(at * rows, rows)]
        stores += run([pltpu.make_async_copy(held.at[at], target, sems.at[at])])
    wait(stores)


def far(value):
    return pltpu.with_memory_space_constraint(value, pltpu.HBM)


def place_of(partner, experts):
    k = lax.axis_index("ex") ^ partner
    spot = jnp.int32(0)
    for at, name in enumerate(far_first(experts)):
        spot = spot + jnp.where(k == name, at * MOST, 0)
    return pl.ds(pl.multiple_of(spot, 8), MOST)


def shifts(experts):
    return list(range(1, experts)) + [0]


def shift(value, axis, step):
    count = lax.axis_size(axis)
    return lax.ppermute(value, axis, [(i, (i + step) % count) for i in range(count)])


def swap(value, axis, bit):
    count = lax.axis_size(axis)
    return lax.ppermute(value, axis, [(i, i ^ bit) for i in range(count)])


def exchange(pieces, axis):
    order = far_first(len(pieces))
    return [swap(piece, axis, k) if k else piece for piece, k in zip(pieces, order)]


def local(inputs, grad_output, routes, gate_probs, gate_up, down_proj):
    experts = lax.axis_size("ex")
    ways = lax.axis_size("ey")
    tokens, width = inputs.shape
    hidden = gate_up.shape[2]
    half = hidden // 2
    capacity = 5 * tokens * experts * routes.shape[1] // (4 * EXPERTS)
    rows = experts * MOST
    weight_bytes = hidden * width * 2
    weight_flops = 2 * capacity * hidden * width
    sds = jax.ShapeDtypeStruct
    piece = [sds((MOST, width), BF)] * experts
    dma = lambda count: pltpu.SemaphoreType.DMA((count,))

    order = far_first(experts)
    pick, prob, grads, *send_in, own_in = call(
        functools.partial(pick_inputs, experts),
        [
            sds((rows, tokens), BF),
            sds((rows, 1), F32),
            pltpu.VMEM((tokens, width), BF),
        ]
        + piece,
        (far(routes.T), far(gate_probs.T), far(inputs), far(grad_output)),
        [HBM] * 4,
        [
            pltpu.VMEM(routes.shape[::-1], jnp.int32),
            pltpu.VMEM(routes.shape[::-1], BF),
            pltpu.VMEM((tokens, width), BF),
            dma(4),
        ],
        flops=2 * rows * tokens * width,
        traffic=4 * tokens * width,
    )
    *send_grad, near_grad, own_grad = call(
        functools.partial(pick_grads, experts),
        piece,
        (pick, prob, grads),
        [VMEM] * 3,
        flops=2 * rows * tokens * width,
        traffic=2 * tokens * width,
    )
    got_in = exchange(send_in + [own_in], "ex")
    held_other, held_mine, *send_grad = call(
        functools.partial(stage, experts - 2),
        [pltpu.VMEM((3, half, width), BF)] * 2 + piece[2:],
        (far(gate_up), far(down_proj), *send_grad),
        [HBM] * 2 + [VMEM] * (experts - 2),
        [dma(6)],
        flops=WCOST * weight_flops,
        traffic=WCOST * weight_bytes,
    )
    got_grad = [swap(part, "ex", k) for part, k in zip(send_grad, order)][::-1]
    pair_other, place, rows_in = call(
        functools.partial(other_pair, experts, capacity),
        [sds((2, capacity, half), BF), sds((rows, capacity), BF), sds((capacity, width), BF)],
        (*got_in, held_other),
        [VMEM] * (experts + 1),
        flops=2 * weight_flops,
        traffic=weight_bytes,
    )
    pair_mine, near_grad = call(
        mine_pair,
        [sds((2, capacity, half), BF), piece[0]],
        (rows_in, held_mine, near_grad),
        [VMEM] * 3,
        flops=C2COST * weight_flops,
        traffic=C2COST * weight_bytes,
    )

    def total(held, sent):
        bit = 2
        while bit * 2 < ways:
            held = held + swap(sent, "ey", bit).astype(F32)
            sent = held.astype(BF)
            bit *= 2
        return held, swap(sent, "ey", bit)

    pair, pair_sent = call(
        pair_sum,
        [sds((2, capacity, half), F32), sds((2, capacity, half), BF)],
        (pair_mine, swap(pair_other, "ey", 1)),
        [VMEM] * 2,
        traffic=10 * capacity * hidden,
    )
    pair, pair_far = total(pair, pair_sent)
    got_grad = got_grad + [swap(near_grad, "ex", 1), own_grad]

    def act_of(own, held, outs, tied, cost):
        return call(
            functools.partial(act_part, experts, own),
            outs + [sds((capacity, half), BF)],
            (*got_grad, place, held, *tied),
            [VMEM] * (experts + 2) + [ANY] * len(tied),
            flops=cost * weight_flops,
            traffic=cost * weight_bytes,
        )

    (act_other,) = act_of(False, held_other, [], [pair_sent], D1COST)
    rows_grad, act_mine = act_of(True, held_mine, [sds((capacity, width), BF)], [], D2COST)
    act = act_mine.astype(F32) + swap(act_other, "ey", 1).astype(F32)
    act, act_far = total(act, act.astype(BF))
    mine_act, by_gate, by_up = call(
        gates,
        [sds((capacity, half), BF)] + [sds((capacity, half), F32)] * 2,
        (pair, pair_far),
        [VMEM] * 2,
        traffic=18 * capacity * half,
        flops=GFLOP * weight_flops,
    )
    other_act = swap(mine_act, "ey", 1)
    mine = call(
        grads_of,
        sds((2, capacity, half), BF),
        (act, act_far, by_gate, by_up, other_act),
        [VMEM] * 4 + [ANY],
        traffic=18 * capacity * half,
    )
    other = swap(mine, "ey", 1)
    own = call(
        own_rows,
        sds((capacity, width), F32),
        (mine, held_mine),
        [VMEM] * 2,
        flops=weight_flops,
        traffic=weight_bytes,
    )
    back = call(
        functools.partial(other_rows, experts),
        piece,
        (own, other, place, held_other),
        [VMEM] * 4,
        [pltpu.VMEM((rows, width), F32)],
        flops=weight_flops,
        traffic=weight_bytes,
    )
    home = [shift(part, "ex", step) if step else part for part, step in zip(back, shifts(experts))]
    pair_grad, down_grad = call(
        weight_grads,
        [sds((1, 2, hidden, width), BF), sds((1, hidden, width), BF)],
        (mine_act, other_act, mine, other, rows_in, rows_grad),
        [VMEM] * 6,
        [pltpu.VMEM((12, half // 2, width), BF), dma(12)],
        limit=24,
        flops=3 * weight_flops,
        traffic=3 * weight_bytes,
        out_specs=[ANY, ANY],
    )
    grad_inputs = call(
        functools.partial(combine, experts),
        sds((tokens, width), BF),
        (pick, *home),
        [VMEM] * (experts + 1),
        [pltpu.VMEM((rows, width), F32), pltpu.VMEM((2, tokens // 2, width), BF), dma(2)],
        flops=2 * rows * tokens * width,
        traffic=4 * tokens * width,
        out_specs=ANY,
    )
    return (grad_inputs, pair_grad, down_grad)


def solution(mesh):
    return jax.shard_map(
        local,
        mesh=mesh,
        in_specs=(
            P(("groups", "ex"), "ey"),
            P(("groups", "ex"), "ey"),
            P(("groups", "ex"), None),
            P(("groups", "ex"), None),
            P("ex", None, None, "ey"),
            P("ex", None, "ey"),
        ),
        out_specs=(
            P(("groups", "ex"), "ey"),
            P("ex", "groups", None, "ey"),
            P("ex", "groups", "ey"),
        ),
        check_vma=False,
    )
```

```python
import functools

import jax
import jax.numpy as jnp
from jax import lax
from jax.experimental import pallas as pl
from jax.experimental.pallas import tpu as pltpu
from jax.sharding import PartitionSpec as P

MOST = 40
EXPERTS = 128
EMPTY = 64.0
BF = jnp.bfloat16
F32 = jnp.float32
MIB = 1 << 20
C2COST = 100
WCOST = 100
GFLOP = 100
D1COST = 1
D2COST = 100
VMEM = pl.BlockSpec(memory_space=pltpu.VMEM)
ANY = pl.BlockSpec(memory_space=pl.ANY)
HBM = pl.BlockSpec(memory_space=pltpu.HBM)
ROWS = (((0,), (0,)), ((), ()))
LANES = (((1,), (1,)), ((), ()))
PLAIN = (((1,), (0,)), ((), ()))


def mm(left, right, dims=PLAIN):
    return lax.dot_general(left, right, dims, preferred_element_type=F32)


def iota(shape, dim):
    return lax.broadcasted_iota(jnp.int32, shape, dim)


def far_first(count):
    return sorted(range(count), key=lambda k: (-k.bit_length(), k))


def cut(source, target, sems, first, pieces):
    rows = target.shape[-2] // pieces
    out = []
    for at in range(pieces):
        part = pl.ds(at * rows, rows)
        out.append(pltpu.make_async_copy(source.at[part], target.at[part], sems.at[first + at]))
    return out


def run(loads):
    for load in loads:
        load.start()
    return loads


def wait(loads):
    for load in loads:
        load.wait()


def block_of(position, names):
    found = jnp.full_like(position, names[0])
    for at in range(1, len(names)):
        found = found + (position >= at * MOST).astype(jnp.int32) * (names[at] - names[at - 1])
    return found


def call(body, outs, operands, specs, scratch=(), limit=16, flops=0, traffic=0, out_specs=None):
    return pl.pallas_call(
        body,
        out_shape=outs,
        in_specs=specs,
        out_specs=out_specs if out_specs is not None else jax.tree.map(lambda _: VMEM, outs),
        scratch_shapes=list(scratch),
        compiler_params=pltpu.CompilerParams(vmem_limit_bytes=limit * MIB),
        cost_estimate=pl.CostEstimate(flops=flops, bytes_accessed=traffic, transcendentals=0),
    )(*operands)


def pick_inputs(experts, routes_in, probs_in, inputs, grads, pick_out, prob_out, grads_out, *refs):
    *pieces, routes, probs, held, sems = refs
    loads = run(
        [
            pltpu.make_async_copy(routes_in, routes, sems.at[0]),
            pltpu.make_async_copy(probs_in, probs, sems.at[1]),
        ]
    )
    input_loads = run(cut(inputs, held, sems, 2, 1))
    grad_loads = run(cut(grads, grads_out, sems, 3, 1))
    me = lax.axis_index("ex")
    tokens = inputs.shape[0]
    rows = experts * MOST
    order = far_first(experts)
    owner = block_of(iota((rows, routes.shape[0]), 0), order)
    named = jnp.zeros((rows, tokens), F32)
    weight = jnp.zeros((rows, tokens), F32)
    earlier = iota((tokens, tokens), 0) < iota((tokens, tokens), 1)
    earlier = jnp.where(earlier, 1.0, 0.0).astype(BF)
    row = iota((rows, tokens), 0)
    slot = row - block_of(row, range(experts)) * MOST
    wait(loads)
    chosen = routes[...]
    wide = probs[...].astype(F32)
    for k in range(experts):
        spread = jnp.where(owner == k, 1.0, 0.0).astype(BF)
        hit = chosen == (me ^ k)
        named = named + mm(spread, jnp.where(hit, 1.0, 0.0).astype(BF))
        weight = weight + mm(spread, jnp.where(hit, wide, 0.0).astype(BF))
    rank = mm(named.astype(BF), earlier).astype(jnp.int32)
    picks = (rank == slot) & (named > 0.5)
    pick = jnp.where(picks, 1.0, 0.0)
    filled = jnp.max(pick, axis=1, keepdims=True) > 0.5
    pick = pick.astype(BF)
    pick_out[...] = pick
    prob_out[...] = jnp.sum(jnp.where(picks, weight, 0.0), axis=1, keepdims=True)
    wait(input_loads)
    sent = jnp.where(filled, mm(pick, held[...]), EMPTY)
    for k in range(experts):
        pieces[k][...] = sent[k * MOST : (k + 1) * MOST].astype(BF)
    wait(grad_loads)


def pick_grads(experts, pick, prob, grads, *refs):
    near_in, near, *pieces = refs
    sent = mm(pick[...], grads[...]) * prob[...]
    parts = [sent[at * MOST : (at + 1) * MOST] for at in range(experts)]
    near[...] = jnp.concatenate([near_in[...].astype(F32), parts[-2]], axis=0).astype(BF)
    for target, part in zip(pieces, parts[:-2] + parts[-1:]):
        target[...] = part.astype(BF)


def stacked(pieces, part=0):
    rows = [piece[...].astype(F32) for piece in pieces]
    rows = [row[part * MOST : (part + 1) * MOST] if row.shape[0] > MOST else row for row in rows]
    return jnp.concatenate(rows, axis=0)


def rows_of(half, own):
    core = lax.axis_index("ey") & 1
    return pl.ds(pl.multiple_of((core if own else 1 - core) * half, 128), half)


def place_rows(experts, capacity, pieces):
    me = lax.axis_index("ex")
    rows = experts * MOST
    got = stacked(pieces)
    full = got[:, :1] < EMPTY / 2
    key = []
    for dim in (0, 1):
        row = iota((rows, rows), dim)
        local_row = row - block_of(row, range(experts)) * MOST
        key.append((me ^ block_of(row, far_first(experts))) * MOST + local_row)
    earlier = jnp.where(key[1] < key[0], 1.0, 0.0).astype(BF)
    wide = jnp.broadcast_to(full, (rows, capacity))
    slot = mm(earlier, jnp.where(wide, 1.0, 0.0).astype(BF)).astype(jnp.int32)
    place = jnp.where((slot == iota((rows, capacity), 1)) & wide, 1.0, 0.0).astype(BF)
    return place, mm(place, got.astype(BF), ROWS).astype(BF)


def stage(count, gate_up, down, *refs):
    pieces, refs = refs[:count], refs[count:]
    held, pieces_out, sems = refs[:2], refs[2:-1], refs[-1]
    half = down.shape[1] // 2
    loads = []
    for own, out in enumerate(held):
        rows = rows_of(half, own == 1)
        for matrix in range(3):
            source = down.at[0, rows] if matrix == 2 else gate_up.at[0, matrix, rows]
            loads.append(pltpu.make_async_copy(source, out.at[matrix], sems.at[len(loads)]))
    run(loads)
    for source, target in zip(pieces, pieces_out):
        target[...] = source[...]
    wait(loads)


def other_pair(experts, capacity, *refs):
    held, out, place_out, rows_out = refs[experts:]
    place, rows_in = place_rows(experts, capacity, refs[:experts])
    place_out[...] = place
    rows_out[...] = rows_in
    for matrix in range(2):
        out[matrix] = mm(held[matrix], rows_in, LANES).T.astype(BF)


def mine_pair(rows_in, held, out):
    for matrix in range(2):
        out[matrix] = mm(held[matrix], rows_in[...], LANES).T.astype(BF)


def pair_sum(mine, other, held_out, sent_out):
    held = mine[...].astype(F32) + other[...].astype(F32)
    held_out[...] = held
    sent_out[...] = held.astype(BF)


def act_part(experts, own, *refs):
    place, held = refs[experts : experts + 2]
    pieces = refs[: experts - 2][::-1] + refs[experts - 2 : experts]
    rows_grad = mm(place[...], stacked(pieces, 1).astype(BF), ROWS).astype(BF)
    if own:
        refs[-2][...] = rows_grad
    refs[-1][...] = mm(held[2], rows_grad, LANES).T.astype(BF)


def gates(pair, pair_far, act_out, by_gate, by_up):
    gate_sum = pair[0] + pair_far[0].astype(F32)
    up_sum = pair[1] + pair_far[1].astype(F32)
    sigmoid_gate = jax.nn.sigmoid(gate_sum)
    silu_gate = gate_sum * sigmoid_gate
    act_out[...] = (silu_gate * up_sum).astype(BF)
    by_gate[...] = up_sum * sigmoid_gate * (1.0 + gate_sum * (1.0 - sigmoid_gate))
    by_up[...] = silu_gate


def grads_of(act, act_far, by_gate, by_up, _, out):
    grad_act = act[...] + act_far[...].astype(F32)
    out[0] = (grad_act * by_gate[...]).astype(BF)
    out[1] = (grad_act * by_up[...]).astype(BF)


def own_rows(mine, held, out):
    out[...] = mm(mine[0], held[0]) + mm(mine[1], held[1])


def other_rows(experts, total, other, place, held, *refs):
    pieces, whole = refs[:experts], refs[experts]
    rows = total[...] + mm(other[0], held[0]) + mm(other[1], held[1])
    whole[...] = mm(place[...], rows.astype(BF))
    me = lax.axis_index("ex")
    for piece, step in zip(pieces, shifts(experts)):
        piece[...] = whole[place_of(lax.rem(me + step, experts), experts)].astype(BF)


def weight_grads(mine_act, other_act, mine, other, rows_in, rows_grad, pair_out, down_out, held, sems):
    core = lax.axis_index("ey") & 1
    half = mine_act.shape[1]
    step = half // 2
    stores = []
    for matrix in range(3):
        right = rows_grad[...] if matrix == 0 else rows_in[...]
        for own in range(2):
            start = (core if own else 1 - core) * half
            for part in range(2):
                columns = slice(part * step, (part + 1) * step)
                if matrix == 0:
                    left = (mine_act if own else other_act)[:, columns]
                else:
                    left = (mine if own else other)[matrix - 1, :, columns]
                at = len(stores)
                held[at] = mm(left, right, ROWS).astype(BF)
                rows = pl.ds(start + part * step, step)
                target = down_out.at[0, rows] if matrix == 0 else pair_out.at[0, matrix - 1, rows]
                store = pltpu.make_async_copy(held.at[at], target, sems.at[at])
                store.start()
                stores.append(store)
    for store in stores:
        store.wait()


def combine(experts, pick, *refs):
    out, whole, held, sems = refs[experts:]
    me = lax.axis_index("ex")
    for piece, step in zip(refs[:experts], shifts(experts)):
        whole[place_of(lax.rem(me + experts - step, experts), experts)] = piece[...].astype(F32)
    home = whole[...].astype(BF)
    rows = out.shape[0] // held.shape[0]
    stores = []
    for at in range(held.shape[0]):
        part = pick[:, at * rows : (at + 1) * rows]
        held[at] = mm(part, home, ROWS).astype(BF)
        target = out.at[pl.ds(at * rows, rows)]
        stores += run([pltpu.make_async_copy(held.at[at], target, sems.at[at])])
    wait(stores)


def far(value):
    return pltpu.with_memory_space_constraint(value, pltpu.HBM)


def place_of(partner, experts):
    k = lax.axis_index("ex") ^ partner
    spot = jnp.int32(0)
    for at, name in enumerate(far_first(experts)):
        spot = spot + jnp.where(k == name, at * MOST, 0)
    return pl.ds(pl.multiple_of(spot, 8), MOST)


def shifts(experts):
    return list(range(1, experts)) + [0]


def shift(value, axis, step):
    count = lax.axis_size(axis)
    return lax.ppermute(value, axis, [(i, (i + step) % count) for i in range(count)])


def swap(value, axis, bit):
    count = lax.axis_size(axis)
    return lax.ppermute(value, axis, [(i, i ^ bit) for i in range(count)])


def exchange(pieces, axis):
    order = far_first(len(pieces))
    return [swap(piece, axis, k) if k else piece for piece, k in zip(pieces, order)]


def local(inputs, grad_output, routes, gate_probs, gate_up, down_proj):
    experts = lax.axis_size("ex")
    ways = lax.axis_size("ey")
    tokens, width = inputs.shape
    hidden = gate_up.shape[2]
    half = hidden // 2
    capacity = 5 * tokens * experts * routes.shape[1] // (4 * EXPERTS)
    rows = experts * MOST
    weight_bytes = hidden * width * 2
    weight_flops = 2 * capacity * hidden * width
    sds = jax.ShapeDtypeStruct
    piece = [sds((MOST, width), BF)] * experts
    dma = lambda count: pltpu.SemaphoreType.DMA((count,))

    order = far_first(experts)
    pick, prob, grads, *send_in, own_in = call(
        functools.partial(pick_inputs, experts),
        [
            sds((rows, tokens), BF),
            sds((rows, 1), F32),
            pltpu.VMEM((tokens, width), BF),
        ]
        + piece,
        (far(routes.T), far(gate_probs.T), far(inputs), far(grad_output)),
        [HBM] * 4,
        [
            pltpu.VMEM(routes.shape[::-1], jnp.int32),
            pltpu.VMEM(routes.shape[::-1], BF),
            pltpu.VMEM((tokens, width), BF),
            dma(4),
        ],
        flops=2 * rows * tokens * width,
        traffic=4 * tokens * width,
    )
    near, *send_grad = call(
        functools.partial(pick_grads, experts),
        [sds((2 * MOST, width), BF)] + piece[1:],
        (pick, prob, grads, send_in[-1]),
        [VMEM] * 4,
        flops=2 * rows * tokens * width,
        traffic=2 * tokens * width,
    )
    near = swap(near, "ex", 1)
    got_in = [swap(part, "ex", k) for part, k in zip(send_in[:-1], order)] + [near, own_in]
    held_other, held_mine, *send_grad = call(
        functools.partial(stage, experts - 1),
        [pltpu.VMEM((3, half, width), BF)] * 2 + piece[1:],
        (far(gate_up), far(down_proj), *send_grad),
        [HBM] * 2 + [VMEM] * (experts - 1),
        [dma(6)],
        flops=WCOST * weight_flops,
        traffic=WCOST * weight_bytes,
    )
    got_grad = [swap(part, "ex", k) for part, k in zip(send_grad[:-1], order)][::-1]
    got_grad = got_grad + [near, send_grad[-1]]
    pair_other, place, rows_in = call(
        functools.partial(other_pair, experts, capacity),
        [sds((2, capacity, half), BF), sds((rows, capacity), BF), sds((capacity, width), BF)],
        (*got_in, held_other),
        [VMEM] * (experts + 1),
        flops=2 * weight_flops,
        traffic=weight_bytes,
    )
    pair_mine = call(
        mine_pair,
        sds((2, capacity, half), BF),
        (rows_in, held_mine),
        [VMEM] * 2,
        flops=C2COST * weight_flops,
        traffic=C2COST * weight_bytes,
    )

    def total(held, sent):
        bit = 2
        while bit * 2 < ways:
            held = held + swap(sent, "ey", bit).astype(F32)
            sent = held.astype(BF)
            bit *= 2
        return held, swap(sent, "ey", bit)

    pair, pair_sent = call(
        pair_sum,
        [sds((2, capacity, half), F32), sds((2, capacity, half), BF)],
        (pair_mine, swap(pair_other, "ey", 1)),
        [VMEM] * 2,
        traffic=10 * capacity * hidden,
    )
    pair, pair_far = total(pair, pair_sent)
    def act_of(own, held, outs, tied, cost):
        return call(
            functools.partial(act_part, experts, own),
            outs + [sds((capacity, half), BF)],
            (*got_grad, place, held, *tied),
            [VMEM] * (experts + 2) + [ANY] * len(tied),
            flops=cost * weight_flops,
            traffic=cost * weight_bytes,
        )

    (act_other,) = act_of(False, held_other, [], [pair_sent], D1COST)
    rows_grad, act_mine = act_of(True, held_mine, [sds((capacity, width), BF)], [], D2COST)
    act = act_mine.astype(F32) + swap(act_other, "ey", 1).astype(F32)
    act, act_far = total(act, act.astype(BF))
    mine_act, by_gate, by_up = call(
        gates,
        [sds((capacity, half), BF)] + [sds((capacity, half), F32)] * 2,
        (pair, pair_far),
        [VMEM] * 2,
        traffic=18 * capacity * half,
        flops=GFLOP * weight_flops,
    )
    other_act = swap(mine_act, "ey", 1)
    mine = call(
        grads_of,
        sds((2, capacity, half), BF),
        (act, act_far, by_gate, by_up, other_act),
        [VMEM] * 4 + [ANY],
        traffic=18 * capacity * half,
    )
    other = swap(mine, "ey", 1)
    own = call(
        own_rows,
        sds((capacity, width), F32),
        (mine, held_mine),
        [VMEM] * 2,
        flops=weight_flops,
        traffic=weight_bytes,
    )
    back = call(
        functools.partial(other_rows, experts),
        piece,
        (own, other, place, held_other),
        [VMEM] * 4,
        [pltpu.VMEM((rows, width), F32)],
        flops=weight_flops,
        traffic=weight_bytes,
    )
    home = [shift(part, "ex", step) if step else part for part, step in zip(back, shifts(experts))]
    pair_grad, down_grad = call(
        weight_grads,
        [sds((1, 2, hidden, width), BF), sds((1, hidden, width), BF)],
        (mine_act, other_act, mine, other, rows_in, rows_grad),
        [VMEM] * 6,
        [pltpu.VMEM((12, half // 2, width), BF), dma(12)],
        limit=24,
        flops=3 * weight_flops,
        traffic=3 * weight_bytes,
        out_specs=[ANY, ANY],
    )
    grad_inputs = call(
        functools.partial(combine, experts),
        sds((tokens, width), BF),
        (pick, *home),
        [VMEM] * (experts + 1),
        [pltpu.VMEM((rows, width), F32), pltpu.VMEM((2, tokens // 2, width), BF), dma(2)],
        flops=2 * rows * tokens * width,
        traffic=4 * tokens * width,
        out_specs=ANY,
    )
    return (grad_inputs, pair_grad, down_grad)


def solution(mesh):
    return jax.shard_map(
        local,
        mesh=mesh,
        in_specs=(
            P(("groups", "ex"), "ey"),
            P(("groups", "ex"), "ey"),
            P(("groups", "ex"), None),
            P(("groups", "ex"), None),
            P("ex", None, None, "ey"),
            P("ex", None, "ey"),
        ),
        out_specs=(
            P(("groups", "ex"), "ey"),
            P("ex", "groups", None, "ey"),
            P("ex", "groups", "ey"),
        ),
        check_vma=False,
    )
```

```python
import functools

import jax
import jax.numpy as jnp
from jax import lax
from jax.experimental import pallas as pl
from jax.experimental.pallas import tpu as pltpu
from jax.sharding import PartitionSpec as P

MOST = 40
EXPERTS = 128
EMPTY = 64.0
BF = jnp.bfloat16
F32 = jnp.float32
MIB = 1 << 20
C2COST = 100
WCOST = 100
GFLOP = 100
D1COST = 1
D2COST = 100
VMEM = pl.BlockSpec(memory_space=pltpu.VMEM)
ANY = pl.BlockSpec(memory_space=pl.ANY)
HBM = pl.BlockSpec(memory_space=pltpu.HBM)
ROWS = (((0,), (0,)), ((), ()))
LANES = (((1,), (1,)), ((), ()))
PLAIN = (((1,), (0,)), ((), ()))


def mm(left, right, dims=PLAIN):
    return lax.dot_general(left, right, dims, preferred_element_type=F32)


def iota(shape, dim):
    return lax.broadcasted_iota(jnp.int32, shape, dim)


def far_first(count):
    return sorted(range(count), key=lambda k: (-k.bit_length(), k))


def cut(source, target, sems, first, pieces):
    rows = target.shape[-2] // pieces
    out = []
    for at in range(pieces):
        part = pl.ds(at * rows, rows)
        out.append(pltpu.make_async_copy(source.at[part], target.at[part], sems.at[first + at]))
    return out


def run(loads):
    for load in loads:
        load.start()
    return loads


def wait(loads):
    for load in loads:
        load.wait()


def block_of(position, names):
    found = jnp.full_like(position, names[0])
    for at in range(1, len(names)):
        found = found + (position >= at * MOST).astype(jnp.int32) * (names[at] - names[at - 1])
    return found


def call(body, outs, operands, specs, scratch=(), limit=16, flops=0, traffic=0, out_specs=None):
    return pl.pallas_call(
        body,
        out_shape=outs,
        in_specs=specs,
        out_specs=out_specs if out_specs is not None else jax.tree.map(lambda _: VMEM, outs),
        scratch_shapes=list(scratch),
        compiler_params=pltpu.CompilerParams(vmem_limit_bytes=limit * MIB),
        cost_estimate=pl.CostEstimate(flops=flops, bytes_accessed=traffic, transcendentals=0),
    )(*operands)


def pick_inputs(experts, routes_in, probs_in, inputs, grads, pick_out, prob_out, grads_out, *refs):
    *pieces, routes, probs, held, sems = refs
    loads = run(
        [
            pltpu.make_async_copy(routes_in, routes, sems.at[0]),
            pltpu.make_async_copy(probs_in, probs, sems.at[1]),
        ]
    )
    input_loads = run(cut(inputs, held, sems, 2, 1))
    grad_loads = run(cut(grads, grads_out, sems, 3, 1))
    me = lax.axis_index("ex")
    tokens = inputs.shape[0]
    rows = experts * MOST
    order = far_first(experts)
    owner = block_of(iota((rows, routes.shape[0]), 0), order)
    named = jnp.zeros((rows, tokens), F32)
    weight = jnp.zeros((rows, tokens), F32)
    earlier = iota((tokens, tokens), 0) < iota((tokens, tokens), 1)
    earlier = jnp.where(earlier, 1.0, 0.0).astype(BF)
    row = iota((rows, tokens), 0)
    slot = row - block_of(row, range(experts)) * MOST
    wait(loads)
    chosen = routes[...]
    wide = probs[...].astype(F32)
    for k in range(experts):
        spread = jnp.where(owner == k, 1.0, 0.0).astype(BF)
        hit = chosen == (me ^ k)
        named = named + mm(spread, jnp.where(hit, 1.0, 0.0).astype(BF))
        weight = weight + mm(spread, jnp.where(hit, wide, 0.0).astype(BF))
    rank = mm(named.astype(BF), earlier).astype(jnp.int32)
    picks = (rank == slot) & (named > 0.5)
    pick = jnp.where(picks, 1.0, 0.0)
    filled = jnp.max(pick, axis=1, keepdims=True) > 0.5
    pick = pick.astype(BF)
    pick_out[...] = pick
    prob_out[...] = jnp.sum(jnp.where(picks, weight, 0.0), axis=1, keepdims=True)
    wait(input_loads)
    sent = jnp.where(filled, mm(pick, held[...]), EMPTY)
    for k in range(experts):
        pieces[k][...] = sent[k * MOST : (k + 1) * MOST].astype(BF)
    wait(grad_loads)


def pick_grads(experts, pick, prob, grads, *refs):
    near_in, near, *pieces = refs
    sent = mm(pick[...], grads[...]) * prob[...]
    parts = [sent[at * MOST : (at + 1) * MOST] for at in range(experts)]
    near[...] = jnp.concatenate([near_in[...].astype(F32), parts[-2]], axis=0).astype(BF)
    for target, part in zip(pieces, parts[:-2] + parts[-1:]):
        target[...] = part.astype(BF)


def stacked(pieces, part=0):
    rows = [piece[...].astype(F32) for piece in pieces]
    rows = [row[part * MOST : (part + 1) * MOST] if row.shape[0] > MOST else row for row in rows]
    return jnp.concatenate(rows, axis=0)


def rows_of(half, own):
    core = lax.axis_index("ey") & 1
    return pl.ds(pl.multiple_of((core if own else 1 - core) * half, 128), half)


def place_rows(experts, capacity, pieces):
    me = lax.axis_index("ex")
    rows = experts * MOST
    got = stacked(pieces)
    full = got[:, :1] < EMPTY / 2
    key = []
    for dim in (0, 1):
        row = iota((rows, rows), dim)
        local_row = row - block_of(row, range(experts)) * MOST
        key.append((me ^ block_of(row, far_first(experts))) * MOST + local_row)
    earlier = jnp.where(key[1] < key[0], 1.0, 0.0).astype(BF)
    wide = jnp.broadcast_to(full, (rows, capacity))
    slot = mm(earlier, jnp.where(wide, 1.0, 0.0).astype(BF)).astype(jnp.int32)
    place = jnp.where((slot == iota((rows, capacity), 1)) & wide, 1.0, 0.0).astype(BF)
    return place, mm(place, got.astype(BF), ROWS).astype(BF)


def stage(count, gate_up, down, *refs):
    pieces, refs = refs[:count], refs[count:]
    held, pieces_out, sems = refs[:2], refs[2:-1], refs[-1]
    half = down.shape[1] // 2
    loads = []
    for own, out in enumerate(held):
        rows = rows_of(half, own == 1)
        for matrix in range(3):
            source = down.at[0, rows] if matrix == 2 else gate_up.at[0, matrix, rows]
            loads.append(pltpu.make_async_copy(source, out.at[matrix], sems.at[len(loads)]))
    run(loads)
    for source, target in zip(pieces, pieces_out):
        target[...] = source[...]
    wait(loads)


def other_pair(experts, capacity, *refs):
    held, out, place_out, rows_out = refs[experts:]
    place, rows_in = place_rows(experts, capacity, refs[:experts])
    place_out[...] = place
    rows_out[...] = rows_in
    for matrix in range(2):
        out[matrix] = mm(rows_in, held[matrix], LANES).astype(BF)


def mine_pair(rows_in, held, out):
    for matrix in range(2):
        out[matrix] = mm(rows_in[...], held[matrix], LANES).astype(BF)


def pair_sum(mine, other, held_out, sent_out):
    held = mine[...].astype(F32) + other[...].astype(F32)
    held_out[...] = held
    sent_out[...] = held.astype(BF)


def act_part(experts, own, *refs):
    place, held = refs[experts : experts + 2]
    pieces = refs[: experts - 2][::-1] + refs[experts - 2 : experts]
    rows_grad = mm(place[...], stacked(pieces, 1).astype(BF), ROWS).astype(BF)
    if own:
        refs[-2][...] = rows_grad
    refs[-1][...] = mm(rows_grad, held[2], LANES).astype(BF)


def gates(pair, pair_far, act_out, by_gate, by_up):
    gate_sum = pair[0] + pair_far[0].astype(F32)
    up_sum = pair[1] + pair_far[1].astype(F32)
    sigmoid_gate = jax.nn.sigmoid(gate_sum)
    silu_gate = gate_sum * sigmoid_gate
    act_out[...] = (silu_gate * up_sum).astype(BF)
    by_gate[...] = up_sum * sigmoid_gate * (1.0 + gate_sum * (1.0 - sigmoid_gate))
    by_up[...] = silu_gate


def grads_of(act, act_far, by_gate, by_up, _, out):
    grad_act = act[...] + act_far[...].astype(F32)
    out[0] = (grad_act * by_gate[...]).astype(BF)
    out[1] = (grad_act * by_up[...]).astype(BF)


def own_rows(mine, held, out):
    out[...] = mm(mine[0], held[0]) + mm(mine[1], held[1])


def other_rows(experts, total, other, place, held, *refs):
    pieces, whole = refs[:experts], refs[experts]
    rows = total[...] + mm(other[0], held[0]) + mm(other[1], held[1])
    whole[...] = mm(place[...], rows.astype(BF))
    for piece, step in zip(pieces, steps(experts)):
        piece[...] = whole[place_of(ahead(step, experts), experts)].astype(BF)


def weight_grads(mine_act, other_act, mine, other, rows_in, rows_grad, pair_out, down_out, held, sems):
    core = lax.axis_index("ey") & 1
    half = mine_act.shape[1]
    step = half // 2
    stores = []
    for matrix in range(3):
        right = rows_grad[...] if matrix == 0 else rows_in[...]
        for own in range(2):
            start = (core if own else 1 - core) * half
            for part in range(2):
                columns = slice(part * step, (part + 1) * step)
                if matrix == 0:
                    left = (mine_act if own else other_act)[:, columns]
                else:
                    left = (mine if own else other)[matrix - 1, :, columns]
                at = len(stores)
                held[at] = mm(left, right, ROWS).astype(BF)
                rows = pl.ds(start + part * step, step)
                target = down_out.at[0, rows] if matrix == 0 else pair_out.at[0, matrix - 1, rows]
                store = pltpu.make_async_copy(held.at[at], target, sems.at[at])
                store.start()
                stores.append(store)
    for store in stores:
        store.wait()


def combine(experts, pick, *refs):
    out, whole, held, sems = refs[experts:]
    for piece, step in zip(refs[:experts], steps(experts)):
        whole[place_of(ahead(experts - step, experts), experts)] = piece[...].astype(F32)
    home = whole[...].astype(BF)
    rows = out.shape[0] // held.shape[0]
    stores = []
    for at in range(held.shape[0]):
        part = pick[:, at * rows : (at + 1) * rows]
        held[at] = mm(part, home, ROWS).astype(BF)
        target = out.at[pl.ds(at * rows, rows)]
        stores += run([pltpu.make_async_copy(held.at[at], target, sems.at[at])])
    wait(stores)


def far(value):
    return pltpu.with_memory_space_constraint(value, pltpu.HBM)


def place_of(partner, experts):
    k = lax.axis_index("ex") ^ partner
    spot = jnp.int32(0)
    for at, name in enumerate(far_first(experts)):
        spot = spot + jnp.where(k == name, at * MOST, 0)
    return pl.ds(pl.multiple_of(spot, 8), MOST)


def tour(count):
    bits = count.bit_length() - 1
    return [sum(((i >> b) & 1) << (bits - 1 - b) for b in range(bits)) for i in range(count)]


def steps(count):
    found = []
    for step in range(1, count // 2 + 1):
        found += [step, count - step]
    return list(dict.fromkeys(found)) + [0]


def ahead(step, count):
    me, names = lax.axis_index("ex"), tour(count)
    found = jnp.int32(0)
    for at, name in enumerate(names):
        found = found + jnp.where(me == name, names[(at + step) % count], 0)
    return found


def shift(value, axis, step):
    count = lax.axis_size(axis)
    names = tour(count)
    return lax.ppermute(
        value, axis, [(name, names[(at + step) % count]) for at, name in enumerate(names)]
    )


def swap(value, axis, bit):
    count = lax.axis_size(axis)
    return lax.ppermute(value, axis, [(i, i ^ bit) for i in range(count)])


def exchange(pieces, axis):
    order = far_first(len(pieces))
    return [swap(piece, axis, k) if k else piece for piece, k in zip(pieces, order)]


def local(inputs, grad_output, routes, gate_probs, gate_up, down_proj):
    experts = lax.axis_size("ex")
    ways = lax.axis_size("ey")
    tokens, width = inputs.shape
    hidden = gate_up.shape[2]
    half = hidden // 2
    capacity = 5 * tokens * experts * routes.shape[1] // (4 * EXPERTS)
    rows = experts * MOST
    weight_bytes = hidden * width * 2
    weight_flops = 2 * capacity * hidden * width
    sds = jax.ShapeDtypeStruct
    piece = [sds((MOST, width), BF)] * experts
    dma = lambda count: pltpu.SemaphoreType.DMA((count,))

    order = far_first(experts)
    pick, prob, grads, *send_in, own_in = call(
        functools.partial(pick_inputs, experts),
        [
            sds((rows, tokens), BF),
            sds((rows, 1), F32),
            pltpu.VMEM((tokens, width), BF),
        ]
        + piece,
        (far(routes.T), far(gate_probs.T), far(inputs), far(grad_output)),
        [HBM] * 4,
        [
            pltpu.VMEM(routes.shape[::-1], jnp.int32),
            pltpu.VMEM(routes.shape[::-1], BF),
            pltpu.VMEM((tokens, width), BF),
            dma(4),
        ],
        flops=2 * rows * tokens * width,
        traffic=4 * tokens * width,
    )
    near, *send_grad = call(
        functools.partial(pick_grads, experts),
        [sds((2 * MOST, width), BF)] + piece[1:],
        (pick, prob, grads, send_in[-1]),
        [VMEM] * 4,
        flops=2 * rows * tokens * width,
        traffic=2 * tokens * width,
    )
    near = swap(near, "ex", 1)
    got_in = [swap(part, "ex", k) for part, k in zip(send_in[:-1], order)] + [near, own_in]
    held_other, held_mine, *send_grad = call(
        functools.partial(stage, experts - 1),
        [pltpu.VMEM((3, half, width), BF)] * 2 + piece[1:],
        (far(gate_up), far(down_proj), *send_grad),
        [HBM] * 2 + [VMEM] * (experts - 1),
        [dma(6)],
        flops=WCOST * weight_flops,
        traffic=WCOST * weight_bytes,
    )
    got_grad = [swap(part, "ex", k) for part, k in zip(send_grad[:-1], order)][::-1]
    got_grad = got_grad + [near, send_grad[-1]]
    pair_other, place, rows_in = call(
        functools.partial(other_pair, experts, capacity),
        [sds((2, capacity, half), BF), sds((rows, capacity), BF), sds((capacity, width), BF)],
        (*got_in, held_other),
        [VMEM] * (experts + 1),
        flops=2 * weight_flops,
        traffic=weight_bytes,
    )
    pair_mine = call(
        mine_pair,
        sds((2, capacity, half), BF),
        (rows_in, held_mine),
        [VMEM] * 2,
        flops=C2COST * weight_flops,
        traffic=C2COST * weight_bytes,
    )

    def total(held, sent):
        bit = 2
        while bit * 2 < ways:
            held = held + swap(sent, "ey", bit).astype(F32)
            sent = held.astype(BF)
            bit *= 2
        return held, swap(sent, "ey", bit)

    pair, pair_sent = call(
        pair_sum,
        [sds((2, capacity, half), F32), sds((2, capacity, half), BF)],
        (pair_mine, swap(pair_other, "ey", 1)),
        [VMEM] * 2,
        traffic=10 * capacity * hidden,
    )
    pair, pair_far = total(pair, pair_sent)
    def act_of(own, held, outs, tied, cost):
        return call(
            functools.partial(act_part, experts, own),
            outs + [sds((capacity, half), BF)],
            (*got_grad, place, held, *tied),
            [VMEM] * (experts + 2) + [ANY] * len(tied),
            flops=cost * weight_flops,
            traffic=cost * weight_bytes,
        )

    (act_other,) = act_of(False, held_other, [], [pair_sent], D1COST)
    rows_grad, act_mine = act_of(True, held_mine, [sds((capacity, width), BF)], [], D2COST)
    act = act_mine.astype(F32) + swap(act_other, "ey", 1).astype(F32)
    act, act_far = total(act, act.astype(BF))
    mine_act, by_gate, by_up = call(
        gates,
        [sds((capacity, half), BF)] + [sds((capacity, half), F32)] * 2,
        (pair, pair_far),
        [VMEM] * 2,
        traffic=18 * capacity * half,
        flops=GFLOP * weight_flops,
    )
    other_act = swap(mine_act, "ey", 1)
    mine = call(
        grads_of,
        sds((2, capacity, half), BF),
        (act, act_far, by_gate, by_up, other_act),
        [VMEM] * 4 + [ANY],
        traffic=18 * capacity * half,
    )
    other = swap(mine, "ey", 1)
    own = call(
        own_rows,
        sds((capacity, width), F32),
        (mine, held_mine),
        [VMEM] * 2,
        flops=weight_flops,
        traffic=weight_bytes,
    )
    back = call(
        functools.partial(other_rows, experts),
        piece,
        (own, other, place, held_other),
        [VMEM] * 4,
        [pltpu.VMEM((rows, width), F32)],
        flops=weight_flops,
        traffic=weight_bytes,
    )
    home = [shift(part, "ex", step) if step else part for part, step in zip(back, steps(experts))]
    pair_grad, down_grad = call(
        weight_grads,
        [sds((1, 2, hidden, width), BF), sds((1, hidden, width), BF)],
        (mine_act, other_act, mine, other, rows_in, rows_grad),
        [VMEM] * 6,
        [pltpu.VMEM((12, half // 2, width), BF), dma(12)],
        limit=24,
        flops=3 * weight_flops,
        traffic=3 * weight_bytes,
        out_specs=[ANY, ANY],
    )
    grad_inputs = call(
        functools.partial(combine, experts),
        sds((tokens, width), BF),
        (pick, *home),
        [VMEM] * (experts + 1),
        [pltpu.VMEM((rows, width), F32), pltpu.VMEM((2, tokens // 2, width), BF), dma(2)],
        flops=2 * rows * tokens * width,
        traffic=4 * tokens * width,
        out_specs=ANY,
    )
    return (grad_inputs, pair_grad, down_grad)


def solution(mesh):
    return jax.shard_map(
        local,
        mesh=mesh,
        in_specs=(
            P(("groups", "ex"), "ey"),
            P(("groups", "ex"), "ey"),
            P(("groups", "ex"), None),
            P(("groups", "ex"), None),
            P("ex", None, None, "ey"),
            P("ex", None, "ey"),
        ),
        out_specs=(
            P(("groups", "ex"), "ey"),
            P("ex", "groups", None, "ey"),
            P("ex", "groups", "ey"),
        ),
        check_vma=False,
    )
```

```python
import functools

import jax
import jax.numpy as jnp
from jax import lax
from jax.experimental import pallas as pl
from jax.experimental.pallas import tpu as pltpu
from jax.sharding import PartitionSpec as P

MOST = 40
EXPERTS = 128
EMPTY = 64.0
BF = jnp.bfloat16
F32 = jnp.float32
MIB = 1 << 20
C2COST = 100
C0COST = 4.75
WCOST = 1
GFLOP = 100
D1COST = 1
D2COST = 100
VMEM = pl.BlockSpec(memory_space=pltpu.VMEM)
ANY = pl.BlockSpec(memory_space=pl.ANY)
HBM = pl.BlockSpec(memory_space=pltpu.HBM)
ROWS = (((0,), (0,)), ((), ()))
LANES = (((1,), (1,)), ((), ()))
PLAIN = (((1,), (0,)), ((), ()))


def mm(left, right, dims=PLAIN):
    return lax.dot_general(left, right, dims, preferred_element_type=F32)


def iota(shape, dim):
    return lax.broadcasted_iota(jnp.int32, shape, dim)


def far_first(count):
    return sorted(range(count), key=lambda k: (-k.bit_length(), k))


def cut(source, target, sems, first, pieces):
    rows = target.shape[-2] // pieces
    out = []
    for at in range(pieces):
        part = pl.ds(at * rows, rows)
        out.append(pltpu.make_async_copy(source.at[part], target.at[part], sems.at[first + at]))
    return out


def run(loads):
    for load in loads:
        load.start()
    return loads


def wait(loads):
    for load in loads:
        load.wait()


def block_of(position, names):
    found = jnp.full_like(position, names[0])
    for at in range(1, len(names)):
        found = found + (position >= at * MOST).astype(jnp.int32) * (names[at] - names[at - 1])
    return found


def call(body, outs, operands, specs, scratch=(), limit=16, flops=0, traffic=0, out_specs=None):
    return pl.pallas_call(
        body,
        out_shape=outs,
        in_specs=specs,
        out_specs=out_specs if out_specs is not None else jax.tree.map(lambda _: VMEM, outs),
        scratch_shapes=list(scratch),
        compiler_params=pltpu.CompilerParams(vmem_limit_bytes=limit * MIB),
        cost_estimate=pl.CostEstimate(flops=flops, bytes_accessed=traffic, transcendentals=0),
    )(*operands)


def pick_inputs(experts, routes_in, probs_in, inputs, grads, pick_out, prob_out, grads_out, *refs):
    *pieces, routes, probs, held, sems = refs
    loads = run(
        [
            pltpu.make_async_copy(routes_in, routes, sems.at[0]),
            pltpu.make_async_copy(probs_in, probs, sems.at[1]),
        ]
    )
    input_loads = run(cut(inputs, held, sems, 2, 1))
    grad_loads = run(cut(grads, grads_out, sems, 3, 1))
    me = lax.axis_index("ex")
    tokens = inputs.shape[0]
    rows = experts * MOST
    order = far_first(experts)
    owner = block_of(iota((rows, routes.shape[0]), 0), order)
    named = jnp.zeros((rows, tokens), F32)
    weight = jnp.zeros((rows, tokens), F32)
    earlier = iota((tokens, tokens), 0) < iota((tokens, tokens), 1)
    earlier = jnp.where(earlier, 1.0, 0.0).astype(BF)
    row = iota((rows, tokens), 0)
    slot = row - block_of(row, range(experts)) * MOST
    wait(loads)
    chosen = routes[...]
    wide = probs[...].astype(F32)
    for k in range(experts):
        spread = jnp.where(owner == k, 1.0, 0.0).astype(BF)
        hit = chosen == (me ^ k)
        named = named + mm(spread, jnp.where(hit, 1.0, 0.0).astype(BF))
        weight = weight + mm(spread, jnp.where(hit, wide, 0.0).astype(BF))
    rank = mm(named.astype(BF), earlier).astype(jnp.int32)
    picks = (rank == slot) & (named > 0.5)
    pick = jnp.where(picks, 1.0, 0.0)
    filled = jnp.max(pick, axis=1, keepdims=True) > 0.5
    pick = pick.astype(BF)
    pick_out[...] = pick
    prob_out[...] = jnp.sum(jnp.where(picks, weight, 0.0), axis=1, keepdims=True)
    wait(input_loads)
    sent = jnp.where(filled, mm(pick, held[...]), EMPTY)
    for k in range(experts):
        pieces[k][...] = sent[k * MOST : (k + 1) * MOST].astype(BF)
    wait(grad_loads)


def pick_grads(experts, pick, prob, grads, *refs):
    near_in, near, *pieces = refs
    sent = mm(pick[...], grads[...]) * prob[...]
    parts = [sent[at * MOST : (at + 1) * MOST] for at in range(experts)]
    near[...] = jnp.concatenate([near_in[...].astype(F32), parts[-2]], axis=0).astype(BF)
    for target, part in zip(pieces, parts[:-2] + parts[-1:]):
        target[...] = part.astype(BF)


def stacked(pieces, part=0):
    rows = [piece[...].astype(F32) for piece in pieces]
    rows = [row[part * MOST : (part + 1) * MOST] if row.shape[0] > MOST else row for row in rows]
    return jnp.concatenate(rows, axis=0)


def rows_of(half, own):
    core = lax.axis_index("ey") & 1
    return pl.ds(pl.multiple_of((core if own else 1 - core) * half, 128), half)


def early_rows(first, out):
    out[...] = first[...]


def place_rows(experts, capacity, pieces):
    me = lax.axis_index("ex")
    rows = experts * MOST
    got = stacked(pieces)
    full = got[:, :1] < EMPTY / 2
    key = []
    for dim in (0, 1):
        row = iota((rows, rows), dim)
        local_row = row - block_of(row, range(experts)) * MOST
        key.append((me ^ block_of(row, far_first(experts))) * MOST + local_row)
    earlier = jnp.where(key[1] < key[0], 1.0, 0.0).astype(BF)
    wide = jnp.broadcast_to(full, (rows, capacity))
    slot = mm(earlier, jnp.where(wide, 1.0, 0.0).astype(BF)).astype(jnp.int32)
    place = jnp.where((slot == iota((rows, capacity), 1)) & wide, 1.0, 0.0).astype(BF)
    return place, mm(place, got.astype(BF), ROWS).astype(BF)


def stage(count, gate_up, down, *refs):
    pieces, refs = refs[:count], refs[count:]
    held, pieces_out, sems = refs[:2], refs[2:-1], refs[-1]
    half = down.shape[1] // 2
    loads = []
    for own, out in enumerate(held):
        rows = rows_of(half, own == 1)
        for matrix in range(3):
            source = down.at[0, rows] if matrix == 2 else gate_up.at[0, matrix, rows]
            loads.append(pltpu.make_async_copy(source, out.at[matrix], sems.at[len(loads)]))
    run(loads)
    for source, target in zip(pieces, pieces_out):
        target[...] = source[...]
    wait(loads)


def other_pair(experts, capacity, *refs):
    held, out, place_out, rows_out = refs[experts:]
    place, rows_in = place_rows(experts, capacity, refs[:experts])
    place_out[...] = place
    rows_out[...] = rows_in
    for matrix in range(2):
        out[matrix] = mm(rows_in, held[matrix], LANES).astype(BF)


def mine_pair(rows_in, held, out):
    for matrix in range(2):
        out[matrix] = mm(rows_in[...], held[matrix], LANES).astype(BF)


def pair_sum(mine, other, held_out, sent_out):
    held = mine[...].astype(F32) + other[...].astype(F32)
    held_out[...] = held
    sent_out[...] = held.astype(BF)


def act_part(experts, own, *refs):
    place, held = refs[experts : experts + 2]
    rows_grad = mm(place[...], stacked(refs[:experts], 1).astype(BF), ROWS).astype(BF)
    if own:
        refs[-2][...] = rows_grad
    refs[-1][...] = mm(rows_grad, held[2], LANES).astype(BF)


def gates(pair, pair_far, act_out, by_gate, by_up):
    gate_sum = pair[0] + pair_far[0].astype(F32)
    up_sum = pair[1] + pair_far[1].astype(F32)
    sigmoid_gate = jax.nn.sigmoid(gate_sum)
    silu_gate = gate_sum * sigmoid_gate
    act_out[...] = (silu_gate * up_sum).astype(BF)
    by_gate[...] = up_sum * sigmoid_gate * (1.0 + gate_sum * (1.0 - sigmoid_gate))
    by_up[...] = silu_gate


def grads_of(act, act_far, by_gate, by_up, _, out):
    grad_act = act[...] + act_far[...].astype(F32)
    out[0] = (grad_act * by_gate[...]).astype(BF)
    out[1] = (grad_act * by_up[...]).astype(BF)


def own_rows(mine, held, out):
    out[...] = mm(mine[0], held[0]) + mm(mine[1], held[1])


def other_rows(experts, total, other, place, held, *refs):
    pieces, whole = refs[:experts], refs[experts]
    rows = total[...] + mm(other[0], held[0]) + mm(other[1], held[1])
    whole[...] = mm(place[...], rows.astype(BF))
    for piece, step in zip(pieces, steps(experts)):
        piece[...] = whole[place_of(ahead(step, experts), experts)].astype(BF)


def weight_grads(mine_act, other_act, mine, other, rows_in, rows_grad, pair_out, down_out, held, sems):
    core = lax.axis_index("ey") & 1
    half = mine_act.shape[1]
    step = half // 2
    stores = []
    for matrix in range(3):
        right = rows_grad[...] if matrix == 0 else rows_in[...]
        for own in range(2):
            start = (core if own else 1 - core) * half
            for part in range(2):
                columns = slice(part * step, (part + 1) * step)
                if matrix == 0:
                    left = (mine_act if own else other_act)[:, columns]
                else:
                    left = (mine if own else other)[matrix - 1, :, columns]
                at = len(stores)
                held[at] = mm(left, right, ROWS).astype(BF)
                rows = pl.ds(start + part * step, step)
                target = down_out.at[0, rows] if matrix == 0 else pair_out.at[0, matrix - 1, rows]
                store = pltpu.make_async_copy(held.at[at], target, sems.at[at])
                store.start()
                stores.append(store)
    for store in stores:
        store.wait()


def combine(experts, pick, *refs):
    out, whole, held, sems = refs[experts:]
    for piece, step in zip(refs[:experts], steps(experts)):
        whole[place_of(ahead(experts - step, experts), experts)] = piece[...].astype(F32)
    home = whole[...].astype(BF)
    rows = out.shape[0] // held.shape[0]
    stores = []
    for at in range(held.shape[0]):
        part = pick[:, at * rows : (at + 1) * rows]
        held[at] = mm(part, home, ROWS).astype(BF)
        target = out.at[pl.ds(at * rows, rows)]
        stores += run([pltpu.make_async_copy(held.at[at], target, sems.at[at])])
    wait(stores)


def far(value):
    return pltpu.with_memory_space_constraint(value, pltpu.HBM)


def place_of(partner, experts):
    k = lax.axis_index("ex") ^ partner
    spot = jnp.int32(0)
    for at, name in enumerate(far_first(experts)):
        spot = spot + jnp.where(k == name, at * MOST, 0)
    return pl.ds(pl.multiple_of(spot, 8), MOST)


def tour(count):
    bits = count.bit_length() - 1
    return [sum(((i >> b) & 1) << (bits - 1 - b) for b in range(bits)) for i in range(count)]


def steps(count):
    found = []
    for step in range(1, count // 2 + 1):
        found += [step, count - step]
    return list(dict.fromkeys(found)) + [0]


def ahead(step, count):
    me, names = lax.axis_index("ex"), tour(count)
    found = jnp.int32(0)
    for at, name in enumerate(names):
        found = found + jnp.where(me == name, names[(at + step) % count], 0)
    return found


def shift(value, axis, step):
    count = lax.axis_size(axis)
    names = tour(count)
    return lax.ppermute(
        value, axis, [(name, names[(at + step) % count]) for at, name in enumerate(names)]
    )


def swap(value, axis, bit):
    count = lax.axis_size(axis)
    return lax.ppermute(value, axis, [(i, i ^ bit) for i in range(count)])


def exchange(pieces, axis):
    order = far_first(len(pieces))
    return [swap(piece, axis, k) if k else piece for piece, k in zip(pieces, order)]


def local(inputs, grad_output, routes, gate_probs, gate_up, down_proj):
    experts = lax.axis_size("ex")
    ways = lax.axis_size("ey")
    tokens, width = inputs.shape
    hidden = gate_up.shape[2]
    half = hidden // 2
    capacity = 5 * tokens * experts * routes.shape[1] // (4 * EXPERTS)
    rows = experts * MOST
    weight_bytes = hidden * width * 2
    weight_flops = 2 * capacity * hidden * width
    sds = jax.ShapeDtypeStruct
    piece = [sds((MOST, width), BF)] * experts
    dma = lambda count: pltpu.SemaphoreType.DMA((count,))

    order = far_first(experts)
    pick, prob, grads, *send_in, own_in = call(
        functools.partial(pick_inputs, experts),
        [
            sds((rows, tokens), BF),
            sds((rows, 1), F32),
            pltpu.VMEM((tokens, width), BF),
        ]
        + piece,
        (far(routes.T), far(gate_probs.T), far(inputs), far(grad_output)),
        [HBM] * 4,
        [
            pltpu.VMEM(routes.shape[::-1], jnp.int32),
            pltpu.VMEM(routes.shape[::-1], BF),
            pltpu.VMEM((tokens, width), BF),
            dma(4),
        ],
        flops=2 * rows * tokens * width,
        traffic=4 * tokens * width,
    )
    near, *send_grad = call(
        functools.partial(pick_grads, experts),
        [sds((2 * MOST, width), BF)] + piece[1:],
        (pick, prob, grads, send_in[-1]),
        [VMEM] * 4,
        flops=2 * rows * tokens * width,
        traffic=2 * tokens * width,
    )
    near = swap(near, "ex", 1)
    got_in = [swap(part, "ex", k) for part, k in zip(send_in[:-1], order)] + [near, own_in]
    got_in[0] = call(
        early_rows,
        piece[0],
        (got_in[0],),
        [VMEM],
        flops=int(C0COST * weight_flops),
        traffic=weight_bytes,
    )
    held_other, held_mine, *send_grad = call(
        functools.partial(stage, experts - 1),
        [pltpu.VMEM((3, half, width), BF)] * 2 + piece[1:],
        (far(gate_up), far(down_proj), *send_grad),
        [HBM] * 2 + [VMEM] * (experts - 1),
        [dma(6)],
        flops=WCOST * weight_flops,
        traffic=WCOST * weight_bytes,
    )
    got_grad = [swap(part, "ex", k) for part, k in zip(send_grad[:-1], order)]
    got_grad = got_grad + [near, send_grad[-1]]
    pair_other, place, rows_in = call(
        functools.partial(other_pair, experts, capacity),
        [sds((2, capacity, half), BF), sds((rows, capacity), BF), sds((capacity, width), BF)],
        (*got_in, held_other),
        [VMEM] * (experts + 1),
        flops=2 * weight_flops,
        traffic=weight_bytes,
    )
    pair_mine = call(
        mine_pair,
        sds((2, capacity, half), BF),
        (rows_in, held_mine),
        [VMEM] * 2,
        flops=C2COST * weight_flops,
        traffic=C2COST * weight_bytes,
    )

    def total(held, sent):
        bit = 2
        while bit * 2 < ways:
            held = held + swap(sent, "ey", bit).astype(F32)
            sent = held.astype(BF)
            bit *= 2
        return held, swap(sent, "ey", bit)

    pair, pair_sent = call(
        pair_sum,
        [sds((2, capacity, half), F32), sds((2, capacity, half), BF)],
        (pair_mine, swap(pair_other, "ey", 1)),
        [VMEM] * 2,
        traffic=10 * capacity * hidden,
    )
    pair, pair_far = total(pair, pair_sent)
    def act_of(own, held, outs, tied, cost):
        return call(
            functools.partial(act_part, experts, own),
            outs + [sds((capacity, half), BF)],
            (*got_grad, place, held, *tied),
            [VMEM] * (experts + 2) + [ANY] * len(tied),
            flops=cost * weight_flops,
            traffic=cost * weight_bytes,
        )

    (act_other,) = act_of(False, held_other, [], [pair_sent], D1COST)
    rows_grad, act_mine = act_of(True, held_mine, [sds((capacity, width), BF)], [], D2COST)
    act = act_mine.astype(F32) + swap(act_other, "ey", 1).astype(F32)
    act, act_far = total(act, act.astype(BF))
    mine_act, by_gate, by_up = call(
        gates,
        [sds((capacity, half), BF)] + [sds((capacity, half), F32)] * 2,
        (pair, pair_far),
        [VMEM] * 2,
        traffic=18 * capacity * half,
        flops=GFLOP * weight_flops,
    )
    other_act = swap(mine_act, "ey", 1)
    mine = call(
        grads_of,
        sds((2, capacity, half), BF),
        (act, act_far, by_gate, by_up, other_act),
        [VMEM] * 4 + [ANY],
        traffic=18 * capacity * half,
    )
    other = swap(mine, "ey", 1)
    own = call(
        own_rows,
        sds((capacity, width), F32),
        (mine, held_mine),
        [VMEM] * 2,
        flops=weight_flops,
        traffic=weight_bytes,
    )
    back = call(
        functools.partial(other_rows, experts),
        piece,
        (own, other, place, held_other),
        [VMEM] * 4,
        [pltpu.VMEM((rows, width), F32)],
        flops=weight_flops,
        traffic=weight_bytes,
    )
    home = [shift(part, "ex", step) if step else part for part, step in zip(back, steps(experts))]
    pair_grad, down_grad = call(
        weight_grads,
        [sds((1, 2, hidden, width), BF), sds((1, hidden, width), BF)],
        (mine_act, other_act, mine, other, rows_in, rows_grad),
        [VMEM] * 6,
        [pltpu.VMEM((12, half // 2, width), BF), dma(12)],
        limit=24,
        flops=3 * weight_flops,
        traffic=3 * weight_bytes,
        out_specs=[ANY, ANY],
    )
    grad_inputs = call(
        functools.partial(combine, experts),
        sds((tokens, width), BF),
        (pick, *home),
        [VMEM] * (experts + 1),
        [pltpu.VMEM((rows, width), F32), pltpu.VMEM((2, tokens // 2, width), BF), dma(2)],
        flops=2 * rows * tokens * width,
        traffic=4 * tokens * width,
        out_specs=ANY,
    )
    return (grad_inputs, pair_grad, down_grad)


def solution(mesh):
    return jax.shard_map(
        local,
        mesh=mesh,
        in_specs=(
            P(("groups", "ex"), "ey"),
            P(("groups", "ex"), "ey"),
            P(("groups", "ex"), None),
            P(("groups", "ex"), None),
            P("ex", None, None, "ey"),
            P("ex", None, "ey"),
        ),
        out_specs=(
            P(("groups", "ex"), "ey"),
            P("ex", "groups", None, "ey"),
            P("ex", "groups", "ey"),
        ),
        check_vma=False,
    )
```

```python
import functools

import jax
import jax.numpy as jnp
from jax import lax
from jax.experimental import pallas as pl
from jax.experimental.pallas import tpu as pltpu
from jax.sharding import PartitionSpec as P

MOST = 40
EXPERTS = 128
EMPTY = 64.0
BF = jnp.bfloat16
F32 = jnp.float32
MIB = 1 << 20
C2COST = 100
C0COST = 4.75
WCOST = 1
GFLOP = 100
D1COST = 1
D2COST = 100
VMEM = pl.BlockSpec(memory_space=pltpu.VMEM)
ANY = pl.BlockSpec(memory_space=pl.ANY)
HBM = pl.BlockSpec(memory_space=pltpu.HBM)
ROWS = (((0,), (0,)), ((), ()))
LANES = (((1,), (1,)), ((), ()))
PLAIN = (((1,), (0,)), ((), ()))


def mm(left, right, dims=PLAIN):
    return lax.dot_general(left, right, dims, preferred_element_type=F32)


def iota(shape, dim):
    return lax.broadcasted_iota(jnp.int32, shape, dim)


def far_first(count):
    return sorted(range(count), key=lambda k: (-k.bit_length(), k))


def cut(source, target, sems, first, pieces):
    rows = target.shape[-2] // pieces
    out = []
    for at in range(pieces):
        part = pl.ds(at * rows, rows)
        out.append(pltpu.make_async_copy(source.at[part], target.at[part], sems.at[first + at]))
    return out


def run(loads):
    for load in loads:
        load.start()
    return loads


def wait(loads):
    for load in loads:
        load.wait()


def block_of(position, names):
    found = jnp.full_like(position, names[0])
    for at in range(1, len(names)):
        found = found + (position >= at * MOST).astype(jnp.int32) * (names[at] - names[at - 1])
    return found


def call(body, outs, operands, specs, scratch=(), limit=16, flops=0, traffic=0, out_specs=None):
    return pl.pallas_call(
        body,
        out_shape=outs,
        in_specs=specs,
        out_specs=out_specs if out_specs is not None else jax.tree.map(lambda _: VMEM, outs),
        scratch_shapes=list(scratch),
        compiler_params=pltpu.CompilerParams(vmem_limit_bytes=limit * MIB),
        cost_estimate=pl.CostEstimate(flops=flops, bytes_accessed=traffic, transcendentals=0),
    )(*operands)


def pick_inputs(experts, routes_in, probs_in, inputs, grads, pick_out, prob_out, grads_out, *refs):
    *pieces, routes, probs, held, sems = refs
    loads = run(
        [
            pltpu.make_async_copy(routes_in, routes, sems.at[0]),
            pltpu.make_async_copy(probs_in, probs, sems.at[1]),
        ]
    )
    input_loads = run(cut(inputs, held, sems, 2, 1))
    grad_loads = run(cut(grads, grads_out, sems, 3, 1))
    me = lax.axis_index("ex")
    tokens = inputs.shape[0]
    rows = experts * MOST
    order = far_first(experts)
    owner = block_of(iota((rows, routes.shape[0]), 0), order)
    named = jnp.zeros((rows, tokens), F32)
    weight = jnp.zeros((rows, tokens), F32)
    earlier = iota((tokens, tokens), 0) < iota((tokens, tokens), 1)
    earlier = jnp.where(earlier, 1.0, 0.0).astype(BF)
    row = iota((rows, tokens), 0)
    slot = row - block_of(row, range(experts)) * MOST
    wait(loads)
    chosen = routes[...]
    wide = probs[...].astype(F32)
    for k in range(experts):
        spread = jnp.where(owner == k, 1.0, 0.0).astype(BF)
        hit = chosen == (me ^ k)
        named = named + mm(spread, jnp.where(hit, 1.0, 0.0).astype(BF))
        weight = weight + mm(spread, jnp.where(hit, wide, 0.0).astype(BF))
    rank = mm(named.astype(BF), earlier).astype(jnp.int32)
    picks = (rank == slot) & (named > 0.5)
    pick = jnp.where(picks, 1.0, 0.0)
    filled = jnp.max(pick, axis=1, keepdims=True) > 0.5
    pick = pick.astype(BF)
    pick_out[...] = pick
    prob_out[...] = jnp.sum(jnp.where(picks, weight, 0.0), axis=1, keepdims=True)
    wait(input_loads)
    sent = jnp.where(filled, mm(pick, held[...]), EMPTY)
    for k in range(experts):
        pieces[k][...] = sent[k * MOST : (k + 1) * MOST].astype(BF)
    wait(grad_loads)


def pick_grads(experts, pick, prob, grads, *refs):
    near_in, near, *pieces = refs
    sent = mm(pick[...], grads[...]) * prob[...]
    parts = [sent[at * MOST : (at + 1) * MOST] for at in range(experts)]
    near[...] = jnp.concatenate([near_in[...].astype(F32), parts[-2]], axis=0).astype(BF)
    for target, part in zip(pieces, parts[:-2] + parts[-1:]):
        target[...] = part.astype(BF)


def stacked(pieces, part=0):
    rows = [piece[...].astype(F32) for piece in pieces]
    rows = [row[part * MOST : (part + 1) * MOST] if row.shape[0] > MOST else row for row in rows]
    return jnp.concatenate(rows, axis=0)


def rows_of(half, own):
    core = lax.axis_index("ey") & 1
    return pl.ds(pl.multiple_of((core if own else 1 - core) * half, 128), half)


def early_rows(first, out):
    out[...] = first[...]


def place_rows(experts, capacity, pieces):
    me = lax.axis_index("ex")
    rows = experts * MOST
    got = stacked(pieces)
    full = got[:, :1] < EMPTY / 2
    key = []
    for dim in (0, 1):
        row = iota((rows, rows), dim)
        local_row = row - block_of(row, range(experts)) * MOST
        key.append((me ^ block_of(row, far_first(experts))) * MOST + local_row)
    earlier = jnp.where(key[1] < key[0], 1.0, 0.0).astype(BF)
    wide = jnp.broadcast_to(full, (rows, capacity))
    slot = mm(earlier, jnp.where(wide, 1.0, 0.0).astype(BF)).astype(jnp.int32)
    place = jnp.where((slot == iota((rows, capacity), 1)) & wide, 1.0, 0.0).astype(BF)
    return place, mm(place, got.astype(BF), ROWS).astype(BF)


def stage(count, gate_up, down, *refs):
    pieces, refs = refs[:count], refs[count:]
    held, pieces_out, sems = refs[:2], refs[2:-1], refs[-1]
    half = down.shape[1] // 2
    loads = []
    for own, out in enumerate(held):
        rows = rows_of(half, own == 1)
        for matrix in range(3):
            source = down.at[0, rows] if matrix == 2 else gate_up.at[0, matrix, rows]
            loads.append(pltpu.make_async_copy(source, out.at[matrix], sems.at[len(loads)]))
    run(loads)
    for source, target in zip(pieces, pieces_out):
        target[...] = source[...]
    wait(loads)


def other_pair(experts, capacity, *refs):
    held, out, place_out, rows_out = refs[experts:]
    place, rows_in = place_rows(experts, capacity, refs[:experts])
    place_out[...] = place
    rows_out[...] = rows_in
    for matrix in range(2):
        out[matrix] = mm(rows_in, held[matrix], LANES).astype(BF)


def mine_pair(rows_in, held, out):
    for matrix in range(2):
        out[matrix] = mm(rows_in[...], held[matrix], LANES).astype(BF)


def pair_sum(mine, other, held_out, sent_out):
    held = mine[...].astype(F32) + other[...].astype(F32)
    held_out[...] = held
    sent_out[...] = held.astype(BF)


def act_part(experts, own, *refs):
    place, held = refs[experts : experts + 2]
    rows_grad = mm(place[...], stacked(refs[:experts], 1).astype(BF), ROWS).astype(BF)
    if own:
        refs[-2][...] = rows_grad
    refs[-1][...] = mm(rows_grad, held[2], LANES).astype(BF)


def gates(pair, pair_far, act_out, by_gate, by_up):
    gate_sum = pair[0] + pair_far[0].astype(F32)
    up_sum = pair[1] + pair_far[1].astype(F32)
    sigmoid_gate = jax.nn.sigmoid(gate_sum)
    silu_gate = gate_sum * sigmoid_gate
    act_out[...] = (silu_gate * up_sum).astype(BF)
    by_gate[...] = up_sum * sigmoid_gate * (1.0 + gate_sum * (1.0 - sigmoid_gate))
    by_up[...] = silu_gate


def grads_of(act, act_far, by_gate, by_up, _, out):
    grad_act = act[...] + act_far[...].astype(F32)
    out[0] = (grad_act * by_gate[...]).astype(BF)
    out[1] = (grad_act * by_up[...]).astype(BF)


def own_rows(mine, held, out):
    out[...] = mm(mine[0], held[0]) + mm(mine[1], held[1])


def other_rows(experts, total, other, place, held, *refs):
    *pieces, whole = refs
    rows = total[...] + mm(other[0], held[0]) + mm(other[1], held[1])
    whole[...] = mm(place[...], rows.astype(BF))
    me = lax.axis_index("ex")
    for piece, trip in zip(pieces, rounds(experts)):
        target = target_of(trip)
        target = jnp.where(target < 0, me, target)
        piece[...] = whole[place_of(target, experts)].astype(BF)
    pieces[-1][...] = whole[place_of(me, experts)].astype(BF)


def weight_grads(mine_act, other_act, mine, other, rows_in, rows_grad, pair_out, down_out, held, sems):
    core = lax.axis_index("ey") & 1
    half = mine_act.shape[1]
    step = half // 2
    stores = []
    for matrix in range(3):
        right = rows_grad[...] if matrix == 0 else rows_in[...]
        for own in range(2):
            start = (core if own else 1 - core) * half
            for part in range(2):
                columns = slice(part * step, (part + 1) * step)
                if matrix == 0:
                    left = (mine_act if own else other_act)[:, columns]
                else:
                    left = (mine if own else other)[matrix - 1, :, columns]
                at = len(stores)
                held[at] = mm(left, right, ROWS).astype(BF)
                rows = pl.ds(start + part * step, step)
                target = down_out.at[0, rows] if matrix == 0 else pair_out.at[0, matrix - 1, rows]
                store = pltpu.make_async_copy(held.at[at], target, sems.at[at])
                store.start()
                stores.append(store)
    for store in stores:
        store.wait()


def combine(experts, pick, *refs):
    *pieces, own, out, whole, held, sems = refs
    me = lax.axis_index("ex")
    spare = pl.ds(experts * MOST, MOST)
    for piece, trip in zip(pieces, rounds(experts)):
        source = source_of(trip)
        spot = place_of(jnp.where(source < 0, me, source), experts).start
        spot = jnp.where(source < 0, spare.start, spot)
        whole[pl.ds(pl.multiple_of(spot, 8), MOST)] = piece[...].astype(F32)
    whole[place_of(me, experts)] = own[...].astype(F32)
    home = whole[: experts * MOST].astype(BF)
    rows = out.shape[0] // held.shape[0]
    stores = []
    for at in range(held.shape[0]):
        part = pick[:, at * rows : (at + 1) * rows]
        held[at] = mm(part, home, ROWS).astype(BF)
        target = out.at[pl.ds(at * rows, rows)]
        stores += run([pltpu.make_async_copy(held.at[at], target, sems.at[at])])
    wait(stores)


def far(value):
    return pltpu.with_memory_space_constraint(value, pltpu.HBM)


def place_of(partner, experts):
    k = lax.axis_index("ex") ^ partner
    spot = jnp.int32(0)
    for at, name in enumerate(far_first(experts)):
        spot = spot + jnp.where(k == name, at * MOST, 0)
    return pl.ds(pl.multiple_of(spot, 8), MOST)


def rounds(count):
    if count == 4:
        return [
            {0: 1, 1: 2, 2: 3, 3: 0},
            {1: 3, 2: 0, 3: 2},
            {0: 2, 2: 1},
            {0: 3, 1: 0, 3: 1},
        ]
    return [{i: (i + step) % count for i in range(count)} for step in range(1, count)]


def partner(pairs):
    me = lax.axis_index("ex")
    found = jnp.int32(-1)
    for name, other in pairs:
        found = jnp.where(me == name, other, found)
    return found


def target_of(trip):
    return partner(trip.items())


def source_of(trip):
    return partner((other, name) for name, other in trip.items())


def swap(value, axis, bit):
    count = lax.axis_size(axis)
    return lax.ppermute(value, axis, [(i, i ^ bit) for i in range(count)])


def exchange(pieces, axis):
    order = far_first(len(pieces))
    return [swap(piece, axis, k) if k else piece for piece, k in zip(pieces, order)]


def local(inputs, grad_output, routes, gate_probs, gate_up, down_proj):
    experts = lax.axis_size("ex")
    ways = lax.axis_size("ey")
    tokens, width = inputs.shape
    hidden = gate_up.shape[2]
    half = hidden // 2
    capacity = 5 * tokens * experts * routes.shape[1] // (4 * EXPERTS)
    rows = experts * MOST
    weight_bytes = hidden * width * 2
    weight_flops = 2 * capacity * hidden * width
    sds = jax.ShapeDtypeStruct
    piece = [sds((MOST, width), BF)] * experts
    dma = lambda count: pltpu.SemaphoreType.DMA((count,))

    order = far_first(experts)
    pick, prob, grads, *send_in, own_in = call(
        functools.partial(pick_inputs, experts),
        [
            sds((rows, tokens), BF),
            sds((rows, 1), F32),
            pltpu.VMEM((tokens, width), BF),
        ]
        + piece,
        (far(routes.T), far(gate_probs.T), far(inputs), far(grad_output)),
        [HBM] * 4,
        [
            pltpu.VMEM(routes.shape[::-1], jnp.int32),
            pltpu.VMEM(routes.shape[::-1], BF),
            pltpu.VMEM((tokens, width), BF),
            dma(4),
        ],
        flops=2 * rows * tokens * width,
        traffic=4 * tokens * width,
    )
    near, *send_grad = call(
        functools.partial(pick_grads, experts),
        [sds((2 * MOST, width), BF)] + piece[1:],
        (pick, prob, grads, send_in[-1]),
        [VMEM] * 4,
        flops=2 * rows * tokens * width,
        traffic=2 * tokens * width,
    )
    near = swap(near, "ex", 1)
    got_in = [swap(part, "ex", k) for part, k in zip(send_in[:-1], order)] + [near, own_in]
    got_in[0] = call(
        early_rows,
        piece[0],
        (got_in[0],),
        [VMEM],
        flops=int(C0COST * weight_flops),
        traffic=weight_bytes,
    )
    held_other, held_mine, *send_grad = call(
        functools.partial(stage, experts - 1),
        [pltpu.VMEM((3, half, width), BF)] * 2 + piece[1:],
        (far(gate_up), far(down_proj), *send_grad),
        [HBM] * 2 + [VMEM] * (experts - 1),
        [dma(6)],
        flops=WCOST * weight_flops,
        traffic=WCOST * weight_bytes,
    )
    got_grad = [swap(part, "ex", k) for part, k in zip(send_grad[:-1], order)]
    got_grad = got_grad + [near, send_grad[-1]]
    pair_other, place, rows_in = call(
        functools.partial(other_pair, experts, capacity),
        [sds((2, capacity, half), BF), sds((rows, capacity), BF), sds((capacity, width), BF)],
        (*got_in, held_other),
        [VMEM] * (experts + 1),
        flops=2 * weight_flops,
        traffic=weight_bytes,
    )
    pair_mine = call(
        mine_pair,
        sds((2, capacity, half), BF),
        (rows_in, held_mine),
        [VMEM] * 2,
        flops=C2COST * weight_flops,
        traffic=C2COST * weight_bytes,
    )

    def total(held, sent):
        bit = 2
        while bit * 2 < ways:
            held = held + swap(sent, "ey", bit).astype(F32)
            sent = held.astype(BF)
            bit *= 2
        return held, swap(sent, "ey", bit)

    pair, pair_sent = call(
        pair_sum,
        [sds((2, capacity, half), F32), sds((2, capacity, half), BF)],
        (pair_mine, swap(pair_other, "ey", 1)),
        [VMEM] * 2,
        traffic=10 * capacity * hidden,
    )
    pair, pair_far = total(pair, pair_sent)
    def act_of(own, held, outs, tied, cost):
        return call(
            functools.partial(act_part, experts, own),
            outs + [sds((capacity, half), BF)],
            (*got_grad, place, held, *tied),
            [VMEM] * (experts + 2) + [ANY] * len(tied),
            flops=cost * weight_flops,
            traffic=cost * weight_bytes,
        )

    (act_other,) = act_of(False, held_other, [], [pair_sent], D1COST)
    rows_grad, act_mine = act_of(True, held_mine, [sds((capacity, width), BF)], [], D2COST)
    act = act_mine.astype(F32) + swap(act_other, "ey", 1).astype(F32)
    act, act_far = total(act, act.astype(BF))
    mine_act, by_gate, by_up = call(
        gates,
        [sds((capacity, half), BF)] + [sds((capacity, half), F32)] * 2,
        (pair, pair_far),
        [VMEM] * 2,
        traffic=18 * capacity * half,
        flops=GFLOP * weight_flops,
    )
    other_act = swap(mine_act, "ey", 1)
    mine = call(
        grads_of,
        sds((2, capacity, half), BF),
        (act, act_far, by_gate, by_up, other_act),
        [VMEM] * 4 + [ANY],
        traffic=18 * capacity * half,
    )
    other = swap(mine, "ey", 1)
    own = call(
        own_rows,
        sds((capacity, width), F32),
        (mine, held_mine),
        [VMEM] * 2,
        flops=weight_flops,
        traffic=weight_bytes,
    )
    trips = rounds(experts)
    back = call(
        functools.partial(other_rows, experts),
        piece[:1] * (len(trips) + 1),
        (own, other, place, held_other),
        [VMEM] * 4,
        [pltpu.VMEM((rows, width), F32)],
        flops=weight_flops,
        traffic=weight_bytes,
    )
    *back, own_back = back
    home = [lax.ppermute(part, "ex", list(trip.items())) for part, trip in zip(back, trips)]
    home = home + [own_back]
    pair_grad, down_grad = call(
        weight_grads,
        [sds((1, 2, hidden, width), BF), sds((1, hidden, width), BF)],
        (mine_act, other_act, mine, other, rows_in, rows_grad),
        [VMEM] * 6,
        [pltpu.VMEM((12, half // 2, width), BF), dma(12)],
        limit=24,
        flops=3 * weight_flops,
        traffic=3 * weight_bytes,
        out_specs=[ANY, ANY],
    )
    grad_inputs = call(
        functools.partial(combine, experts),
        sds((tokens, width), BF),
        (pick, *home),
        [VMEM] * (len(home) + 1),
        [pltpu.VMEM((rows + MOST, width), F32), pltpu.VMEM((2, tokens // 2, width), BF), dma(2)],
        flops=2 * rows * tokens * width,
        traffic=4 * tokens * width,
        out_specs=ANY,
    )
    return (grad_inputs, pair_grad, down_grad)


def solution(mesh):
    return jax.shard_map(
        local,
        mesh=mesh,
        in_specs=(
            P(("groups", "ex"), "ey"),
            P(("groups", "ex"), "ey"),
            P(("groups", "ex"), None),
            P(("groups", "ex"), None),
            P("ex", None, None, "ey"),
            P("ex", None, "ey"),
        ),
        out_specs=(
            P(("groups", "ex"), "ey"),
            P("ex", "groups", None, "ey"),
            P("ex", "groups", "ey"),
        ),
        check_vma=False,
    )
```

```python
import functools

import jax
import jax.numpy as jnp
from jax import lax
from jax.experimental import pallas as pl
from jax.experimental.pallas import tpu as pltpu
from jax.sharding import PartitionSpec as P

MOST = 40
EXPERTS = 128
EMPTY = 64.0
BF = jnp.bfloat16
F32 = jnp.float32
MIB = 1 << 20
C2COST = 100
WCOST = 100
GFLOP = 100
D1COST = 1
D2COST = 100
VMEM = pl.BlockSpec(memory_space=pltpu.VMEM)
ANY = pl.BlockSpec(memory_space=pl.ANY)
HBM = pl.BlockSpec(memory_space=pltpu.HBM)
ROWS = (((0,), (0,)), ((), ()))
LANES = (((1,), (1,)), ((), ()))
PLAIN = (((1,), (0,)), ((), ()))


def mm(left, right, dims=PLAIN):
    return lax.dot_general(left, right, dims, preferred_element_type=F32)


def iota(shape, dim):
    return lax.broadcasted_iota(jnp.int32, shape, dim)


def far_first(count):
    return sorted(range(count), key=lambda k: (-k.bit_length(), k))


def cut(source, target, sems, first, pieces):
    rows = target.shape[-2] // pieces
    out = []
    for at in range(pieces):
        part = pl.ds(at * rows, rows)
        out.append(pltpu.make_async_copy(source.at[part], target.at[part], sems.at[first + at]))
    return out


def run(loads):
    for load in loads:
        load.start()
    return loads


def wait(loads):
    for load in loads:
        load.wait()


def block_of(position, names):
    found = jnp.full_like(position, names[0])
    for at in range(1, len(names)):
        found = found + (position >= at * MOST).astype(jnp.int32) * (names[at] - names[at - 1])
    return found


def call(body, outs, operands, specs, scratch=(), limit=16, flops=0, traffic=0, out_specs=None):
    return pl.pallas_call(
        body,
        out_shape=outs,
        in_specs=specs,
        out_specs=out_specs if out_specs is not None else jax.tree.map(lambda _: VMEM, outs),
        scratch_shapes=list(scratch),
        compiler_params=pltpu.CompilerParams(vmem_limit_bytes=limit * MIB),
        cost_estimate=pl.CostEstimate(flops=flops, bytes_accessed=traffic, transcendentals=0),
    )(*operands)


def pick_inputs(experts, routes_in, probs_in, inputs, grads, pick_out, prob_out, grads_out, *refs):
    *pieces, routes, probs, held, sems = refs
    loads = run(
        [
            pltpu.make_async_copy(routes_in, routes, sems.at[0]),
            pltpu.make_async_copy(probs_in, probs, sems.at[1]),
        ]
    )
    input_loads = run(cut(inputs, held, sems, 2, 1))
    grad_loads = run(cut(grads, grads_out, sems, 3, 1))
    me = lax.axis_index("ex")
    tokens = inputs.shape[0]
    rows = experts * MOST
    order = far_first(experts)
    width = routes.shape[0]
    cells = (rows, experts * width)
    spread = block_of(iota(cells, 0), range(experts)) == lax.shift_right_logical(
        iota(cells, 1), width.bit_length() - 1
    )
    spread = jnp.where(spread, 1.0, 0.0).astype(BF)
    earlier = iota((tokens, tokens), 0) < iota((tokens, tokens), 1)
    earlier = jnp.where(earlier, 1.0, 0.0).astype(BF)
    row = iota((rows, tokens), 0)
    slot = row - block_of(row, range(experts)) * MOST
    wait(loads)
    chosen = routes[...]
    wide = probs[...].astype(F32)
    hits = jnp.concatenate([jnp.where(chosen == (me ^ k), 1.0, 0.0) for k in order], axis=0)
    odds = hits * jnp.concatenate([wide] * experts, axis=0)
    both = mm(spread, jnp.concatenate([hits, odds], axis=1).astype(BF))
    named, weight = both[:, :tokens], both[:, tokens:]
    rank = mm(named.astype(BF), earlier).astype(jnp.int32)
    picks = (rank == slot) & (named > 0.5)
    pick = jnp.where(picks, 1.0, 0.0)
    filled = jnp.max(pick, axis=1, keepdims=True) > 0.5
    pick = pick.astype(BF)
    pick_out[...] = pick
    prob_out[...] = jnp.sum(jnp.where(picks, weight, 0.0), axis=1, keepdims=True)
    wait(input_loads)
    sent = jnp.where(filled, mm(pick, held[...]), EMPTY)
    for k in range(experts):
        pieces[k][...] = sent[k * MOST : (k + 1) * MOST].astype(BF)
    wait(grad_loads)


def pick_grads(experts, pick, prob, grads, *refs):
    near_in, near, *pieces = refs
    sent = mm(pick[...], grads[...]) * prob[...]
    parts = [sent[at * MOST : (at + 1) * MOST] for at in range(experts)]
    near[...] = jnp.concatenate([near_in[...].astype(F32), parts[-2]], axis=0).astype(BF)
    for target, part in zip(pieces, parts[:-2] + parts[-1:]):
        target[...] = part.astype(BF)


def stacked(pieces, part=0):
    rows = [piece[...].astype(F32) for piece in pieces]
    rows = [row[part * MOST : (part + 1) * MOST] if row.shape[0] > MOST else row for row in rows]
    return jnp.concatenate(rows, axis=0)


def rows_of(half, own):
    core = lax.axis_index("ey") & 1
    return pl.ds(pl.multiple_of((core if own else 1 - core) * half, 128), half)


def place_rows(experts, capacity, pieces):
    me = lax.axis_index("ex")
    rows = experts * MOST
    got = stacked(pieces)
    full = got[:, :1] < EMPTY / 2
    key = []
    for shape, dim in (((rows, 1), 0), ((1, rows), 1)):
        row = iota(shape, dim)
        local_row = row - block_of(row, range(experts)) * MOST
        key.append((me ^ block_of(row, far_first(experts))) * MOST + local_row)
    earlier = jnp.where(key[1] < key[0], 1.0, 0.0).astype(BF)
    wide = jnp.broadcast_to(full, (rows, capacity))
    slot = mm(earlier, jnp.where(wide, 1.0, 0.0).astype(BF)).astype(jnp.int32)
    place = jnp.where((slot == iota((rows, capacity), 1)) & wide, 1.0, 0.0).astype(BF)
    return place, mm(place, got.astype(BF), ROWS).astype(BF)


def stage(count, gate_up, down, *refs):
    pieces, refs = refs[:count], refs[count:]
    held, pieces_out, sems = refs[:2], refs[2:-1], refs[-1]
    half = down.shape[1] // 2
    loads = []
    for own, out in enumerate(held):
        rows = rows_of(half, own == 1)
        for matrix in range(3):
            source = down.at[0, rows] if matrix == 2 else gate_up.at[0, matrix, rows]
            loads.append(pltpu.make_async_copy(source, out.at[matrix], sems.at[len(loads)]))
    run(loads)
    for source, target in zip(pieces, pieces_out):
        target[...] = source[...]
    wait(loads)


def other_pair(experts, capacity, *refs):
    held, out, place_out, rows_out = refs[experts:]
    place, rows_in = place_rows(experts, capacity, refs[:experts])
    place_out[...] = place
    rows_out[...] = rows_in
    for matrix in range(2):
        out[matrix] = mm(rows_in, held[matrix], LANES).astype(BF)


def mine_pair(rows_in, held, out):
    for matrix in range(2):
        out[matrix] = mm(rows_in[...], held[matrix], LANES).astype(BF)


def pair_sum(mine, other, held_out, sent_out):
    held = mine[...].astype(F32) + other[...].astype(F32)
    held_out[...] = held
    sent_out[...] = held.astype(BF)


def act_part(experts, own, *refs):
    place, held = refs[experts : experts + 2]
    pieces = refs[: experts - 2][::-1] + refs[experts - 2 : experts]
    rows_grad = mm(place[...], stacked(pieces, 1).astype(BF), ROWS).astype(BF)
    if own:
        refs[-2][...] = rows_grad
    refs[-1][...] = mm(rows_grad, held[2], LANES).astype(BF)


def gates(pair, pair_far, act_out, by_gate, by_up):
    gate_sum = pair[0] + pair_far[0].astype(F32)
    up_sum = pair[1] + pair_far[1].astype(F32)
    sigmoid_gate = jax.nn.sigmoid(gate_sum)
    silu_gate = gate_sum * sigmoid_gate
    act_out[...] = (silu_gate * up_sum).astype(BF)
    by_gate[...] = up_sum * sigmoid_gate * (1.0 + gate_sum * (1.0 - sigmoid_gate))
    by_up[...] = silu_gate


def grads_of(act, act_far, by_gate, by_up, _, out):
    grad_act = act[...] + act_far[...].astype(F32)
    out[0] = (grad_act * by_gate[...]).astype(BF)
    out[1] = (grad_act * by_up[...]).astype(BF)


def own_rows(mine, held, out):
    out[...] = mm(mine[0], held[0]) + mm(mine[1], held[1])


def other_rows(experts, total, other, place, held, *refs):
    pieces, whole = refs[:experts], refs[experts]
    rows = total[...] + mm(other[0], held[0]) + mm(other[1], held[1])
    whole[...] = mm(place[...], rows.astype(BF))
    for piece, step in zip(pieces, steps(experts)):
        piece[...] = whole[place_of(ahead(step, experts), experts)].astype(BF)


def weight_grads(mine_act, other_act, mine, other, rows_in, rows_grad, pair_out, down_out, held, sems):
    core = lax.axis_index("ey") & 1
    half = mine_act.shape[1]
    step = half // 2
    stores = []
    for matrix in range(3):
        right = rows_grad[...] if matrix == 0 else rows_in[...]
        for own in range(2):
            start = (core if own else 1 - core) * half
            for part in range(2):
                columns = slice(part * step, (part + 1) * step)
                if matrix == 0:
                    left = (mine_act if own else other_act)[:, columns]
                else:
                    left = (mine if own else other)[matrix - 1, :, columns]
                at = len(stores)
                held[at] = mm(left, right, ROWS).astype(BF)
                rows = pl.ds(start + part * step, step)
                target = down_out.at[0, rows] if matrix == 0 else pair_out.at[0, matrix - 1, rows]
                store = pltpu.make_async_copy(held.at[at], target, sems.at[at])
                store.start()
                stores.append(store)
    for store in stores:
        store.wait()


def combine(experts, pick, *refs):
    out, whole, held, sems = refs[experts:]
    for piece, step in zip(refs[:experts], steps(experts)):
        whole[place_of(ahead(experts - step, experts), experts)] = piece[...].astype(F32)
    home = whole[...].astype(BF)
    rows = out.shape[0] // held.shape[0]
    stores = []
    for at in range(held.shape[0]):
        part = pick[:, at * rows : (at + 1) * rows]
        held[at] = mm(part, home, ROWS).astype(BF)
        target = out.at[pl.ds(at * rows, rows)]
        stores += run([pltpu.make_async_copy(held.at[at], target, sems.at[at])])
    wait(stores)


def far(value):
    return pltpu.with_memory_space_constraint(value, pltpu.HBM)


def place_of(partner, experts):
    k = lax.axis_index("ex") ^ partner
    spot = jnp.int32(0)
    for at, name in enumerate(far_first(experts)):
        spot = spot + jnp.where(k == name, at * MOST, 0)
    return pl.ds(pl.multiple_of(spot, 8), MOST)


def tour(count):
    bits = count.bit_length() - 1
    return [sum(((i >> b) & 1) << (bits - 1 - b) for b in range(bits)) for i in range(count)]


def steps(count):
    found = []
    for step in range(1, count // 2 + 1):
        found += [step, count - step]
    return list(dict.fromkeys(found)) + [0]


def ahead(step, count):
    me, names = lax.axis_index("ex"), tour(count)
    found = jnp.int32(0)
    for at, name in enumerate(names):
        found = found + jnp.where(me == name, names[(at + step) % count], 0)
    return found


def shift(value, axis, step):
    count = lax.axis_size(axis)
    names = tour(count)
    return lax.ppermute(
        value, axis, [(name, names[(at + step) % count]) for at, name in enumerate(names)]
    )


def swap(value, axis, bit):
    count = lax.axis_size(axis)
    return lax.ppermute(value, axis, [(i, i ^ bit) for i in range(count)])


def exchange(pieces, axis):
    order = far_first(len(pieces))
    return [swap(piece, axis, k) if k else piece for piece, k in zip(pieces, order)]


def local(inputs, grad_output, routes, gate_probs, gate_up, down_proj):
    experts = lax.axis_size("ex")
    ways = lax.axis_size("ey")
    tokens, width = inputs.shape
    hidden = gate_up.shape[2]
    half = hidden // 2
    capacity = 5 * tokens * experts * routes.shape[1] // (4 * EXPERTS)
    rows = experts * MOST
    weight_bytes = hidden * width * 2
    weight_flops = 2 * capacity * hidden * width
    sds = jax.ShapeDtypeStruct
    piece = [sds((MOST, width), BF)] * experts
    dma = lambda count: pltpu.SemaphoreType.DMA((count,))

    order = far_first(experts)
    pick, prob, grads, *send_in, own_in = call(
        functools.partial(pick_inputs, experts),
        [
            sds((rows, tokens), BF),
            sds((rows, 1), F32),
            pltpu.VMEM((tokens, width), BF),
        ]
        + piece,
        (far(routes.T), far(gate_probs.T), far(inputs), far(grad_output)),
        [HBM] * 4,
        [
            pltpu.VMEM(routes.shape[::-1], jnp.int32),
            pltpu.VMEM(routes.shape[::-1], BF),
            pltpu.VMEM((tokens, width), BF),
            dma(4),
        ],
        flops=2 * rows * tokens * width,
        traffic=4 * tokens * width,
    )
    near, *send_grad = call(
        functools.partial(pick_grads, experts),
        [sds((2 * MOST, width), BF)] + piece[1:],
        (pick, prob, grads, send_in[-1]),
        [VMEM] * 4,
        flops=2 * rows * tokens * width,
        traffic=2 * tokens * width,
    )
    near = swap(near, "ex", 1)
    got_in = [swap(part, "ex", k) for part, k in zip(send_in[:-1], order)] + [near, own_in]
    held_other, held_mine, *send_grad = call(
        functools.partial(stage, experts - 1),
        [pltpu.VMEM((3, half, width), BF)] * 2 + piece[1:],
        (far(gate_up), far(down_proj), *send_grad),
        [HBM] * 2 + [VMEM] * (experts - 1),
        [dma(6)],
        flops=WCOST * weight_flops,
        traffic=WCOST * weight_bytes,
    )
    got_grad = [swap(part, "ex", k) for part, k in zip(send_grad[:-1], order)][::-1]
    got_grad = got_grad + [near, send_grad[-1]]
    pair_other, place, rows_in = call(
        functools.partial(other_pair, experts, capacity),
        [sds((2, capacity, half), BF), sds((rows, capacity), BF), sds((capacity, width), BF)],
        (*got_in, held_other),
        [VMEM] * (experts + 1),
        flops=2 * weight_flops,
        traffic=weight_bytes,
    )
    pair_mine = call(
        mine_pair,
        sds((2, capacity, half), BF),
        (rows_in, held_mine),
        [VMEM] * 2,
        flops=C2COST * weight_flops,
        traffic=C2COST * weight_bytes,
    )

    def total(held, sent):
        bit = 2
        while bit * 2 < ways:
            held = held + swap(sent, "ey", bit).astype(F32)
            sent = held.astype(BF)
            bit *= 2
        return held, swap(sent, "ey", bit)

    pair, pair_sent = call(
        pair_sum,
        [sds((2, capacity, half), F32), sds((2, capacity, half), BF)],
        (pair_mine, swap(pair_other, "ey", 1)),
        [VMEM] * 2,
        traffic=10 * capacity * hidden,
    )
    pair, pair_far = total(pair, pair_sent)
    def act_of(own, held, outs, tied, cost):
        return call(
            functools.partial(act_part, experts, own),
            outs + [sds((capacity, half), BF)],
            (*got_grad, place, held, *tied),
            [VMEM] * (experts + 2) + [ANY] * len(tied),
            flops=cost * weight_flops,
            traffic=cost * weight_bytes,
        )

    (act_other,) = act_of(False, held_other, [], [pair_sent], D1COST)
    rows_grad, act_mine = act_of(True, held_mine, [sds((capacity, width), BF)], [], D2COST)
    act = act_mine.astype(F32) + swap(act_other, "ey", 1).astype(F32)
    act, act_far = total(act, act.astype(BF))
    mine_act, by_gate, by_up = call(
        gates,
        [sds((capacity, half), BF)] + [sds((capacity, half), F32)] * 2,
        (pair, pair_far),
        [VMEM] * 2,
        traffic=18 * capacity * half,
        flops=GFLOP * weight_flops,
    )
    other_act = swap(mine_act, "ey", 1)
    mine = call(
        grads_of,
        sds((2, capacity, half), BF),
        (act, act_far, by_gate, by_up, other_act),
        [VMEM] * 4 + [ANY],
        traffic=18 * capacity * half,
    )
    other = swap(mine, "ey", 1)
    own = call(
        own_rows,
        sds((capacity, width), F32),
        (mine, held_mine),
        [VMEM] * 2,
        flops=weight_flops,
        traffic=weight_bytes,
    )
    back = call(
        functools.partial(other_rows, experts),
        piece,
        (own, other, place, held_other),
        [VMEM] * 4,
        [pltpu.VMEM((rows, width), F32)],
        flops=weight_flops,
        traffic=weight_bytes,
    )
    home = [shift(part, "ex", step) if step else part for part, step in zip(back, steps(experts))]
    pair_grad, down_grad = call(
        weight_grads,
        [sds((1, 2, hidden, width), BF), sds((1, hidden, width), BF)],
        (mine_act, other_act, mine, other, rows_in, rows_grad),
        [VMEM] * 6,
        [pltpu.VMEM((12, half // 2, width), BF), dma(12)],
        limit=24,
        flops=3 * weight_flops,
        traffic=3 * weight_bytes,
        out_specs=[ANY, ANY],
    )
    grad_inputs = call(
        functools.partial(combine, experts),
        sds((tokens, width), BF),
        (pick, *home),
        [VMEM] * (experts + 1),
        [pltpu.VMEM((rows, width), F32), pltpu.VMEM((2, tokens // 2, width), BF), dma(2)],
        flops=2 * rows * tokens * width,
        traffic=4 * tokens * width,
        out_specs=ANY,
    )
    return (grad_inputs, pair_grad, down_grad)


def solution(mesh):
    return jax.shard_map(
        local,
        mesh=mesh,
        in_specs=(
            P(("groups", "ex"), "ey"),
            P(("groups", "ex"), "ey"),
            P(("groups", "ex"), None),
            P(("groups", "ex"), None),
            P("ex", None, None, "ey"),
            P("ex", None, "ey"),
        ),
        out_specs=(
            P(("groups", "ex"), "ey"),
            P("ex", "groups", None, "ey"),
            P("ex", "groups", "ey"),
        ),
        check_vma=False,
    )
```

```python
import functools

import jax
import jax.numpy as jnp
from jax import lax
from jax.experimental import pallas as pl
from jax.experimental.pallas import tpu as pltpu
from jax.sharding import PartitionSpec as P

MOST = 40
EXPERTS = 128
EMPTY = 64.0
BF = jnp.bfloat16
F32 = jnp.float32
MIB = 1 << 20
C2COST = 100
C0COST = 4.75
WCOST = 1
GFLOP = 100
D1COST = 1
D2COST = 100
VMEM = pl.BlockSpec(memory_space=pltpu.VMEM)
ANY = pl.BlockSpec(memory_space=pl.ANY)
HBM = pl.BlockSpec(memory_space=pltpu.HBM)
ROWS = (((0,), (0,)), ((), ()))
LANES = (((1,), (1,)), ((), ()))
PLAIN = (((1,), (0,)), ((), ()))


def mm(left, right, dims=PLAIN):
    return lax.dot_general(left, right, dims, preferred_element_type=F32)


def iota(shape, dim):
    return lax.broadcasted_iota(jnp.int32, shape, dim)


def far_first(count):
    return sorted(range(count), key=lambda k: (-k.bit_length(), k))


def cut(source, target, sems, first, pieces):
    rows = target.shape[-2] // pieces
    out = []
    for at in range(pieces):
        part = pl.ds(at * rows, rows)
        out.append(pltpu.make_async_copy(source.at[part], target.at[part], sems.at[first + at]))
    return out


def run(loads):
    for load in loads:
        load.start()
    return loads


def wait(loads):
    for load in loads:
        load.wait()


def block_of(position, names):
    found = jnp.full_like(position, names[0])
    for at in range(1, len(names)):
        found = found + (position >= at * MOST).astype(jnp.int32) * (names[at] - names[at - 1])
    return found


def call(body, outs, operands, specs, scratch=(), limit=16, flops=0, traffic=0, out_specs=None):
    return pl.pallas_call(
        body,
        out_shape=outs,
        in_specs=specs,
        out_specs=out_specs if out_specs is not None else jax.tree.map(lambda _: VMEM, outs),
        scratch_shapes=list(scratch),
        compiler_params=pltpu.CompilerParams(vmem_limit_bytes=limit * MIB),
        cost_estimate=pl.CostEstimate(flops=flops, bytes_accessed=traffic, transcendentals=0),
    )(*operands)


def pick_inputs(experts, routes_in, probs_in, inputs, grads, pick_out, prob_out, grads_out, *refs):
    *pieces, routes, probs, held, sems = refs
    loads = run(
        [
            pltpu.make_async_copy(routes_in, routes, sems.at[0]),
            pltpu.make_async_copy(probs_in, probs, sems.at[1]),
        ]
    )
    input_loads = run(cut(inputs, held, sems, 2, 1))
    grad_loads = run(cut(grads, grads_out, sems, 3, 1))
    me = lax.axis_index("ex")
    tokens = inputs.shape[0]
    rows = experts * MOST
    order = far_first(experts)
    width = routes.shape[0]
    cells = (rows, experts * width)
    spread = block_of(iota(cells, 0), range(experts)) == lax.shift_right_logical(
        iota(cells, 1), width.bit_length() - 1
    )
    spread = jnp.where(spread, 1.0, 0.0).astype(BF)
    earlier = iota((tokens, tokens), 0) < iota((tokens, tokens), 1)
    earlier = jnp.where(earlier, 1.0, 0.0).astype(BF)
    row = iota((rows, tokens), 0)
    slot = row - block_of(row, range(experts)) * MOST
    wait(loads)
    chosen = routes[...]
    wide = probs[...].astype(F32)
    hits = jnp.concatenate([jnp.where(chosen == (me ^ k), 1.0, 0.0) for k in order], axis=0)
    odds = hits * jnp.concatenate([wide] * experts, axis=0)
    both = mm(spread, jnp.concatenate([hits, odds], axis=1).astype(BF))
    named, weight = both[:, :tokens], both[:, tokens:]
    rank = mm(named.astype(BF), earlier).astype(jnp.int32)
    picks = (rank == slot) & (named > 0.5)
    pick = jnp.where(picks, 1.0, 0.0)
    filled = jnp.max(pick, axis=1, keepdims=True) > 0.5
    pick = pick.astype(BF)
    pick_out[...] = pick
    prob_out[...] = jnp.sum(jnp.where(picks, weight, 0.0), axis=1, keepdims=True)
    wait(input_loads)
    sent = jnp.where(filled, mm(pick, held[...]), EMPTY)
    for k in range(experts):
        pieces[k][...] = sent[k * MOST : (k + 1) * MOST].astype(BF)
    wait(grad_loads)


def pick_grads(experts, pick, prob, grads, *refs):
    near_in, near, *pieces = refs
    sent = mm(pick[...], grads[...]) * prob[...]
    parts = [sent[at * MOST : (at + 1) * MOST] for at in range(experts)]
    near[...] = jnp.concatenate([near_in[...].astype(F32), parts[-2]], axis=0).astype(BF)
    for target, part in zip(pieces, parts[:-2] + parts[-1:]):
        target[...] = part.astype(BF)


def stacked(pieces, part=0):
    rows = [piece[...].astype(F32) for piece in pieces]
    rows = [row[part * MOST : (part + 1) * MOST] if row.shape[0] > MOST else row for row in rows]
    return jnp.concatenate(rows, axis=0)


def rows_of(half, own):
    core = lax.axis_index("ey") & 1
    return pl.ds(pl.multiple_of((core if own else 1 - core) * half, 128), half)


def early_rows(first, out):
    out[...] = first[...]


def place_rows(experts, capacity, pieces):
    me = lax.axis_index("ex")
    rows = experts * MOST
    got = stacked(pieces)
    full = got[:, :1] < EMPTY / 2
    key = []
    for shape, dim in (((rows, 1), 0), ((1, rows), 1)):
        row = iota(shape, dim)
        local_row = row - block_of(row, range(experts)) * MOST
        key.append((me ^ block_of(row, far_first(experts))) * MOST + local_row)
    earlier = jnp.where(key[1] < key[0], 1.0, 0.0).astype(BF)
    wide = jnp.broadcast_to(full, (rows, capacity))
    slot = mm(earlier, jnp.where(wide, 1.0, 0.0).astype(BF)).astype(jnp.int32)
    place = jnp.where((slot == iota((rows, capacity), 1)) & wide, 1.0, 0.0).astype(BF)
    return place, mm(place, got.astype(BF), ROWS).astype(BF)


def stage(count, gate_up, down, *refs):
    pieces, refs = refs[:count], refs[count:]
    held, pieces_out, sems = refs[:2], refs[2:-1], refs[-1]
    half = down.shape[1] // 2
    loads = []
    for own, out in enumerate(held):
        rows = rows_of(half, own == 1)
        for matrix in range(3):
            source = down.at[0, rows] if matrix == 2 else gate_up.at[0, matrix, rows]
            loads.append(pltpu.make_async_copy(source, out.at[matrix], sems.at[len(loads)]))
    run(loads)
    for source, target in zip(pieces, pieces_out):
        target[...] = source[...]
    wait(loads)


def other_pair(experts, capacity, *refs):
    held, out, place_out, rows_out = refs[experts:]
    place, rows_in = place_rows(experts, capacity, refs[:experts])
    place_out[...] = place
    rows_out[...] = rows_in
    for matrix in range(2):
        out[matrix] = mm(rows_in, held[matrix], LANES).astype(BF)


def mine_pair(rows_in, held, out):
    for matrix in range(2):
        out[matrix] = mm(rows_in[...], held[matrix], LANES).astype(BF)


def pair_sum(mine, other, held_out, sent_out):
    held = mine[...].astype(F32) + other[...].astype(F32)
    held_out[...] = held
    sent_out[...] = held.astype(BF)


def act_part(experts, own, *refs):
    place, held = refs[experts : experts + 2]
    rows_grad = mm(place[...], stacked(refs[:experts], 1).astype(BF), ROWS).astype(BF)
    if own:
        refs[-2][...] = rows_grad
    refs[-1][...] = mm(rows_grad, held[2], LANES).astype(BF)


def gates(pair, pair_far, act_out, by_gate, by_up):
    gate_sum = pair[0] + pair_far[0].astype(F32)
    up_sum = pair[1] + pair_far[1].astype(F32)
    sigmoid_gate = jax.nn.sigmoid(gate_sum)
    silu_gate = gate_sum * sigmoid_gate
    act_out[...] = (silu_gate * up_sum).astype(BF)
    by_gate[...] = up_sum * sigmoid_gate * (1.0 + gate_sum * (1.0 - sigmoid_gate))
    by_up[...] = silu_gate


def grads_of(act, act_far, by_gate, by_up, _, out):
    grad_act = act[...] + act_far[...].astype(F32)
    out[0] = (grad_act * by_gate[...]).astype(BF)
    out[1] = (grad_act * by_up[...]).astype(BF)


def own_rows(mine, held, out):
    out[...] = mm(mine[0], held[0]) + mm(mine[1], held[1])


def other_rows(experts, total, other, place, held, *refs):
    pieces, whole = refs[:experts], refs[experts]
    rows = total[...] + mm(other[0], held[0]) + mm(other[1], held[1])
    whole[...] = mm(place[...], rows.astype(BF))
    for piece, step in zip(pieces, steps(experts)):
        piece[...] = whole[place_of(ahead(step, experts), experts)].astype(BF)


def weight_grads(mine_act, other_act, mine, other, rows_in, rows_grad, pair_out, down_out, held, sems):
    core = lax.axis_index("ey") & 1
    half = mine_act.shape[1]
    step = half // 2
    stores = []
    for matrix in range(3):
        right = rows_grad[...] if matrix == 0 else rows_in[...]
        for own in range(2):
            start = (core if own else 1 - core) * half
            for part in range(2):
                columns = slice(part * step, (part + 1) * step)
                if matrix == 0:
                    left = (mine_act if own else other_act)[:, columns]
                else:
                    left = (mine if own else other)[matrix - 1, :, columns]
                at = len(stores)
                held[at] = mm(left, right, ROWS).astype(BF)
                rows = pl.ds(start + part * step, step)
                target = down_out.at[0, rows] if matrix == 0 else pair_out.at[0, matrix - 1, rows]
                store = pltpu.make_async_copy(held.at[at], target, sems.at[at])
                store.start()
                stores.append(store)
    for store in stores:
        store.wait()


def combine(experts, pick, *refs):
    out, whole, held, sems = refs[experts:]
    for piece, step in zip(refs[:experts], steps(experts)):
        whole[place_of(ahead(experts - step, experts), experts)] = piece[...].astype(F32)
    home = whole[...].astype(BF)
    rows = out.shape[0] // held.shape[0]
    stores = []
    for at in range(held.shape[0]):
        part = pick[:, at * rows : (at + 1) * rows]
        held[at] = mm(part, home, ROWS).astype(BF)
        target = out.at[pl.ds(at * rows, rows)]
        stores += run([pltpu.make_async_copy(held.at[at], target, sems.at[at])])
    wait(stores)


def far(value):
    return pltpu.with_memory_space_constraint(value, pltpu.HBM)


def place_of(partner, experts):
    k = lax.axis_index("ex") ^ partner
    spot = jnp.int32(0)
    for at, name in enumerate(far_first(experts)):
        spot = spot + jnp.where(k == name, at * MOST, 0)
    return pl.ds(pl.multiple_of(spot, 8), MOST)


def tour(count):
    return list(range(count))


def steps(count):
    return list(range(1, count)) + [0]


def ahead(step, count):
    me, names = lax.axis_index("ex"), tour(count)
    found = jnp.int32(0)
    for at, name in enumerate(names):
        found = found + jnp.where(me == name, names[(at + step) % count], 0)
    return found


def shift(value, axis, step):
    count = lax.axis_size(axis)
    names = tour(count)
    return lax.ppermute(
        value, axis, [(name, names[(at + step) % count]) for at, name in enumerate(names)]
    )


def swap(value, axis, bit):
    count = lax.axis_size(axis)
    return lax.ppermute(value, axis, [(i, i ^ bit) for i in range(count)])


def exchange(pieces, axis):
    order = far_first(len(pieces))
    return [swap(piece, axis, k) if k else piece for piece, k in zip(pieces, order)]


def local(inputs, grad_output, routes, gate_probs, gate_up, down_proj):
    experts = lax.axis_size("ex")
    ways = lax.axis_size("ey")
    tokens, width = inputs.shape
    hidden = gate_up.shape[2]
    half = hidden // 2
    capacity = 5 * tokens * experts * routes.shape[1] // (4 * EXPERTS)
    rows = experts * MOST
    weight_bytes = hidden * width * 2
    weight_flops = 2 * capacity * hidden * width
    sds = jax.ShapeDtypeStruct
    piece = [sds((MOST, width), BF)] * experts
    dma = lambda count: pltpu.SemaphoreType.DMA((count,))

    order = far_first(experts)
    pick, prob, grads, *send_in, own_in = call(
        functools.partial(pick_inputs, experts),
        [
            sds((rows, tokens), BF),
            sds((rows, 1), F32),
            pltpu.VMEM((tokens, width), BF),
        ]
        + piece,
        (far(routes.T), far(gate_probs.T), far(inputs), far(grad_output)),
        [HBM] * 4,
        [
            pltpu.VMEM(routes.shape[::-1], jnp.int32),
            pltpu.VMEM(routes.shape[::-1], BF),
            pltpu.VMEM((tokens, width), BF),
            dma(4),
        ],
        flops=2 * rows * tokens * width,
        traffic=4 * tokens * width,
    )
    near, *send_grad = call(
        functools.partial(pick_grads, experts),
        [sds((2 * MOST, width), BF)] + piece[1:],
        (pick, prob, grads, send_in[-1]),
        [VMEM] * 4,
        flops=2 * rows * tokens * width,
        traffic=2 * tokens * width,
    )
    near = swap(near, "ex", 1)
    got_in = [swap(part, "ex", k) for part, k in zip(send_in[:-1], order)] + [near, own_in]
    got_in[0] = call(
        early_rows,
        piece[0],
        (got_in[0],),
        [VMEM],
        flops=int(C0COST * weight_flops),
        traffic=weight_bytes,
    )
    held_other, held_mine, *send_grad = call(
        functools.partial(stage, experts - 1),
        [pltpu.VMEM((3, half, width), BF)] * 2 + piece[1:],
        (far(gate_up), far(down_proj), *send_grad),
        [HBM] * 2 + [VMEM] * (experts - 1),
        [dma(6)],
        flops=WCOST * weight_flops,
        traffic=WCOST * weight_bytes,
    )
    got_grad = [swap(part, "ex", k) for part, k in zip(send_grad[:-1], order)]
    got_grad = got_grad + [near, send_grad[-1]]
    pair_other, place, rows_in = call(
        functools.partial(other_pair, experts, capacity),
        [sds((2, capacity, half), BF), sds((rows, capacity), BF), sds((capacity, width), BF)],
        (*got_in, held_other),
        [VMEM] * (experts + 1),
        flops=2 * weight_flops,
        traffic=weight_bytes,
    )
    pair_mine = call(
        mine_pair,
        sds((2, capacity, half), BF),
        (rows_in, held_mine),
        [VMEM] * 2,
        flops=C2COST * weight_flops,
        traffic=C2COST * weight_bytes,
    )

    def total(held, sent):
        bit = 2
        while bit * 2 < ways:
            held = held + swap(sent, "ey", bit).astype(F32)
            sent = held.astype(BF)
            bit *= 2
        return held, swap(sent, "ey", bit)

    pair, pair_sent = call(
        pair_sum,
        [sds((2, capacity, half), F32), sds((2, capacity, half), BF)],
        (pair_mine, swap(pair_other, "ey", 1)),
        [VMEM] * 2,
        traffic=10 * capacity * hidden,
    )
    pair, pair_far = total(pair, pair_sent)
    def act_of(own, held, outs, tied, cost):
        return call(
            functools.partial(act_part, experts, own),
            outs + [sds((capacity, half), BF)],
            (*got_grad, place, held, *tied),
            [VMEM] * (experts + 2) + [ANY] * len(tied),
            flops=cost * weight_flops,
            traffic=cost * weight_bytes,
        )

    (act_other,) = act_of(False, held_other, [], [pair_sent], D1COST)
    rows_grad, act_mine = act_of(True, held_mine, [sds((capacity, width), BF)], [], D2COST)
    act = act_mine.astype(F32) + swap(act_other, "ey", 1).astype(F32)
    act, act_far = total(act, act.astype(BF))
    mine_act, by_gate, by_up = call(
        gates,
        [sds((capacity, half), BF)] + [sds((capacity, half), F32)] * 2,
        (pair, pair_far),
        [VMEM] * 2,
        traffic=18 * capacity * half,
        flops=GFLOP * weight_flops,
    )
    other_act = swap(mine_act, "ey", 1)
    mine = call(
        grads_of,
        sds((2, capacity, half), BF),
        (act, act_far, by_gate, by_up, other_act),
        [VMEM] * 4 + [ANY],
        traffic=18 * capacity * half,
    )
    other = swap(mine, "ey", 1)
    own = call(
        own_rows,
        sds((capacity, width), F32),
        (mine, held_mine),
        [VMEM] * 2,
        flops=weight_flops,
        traffic=weight_bytes,
    )
    back = call(
        functools.partial(other_rows, experts),
        piece,
        (own, other, place, held_other),
        [VMEM] * 4,
        [pltpu.VMEM((rows, width), F32)],
        flops=weight_flops,
        traffic=weight_bytes,
    )
    home = [shift(part, "ex", step) if step else part for part, step in zip(back, steps(experts))]
    pair_grad, down_grad = call(
        weight_grads,
        [sds((1, 2, hidden, width), BF), sds((1, hidden, width), BF)],
        (mine_act, other_act, mine, other, rows_in, rows_grad),
        [VMEM] * 6,
        [pltpu.VMEM((12, half // 2, width), BF), dma(12)],
        limit=24,
        flops=3 * weight_flops,
        traffic=3 * weight_bytes,
        out_specs=[ANY, ANY],
    )
    grad_inputs = call(
        functools.partial(combine, experts),
        sds((tokens, width), BF),
        (pick, *home),
        [VMEM] * (experts + 1),
        [pltpu.VMEM((rows, width), F32), pltpu.VMEM((2, tokens // 2, width), BF), dma(2)],
        flops=2 * rows * tokens * width,
        traffic=4 * tokens * width,
        out_specs=ANY,
    )
    return (grad_inputs, pair_grad, down_grad)


def solution(mesh):
    return jax.shard_map(
        local,
        mesh=mesh,
        in_specs=(
            P(("groups", "ex"), "ey"),
            P(("groups", "ex"), "ey"),
            P(("groups", "ex"), None),
            P(("groups", "ex"), None),
            P("ex", None, None, "ey"),
            P("ex", None, "ey"),
        ),
        out_specs=(
            P(("groups", "ex"), "ey"),
            P("ex", "groups", None, "ey"),
            P("ex", "groups", "ey"),
        ),
        check_vma=False,
    )
```

```python
import functools

import jax
import jax.numpy as jnp
from jax import lax
from jax.experimental import pallas as pl
from jax.experimental.pallas import tpu as pltpu
from jax.sharding import PartitionSpec as P

MOST = 40
EXPERTS = 128
EMPTY = 64.0
BF = jnp.bfloat16
F32 = jnp.float32
MIB = 1 << 20
C2COST = 100
C0COST = 4.75
WCOST = 1
CUTS = 3
GFLOP = 100
D1COST = 1
D2COST = 100
VMEM = pl.BlockSpec(memory_space=pltpu.VMEM)
ANY = pl.BlockSpec(memory_space=pl.ANY)
HBM = pl.BlockSpec(memory_space=pltpu.HBM)
ROWS = (((0,), (0,)), ((), ()))
LANES = (((1,), (1,)), ((), ()))
PLAIN = (((1,), (0,)), ((), ()))


def mm(left, right, dims=PLAIN):
    return lax.dot_general(left, right, dims, preferred_element_type=F32)


def iota(shape, dim):
    return lax.broadcasted_iota(jnp.int32, shape, dim)


def far_first(count):
    return sorted(range(count), key=lambda k: (-k.bit_length(), k))


def cut(source, target, sems, first, pieces):
    rows = target.shape[-2] // pieces
    out = []
    for at in range(pieces):
        part = pl.ds(at * rows, rows)
        out.append(pltpu.make_async_copy(source.at[part], target.at[part], sems.at[first + at]))
    return out


def run(loads):
    for load in loads:
        load.start()
    return loads


def wait(loads):
    for load in loads:
        load.wait()


def block_of(position, names):
    found = jnp.full_like(position, names[0])
    for at in range(1, len(names)):
        found = found + (position >= at * MOST).astype(jnp.int32) * (names[at] - names[at - 1])
    return found


def call(body, outs, operands, specs, scratch=(), limit=16, flops=0, traffic=0, out_specs=None):
    return pl.pallas_call(
        body,
        out_shape=outs,
        in_specs=specs,
        out_specs=out_specs if out_specs is not None else jax.tree.map(lambda _: VMEM, outs),
        scratch_shapes=list(scratch),
        compiler_params=pltpu.CompilerParams(vmem_limit_bytes=limit * MIB),
        cost_estimate=pl.CostEstimate(flops=flops, bytes_accessed=traffic, transcendentals=0),
    )(*operands)


def pick_inputs(experts, routes_in, probs_in, inputs, grads, pick_out, prob_out, grads_out, *refs):
    *pieces, routes, probs, held, sems = refs
    loads = run(
        [
            pltpu.make_async_copy(routes_in, routes, sems.at[0]),
            pltpu.make_async_copy(probs_in, probs, sems.at[1]),
        ]
    )
    input_loads = run(cut(inputs, held, sems, 2, 1))
    grad_loads = run(cut(grads, grads_out, sems, 3, 1))
    me = lax.axis_index("ex")
    tokens = inputs.shape[0]
    rows = experts * MOST
    order = far_first(experts)
    width = routes.shape[0]
    cells = (rows, experts * width)
    spread = block_of(iota(cells, 0), range(experts)) == lax.shift_right_logical(
        iota(cells, 1), width.bit_length() - 1
    )
    spread = jnp.where(spread, 1.0, 0.0).astype(BF)
    earlier = iota((tokens, tokens), 0) < iota((tokens, tokens), 1)
    earlier = jnp.where(earlier, 1.0, 0.0).astype(BF)
    row = iota((rows, tokens), 0)
    slot = row - block_of(row, range(experts)) * MOST
    wait(loads)
    chosen = routes[...]
    wide = probs[...].astype(F32)
    hits = jnp.concatenate([jnp.where(chosen == (me ^ k), 1.0, 0.0) for k in order], axis=0)
    odds = hits * jnp.concatenate([wide] * experts, axis=0)
    both = mm(spread, jnp.concatenate([hits, odds], axis=1).astype(BF))
    named, weight = both[:, :tokens], both[:, tokens:]
    rank = mm(named.astype(BF), earlier).astype(jnp.int32)
    picks = (rank == slot) & (named > 0.5)
    pick = jnp.where(picks, 1.0, 0.0)
    filled = jnp.max(pick, axis=1, keepdims=True) > 0.5
    pick = pick.astype(BF)
    pick_out[...] = pick
    prob_out[...] = jnp.sum(jnp.where(picks, weight, 0.0), axis=1, keepdims=True)
    wait(input_loads)
    sent = jnp.where(filled, mm(pick, held[...]), EMPTY)
    for k in range(experts):
        pieces[k][...] = sent[k * MOST : (k + 1) * MOST].astype(BF)
    wait(grad_loads)


def pick_grads(experts, pick, prob, grads, *refs):
    near_in, near, *pieces = refs
    sent = mm(pick[...], grads[...]) * prob[...]
    parts = [sent[at * MOST : (at + 1) * MOST] for at in range(experts)]
    near[...] = jnp.concatenate([near_in[...].astype(F32), parts[-2]], axis=0).astype(BF)
    for target, part in zip(pieces, parts[:-2] + parts[-1:]):
        target[...] = part.astype(BF)


def stacked(pieces, part=0):
    rows = [piece[...].astype(F32) for piece in pieces]
    rows = [row[part * MOST : (part + 1) * MOST] if row.shape[0] > MOST else row for row in rows]
    return jnp.concatenate(rows, axis=0)


def rows_of(half, own):
    core = lax.axis_index("ey") & 1
    return pl.ds(pl.multiple_of((core if own else 1 - core) * half, 128), half)


def early_rows(first, out):
    out[...] = first[...]


def place_rows(experts, capacity, pieces):
    me = lax.axis_index("ex")
    rows = experts * MOST
    got = stacked(pieces)
    full = got[:, :1] < EMPTY / 2
    key = []
    for shape, dim in (((rows, 1), 0), ((1, rows), 1)):
        row = iota(shape, dim)
        local_row = row - block_of(row, range(experts)) * MOST
        key.append((me ^ block_of(row, far_first(experts))) * MOST + local_row)
    earlier = jnp.where(key[1] < key[0], 1.0, 0.0).astype(BF)
    wide = jnp.broadcast_to(full, (rows, capacity))
    slot = mm(earlier, jnp.where(wide, 1.0, 0.0).astype(BF)).astype(jnp.int32)
    place = jnp.where((slot == iota((rows, capacity), 1)) & wide, 1.0, 0.0).astype(BF)
    return place, mm(place, got.astype(BF), ROWS).astype(BF)


def stage(count, gate_up, down, *refs):
    pieces, refs = refs[:count], refs[count:]
    held, pieces_out, sems = refs[:2], refs[2:-1], refs[-1]
    half = down.shape[1] // 2
    loads = []
    for own, out in enumerate(held):
        rows = rows_of(half, own == 1)
        for matrix in range(3):
            source = down.at[0, rows] if matrix == 2 else gate_up.at[0, matrix, rows]
            loads += cut(source, out.at[matrix], sems, len(loads), CUTS)
    run(loads)
    for source, target in zip(pieces, pieces_out):
        target[...] = source[...]
    wait(loads)


def other_pair(experts, capacity, *refs):
    held, out, place_out, rows_out = refs[experts:]
    place, rows_in = place_rows(experts, capacity, refs[:experts])
    place_out[...] = place
    rows_out[...] = rows_in
    for matrix in range(2):
        out[matrix] = mm(rows_in, held[matrix], LANES).astype(BF)


def mine_pair(rows_in, held, out):
    for matrix in range(2):
        out[matrix] = mm(rows_in[...], held[matrix], LANES).astype(BF)


def pair_sum(mine, other, held_out, sent_out):
    held = mine[...].astype(F32) + other[...].astype(F32)
    held_out[...] = held
    sent_out[...] = held.astype(BF)


def act_part(experts, own, *refs):
    place, held = refs[experts : experts + 2]
    rows_grad = mm(place[...], stacked(refs[:experts], 1).astype(BF), ROWS).astype(BF)
    if own:
        refs[-2][...] = rows_grad
    refs[-1][...] = mm(rows_grad, held[2], LANES).astype(BF)


def gates(pair, pair_far, act_out, by_gate, by_up):
    gate_sum = pair[0] + pair_far[0].astype(F32)
    up_sum = pair[1] + pair_far[1].astype(F32)
    sigmoid_gate = jax.nn.sigmoid(gate_sum)
    silu_gate = gate_sum * sigmoid_gate
    act_out[...] = (silu_gate * up_sum).astype(BF)
    by_gate[...] = up_sum * sigmoid_gate * (1.0 + gate_sum * (1.0 - sigmoid_gate))
    by_up[...] = silu_gate


def grads_of(act, act_far, by_gate, by_up, _, out):
    grad_act = act[...] + act_far[...].astype(F32)
    out[0] = (grad_act * by_gate[...]).astype(BF)
    out[1] = (grad_act * by_up[...]).astype(BF)


def own_rows(mine, held, out):
    out[...] = mm(mine[0], held[0]) + mm(mine[1], held[1])


def other_rows(experts, total, other, place, held, *refs):
    pieces, whole = refs[:experts], refs[experts]
    rows = total[...] + mm(other[0], held[0]) + mm(other[1], held[1])
    whole[...] = mm(place[...], rows.astype(BF))
    for piece, step in zip(pieces, steps(experts)):
        piece[...] = whole[place_of(ahead(step, experts), experts)].astype(BF)


def weight_grads(mine_act, other_act, mine, other, rows_in, rows_grad, pair_out, down_out, held, sems):
    core = lax.axis_index("ey") & 1
    half = mine_act.shape[1]
    step = half // 2
    stores = []
    for matrix in range(3):
        right = rows_grad[...] if matrix == 0 else rows_in[...]
        for own in range(2):
            start = (core if own else 1 - core) * half
            for part in range(2):
                columns = slice(part * step, (part + 1) * step)
                if matrix == 0:
                    left = (mine_act if own else other_act)[:, columns]
                else:
                    left = (mine if own else other)[matrix - 1, :, columns]
                at = len(stores)
                held[at] = mm(left, right, ROWS).astype(BF)
                rows = pl.ds(start + part * step, step)
                target = down_out.at[0, rows] if matrix == 0 else pair_out.at[0, matrix - 1, rows]
                store = pltpu.make_async_copy(held.at[at], target, sems.at[at])
                store.start()
                stores.append(store)
    for store in stores:
        store.wait()


def combine(experts, pick, *refs):
    out, whole, held, sems = refs[experts:]
    for piece, step in zip(refs[:experts], steps(experts)):
        whole[place_of(ahead(experts - step, experts), experts)] = piece[...].astype(F32)
    home = whole[...].astype(BF)
    rows = out.shape[0] // held.shape[0]
    stores = []
    for at in range(held.shape[0]):
        part = pick[:, at * rows : (at + 1) * rows]
        held[at] = mm(part, home, ROWS).astype(BF)
        target = out.at[pl.ds(at * rows, rows)]
        stores += run([pltpu.make_async_copy(held.at[at], target, sems.at[at])])
    wait(stores)


def far(value):
    return pltpu.with_memory_space_constraint(value, pltpu.HBM)


def place_of(partner, experts):
    k = lax.axis_index("ex") ^ partner
    spot = jnp.int32(0)
    for at, name in enumerate(far_first(experts)):
        spot = spot + jnp.where(k == name, at * MOST, 0)
    return pl.ds(pl.multiple_of(spot, 8), MOST)


def tour(count):
    return list(range(count))


def steps(count):
    return list(range(1, count)) + [0]


def ahead(step, count):
    me, names = lax.axis_index("ex"), tour(count)
    found = jnp.int32(0)
    for at, name in enumerate(names):
        found = found + jnp.where(me == name, names[(at + step) % count], 0)
    return found


def shift(value, axis, step):
    count = lax.axis_size(axis)
    names = tour(count)
    return lax.ppermute(
        value, axis, [(name, names[(at + step) % count]) for at, name in enumerate(names)]
    )


def swap(value, axis, bit):
    count = lax.axis_size(axis)
    return lax.ppermute(value, axis, [(i, i ^ bit) for i in range(count)])


def exchange(pieces, axis):
    order = far_first(len(pieces))
    return [swap(piece, axis, k) if k else piece for piece, k in zip(pieces, order)]


def local(inputs, grad_output, routes, gate_probs, gate_up, down_proj):
    experts = lax.axis_size("ex")
    ways = lax.axis_size("ey")
    tokens, width = inputs.shape
    hidden = gate_up.shape[2]
    half = hidden // 2
    capacity = 5 * tokens * experts * routes.shape[1] // (4 * EXPERTS)
    rows = experts * MOST
    weight_bytes = hidden * width * 2
    weight_flops = 2 * capacity * hidden * width
    sds = jax.ShapeDtypeStruct
    piece = [sds((MOST, width), BF)] * experts
    dma = lambda count: pltpu.SemaphoreType.DMA((count,))

    order = far_first(experts)
    pick, prob, grads, *send_in, own_in = call(
        functools.partial(pick_inputs, experts),
        [
            sds((rows, tokens), BF),
            sds((rows, 1), F32),
            pltpu.VMEM((tokens, width), BF),
        ]
        + piece,
        (far(routes.T), far(gate_probs.T), far(inputs), far(grad_output)),
        [HBM] * 4,
        [
            pltpu.VMEM(routes.shape[::-1], jnp.int32),
            pltpu.VMEM(routes.shape[::-1], BF),
            pltpu.VMEM((tokens, width), BF),
            dma(4),
        ],
        flops=2 * rows * tokens * width,
        traffic=4 * tokens * width,
    )
    near, *send_grad = call(
        functools.partial(pick_grads, experts),
        [sds((2 * MOST, width), BF)] + piece[1:],
        (pick, prob, grads, send_in[-1]),
        [VMEM] * 4,
        flops=2 * rows * tokens * width,
        traffic=2 * tokens * width,
    )
    near = swap(near, "ex", 1)
    got_in = [swap(part, "ex", k) for part, k in zip(send_in[:-1], order)] + [near, own_in]
    got_in[0] = call(
        early_rows,
        piece[0],
        (got_in[0],),
        [VMEM],
        flops=int(C0COST * weight_flops),
        traffic=weight_bytes,
    )
    held_other, held_mine, *send_grad = call(
        functools.partial(stage, experts - 1),
        [pltpu.VMEM((3, half, width), BF)] * 2 + piece[1:],
        (far(gate_up), far(down_proj), *send_grad),
        [HBM] * 2 + [VMEM] * (experts - 1),
        [dma(6 * CUTS)],
        flops=WCOST * weight_flops,
        traffic=WCOST * weight_bytes,
    )
    got_grad = [swap(part, "ex", k) for part, k in zip(send_grad[:-1], order)]
    got_grad = got_grad + [near, send_grad[-1]]
    pair_other, place, rows_in = call(
        functools.partial(other_pair, experts, capacity),
        [sds((2, capacity, half), BF), sds((rows, capacity), BF), sds((capacity, width), BF)],
        (*got_in, held_other),
        [VMEM] * (experts + 1),
        flops=2 * weight_flops,
        traffic=weight_bytes,
    )
    pair_mine = call(
        mine_pair,
        sds((2, capacity, half), BF),
        (rows_in, held_mine),
        [VMEM] * 2,
        flops=C2COST * weight_flops,
        traffic=C2COST * weight_bytes,
    )

    def total(held, sent):
        bit = 2
        while bit * 2 < ways:
            held = held + swap(sent, "ey", bit).astype(F32)
            sent = held.astype(BF)
            bit *= 2
        return held, swap(sent, "ey", bit)

    pair, pair_sent = call(
        pair_sum,
        [sds((2, capacity, half), F32), sds((2, capacity, half), BF)],
        (pair_mine, swap(pair_other, "ey", 1)),
        [VMEM] * 2,
        traffic=10 * capacity * hidden,
    )
    pair, pair_far = total(pair, pair_sent)
    def act_of(own, held, outs, tied, cost):
        return call(
            functools.partial(act_part, experts, own),
            outs + [sds((capacity, half), BF)],
            (*got_grad, place, held, *tied),
            [VMEM] * (experts + 2) + [ANY] * len(tied),
            flops=cost * weight_flops,
            traffic=cost * weight_bytes,
        )

    (act_other,) = act_of(False, held_other, [], [pair_sent], D1COST)
    rows_grad, act_mine = act_of(True, held_mine, [sds((capacity, width), BF)], [], D2COST)
    act = act_mine.astype(F32) + swap(act_other, "ey", 1).astype(F32)
    act, act_far = total(act, act.astype(BF))
    mine_act, by_gate, by_up = call(
        gates,
        [sds((capacity, half), BF)] + [sds((capacity, half), F32)] * 2,
        (pair, pair_far),
        [VMEM] * 2,
        traffic=18 * capacity * half,
        flops=GFLOP * weight_flops,
    )
    other_act = swap(mine_act, "ey", 1)
    mine = call(
        grads_of,
        sds((2, capacity, half), BF),
        (act, act_far, by_gate, by_up, other_act),
        [VMEM] * 4 + [ANY],
        traffic=18 * capacity * half,
    )
    other = swap(mine, "ey", 1)
    own = call(
        own_rows,
        sds((capacity, width), F32),
        (mine, held_mine),
        [VMEM] * 2,
        flops=weight_flops,
        traffic=weight_bytes,
    )
    back = call(
        functools.partial(other_rows, experts),
        piece,
        (own, other, place, held_other),
        [VMEM] * 4,
        [pltpu.VMEM((rows, width), F32)],
        flops=weight_flops,
        traffic=weight_bytes,
    )
    home = [shift(part, "ex", step) if step else part for part, step in zip(back, steps(experts))]
    pair_grad, down_grad = call(
        weight_grads,
        [sds((1, 2, hidden, width), BF), sds((1, hidden, width), BF)],
        (mine_act, other_act, mine, other, rows_in, rows_grad),
        [VMEM] * 6,
        [pltpu.VMEM((12, half // 2, width), BF), dma(12)],
        limit=24,
        flops=3 * weight_flops,
        traffic=3 * weight_bytes,
        out_specs=[ANY, ANY],
    )
    grad_inputs = call(
        functools.partial(combine, experts),
        sds((tokens, width), BF),
        (pick, *home),
        [VMEM] * (experts + 1),
        [pltpu.VMEM((rows, width), F32), pltpu.VMEM((4, tokens // 4, width), BF), dma(4)],
        flops=2 * rows * tokens * width,
        traffic=4 * tokens * width,
        out_specs=ANY,
    )
    return (grad_inputs, pair_grad, down_grad)


def solution(mesh):
    return jax.shard_map(
        local,
        mesh=mesh,
        in_specs=(
            P(("groups", "ex"), "ey"),
            P(("groups", "ex"), "ey"),
            P(("groups", "ex"), None),
            P(("groups", "ex"), None),
            P("ex", None, None, "ey"),
            P("ex", None, "ey"),
        ),
        out_specs=(
            P(("groups", "ex"), "ey"),
            P("ex", "groups", None, "ey"),
            P("ex", "groups", "ey"),
        ),
        check_vma=False,
    )
```

```python
import functools

import jax
import jax.numpy as jnp
from jax import lax
from jax.experimental import pallas as pl
from jax.experimental.pallas import tpu as pltpu
from jax.sharding import PartitionSpec as P

MOST = 40
EXPERTS = 128
EMPTY = 64.0
BF = jnp.bfloat16
F32 = jnp.float32
MIB = 1 << 20
C2COST = 100
C0COST = 4.75
WCOST = 1
GFLOP = 100
D1COST = 1
D2COST = 100
VMEM = pl.BlockSpec(memory_space=pltpu.VMEM)
ANY = pl.BlockSpec(memory_space=pl.ANY)
HBM = pl.BlockSpec(memory_space=pltpu.HBM)
ROWS = (((0,), (0,)), ((), ()))
LANES = (((1,), (1,)), ((), ()))
PLAIN = (((1,), (0,)), ((), ()))


def mm(left, right, dims=PLAIN):
    return lax.dot_general(left, right, dims, preferred_element_type=F32)


def iota(shape, dim):
    return lax.broadcasted_iota(jnp.int32, shape, dim)


def far_first(count):
    return sorted(range(count), key=lambda k: (-k.bit_length(), k))


def cut(source, target, sems, first, pieces):
    rows = target.shape[-2] // pieces
    out = []
    for at in range(pieces):
        part = pl.ds(at * rows, rows)
        out.append(pltpu.make_async_copy(source.at[part], target.at[part], sems.at[first + at]))
    return out


def run(loads):
    for load in loads:
        load.start()
    return loads


def wait(loads):
    for load in loads:
        load.wait()


def block_of(position, names):
    found = jnp.full_like(position, names[0])
    for at in range(1, len(names)):
        found = found + (position >= at * MOST).astype(jnp.int32) * (names[at] - names[at - 1])
    return found


def call(body, outs, operands, specs, scratch=(), limit=16, flops=0, traffic=0, out_specs=None):
    return pl.pallas_call(
        body,
        out_shape=outs,
        in_specs=specs,
        out_specs=out_specs if out_specs is not None else jax.tree.map(lambda _: VMEM, outs),
        scratch_shapes=list(scratch),
        compiler_params=pltpu.CompilerParams(vmem_limit_bytes=limit * MIB),
        cost_estimate=pl.CostEstimate(flops=flops, bytes_accessed=traffic, transcendentals=0),
    )(*operands)


def pick_inputs(experts, routes_in, probs_in, inputs, grads, pick_out, prob_out, grads_out, *refs):
    *pieces, routes, probs, held, sems = refs
    loads = run(
        [
            pltpu.make_async_copy(routes_in, routes, sems.at[0]),
            pltpu.make_async_copy(probs_in, probs, sems.at[1]),
        ]
    )
    input_loads = run(cut(inputs, held, sems, 2, 1))
    grad_loads = run(cut(grads, grads_out, sems, 3, 1))
    me = lax.axis_index("ex")
    tokens = inputs.shape[0]
    rows = experts * MOST
    order = far_first(experts)
    width = routes.shape[0]
    cells = (rows, experts * width)
    spread = block_of(iota(cells, 0), range(experts)) == lax.shift_right_logical(
        iota(cells, 1), width.bit_length() - 1
    )
    spread = jnp.where(spread, 1.0, 0.0).astype(BF)
    earlier = iota((tokens, tokens), 0) < iota((tokens, tokens), 1)
    earlier = jnp.where(earlier, 1.0, 0.0).astype(BF)
    row = iota((rows, tokens), 0)
    slot = row - block_of(row, range(experts)) * MOST
    wait(loads)
    chosen = routes[...]
    wide = probs[...].astype(F32)
    hits = jnp.concatenate([jnp.where(chosen == (me ^ k), 1.0, 0.0) for k in order], axis=0)
    odds = hits * jnp.concatenate([wide] * experts, axis=0)
    both = mm(spread, jnp.concatenate([hits, odds], axis=1).astype(BF))
    named, weight = both[:, :tokens], both[:, tokens:]
    rank = mm(named.astype(BF), earlier).astype(jnp.int32)
    picks = (rank == slot) & (named > 0.5)
    pick = jnp.where(picks, 1.0, 0.0)
    filled = jnp.max(pick, axis=1, keepdims=True) > 0.5
    pick = pick.astype(BF)
    pick_out[...] = pick
    prob_out[...] = jnp.sum(jnp.where(picks, weight, 0.0), axis=1, keepdims=True)
    wait(input_loads)
    sent = jnp.where(filled, mm(pick, held[...]), EMPTY)
    for k in range(experts):
        pieces[k][...] = sent[k * MOST : (k + 1) * MOST].astype(BF)
    wait(grad_loads)


def pick_grads(experts, pick, prob, grads, *refs):
    near_in, near, *pieces = refs
    sent = mm(pick[...], grads[...]) * prob[...]
    parts = [sent[at * MOST : (at + 1) * MOST] for at in range(experts)]
    near[...] = jnp.concatenate([near_in[...].astype(F32), parts[-2]], axis=0).astype(BF)
    for target, part in zip(pieces, parts[:-2] + parts[-1:]):
        target[...] = part.astype(BF)


def rows_of(half, own):
    core = lax.axis_index("ey") & 1
    return pl.ds(pl.multiple_of((core if own else 1 - core) * half, 128), half)


def early_rows(first, out):
    out[...] = first[...]


def joined(place, pieces, part):
    total = None
    for at, piece in enumerate(pieces):
        rows = place[at * MOST : (at + 1) * MOST]
        if piece.shape[0] > MOST:
            blank = jnp.zeros_like(rows)
            rows = jnp.concatenate([blank, rows] if part else [rows, blank], axis=0)
        term = mm(rows.astype(BF), piece[...], ROWS)
        total = term if total is None else total + term
    return total.astype(BF)


def place_rows(experts, capacity, pieces):
    me = lax.axis_index("ex")
    rows = experts * MOST
    first = [piece[:, :128].astype(F32)[:MOST] for piece in pieces]
    full = jnp.concatenate(first, axis=0)[:, :1] < EMPTY / 2
    key = []
    for shape, dim in (((rows, 1), 0), ((1, rows), 1)):
        row = iota(shape, dim)
        local_row = row - block_of(row, range(experts)) * MOST
        key.append((me ^ block_of(row, far_first(experts))) * MOST + local_row)
    earlier = jnp.where(key[1] < key[0], 1.0, 0.0).astype(BF)
    wide = jnp.broadcast_to(full, (rows, capacity))
    slot = mm(earlier, jnp.where(wide, 1.0, 0.0).astype(BF)).astype(jnp.int32)
    place = jnp.where((slot == iota((rows, capacity), 1)) & wide, 1.0, 0.0)
    return place.astype(BF), joined(place, pieces, 0)


def stage(count, gate_up, down, *refs):
    pieces, refs = refs[:count], refs[count:]
    held, pieces_out, sems = refs[:2], refs[2:-1], refs[-1]
    half = down.shape[1] // 2
    loads = []
    for own, out in enumerate(held):
        rows = rows_of(half, own == 1)
        for matrix in range(3):
            source = down.at[0, rows] if matrix == 2 else gate_up.at[0, matrix, rows]
            loads.append(pltpu.make_async_copy(source, out.at[matrix], sems.at[len(loads)]))
    run(loads)
    for source, target in zip(pieces, pieces_out):
        target[...] = source[...]
    wait(loads)


def other_pair(experts, capacity, *refs):
    held, out, place_out, rows_out = refs[experts:]
    place, rows_in = place_rows(experts, capacity, refs[:experts])
    place_out[...] = place
    rows_out[...] = rows_in
    for matrix in range(2):
        out[matrix] = mm(rows_in, held[matrix], LANES).astype(BF)


def mine_pair(rows_in, held, out):
    for matrix in range(2):
        out[matrix] = mm(rows_in[...], held[matrix], LANES).astype(BF)


def pair_sum(mine, other, held_out, sent_out):
    held = mine[...].astype(F32) + other[...].astype(F32)
    held_out[...] = held
    sent_out[...] = held.astype(BF)


def act_part(experts, own, *refs):
    place, held = refs[experts : experts + 2]
    rows_grad = joined(place[...].astype(F32), refs[:experts], 1)
    if own:
        refs[-2][...] = rows_grad
    refs[-1][...] = mm(rows_grad, held[2], LANES).astype(BF)


def gates(pair, pair_far, act_out, by_gate, by_up):
    gate_sum = pair[0] + pair_far[0].astype(F32)
    up_sum = pair[1] + pair_far[1].astype(F32)
    sigmoid_gate = jax.nn.sigmoid(gate_sum)
    silu_gate = gate_sum * sigmoid_gate
    act_out[...] = (silu_gate * up_sum).astype(BF)
    by_gate[...] = up_sum * sigmoid_gate * (1.0 + gate_sum * (1.0 - sigmoid_gate))
    by_up[...] = silu_gate


def grads_of(act, act_far, by_gate, by_up, _, out):
    grad_act = act[...] + act_far[...].astype(F32)
    out[0] = (grad_act * by_gate[...]).astype(BF)
    out[1] = (grad_act * by_up[...]).astype(BF)


def own_rows(mine, held, out):
    out[...] = mm(mine[0], held[0]) + mm(mine[1], held[1])


def other_rows(experts, total, other, place, held, *refs):
    pieces, whole = refs[:experts], refs[experts]
    rows = total[...] + mm(other[0], held[0]) + mm(other[1], held[1])
    whole[...] = mm(place[...], rows.astype(BF))
    for piece, step in zip(pieces, steps(experts)):
        piece[...] = whole[place_of(ahead(step, experts), experts)].astype(BF)


def weight_grads(mine_act, other_act, mine, other, rows_in, rows_grad, pair_out, down_out, held, sems):
    core = lax.axis_index("ey") & 1
    half = mine_act.shape[1]
    step = half // 2
    stores = []
    for matrix in range(3):
        right = rows_grad[...] if matrix == 0 else rows_in[...]
        for own in range(2):
            start = (core if own else 1 - core) * half
            for part in range(2):
                columns = slice(part * step, (part + 1) * step)
                if matrix == 0:
                    left = (mine_act if own else other_act)[:, columns]
                else:
                    left = (mine if own else other)[matrix - 1, :, columns]
                at = len(stores)
                held[at] = mm(left, right, ROWS).astype(BF)
                rows = pl.ds(start + part * step, step)
                target = down_out.at[0, rows] if matrix == 0 else pair_out.at[0, matrix - 1, rows]
                store = pltpu.make_async_copy(held.at[at], target, sems.at[at])
                store.start()
                stores.append(store)
    for store in stores:
        store.wait()


def combine(experts, pick, *refs):
    out, whole, held, sems = refs[experts:]
    for piece, step in zip(refs[:experts], steps(experts)):
        whole[place_of(ahead(experts - step, experts), experts)] = piece[...].astype(F32)
    home = whole[...].astype(BF)
    rows = out.shape[0] // held.shape[0]
    stores = []
    for at in range(held.shape[0]):
        part = pick[:, at * rows : (at + 1) * rows]
        held[at] = mm(part, home, ROWS).astype(BF)
        target = out.at[pl.ds(at * rows, rows)]
        stores += run([pltpu.make_async_copy(held.at[at], target, sems.at[at])])
    wait(stores)


def far(value):
    return pltpu.with_memory_space_constraint(value, pltpu.HBM)


def place_of(partner, experts):
    k = lax.axis_index("ex") ^ partner
    spot = jnp.int32(0)
    for at, name in enumerate(far_first(experts)):
        spot = spot + jnp.where(k == name, at * MOST, 0)
    return pl.ds(pl.multiple_of(spot, 8), MOST)


def tour(count):
    return list(range(count))


def steps(count):
    return list(range(1, count)) + [0]


def ahead(step, count):
    me, names = lax.axis_index("ex"), tour(count)
    found = jnp.int32(0)
    for at, name in enumerate(names):
        found = found + jnp.where(me == name, names[(at + step) % count], 0)
    return found


def shift(value, axis, step):
    count = lax.axis_size(axis)
    names = tour(count)
    return lax.ppermute(
        value, axis, [(name, names[(at + step) % count]) for at, name in enumerate(names)]
    )


def swap(value, axis, bit):
    count = lax.axis_size(axis)
    return lax.ppermute(value, axis, [(i, i ^ bit) for i in range(count)])


def exchange(pieces, axis):
    order = far_first(len(pieces))
    return [swap(piece, axis, k) if k else piece for piece, k in zip(pieces, order)]


def local(inputs, grad_output, routes, gate_probs, gate_up, down_proj):
    experts = lax.axis_size("ex")
    ways = lax.axis_size("ey")
    tokens, width = inputs.shape
    hidden = gate_up.shape[2]
    half = hidden // 2
    capacity = 5 * tokens * experts * routes.shape[1] // (4 * EXPERTS)
    rows = experts * MOST
    weight_bytes = hidden * width * 2
    weight_flops = 2 * capacity * hidden * width
    sds = jax.ShapeDtypeStruct
    piece = [sds((MOST, width), BF)] * experts
    dma = lambda count: pltpu.SemaphoreType.DMA((count,))

    order = far_first(experts)
    pick, prob, grads, *send_in, own_in = call(
        functools.partial(pick_inputs, experts),
        [
            sds((rows, tokens), BF),
            sds((rows, 1), F32),
            pltpu.VMEM((tokens, width), BF),
        ]
        + piece,
        (far(routes.T), far(gate_probs.T), far(inputs), far(grad_output)),
        [HBM] * 4,
        [
            pltpu.VMEM(routes.shape[::-1], jnp.int32),
            pltpu.VMEM(routes.shape[::-1], BF),
            pltpu.VMEM((tokens, width), BF),
            dma(4),
        ],
        flops=2 * rows * tokens * width,
        traffic=4 * tokens * width,
    )
    near, *send_grad = call(
        functools.partial(pick_grads, experts),
        [sds((2 * MOST, width), BF)] + piece[1:],
        (pick, prob, grads, send_in[-1]),
        [VMEM] * 4,
        flops=2 * rows * tokens * width,
        traffic=2 * tokens * width,
    )
    near = swap(near, "ex", 1)
    got_in = [swap(part, "ex", k) for part, k in zip(send_in[:-1], order)] + [near, own_in]
    got_in[0] = call(
        early_rows,
        piece[0],
        (got_in[0],),
        [VMEM],
        flops=int(C0COST * weight_flops),
        traffic=weight_bytes,
    )
    held_other, held_mine, *send_grad = call(
        functools.partial(stage, experts - 1),
        [pltpu.VMEM((3, half, width), BF)] * 2 + piece[1:],
        (far(gate_up), far(down_proj), *send_grad),
        [HBM] * 2 + [VMEM] * (experts - 1),
        [dma(6)],
        flops=WCOST * weight_flops,
        traffic=WCOST * weight_bytes,
    )
    got_grad = [swap(part, "ex", k) for part, k in zip(send_grad[:-1], order)]
    got_grad = got_grad + [near, send_grad[-1]]
    pair_other, place, rows_in = call(
        functools.partial(other_pair, experts, capacity),
        [sds((2, capacity, half), BF), sds((rows, capacity), BF), sds((capacity, width), BF)],
        (*got_in, held_other),
        [VMEM] * (experts + 1),
        flops=2 * weight_flops,
        traffic=weight_bytes,
    )
    pair_mine = call(
        mine_pair,
        sds((2, capacity, half), BF),
        (rows_in, held_mine),
        [VMEM] * 2,
        flops=C2COST * weight_flops,
        traffic=C2COST * weight_bytes,
    )

    def total(held, sent):
        bit = 2
        while bit * 2 < ways:
            held = held + swap(sent, "ey", bit).astype(F32)
            sent = held.astype(BF)
            bit *= 2
        return held, swap(sent, "ey", bit)

    pair, pair_sent = call(
        pair_sum,
        [sds((2, capacity, half), F32), sds((2, capacity, half), BF)],
        (pair_mine, swap(pair_other, "ey", 1)),
        [VMEM] * 2,
        traffic=10 * capacity * hidden,
    )
    pair, pair_far = total(pair, pair_sent)
    def act_of(own, held, outs, tied, cost):
        return call(
            functools.partial(act_part, experts, own),
            outs + [sds((capacity, half), BF)],
            (*got_grad, place, held, *tied),
            [VMEM] * (experts + 2) + [ANY] * len(tied),
            flops=cost * weight_flops,
            traffic=cost * weight_bytes,
        )

    (act_other,) = act_of(False, held_other, [], [pair_sent], D1COST)
    rows_grad, act_mine = act_of(True, held_mine, [sds((capacity, width), BF)], [], D2COST)
    act = act_mine.astype(F32) + swap(act_other, "ey", 1).astype(F32)
    act, act_far = total(act, act.astype(BF))
    mine_act, by_gate, by_up = call(
        gates,
        [sds((capacity, half), BF)] + [sds((capacity, half), F32)] * 2,
        (pair, pair_far),
        [VMEM] * 2,
        traffic=18 * capacity * half,
        flops=GFLOP * weight_flops,
    )
    other_act = swap(mine_act, "ey", 1)
    mine = call(
        grads_of,
        sds((2, capacity, half), BF),
        (act, act_far, by_gate, by_up, other_act),
        [VMEM] * 4 + [ANY],
        traffic=18 * capacity * half,
    )
    other = swap(mine, "ey", 1)
    own = call(
        own_rows,
        sds((capacity, width), F32),
        (mine, held_mine),
        [VMEM] * 2,
        flops=weight_flops,
        traffic=weight_bytes,
    )
    back = call(
        functools.partial(other_rows, experts),
        piece,
        (own, other, place, held_other),
        [VMEM] * 4,
        [pltpu.VMEM((rows, width), F32)],
        flops=weight_flops,
        traffic=weight_bytes,
    )
    home = [shift(part, "ex", step) if step else part for part, step in zip(back, steps(experts))]
    pair_grad, down_grad = call(
        weight_grads,
        [sds((1, 2, hidden, width), BF), sds((1, hidden, width), BF)],
        (mine_act, other_act, mine, other, rows_in, rows_grad),
        [VMEM] * 6,
        [pltpu.VMEM((12, half // 2, width), BF), dma(12)],
        limit=24,
        flops=3 * weight_flops,
        traffic=3 * weight_bytes,
        out_specs=[ANY, ANY],
    )
    grad_inputs = call(
        functools.partial(combine, experts),
        sds((tokens, width), BF),
        (pick, *home),
        [VMEM] * (experts + 1),
        [pltpu.VMEM((rows, width), F32), pltpu.VMEM((2, tokens // 2, width), BF), dma(2)],
        flops=2 * rows * tokens * width,
        traffic=4 * tokens * width,
        out_specs=ANY,
    )
    return (grad_inputs, pair_grad, down_grad)


def solution(mesh):
    return jax.shard_map(
        local,
        mesh=mesh,
        in_specs=(
            P(("groups", "ex"), "ey"),
            P(("groups", "ex"), "ey"),
            P(("groups", "ex"), None),
            P(("groups", "ex"), None),
            P("ex", None, None, "ey"),
            P("ex", None, "ey"),
        ),
        out_specs=(
            P(("groups", "ex"), "ey"),
            P("ex", "groups", None, "ey"),
            P("ex", "groups", "ey"),
        ),
        check_vma=False,
    )
```

```python
import functools

import jax
import jax.numpy as jnp
from jax import lax
from jax.experimental import pallas as pl
from jax.experimental.pallas import tpu as pltpu
from jax.sharding import PartitionSpec as P

MOST = 40
EXPERTS = 128
EMPTY = 64.0
BF = jnp.bfloat16
F32 = jnp.float32
MIB = 1 << 20
C2COST = 100
C0COST = 4.75
WCOST = 1
GFLOP = 100
D1COST = 1
D2COST = 100
VMEM = pl.BlockSpec(memory_space=pltpu.VMEM)
ANY = pl.BlockSpec(memory_space=pl.ANY)
HBM = pl.BlockSpec(memory_space=pltpu.HBM)
ROWS = (((0,), (0,)), ((), ()))
LANES = (((1,), (1,)), ((), ()))
PLAIN = (((1,), (0,)), ((), ()))


def mm(left, right, dims=PLAIN):
    return lax.dot_general(left, right, dims, preferred_element_type=F32)


def iota(shape, dim):
    return lax.broadcasted_iota(jnp.int32, shape, dim)


def far_first(count):
    return sorted(range(count), key=lambda k: (-k.bit_length(), k))


def cut(source, target, sems, first, pieces):
    rows = target.shape[-2] // pieces
    out = []
    for at in range(pieces):
        part = pl.ds(at * rows, rows)
        out.append(pltpu.make_async_copy(source.at[part], target.at[part], sems.at[first + at]))
    return out


def run(loads):
    for load in loads:
        load.start()
    return loads


def wait(loads):
    for load in loads:
        load.wait()


def block_of(position, names):
    found = jnp.full_like(position, names[0])
    for at in range(1, len(names)):
        found = found + (position >= at * MOST).astype(jnp.int32) * (names[at] - names[at - 1])
    return found


def call(body, outs, operands, specs, scratch=(), limit=16, flops=0, traffic=0, out_specs=None):
    return pl.pallas_call(
        body,
        out_shape=outs,
        in_specs=specs,
        out_specs=out_specs if out_specs is not None else jax.tree.map(lambda _: VMEM, outs),
        scratch_shapes=list(scratch),
        compiler_params=pltpu.CompilerParams(vmem_limit_bytes=limit * MIB),
        cost_estimate=pl.CostEstimate(flops=flops, bytes_accessed=traffic, transcendentals=0),
    )(*operands)


def pick_inputs(experts, routes_in, probs_in, inputs, grads, pick_out, prob_out, grads_out, *refs):
    *pieces, routes, probs, held, sems = refs
    loads = run(
        [
            pltpu.make_async_copy(routes_in, routes, sems.at[0]),
            pltpu.make_async_copy(probs_in, probs, sems.at[1]),
        ]
    )
    input_loads = run(cut(inputs, held, sems, 2, 1))
    grad_loads = run(cut(grads, grads_out, sems, 3, 1))
    me = lax.axis_index("ex")
    tokens = inputs.shape[0]
    rows = experts * MOST
    order = far_first(experts)
    width = routes.shape[0]
    cells = (rows, experts * width)
    spread = block_of(iota(cells, 0), range(experts)) == lax.shift_right_logical(
        iota(cells, 1), width.bit_length() - 1
    )
    spread = jnp.where(spread, 1.0, 0.0).astype(BF)
    earlier = iota((tokens, tokens), 0) < iota((tokens, tokens), 1)
    earlier = jnp.where(earlier, 1.0, 0.0).astype(BF)
    row = iota((rows, tokens), 0)
    slot = row - block_of(row, range(experts)) * MOST
    wait(loads)
    chosen = routes[...]
    wide = probs[...].astype(F32)
    hits = jnp.concatenate([jnp.where(chosen == (me ^ k), 1.0, 0.0) for k in order], axis=0)
    odds = hits * jnp.concatenate([wide] * experts, axis=0)
    both = mm(spread, jnp.concatenate([hits, odds], axis=1).astype(BF))
    named, weight = both[:, :tokens], both[:, tokens:]
    rank = mm(named.astype(BF), earlier).astype(jnp.int32)
    picks = (rank == slot) & (named > 0.5)
    pick = jnp.where(picks, 1.0, 0.0)
    filled = jnp.max(pick, axis=1, keepdims=True) > 0.5
    pick = pick.astype(BF)
    pick_out[...] = pick
    prob_out[...] = jnp.sum(jnp.where(picks, weight, 0.0), axis=1, keepdims=True)
    wait(input_loads)
    sent = jnp.where(filled, mm(pick, held[...]), EMPTY)
    for k in range(experts):
        pieces[k][...] = sent[k * MOST : (k + 1) * MOST].astype(BF)
    wait(grad_loads)


def pick_grads(experts, pick, prob, grads, *refs):
    near_in, near, *pieces = refs
    sent = mm(pick[...], grads[...]) * prob[...]
    parts = [sent[at * MOST : (at + 1) * MOST] for at in range(experts)]
    near[...] = jnp.concatenate([near_in[...].astype(F32), parts[-2]], axis=0).astype(BF)
    for target, part in zip(pieces, parts[:-2] + parts[-1:]):
        target[...] = part.astype(BF)


def stacked(pieces, part=0):
    rows = [piece[...].astype(F32) for piece in pieces]
    rows = [row[part * MOST : (part + 1) * MOST] if row.shape[0] > MOST else row for row in rows]
    return jnp.concatenate(rows, axis=0)


def rows_of(half, own):
    core = lax.axis_index("ey") & 1
    return pl.ds(pl.multiple_of((core if own else 1 - core) * half, 128), half)


def early_rows(first, out):
    out[...] = first[...]


def place_rows(experts, capacity, pieces):
    me = lax.axis_index("ex")
    rows = experts * MOST
    got = stacked(pieces)
    full = got[:, :1] < EMPTY / 2
    key = []
    for shape, dim in (((rows, 1), 0), ((1, rows), 1)):
        row = iota(shape, dim)
        local_row = row - block_of(row, range(experts)) * MOST
        key.append((me ^ block_of(row, far_first(experts))) * MOST + local_row)
    earlier = jnp.where(key[1] < key[0], 1.0, 0.0).astype(BF)
    wide = jnp.broadcast_to(full, (rows, capacity))
    slot = mm(earlier, jnp.where(wide, 1.0, 0.0).astype(BF)).astype(jnp.int32)
    place = jnp.where((slot == iota((rows, capacity), 1)) & wide, 1.0, 0.0).astype(BF)
    return place, mm(place, got.astype(BF), ROWS).astype(BF)


def stage(count, gate_up, down, *refs):
    pieces, refs = refs[:count], refs[count:]
    held, pieces_out, sems = refs[:2], refs[2:-1], refs[-1]
    half = down.shape[1] // 2
    loads = []
    for own, out in enumerate(held):
        rows = rows_of(half, own == 1)
        for matrix in range(3):
            source = down.at[0, rows] if matrix == 2 else gate_up.at[0, matrix, rows]
            loads.append(pltpu.make_async_copy(source, out.at[matrix], sems.at[len(loads)]))
    run(loads)
    for source, target in zip(pieces, pieces_out):
        target[...] = source[...]
    wait(loads)


def other_pair(experts, capacity, *refs):
    held, out, place_out, rows_out = refs[experts:]
    place, rows_in = place_rows(experts, capacity, refs[:experts])
    place_out[...] = place
    rows_out[...] = rows_in
    for matrix in range(2):
        out[matrix] = mm(rows_in, held[matrix], LANES).astype(BF)


def mine_pair(rows_in, held, out):
    for matrix in range(2):
        out[matrix] = mm(rows_in[...], held[matrix], LANES).astype(BF)


def pair_sum(mine, other, held_out, sent_out):
    held = mine[...].astype(F32) + other[...].astype(F32)
    held_out[...] = held
    sent_out[...] = held.astype(BF)


def act_part(experts, own, *refs):
    place, held = refs[experts : experts + 2]
    rows_grad = mm(place[...], stacked(refs[:experts], 1).astype(BF), ROWS).astype(BF)
    if own:
        refs[-2][...] = rows_grad
    refs[-1][...] = mm(rows_grad, held[2], LANES).astype(BF)


def gates(pair, pair_far, act_out, by_gate, by_up):
    gate_sum = pair[0] + pair_far[0].astype(F32)
    up_sum = pair[1] + pair_far[1].astype(F32)
    sigmoid_gate = jax.nn.sigmoid(gate_sum)
    silu_gate = gate_sum * sigmoid_gate
    act_out[...] = (silu_gate * up_sum).astype(BF)
    by_gate[...] = up_sum * sigmoid_gate * (1.0 + gate_sum * (1.0 - sigmoid_gate))
    by_up[...] = silu_gate


def grads_of(act, act_far, by_gate, by_up, _, out):
    grad_act = act[...] + act_far[...].astype(F32)
    out[0] = (grad_act * by_gate[...]).astype(BF)
    out[1] = (grad_act * by_up[...]).astype(BF)


def own_rows(mine, held, out):
    out[...] = mm(mine[0], held[0]) + mm(mine[1], held[1])


def other_rows(experts, total, other, place, held, *refs):
    pieces, whole = refs[:experts], refs[experts]
    rows = total[...] + mm(other[0], held[0]) + mm(other[1], held[1])
    whole[...] = mm(place[...], rows.astype(BF))
    for piece, step in zip(pieces, steps(experts)):
        piece[...] = whole[place_of(ahead(step, experts), experts)].astype(BF)


def weight_grads(mine_act, other_act, mine, other, rows_in, rows_grad, pair_out, down_out, held, sems):
    core = lax.axis_index("ey") & 1
    half = mine_act.shape[1]
    step = half // 2
    stores = []
    for matrix in range(3):
        right = rows_grad[...] if matrix == 0 else rows_in[...]
        for own in range(2):
            start = (core if own else 1 - core) * half
            for part in range(2):
                columns = slice(part * step, (part + 1) * step)
                if matrix == 0:
                    left = (mine_act if own else other_act)[:, columns]
                else:
                    left = (mine if own else other)[matrix - 1, :, columns]
                at = len(stores)
                held[at] = mm(left, right, ROWS).astype(BF)
                rows = pl.ds(start + part * step, step)
                target = down_out.at[0, rows] if matrix == 0 else pair_out.at[0, matrix - 1, rows]
                store = pltpu.make_async_copy(held.at[at], target, sems.at[at])
                store.start()
                stores.append(store)
    for store in stores:
        store.wait()


def combine(experts, pick, *refs):
    out, whole, held, sems = refs[experts:]
    for piece, step in zip(refs[:experts], steps(experts)):
        whole[place_of(ahead(experts - step, experts), experts)] = piece[...].astype(F32)
    home = whole[...].astype(BF)
    rows = out.shape[0] // held.shape[0]
    stores = []
    for at in range(held.shape[0]):
        part = pick[:, at * rows : (at + 1) * rows]
        held[at] = mm(part, home, ROWS).astype(BF)
        target = out.at[pl.ds(at * rows, rows)]
        stores += run([pltpu.make_async_copy(held.at[at], target, sems.at[at])])
    wait(stores)


def far(value):
    return pltpu.with_memory_space_constraint(value, pltpu.HBM)


def place_of(partner, experts):
    k = lax.axis_index("ex") ^ partner
    spot = jnp.int32(0)
    for at, name in enumerate(far_first(experts)):
        spot = spot + jnp.where(k == name, at * MOST, 0)
    return pl.ds(pl.multiple_of(spot, 8), MOST)


def tour(count):
    return [i ^ (i >> 1) for i in range(count)]


def steps(count):
    return list(range(2, count)) + [1, 0]


def ahead(step, count):
    me, names = lax.axis_index("ex"), tour(count)
    found = jnp.int32(0)
    for at, name in enumerate(names):
        found = found + jnp.where(me == name, names[(at + step) % count], 0)
    return found


def shift(value, axis, step):
    count = lax.axis_size(axis)
    names = tour(count)
    return lax.ppermute(
        value, axis, [(name, names[(at + step) % count]) for at, name in enumerate(names)]
    )


def swap(value, axis, bit):
    count = lax.axis_size(axis)
    return lax.ppermute(value, axis, [(i, i ^ bit) for i in range(count)])


def exchange(pieces, axis):
    order = far_first(len(pieces))
    return [swap(piece, axis, k) if k else piece for piece, k in zip(pieces, order)]


def local(inputs, grad_output, routes, gate_probs, gate_up, down_proj):
    experts = lax.axis_size("ex")
    ways = lax.axis_size("ey")
    tokens, width = inputs.shape
    hidden = gate_up.shape[2]
    half = hidden // 2
    capacity = 5 * tokens * experts * routes.shape[1] // (4 * EXPERTS)
    rows = experts * MOST
    weight_bytes = hidden * width * 2
    weight_flops = 2 * capacity * hidden * width
    sds = jax.ShapeDtypeStruct
    piece = [sds((MOST, width), BF)] * experts
    dma = lambda count: pltpu.SemaphoreType.DMA((count,))

    order = far_first(experts)
    pick, prob, grads, *send_in, own_in = call(
        functools.partial(pick_inputs, experts),
        [
            sds((rows, tokens), BF),
            sds((rows, 1), F32),
            pltpu.VMEM((tokens, width), BF),
        ]
        + piece,
        (far(routes.T), far(gate_probs.T), far(inputs), far(grad_output)),
        [HBM] * 4,
        [
            pltpu.VMEM(routes.shape[::-1], jnp.int32),
            pltpu.VMEM(routes.shape[::-1], BF),
            pltpu.VMEM((tokens, width), BF),
            dma(4),
        ],
        flops=2 * rows * tokens * width,
        traffic=4 * tokens * width,
    )
    near, *send_grad = call(
        functools.partial(pick_grads, experts),
        [sds((2 * MOST, width), BF)] + piece[1:],
        (pick, prob, grads, send_in[-1]),
        [VMEM] * 4,
        flops=2 * rows * tokens * width,
        traffic=2 * tokens * width,
    )
    near = swap(near, "ex", 1)
    got_in = [swap(part, "ex", k) for part, k in zip(send_in[:-1], order)] + [near, own_in]
    got_in[0] = call(
        early_rows,
        piece[0],
        (got_in[0],),
        [VMEM],
        flops=int(C0COST * weight_flops),
        traffic=weight_bytes,
    )
    held_other, held_mine, *send_grad = call(
        functools.partial(stage, experts - 1),
        [pltpu.VMEM((3, half, width), BF)] * 2 + piece[1:],
        (far(gate_up), far(down_proj), *send_grad),
        [HBM] * 2 + [VMEM] * (experts - 1),
        [dma(6)],
        flops=WCOST * weight_flops,
        traffic=WCOST * weight_bytes,
    )
    got_grad = [swap(part, "ex", k) for part, k in zip(send_grad[:-1], order)]
    got_grad = got_grad + [near, send_grad[-1]]
    pair_other, place, rows_in = call(
        functools.partial(other_pair, experts, capacity),
        [sds((2, capacity, half), BF), sds((rows, capacity), BF), sds((capacity, width), BF)],
        (*got_in, held_other),
        [VMEM] * (experts + 1),
        flops=2 * weight_flops,
        traffic=weight_bytes,
    )
    pair_mine = call(
        mine_pair,
        sds((2, capacity, half), BF),
        (rows_in, held_mine),
        [VMEM] * 2,
        flops=C2COST * weight_flops,
        traffic=C2COST * weight_bytes,
    )

    def total(held, sent):
        bit = 2
        while bit * 2 < ways:
            held = held + swap(sent, "ey", bit).astype(F32)
            sent = held.astype(BF)
            bit *= 2
        return held, swap(sent, "ey", bit)

    pair, pair_sent = call(
        pair_sum,
        [sds((2, capacity, half), F32), sds((2, capacity, half), BF)],
        (pair_mine, swap(pair_other, "ey", 1)),
        [VMEM] * 2,
        traffic=10 * capacity * hidden,
    )
    pair, pair_far = total(pair, pair_sent)
    def act_of(own, held, outs, tied, cost):
        return call(
            functools.partial(act_part, experts, own),
            outs + [sds((capacity, half), BF)],
            (*got_grad, place, held, *tied),
            [VMEM] * (experts + 2) + [ANY] * len(tied),
            flops=cost * weight_flops,
            traffic=cost * weight_bytes,
        )

    (act_other,) = act_of(False, held_other, [], [pair_sent], D1COST)
    rows_grad, act_mine = act_of(True, held_mine, [sds((capacity, width), BF)], [], D2COST)
    act = act_mine.astype(F32) + swap(act_other, "ey", 1).astype(F32)
    act, act_far = total(act, act.astype(BF))
    mine_act, by_gate, by_up = call(
        gates,
        [sds((capacity, half), BF)] + [sds((capacity, half), F32)] * 2,
        (pair, pair_far),
        [VMEM] * 2,
        traffic=18 * capacity * half,
        flops=GFLOP * weight_flops,
    )
    other_act = swap(mine_act, "ey", 1)
    mine = call(
        grads_of,
        sds((2, capacity, half), BF),
        (act, act_far, by_gate, by_up, other_act),
        [VMEM] * 4 + [ANY],
        traffic=18 * capacity * half,
    )
    other = swap(mine, "ey", 1)
    own = call(
        own_rows,
        sds((capacity, width), F32),
        (mine, held_mine),
        [VMEM] * 2,
        flops=weight_flops,
        traffic=weight_bytes,
    )
    back = call(
        functools.partial(other_rows, experts),
        piece,
        (own, other, place, held_other),
        [VMEM] * 4,
        [pltpu.VMEM((rows, width), F32)],
        flops=weight_flops,
        traffic=weight_bytes,
    )
    home = [shift(part, "ex", step) if step else part for part, step in zip(back, steps(experts))]
    pair_grad, down_grad = call(
        weight_grads,
        [sds((1, 2, hidden, width), BF), sds((1, hidden, width), BF)],
        (mine_act, other_act, mine, other, rows_in, rows_grad),
        [VMEM] * 6,
        [pltpu.VMEM((12, half // 2, width), BF), dma(12)],
        limit=24,
        flops=3 * weight_flops,
        traffic=3 * weight_bytes,
        out_specs=[ANY, ANY],
    )
    grad_inputs = call(
        functools.partial(combine, experts),
        sds((tokens, width), BF),
        (pick, *home),
        [VMEM] * (experts + 1),
        [pltpu.VMEM((rows, width), F32), pltpu.VMEM((2, tokens // 2, width), BF), dma(2)],
        flops=2 * rows * tokens * width,
        traffic=4 * tokens * width,
        out_specs=ANY,
    )
    return (grad_inputs, pair_grad, down_grad)


def solution(mesh):
    return jax.shard_map(
        local,
        mesh=mesh,
        in_specs=(
            P(("groups", "ex"), "ey"),
            P(("groups", "ex"), "ey"),
            P(("groups", "ex"), None),
            P(("groups", "ex"), None),
            P("ex", None, None, "ey"),
            P("ex", None, "ey"),
        ),
        out_specs=(
            P(("groups", "ex"), "ey"),
            P("ex", "groups", None, "ey"),
            P("ex", "groups", "ey"),
        ),
        check_vma=False,
    )
```

```python
import functools

import jax
import jax.numpy as jnp
from jax import lax
from jax.experimental import pallas as pl
from jax.experimental.pallas import tpu as pltpu
from jax.sharding import PartitionSpec as P

MOST = 40
EXPERTS = 128
EMPTY = 64.0
BF = jnp.bfloat16
F32 = jnp.float32
MIB = 1 << 20
C2COST = 100
C0COST = 4.75
WCOST = 1
GFLOP = 100
D1COST = 1
D2COST = 100
VMEM = pl.BlockSpec(memory_space=pltpu.VMEM)
ANY = pl.BlockSpec(memory_space=pl.ANY)
HBM = pl.BlockSpec(memory_space=pltpu.HBM)
ROWS = (((0,), (0,)), ((), ()))
LANES = (((1,), (1,)), ((), ()))
PLAIN = (((1,), (0,)), ((), ()))


def mm(left, right, dims=PLAIN):
    return lax.dot_general(left, right, dims, preferred_element_type=F32)


def iota(shape, dim):
    return lax.broadcasted_iota(jnp.int32, shape, dim)


def far_first(count):
    return sorted(range(count), key=lambda k: (-k.bit_length(), k))


def cut(source, target, sems, first, pieces):
    rows = target.shape[-2] // pieces
    out = []
    for at in range(pieces):
        part = pl.ds(at * rows, rows)
        out.append(pltpu.make_async_copy(source.at[part], target.at[part], sems.at[first + at]))
    return out


def run(loads):
    for load in loads:
        load.start()
    return loads


def wait(loads):
    for load in loads:
        load.wait()


def block_of(position, names):
    found = jnp.full_like(position, names[0])
    for at in range(1, len(names)):
        found = found + (position >= at * MOST).astype(jnp.int32) * (names[at] - names[at - 1])
    return found


def call(body, outs, operands, specs, scratch=(), limit=16, flops=0, traffic=0, out_specs=None):
    return pl.pallas_call(
        body,
        out_shape=outs,
        in_specs=specs,
        out_specs=out_specs if out_specs is not None else jax.tree.map(lambda _: VMEM, outs),
        scratch_shapes=list(scratch),
        compiler_params=pltpu.CompilerParams(vmem_limit_bytes=limit * MIB),
        cost_estimate=pl.CostEstimate(flops=flops, bytes_accessed=traffic, transcendentals=0),
    )(*operands)


def pick_inputs(experts, routes_in, probs_in, inputs, grads, pick_out, prob_out, grads_out, *refs):
    *pieces, routes, probs, held, sems = refs
    loads = run(
        [
            pltpu.make_async_copy(routes_in, routes, sems.at[0]),
            pltpu.make_async_copy(probs_in, probs, sems.at[1]),
        ]
    )
    input_loads = run(cut(inputs, held, sems, 2, 1))
    grad_loads = run(cut(grads, grads_out, sems, 3, 1))
    me = lax.axis_index("ex")
    tokens = inputs.shape[0]
    rows = experts * MOST
    order = far_first(experts)
    width = routes.shape[0]
    cells = (rows, experts * width)
    spread = block_of(iota(cells, 0), range(experts)) == lax.shift_right_logical(
        iota(cells, 1), width.bit_length() - 1
    )
    spread = jnp.where(spread, 1.0, 0.0).astype(BF)
    earlier = iota((tokens, tokens), 0) < iota((tokens, tokens), 1)
    earlier = jnp.where(earlier, 1.0, 0.0).astype(BF)
    row = iota((rows, tokens), 0)
    slot = row - block_of(row, range(experts)) * MOST
    wait(loads)
    chosen = routes[...]
    wide = probs[...].astype(F32)
    hits = jnp.concatenate([jnp.where(chosen == (me ^ k), 1.0, 0.0) for k in order], axis=0)
    odds = hits * jnp.concatenate([wide] * experts, axis=0)
    both = mm(spread, jnp.concatenate([hits, odds], axis=1).astype(BF))
    named, weight = both[:, :tokens], both[:, tokens:]
    rank = mm(named.astype(BF), earlier).astype(jnp.int32)
    picks = (rank == slot) & (named > 0.5)
    pick = jnp.where(picks, 1.0, 0.0)
    filled = jnp.max(pick, axis=1, keepdims=True) > 0.5
    pick = pick.astype(BF)
    pick_out[...] = pick
    prob_out[...] = jnp.sum(jnp.where(picks, weight, 0.0), axis=1, keepdims=True)
    wait(input_loads)
    sent = jnp.where(filled, mm(pick, held[...]), EMPTY)
    for k in range(experts):
        pieces[k][...] = sent[k * MOST : (k + 1) * MOST].astype(BF)
    wait(grad_loads)


def pick_grads(experts, pick, prob, grads, *refs):
    near_in, near, *pieces = refs
    sent = mm(pick[...], grads[...]) * prob[...]
    parts = [sent[at * MOST : (at + 1) * MOST] for at in range(experts)]
    near[...] = jnp.concatenate([near_in[...].astype(F32), parts[-2]], axis=0).astype(BF)
    for target, part in zip(pieces, parts[:-2] + parts[-1:]):
        target[...] = part.astype(BF)


def stacked(pieces, part=0):
    rows = [piece[...].astype(F32) for piece in pieces]
    rows = [row[part * MOST : (part + 1) * MOST] if row.shape[0] > MOST else row for row in rows]
    return jnp.concatenate(rows, axis=0)


def rows_of(half, own):
    core = lax.axis_index("ey") & 1
    return pl.ds(pl.multiple_of((core if own else 1 - core) * half, 128), half)


def early_rows(first, out):
    out[...] = first[...]


def place_rows(experts, capacity, pieces):
    me = lax.axis_index("ex")
    rows = experts * MOST
    got = stacked(pieces)
    full = got[:, :1] < EMPTY / 2
    key = []
    for shape, dim in (((rows, 1), 0), ((1, rows), 1)):
        row = iota(shape, dim)
        local_row = row - block_of(row, range(experts)) * MOST
        key.append((me ^ block_of(row, far_first(experts))) * MOST + local_row)
    earlier = jnp.where(key[1] < key[0], 1.0, 0.0).astype(BF)
    wide = jnp.broadcast_to(full, (rows, capacity))
    slot = mm(earlier, jnp.where(wide, 1.0, 0.0).astype(BF)).astype(jnp.int32)
    place = jnp.where((slot == iota((rows, capacity), 1)) & wide, 1.0, 0.0).astype(BF)
    return place, mm(place, got.astype(BF), ROWS).astype(BF)


def stage(count, gate_up, down, *refs):
    pieces, refs = refs[:count], refs[count:]
    held, pieces_out, sems = refs[:2], refs[2:-1], refs[-1]
    half = down.shape[1] // 2
    loads = []
    for own, out in enumerate(held):
        rows = rows_of(half, own == 1)
        for matrix in range(3):
            source = down.at[0, rows] if matrix == 2 else gate_up.at[0, matrix, rows]
            loads.append(pltpu.make_async_copy(source, out.at[matrix], sems.at[len(loads)]))
    run(loads)
    for source, target in zip(pieces, pieces_out):
        target[...] = source[...]
    wait(loads)


def other_pair(experts, capacity, *refs):
    held, out, place_out, rows_out = refs[experts:]
    place, rows_in = place_rows(experts, capacity, refs[:experts])
    place_out[...] = place
    rows_out[...] = rows_in
    for matrix in range(2):
        out[matrix] = mm(rows_in, held[matrix], LANES).astype(BF)


def mine_pair(rows_in, held, out):
    for matrix in range(2):
        out[matrix] = mm(rows_in[...], held[matrix], LANES).astype(BF)


def pair_sum(mine, other, held_out, sent_out):
    held = mine[...].astype(F32) + other[...].astype(F32)
    held_out[...] = held
    sent_out[...] = held.astype(BF)


def act_part(experts, own, *refs):
    place, held = refs[experts : experts + 2]
    pieces = refs[: experts - 2][::-1] + refs[experts - 2 : experts]
    rows_grad = mm(place[...], stacked(pieces, 1).astype(BF), ROWS).astype(BF)
    if own:
        refs[-2][...] = rows_grad
    refs[-1][...] = mm(rows_grad, held[2], LANES).astype(BF)


def gates(pair, pair_far, act_out, by_gate, by_up):
    gate_sum = pair[0] + pair_far[0].astype(F32)
    up_sum = pair[1] + pair_far[1].astype(F32)
    sigmoid_gate = jax.nn.sigmoid(gate_sum)
    silu_gate = gate_sum * sigmoid_gate
    act_out[...] = (silu_gate * up_sum).astype(BF)
    by_gate[...] = up_sum * sigmoid_gate * (1.0 + gate_sum * (1.0 - sigmoid_gate))
    by_up[...] = silu_gate


def grads_of(act, act_far, by_gate, by_up, _, out):
    grad_act = act[...] + act_far[...].astype(F32)
    out[0] = (grad_act * by_gate[...]).astype(BF)
    out[1] = (grad_act * by_up[...]).astype(BF)


def own_rows(mine, held, out):
    out[...] = mm(mine[0], held[0]) + mm(mine[1], held[1])


def other_rows(experts, total, other, place, held, *refs):
    pieces, whole = refs[:experts], refs[experts]
    rows = total[...] + mm(other[0], held[0]) + mm(other[1], held[1])
    whole[...] = mm(place[...], rows.astype(BF))
    for piece, step in zip(pieces, steps(experts)):
        piece[...] = whole[place_of(ahead(step, experts), experts)].astype(BF)


def weight_grads(mine_act, other_act, mine, other, rows_in, rows_grad, pair_out, down_out, held, sems):
    core = lax.axis_index("ey") & 1
    half = mine_act.shape[1]
    step = half // 2
    stores = []
    for matrix in range(3):
        right = rows_grad[...] if matrix == 0 else rows_in[...]
        for own in range(2):
            start = (core if own else 1 - core) * half
            for part in range(2):
                columns = slice(part * step, (part + 1) * step)
                if matrix == 0:
                    left = (mine_act if own else other_act)[:, columns]
                else:
                    left = (mine if own else other)[matrix - 1, :, columns]
                at = len(stores)
                held[at] = mm(left, right, ROWS).astype(BF)
                rows = pl.ds(start + part * step, step)
                target = down_out.at[0, rows] if matrix == 0 else pair_out.at[0, matrix - 1, rows]
                store = pltpu.make_async_copy(held.at[at], target, sems.at[at])
                store.start()
                stores.append(store)
    for store in stores:
        store.wait()


def combine(experts, pick, *refs):
    out, whole, held, sems = refs[experts:]
    for piece, step in zip(refs[:experts], steps(experts)):
        whole[place_of(ahead(experts - step, experts), experts)] = piece[...].astype(F32)
    home = whole[...].astype(BF)
    rows = out.shape[0] // held.shape[0]
    stores = []
    for at in range(held.shape[0]):
        part = pick[:, at * rows : (at + 1) * rows]
        held[at] = mm(part, home, ROWS).astype(BF)
        target = out.at[pl.ds(at * rows, rows)]
        stores += run([pltpu.make_async_copy(held.at[at], target, sems.at[at])])
    wait(stores)


def far(value):
    return pltpu.with_memory_space_constraint(value, pltpu.HBM)


def place_of(partner, experts):
    k = lax.axis_index("ex") ^ partner
    spot = jnp.int32(0)
    for at, name in enumerate(far_first(experts)):
        spot = spot + jnp.where(k == name, at * MOST, 0)
    return pl.ds(pl.multiple_of(spot, 8), MOST)


def tour(count):
    return list(range(count))


def steps(count):
    return list(range(1, count)) + [0]


def ahead(step, count):
    me, names = lax.axis_index("ex"), tour(count)
    found = jnp.int32(0)
    for at, name in enumerate(names):
        found = found + jnp.where(me == name, names[(at + step) % count], 0)
    return found


def shift(value, axis, step):
    count = lax.axis_size(axis)
    names = tour(count)
    return lax.ppermute(
        value, axis, [(name, names[(at + step) % count]) for at, name in enumerate(names)]
    )


def swap(value, axis, bit):
    count = lax.axis_size(axis)
    return lax.ppermute(value, axis, [(i, i ^ bit) for i in range(count)])


def exchange(pieces, axis):
    order = far_first(len(pieces))
    return [swap(piece, axis, k) if k else piece for piece, k in zip(pieces, order)]


def local(inputs, grad_output, routes, gate_probs, gate_up, down_proj):
    experts = lax.axis_size("ex")
    ways = lax.axis_size("ey")
    tokens, width = inputs.shape
    hidden = gate_up.shape[2]
    half = hidden // 2
    capacity = 5 * tokens * experts * routes.shape[1] // (4 * EXPERTS)
    rows = experts * MOST
    weight_bytes = hidden * width * 2
    weight_flops = 2 * capacity * hidden * width
    sds = jax.ShapeDtypeStruct
    piece = [sds((MOST, width), BF)] * experts
    dma = lambda count: pltpu.SemaphoreType.DMA((count,))

    order = far_first(experts)
    pick, prob, grads, *send_in, own_in = call(
        functools.partial(pick_inputs, experts),
        [
            sds((rows, tokens), BF),
            sds((rows, 1), F32),
            pltpu.VMEM((tokens, width), BF),
        ]
        + piece,
        (far(routes.T), far(gate_probs.T), far(inputs), far(grad_output)),
        [HBM] * 4,
        [
            pltpu.VMEM(routes.shape[::-1], jnp.int32),
            pltpu.VMEM(routes.shape[::-1], BF),
            pltpu.VMEM((tokens, width), BF),
            dma(4),
        ],
        flops=2 * rows * tokens * width,
        traffic=4 * tokens * width,
    )
    near, *send_grad = call(
        functools.partial(pick_grads, experts),
        [sds((2 * MOST, width), BF)] + piece[1:],
        (pick, prob, grads, send_in[-1]),
        [VMEM] * 4,
        flops=2 * rows * tokens * width,
        traffic=2 * tokens * width,
    )
    near = swap(near, "ex", 1)
    got_in = [swap(part, "ex", k) for part, k in zip(send_in[:-1], order)] + [near, own_in]
    got_in[0] = call(
        early_rows,
        piece[0],
        (got_in[0],),
        [VMEM],
        flops=int(C0COST * weight_flops),
        traffic=weight_bytes,
    )
    held_other, held_mine, *send_grad = call(
        functools.partial(stage, experts - 1),
        [pltpu.VMEM((3, half, width), BF)] * 2 + piece[1:],
        (far(gate_up), far(down_proj), *send_grad),
        [HBM] * 2 + [VMEM] * (experts - 1),
        [dma(6)],
        flops=WCOST * weight_flops,
        traffic=WCOST * weight_bytes,
    )
    got_grad = [swap(part, "ex", k) for part, k in zip(send_grad[:-1], order)][::-1]
    got_grad = got_grad + [near, send_grad[-1]]
    pair_other, place, rows_in = call(
        functools.partial(other_pair, experts, capacity),
        [sds((2, capacity, half), BF), sds((rows, capacity), BF), sds((capacity, width), BF)],
        (*got_in, held_other),
        [VMEM] * (experts + 1),
        flops=2 * weight_flops,
        traffic=weight_bytes,
    )
    pair_mine = call(
        mine_pair,
        sds((2, capacity, half), BF),
        (rows_in, held_mine),
        [VMEM] * 2,
        flops=C2COST * weight_flops,
        traffic=C2COST * weight_bytes,
    )

    def total(held, sent):
        bit = 2
        while bit * 2 < ways:
            held = held + swap(sent, "ey", bit).astype(F32)
            sent = held.astype(BF)
            bit *= 2
        return held, swap(sent, "ey", bit)

    pair, pair_sent = call(
        pair_sum,
        [sds((2, capacity, half), F32), sds((2, capacity, half), BF)],
        (pair_mine, swap(pair_other, "ey", 1)),
        [VMEM] * 2,
        traffic=10 * capacity * hidden,
    )
    pair, pair_far = total(pair, pair_sent)
    def act_of(own, held, outs, tied, cost):
        return call(
            functools.partial(act_part, experts, own),
            outs + [sds((capacity, half), BF)],
            (*got_grad, place, held, *tied),
            [VMEM] * (experts + 2) + [ANY] * len(tied),
            flops=cost * weight_flops,
            traffic=cost * weight_bytes,
        )

    (act_other,) = act_of(False, held_other, [], [pair_sent], D1COST)
    rows_grad, act_mine = act_of(True, held_mine, [sds((capacity, width), BF)], [], D2COST)
    act = act_mine.astype(F32) + swap(act_other, "ey", 1).astype(F32)
    act, act_far = total(act, act.astype(BF))
    mine_act, by_gate, by_up = call(
        gates,
        [sds((capacity, half), BF)] + [sds((capacity, half), F32)] * 2,
        (pair, pair_far),
        [VMEM] * 2,
        traffic=18 * capacity * half,
        flops=GFLOP * weight_flops,
    )
    other_act = swap(mine_act, "ey", 1)
    mine = call(
        grads_of,
        sds((2, capacity, half), BF),
        (act, act_far, by_gate, by_up, other_act),
        [VMEM] * 4 + [ANY],
        traffic=18 * capacity * half,
    )
    other = swap(mine, "ey", 1)
    own = call(
        own_rows,
        sds((capacity, width), F32),
        (mine, held_mine),
        [VMEM] * 2,
        flops=weight_flops,
        traffic=weight_bytes,
    )
    back = call(
        functools.partial(other_rows, experts),
        piece,
        (own, other, place, held_other),
        [VMEM] * 4,
        [pltpu.VMEM((rows, width), F32)],
        flops=weight_flops,
        traffic=weight_bytes,
    )
    home = [shift(part, "ex", step) if step else part for part, step in zip(back, steps(experts))]
    pair_grad, down_grad = call(
        weight_grads,
        [sds((1, 2, hidden, width), BF), sds((1, hidden, width), BF)],
        (mine_act, other_act, mine, other, rows_in, rows_grad),
        [VMEM] * 6,
        [pltpu.VMEM((12, half // 2, width), BF), dma(12)],
        limit=24,
        flops=3 * weight_flops,
        traffic=3 * weight_bytes,
        out_specs=[ANY, ANY],
    )
    grad_inputs = call(
        functools.partial(combine, experts),
        sds((tokens, width), BF),
        (pick, *home),
        [VMEM] * (experts + 1),
        [pltpu.VMEM((rows, width), F32), pltpu.VMEM((2, tokens // 2, width), BF), dma(2)],
        flops=2 * rows * tokens * width,
        traffic=4 * tokens * width,
        out_specs=ANY,
    )
    return (grad_inputs, pair_grad, down_grad)


def solution(mesh):
    return jax.shard_map(
        local,
        mesh=mesh,
        in_specs=(
            P(("groups", "ex"), "ey"),
            P(("groups", "ex"), "ey"),
            P(("groups", "ex"), None),
            P(("groups", "ex"), None),
            P("ex", None, None, "ey"),
            P("ex", None, "ey"),
        ),
        out_specs=(
            P(("groups", "ex"), "ey"),
            P("ex", "groups", None, "ey"),
            P("ex", "groups", "ey"),
        ),
        check_vma=False,
    )
```

```python
import functools

import jax
import jax.numpy as jnp
from jax import lax
from jax.experimental import pallas as pl
from jax.experimental.pallas import tpu as pltpu
from jax.sharding import PartitionSpec as P

MOST = 40
EXPERTS = 128
EMPTY = 64.0
BF = jnp.bfloat16
F32 = jnp.float32
MIB = 1 << 20
C2COST = 100
C0COST = 4.75
WCOST = 1
GFLOP = 100
D1COST = 1
D2COST = 100
VMEM = pl.BlockSpec(memory_space=pltpu.VMEM)
ANY = pl.BlockSpec(memory_space=pl.ANY)
HBM = pl.BlockSpec(memory_space=pltpu.HBM)
ROWS = (((0,), (0,)), ((), ()))
LANES = (((1,), (1,)), ((), ()))
PLAIN = (((1,), (0,)), ((), ()))


def mm(left, right, dims=PLAIN):
    return lax.dot_general(left, right, dims, preferred_element_type=F32)


def iota(shape, dim):
    return lax.broadcasted_iota(jnp.int32, shape, dim)


def far_first(count):
    return sorted(range(count), key=lambda k: (-k.bit_length(), k))


def cut(source, target, sems, first, pieces):
    rows = target.shape[-2] // pieces
    out = []
    for at in range(pieces):
        part = pl.ds(at * rows, rows)
        out.append(pltpu.make_async_copy(source.at[part], target.at[part], sems.at[first + at]))
    return out


def run(loads):
    for load in loads:
        load.start()
    return loads


def wait(loads):
    for load in loads:
        load.wait()


def block_of(position, names):
    found = jnp.full_like(position, names[0])
    for at in range(1, len(names)):
        found = found + (position >= at * MOST).astype(jnp.int32) * (names[at] - names[at - 1])
    return found


def call(body, outs, operands, specs, scratch=(), limit=16, flops=0, traffic=0, out_specs=None):
    return pl.pallas_call(
        body,
        out_shape=outs,
        in_specs=specs,
        out_specs=out_specs if out_specs is not None else jax.tree.map(lambda _: VMEM, outs),
        scratch_shapes=list(scratch),
        compiler_params=pltpu.CompilerParams(vmem_limit_bytes=limit * MIB),
        cost_estimate=pl.CostEstimate(flops=flops, bytes_accessed=traffic, transcendentals=0),
    )(*operands)


def pick_inputs(experts, routes_in, probs_in, inputs, grads, pick_out, prob_out, grads_out, *refs):
    *pieces, routes, probs, held, sems = refs
    loads = run(
        [
            pltpu.make_async_copy(routes_in, routes, sems.at[0]),
            pltpu.make_async_copy(probs_in, probs, sems.at[1]),
        ]
    )
    input_loads = run(cut(inputs, held, sems, 2, 1))
    grad_loads = run(cut(grads, grads_out, sems, 3, 1))
    me = lax.axis_index("ex")
    tokens = inputs.shape[0]
    rows = experts * MOST
    order = far_first(experts)
    width = routes.shape[0]
    cells = (rows, experts * width)
    spread = block_of(iota(cells, 0), range(experts)) == lax.shift_right_logical(
        iota(cells, 1), width.bit_length() - 1
    )
    spread = jnp.where(spread, 1.0, 0.0).astype(BF)
    earlier = iota((tokens, tokens), 0) < iota((tokens, tokens), 1)
    earlier = jnp.where(earlier, 1.0, 0.0).astype(BF)
    row = iota((rows, tokens), 0)
    slot = row - block_of(row, range(experts)) * MOST
    wait(loads)
    chosen = routes[...]
    wide = probs[...].astype(F32)
    hits = jnp.concatenate([jnp.where(chosen == (me ^ k), 1.0, 0.0) for k in order], axis=0)
    odds = hits * jnp.concatenate([wide] * experts, axis=0)
    both = mm(spread, jnp.concatenate([hits, odds], axis=1).astype(BF))
    named, weight = both[:, :tokens], both[:, tokens:]
    rank = mm(named.astype(BF), earlier).astype(jnp.int32)
    picks = (rank == slot) & (named > 0.5)
    pick = jnp.where(picks, 1.0, 0.0)
    filled = jnp.max(pick, axis=1, keepdims=True) > 0.5
    pick = pick.astype(BF)
    pick_out[...] = pick
    prob_out[...] = jnp.sum(jnp.where(picks, weight, 0.0), axis=1, keepdims=True)
    wait(input_loads)
    sent = jnp.where(filled, mm(pick, held[...]), EMPTY)
    for k in range(experts):
        pieces[k][...] = sent[k * MOST : (k + 1) * MOST].astype(BF)
    wait(grad_loads)


def pick_grads(experts, pick, prob, grads, *refs):
    near_in, near, *pieces = refs
    sent = mm(pick[...], grads[...]) * prob[...]
    parts = [sent[at * MOST : (at + 1) * MOST] for at in range(experts)]
    near[...] = jnp.concatenate([near_in[...].astype(F32), parts[-2]], axis=0).astype(BF)
    for target, part in zip(pieces, parts[:-2] + parts[-1:]):
        target[...] = part.astype(BF)


def stacked(pieces, part=0):
    rows = [piece[...].astype(F32) for piece in pieces]
    rows = [row[part * MOST : (part + 1) * MOST] if row.shape[0] > MOST else row for row in rows]
    return jnp.concatenate(rows, axis=0)


def rows_of(half, own):
    core = lax.axis_index("ey") & 1
    return pl.ds(pl.multiple_of((core if own else 1 - core) * half, 128), half)


def early_rows(first, out):
    out[...] = first[...]


def place_rows(experts, capacity, pieces):
    me = lax.axis_index("ex")
    rows = experts * MOST
    got = stacked(pieces)
    full = got[:, :1] < EMPTY / 2
    key = []
    for shape, dim in (((rows, 1), 0), ((1, rows), 1)):
        row = iota(shape, dim)
        local_row = row - block_of(row, range(experts)) * MOST
        key.append((me ^ block_of(row, far_first(experts))) * MOST + local_row)
    earlier = jnp.where(key[1] < key[0], 1.0, 0.0).astype(BF)
    wide = jnp.broadcast_to(full, (rows, capacity))
    slot = mm(earlier, jnp.where(wide, 1.0, 0.0).astype(BF)).astype(jnp.int32)
    place = jnp.where((slot == iota((rows, capacity), 1)) & wide, 1.0, 0.0).astype(BF)
    return place, mm(place, got.astype(BF), ROWS).astype(BF)


def stage(count, gate_up, down, *refs):
    pieces, refs = refs[:count], refs[count:]
    held, pieces_out, sems = refs[:2], refs[2:-1], refs[-1]
    half = down.shape[1] // 2
    loads = []
    for own, out in enumerate(held):
        rows = rows_of(half, own == 1)
        for matrix in range(3):
            source = down.at[0, rows] if matrix == 2 else gate_up.at[0, matrix, rows]
            loads.append(pltpu.make_async_copy(source, out.at[matrix], sems.at[len(loads)]))
    run(loads)
    for source, target in zip(pieces, pieces_out):
        target[...] = source[...]
    wait(loads)


def other_pair(experts, capacity, *refs):
    held, out, place_out, rows_out = refs[experts:]
    place, rows_in = place_rows(experts, capacity, refs[:experts])
    place_out[...] = place
    rows_out[...] = rows_in
    for matrix in range(2):
        out[matrix] = mm(rows_in, held[matrix], LANES).astype(BF)


def mine_pair(rows_in, held, out):
    for matrix in range(2):
        out[matrix] = mm(rows_in[...], held[matrix], LANES).astype(BF)


def pair_sum(mine, other, held_out, sent_out):
    held = mine[...].astype(F32) + other[...].astype(F32)
    held_out[...] = held
    sent_out[...] = held.astype(BF)


def act_part(experts, own, *refs):
    place, held = refs[experts : experts + 2]
    pieces = refs[: experts - 2][::-1] + refs[experts - 2 : experts]
    rows_grad = mm(place[...], stacked(pieces, 1).astype(BF), ROWS).astype(BF)
    if own:
        refs[-2][...] = rows_grad
    refs[-1][...] = mm(rows_grad, held[2], LANES).astype(BF)


def gates(pair, pair_far, act_out, by_gate, by_up):
    gate_sum = pair[0] + pair_far[0].astype(F32)
    up_sum = pair[1] + pair_far[1].astype(F32)
    sigmoid_gate = jax.nn.sigmoid(gate_sum)
    silu_gate = gate_sum * sigmoid_gate
    act_out[...] = (silu_gate * up_sum).astype(BF)
    by_gate[...] = up_sum * sigmoid_gate * (1.0 + gate_sum * (1.0 - sigmoid_gate))
    by_up[...] = silu_gate


def grads_of(act, act_far, by_gate, by_up, _, out):
    grad_act = act[...] + act_far[...].astype(F32)
    out[0] = (grad_act * by_gate[...]).astype(BF)
    out[1] = (grad_act * by_up[...]).astype(BF)


def own_rows(mine, held, out):
    out[...] = mm(mine[0], held[0]) + mm(mine[1], held[1])


def other_rows(experts, total, other, place, held, *refs):
    pieces, whole = refs[:experts], refs[experts]
    rows = total[...] + mm(other[0], held[0]) + mm(other[1], held[1])
    whole[...] = mm(place[...], rows.astype(BF))
    for piece, step in zip(pieces, steps(experts)):
        piece[...] = whole[place_of(ahead(step, experts), experts)].astype(BF)


def weight_grads(mine_act, other_act, mine, other, rows_in, rows_grad, pair_out, down_out, held, sems):
    core = lax.axis_index("ey") & 1
    half = mine_act.shape[1]
    stores = []
    for matrix in range(3):
        right = rows_grad[...] if matrix == 0 else rows_in[...]
        for own in range(2):
            start = (core if own else 1 - core) * half
            parts = 2 if (matrix, own) == (2, 1) else 1
            step = half // parts
            for part in range(parts):
                columns = slice(part * step, (part + 1) * step)
                if matrix == 0:
                    left = (mine_act if own else other_act)[:, columns]
                else:
                    left = (mine if own else other)[matrix - 1, :, columns]
                at = len(stores)
                block = held.at[2 * matrix + own, pl.ds(part * step, step)]
                block[...] = mm(left, right, ROWS).astype(BF)
                rows = pl.ds(start + part * step, step)
                target = down_out.at[0, rows] if matrix == 0 else pair_out.at[0, matrix - 1, rows]
                store = pltpu.make_async_copy(block, target, sems.at[at])
                store.start()
                stores.append(store)
    for store in stores:
        store.wait()


def combine(experts, pick, *refs):
    out, whole, held, sems = refs[experts:]
    for piece, step in zip(refs[:experts], steps(experts)):
        whole[place_of(ahead(experts - step, experts), experts)] = piece[...].astype(F32)
    home = whole[...].astype(BF)
    rows = out.shape[0] // held.shape[0]
    stores = []
    for at in range(held.shape[0]):
        part = pick[:, at * rows : (at + 1) * rows]
        held[at] = mm(part, home, ROWS).astype(BF)
        target = out.at[pl.ds(at * rows, rows)]
        stores += run([pltpu.make_async_copy(held.at[at], target, sems.at[at])])
    wait(stores)


def far(value):
    return pltpu.with_memory_space_constraint(value, pltpu.HBM)


def place_of(partner, experts):
    k = lax.axis_index("ex") ^ partner
    spot = jnp.int32(0)
    for at, name in enumerate(far_first(experts)):
        spot = spot + jnp.where(k == name, at * MOST, 0)
    return pl.ds(pl.multiple_of(spot, 8), MOST)


def tour(count):
    return list(range(count))


def steps(count):
    return list(range(1, count)) + [0]


def ahead(step, count):
    me, names = lax.axis_index("ex"), tour(count)
    found = jnp.int32(0)
    for at, name in enumerate(names):
        found = found + jnp.where(me == name, names[(at + step) % count], 0)
    return found


def shift(value, axis, step):
    count = lax.axis_size(axis)
    names = tour(count)
    return lax.ppermute(
        value, axis, [(name, names[(at + step) % count]) for at, name in enumerate(names)]
    )


def swap(value, axis, bit):
    count = lax.axis_size(axis)
    return lax.ppermute(value, axis, [(i, i ^ bit) for i in range(count)])


def exchange(pieces, axis):
    order = far_first(len(pieces))
    return [swap(piece, axis, k) if k else piece for piece, k in zip(pieces, order)]


def local(inputs, grad_output, routes, gate_probs, gate_up, down_proj):
    experts = lax.axis_size("ex")
    ways = lax.axis_size("ey")
    tokens, width = inputs.shape
    hidden = gate_up.shape[2]
    half = hidden // 2
    capacity = 5 * tokens * experts * routes.shape[1] // (4 * EXPERTS)
    rows = experts * MOST
    weight_bytes = hidden * width * 2
    weight_flops = 2 * capacity * hidden * width
    sds = jax.ShapeDtypeStruct
    piece = [sds((MOST, width), BF)] * experts
    dma = lambda count: pltpu.SemaphoreType.DMA((count,))

    order = far_first(experts)
    pick, prob, grads, *send_in, own_in = call(
        functools.partial(pick_inputs, experts),
        [
            sds((rows, tokens), BF),
            sds((rows, 1), F32),
            pltpu.VMEM((tokens, width), BF),
        ]
        + piece,
        (far(routes.T), far(gate_probs.T), far(inputs), far(grad_output)),
        [HBM] * 4,
        [
            pltpu.VMEM(routes.shape[::-1], jnp.int32),
            pltpu.VMEM(routes.shape[::-1], BF),
            pltpu.VMEM((tokens, width), BF),
            dma(4),
        ],
        flops=2 * rows * tokens * width,
        traffic=4 * tokens * width,
    )
    near, *send_grad = call(
        functools.partial(pick_grads, experts),
        [sds((2 * MOST, width), BF)] + piece[1:],
        (pick, prob, grads, send_in[-1]),
        [VMEM] * 4,
        flops=2 * rows * tokens * width,
        traffic=2 * tokens * width,
    )
    near = swap(near, "ex", 1)
    got_in = [swap(part, "ex", k) for part, k in zip(send_in[:-1], order)] + [near, own_in]
    got_in[0] = call(
        early_rows,
        piece[0],
        (got_in[0],),
        [VMEM],
        flops=int(C0COST * weight_flops),
        traffic=weight_bytes,
    )
    held_other, held_mine, *send_grad = call(
        functools.partial(stage, experts - 1),
        [pltpu.VMEM((3, half, width), BF)] * 2 + piece[1:],
        (far(gate_up), far(down_proj), *send_grad),
        [HBM] * 2 + [VMEM] * (experts - 1),
        [dma(6)],
        flops=WCOST * weight_flops,
        traffic=WCOST * weight_bytes,
    )
    got_grad = [swap(part, "ex", k) for part, k in zip(send_grad[:-1], order)][::-1]
    got_grad = got_grad + [near, send_grad[-1]]
    pair_other, place, rows_in = call(
        functools.partial(other_pair, experts, capacity),
        [sds((2, capacity, half), BF), sds((rows, capacity), BF), sds((capacity, width), BF)],
        (*got_in, held_other),
        [VMEM] * (experts + 1),
        flops=2 * weight_flops,
        traffic=weight_bytes,
    )
    pair_mine = call(
        mine_pair,
        sds((2, capacity, half), BF),
        (rows_in, held_mine),
        [VMEM] * 2,
        flops=C2COST * weight_flops,
        traffic=C2COST * weight_bytes,
    )

    def total(held, sent):
        bit = 2
        while bit * 2 < ways:
            held = held + swap(sent, "ey", bit).astype(F32)
            sent = held.astype(BF)
            bit *= 2
        return held, swap(sent, "ey", bit)

    pair, pair_sent = call(
        pair_sum,
        [sds((2, capacity, half), F32), sds((2, capacity, half), BF)],
        (pair_mine, swap(pair_other, "ey", 1)),
        [VMEM] * 2,
        traffic=10 * capacity * hidden,
    )
    pair, pair_far = total(pair, pair_sent)
    def act_of(own, held, outs, tied, cost):
        return call(
            functools.partial(act_part, experts, own),
            outs + [sds((capacity, half), BF)],
            (*got_grad, place, held, *tied),
            [VMEM] * (experts + 2) + [ANY] * len(tied),
            flops=cost * weight_flops,
            traffic=cost * weight_bytes,
        )

    (act_other,) = act_of(False, held_other, [], [pair_sent], D1COST)
    rows_grad, act_mine = act_of(True, held_mine, [sds((capacity, width), BF)], [], D2COST)
    act = act_mine.astype(F32) + swap(act_other, "ey", 1).astype(F32)
    act, act_far = total(act, act.astype(BF))
    mine_act, by_gate, by_up = call(
        gates,
        [sds((capacity, half), BF)] + [sds((capacity, half), F32)] * 2,
        (pair, pair_far),
        [VMEM] * 2,
        traffic=18 * capacity * half,
        flops=GFLOP * weight_flops,
    )
    other_act = swap(mine_act, "ey", 1)
    mine = call(
        grads_of,
        sds((2, capacity, half), BF),
        (act, act_far, by_gate, by_up, other_act),
        [VMEM] * 4 + [ANY],
        traffic=18 * capacity * half,
    )
    other = swap(mine, "ey", 1)
    own = call(
        own_rows,
        sds((capacity, width), F32),
        (mine, held_mine),
        [VMEM] * 2,
        flops=weight_flops,
        traffic=weight_bytes,
    )
    back = call(
        functools.partial(other_rows, experts),
        piece,
        (own, other, place, held_other),
        [VMEM] * 4,
        [pltpu.VMEM((rows, width), F32)],
        flops=weight_flops,
        traffic=weight_bytes,
    )
    home = [shift(part, "ex", step) if step else part for part, step in zip(back, steps(experts))]
    pair_grad, down_grad = call(
        weight_grads,
        [sds((1, 2, hidden, width), BF), sds((1, hidden, width), BF)],
        (mine_act, other_act, mine, other, rows_in, rows_grad),
        [VMEM] * 6,
        [pltpu.VMEM((6, half, width), BF), dma(7)],
        limit=24,
        flops=3 * weight_flops,
        traffic=3 * weight_bytes,
        out_specs=[ANY, ANY],
    )
    grad_inputs = call(
        functools.partial(combine, experts),
        sds((tokens, width), BF),
        (pick, *home),
        [VMEM] * (experts + 1),
        [pltpu.VMEM((rows, width), F32), pltpu.VMEM((2, tokens // 2, width), BF), dma(2)],
        flops=2 * rows * tokens * width,
        traffic=4 * tokens * width,
        out_specs=ANY,
    )
    return (grad_inputs, pair_grad, down_grad)


def solution(mesh):
    return jax.shard_map(
        local,
        mesh=mesh,
        in_specs=(
            P(("groups", "ex"), "ey"),
            P(("groups", "ex"), "ey"),
            P(("groups", "ex"), None),
            P(("groups", "ex"), None),
            P("ex", None, None, "ey"),
            P("ex", None, "ey"),
        ),
        out_specs=(
            P(("groups", "ex"), "ey"),
            P("ex", "groups", None, "ey"),
            P("ex", "groups", "ey"),
        ),
        check_vma=False,
    )
```

```python
import functools

import jax
import jax.numpy as jnp
from jax import lax
from jax.experimental import pallas as pl
from jax.experimental.pallas import tpu as pltpu
from jax.sharding import PartitionSpec as P

MOST = 40
EXPERTS = 128
EMPTY = 64.0
BF = jnp.bfloat16
F32 = jnp.float32
MIB = 1 << 20
C2COST = 100
C0COST = 4.75
WCOST = 1
GFLOP = 100
D1COST = 1
D2COST = 100
VMEM = pl.BlockSpec(memory_space=pltpu.VMEM)
ANY = pl.BlockSpec(memory_space=pl.ANY)
HBM = pl.BlockSpec(memory_space=pltpu.HBM)
ROWS = (((0,), (0,)), ((), ()))
LANES = (((1,), (1,)), ((), ()))
PLAIN = (((1,), (0,)), ((), ()))


def mm(left, right, dims=PLAIN):
    return lax.dot_general(left, right, dims, preferred_element_type=F32)


def iota(shape, dim):
    return lax.broadcasted_iota(jnp.int32, shape, dim)


def far_first(count):
    return sorted(range(count), key=lambda k: (-k.bit_length(), k))


def cut(source, target, sems, first, pieces):
    rows = target.shape[-2] // pieces
    out = []
    for at in range(pieces):
        part = pl.ds(at * rows, rows)
        out.append(pltpu.make_async_copy(source.at[part], target.at[part], sems.at[first + at]))
    return out


def run(loads):
    for load in loads:
        load.start()
    return loads


def wait(loads):
    for load in loads:
        load.wait()


def block_of(position, names):
    found = jnp.full_like(position, names[0])
    for at in range(1, len(names)):
        found = found + (position >= at * MOST).astype(jnp.int32) * (names[at] - names[at - 1])
    return found


def call(body, outs, operands, specs, scratch=(), limit=16, flops=0, traffic=0, out_specs=None):
    return pl.pallas_call(
        body,
        out_shape=outs,
        in_specs=specs,
        out_specs=out_specs if out_specs is not None else jax.tree.map(lambda _: VMEM, outs),
        scratch_shapes=list(scratch),
        compiler_params=pltpu.CompilerParams(vmem_limit_bytes=limit * MIB),
        cost_estimate=pl.CostEstimate(flops=flops, bytes_accessed=traffic, transcendentals=0),
    )(*operands)


def pick_inputs(experts, routes_in, probs_in, inputs, grads, pick_out, prob_out, grads_out, *refs):
    *pieces, routes, probs, held, sems = refs
    loads = run(
        [
            pltpu.make_async_copy(routes_in, routes, sems.at[0]),
            pltpu.make_async_copy(probs_in, probs, sems.at[1]),
        ]
    )
    input_loads = run(cut(inputs, held, sems, 2, 1))
    grad_loads = run(cut(grads, grads_out, sems, 3, 1))
    me = lax.axis_index("ex")
    tokens = inputs.shape[0]
    rows = experts * MOST
    order = far_first(experts)
    width = routes.shape[0]
    cells = (rows, experts * width)
    spread = block_of(iota(cells, 0), range(experts)) == lax.shift_right_logical(
        iota(cells, 1), width.bit_length() - 1
    )
    spread = jnp.where(spread, 1.0, 0.0).astype(BF)
    earlier = iota((tokens, tokens), 0) < iota((tokens, tokens), 1)
    earlier = jnp.where(earlier, 1.0, 0.0).astype(BF)
    row = iota((rows, tokens), 0)
    slot = row - block_of(row, range(experts)) * MOST
    wait(loads)
    chosen = routes[...]
    wide = probs[...].astype(F32)
    hits = jnp.concatenate([jnp.where(chosen == (me ^ k), 1.0, 0.0) for k in order], axis=0)
    odds = hits * jnp.concatenate([wide] * experts, axis=0)
    both = mm(spread, jnp.concatenate([hits, odds], axis=1).astype(BF))
    named, weight = both[:, :tokens], both[:, tokens:]
    rank = mm(named.astype(BF), earlier).astype(jnp.int32)
    picks = (rank == slot) & (named > 0.5)
    pick = jnp.where(picks, 1.0, 0.0)
    filled = jnp.max(pick, axis=1, keepdims=True) > 0.5
    pick = pick.astype(BF)
    pick_out[...] = pick
    prob_out[...] = jnp.sum(jnp.where(picks, weight, 0.0), axis=1, keepdims=True)
    wait(input_loads)
    sent = jnp.where(filled, mm(pick, held[...]), EMPTY)
    for k in range(experts):
        pieces[k][...] = sent[k * MOST : (k + 1) * MOST].astype(BF)
    wait(grad_loads)


def pick_grads(experts, pick, prob, grads, *refs):
    near_in, near, *pieces = refs
    sent = mm(pick[...], grads[...]) * prob[...]
    parts = [sent[at * MOST : (at + 1) * MOST] for at in range(experts)]
    near[...] = jnp.concatenate([near_in[...].astype(F32), parts[-2]], axis=0).astype(BF)
    for target, part in zip(pieces, parts[:-2] + parts[-1:]):
        target[...] = part.astype(BF)


def stacked(pieces, part=0):
    rows = [piece[...].astype(F32) for piece in pieces]
    rows = [row[part * MOST : (part + 1) * MOST] if row.shape[0] > MOST else row for row in rows]
    return jnp.concatenate(rows, axis=0)


def rows_of(half, own):
    core = lax.axis_index("ey") & 1
    return pl.ds(pl.multiple_of((core if own else 1 - core) * half, 128), half)


def early_rows(first, out):
    out[...] = first[...]


def place_rows(experts, capacity, pieces):
    me = lax.axis_index("ex")
    rows = experts * MOST
    got = stacked(pieces)
    full = got[:, :1] < EMPTY / 2
    key = []
    for shape, dim in (((rows, 1), 0), ((1, rows), 1)):
        row = iota(shape, dim)
        local_row = row - block_of(row, range(experts)) * MOST
        key.append((me ^ block_of(row, far_first(experts))) * MOST + local_row)
    earlier = jnp.where(key[1] < key[0], 1.0, 0.0).astype(BF)
    wide = jnp.broadcast_to(full, (rows, capacity))
    slot = mm(earlier, jnp.where(wide, 1.0, 0.0).astype(BF)).astype(jnp.int32)
    place = jnp.where((slot == iota((rows, capacity), 1)) & wide, 1.0, 0.0).astype(BF)
    return place, mm(place, got.astype(BF), ROWS).astype(BF)


def stage(count, gate_up, down, *refs):
    pieces, refs = refs[:count], refs[count:]
    held, pieces_out, sems = refs[:2], refs[2:-1], refs[-1]
    half = down.shape[1] // 2
    loads = []
    for own, out in enumerate(held):
        rows = rows_of(half, own == 1)
        for matrix in range(3):
            source = down.at[0, rows] if matrix == 2 else gate_up.at[0, matrix, rows]
            loads.append(pltpu.make_async_copy(source, out.at[matrix], sems.at[len(loads)]))
    run(loads)
    for source, target in zip(pieces, pieces_out):
        target[...] = source[...]
    wait(loads)


def other_pair(experts, capacity, *refs):
    held, out, place_out, rows_out = refs[experts:]
    place, rows_in = place_rows(experts, capacity, refs[:experts])
    place_out[...] = place
    rows_out[...] = rows_in
    for matrix in range(2):
        out[matrix] = mm(rows_in, held[matrix], LANES).astype(BF)


def mine_pair(rows_in, held, out):
    for matrix in range(2):
        out[matrix] = mm(rows_in[...], held[matrix], LANES).astype(BF)


def pair_sum(mine, other, held_out, sent_out):
    held = mine[...].astype(F32) + other[...].astype(F32)
    held_out[...] = held
    sent_out[...] = held.astype(BF)


def act_part(experts, own, *refs):
    place, held = refs[experts : experts + 2]
    pieces = refs[: experts - 2][::-1] + refs[experts - 2 : experts]
    rows_grad = mm(place[...], stacked(pieces, 1).astype(BF), ROWS).astype(BF)
    if own:
        refs[-2][...] = rows_grad
    refs[-1][...] = mm(rows_grad, held[2], LANES).astype(BF)


def gates(pair, pair_far, act_out, by_gate, by_up):
    gate_sum = pair[0] + pair_far[0].astype(F32)
    up_sum = pair[1] + pair_far[1].astype(F32)
    sigmoid_gate = jax.nn.sigmoid(gate_sum)
    silu_gate = gate_sum * sigmoid_gate
    act_out[...] = (silu_gate * up_sum).astype(BF)
    by_gate[...] = up_sum * sigmoid_gate * (1.0 + gate_sum * (1.0 - sigmoid_gate))
    by_up[...] = silu_gate


def grads_of(act, act_far, by_gate, by_up, _, out):
    grad_act = act[...] + act_far[...].astype(F32)
    out[0] = (grad_act * by_gate[...]).astype(BF)
    out[1] = (grad_act * by_up[...]).astype(BF)


def own_rows(mine, held, out):
    out[...] = mm(mine[0], held[0]) + mm(mine[1], held[1])


def other_rows(experts, total, other, place, held, *refs):
    pieces, whole = refs[:experts], refs[experts]
    rows = total[...] + mm(other[0], held[0]) + mm(other[1], held[1])
    whole[...] = mm(place[...], rows.astype(BF))
    for piece, step in zip(pieces, steps(experts)):
        piece[...] = whole[place_of(ahead(step, experts), experts)].astype(BF)


def weight_grads(mine_act, other_act, mine, other, rows_in, rows_grad, pair_out, down_out, held, sems):
    core = lax.axis_index("ey") & 1
    half = mine_act.shape[1]
    step = half // 4
    stores = []
    for matrix in range(3):
        right = rows_grad[...] if matrix == 0 else rows_in[...]
        for own in range(2):
            start = (core if own else 1 - core) * half
            for part in range(4):
                columns = slice(part * step, (part + 1) * step)
                if matrix == 0:
                    left = (mine_act if own else other_act)[:, columns]
                else:
                    left = (mine if own else other)[matrix - 1, :, columns]
                at = len(stores)
                held[at] = mm(left, right, ROWS).astype(BF)
                rows = pl.ds(start + part * step, step)
                target = down_out.at[0, rows] if matrix == 0 else pair_out.at[0, matrix - 1, rows]
                store = pltpu.make_async_copy(held.at[at], target, sems.at[at])
                store.start()
                stores.append(store)
    for store in stores:
        store.wait()


def combine(experts, pick, *refs):
    out, whole, held, sems = refs[experts:]
    for piece, step in zip(refs[:experts], steps(experts)):
        whole[place_of(ahead(experts - step, experts), experts)] = piece[...].astype(F32)
    home = whole[...].astype(BF)
    rows = out.shape[0] // held.shape[0]
    stores = []
    for at in range(held.shape[0]):
        part = pick[:, at * rows : (at + 1) * rows]
        held[at] = mm(part, home, ROWS).astype(BF)
        target = out.at[pl.ds(at * rows, rows)]
        stores += run([pltpu.make_async_copy(held.at[at], target, sems.at[at])])
    wait(stores)


def far(value):
    return pltpu.with_memory_space_constraint(value, pltpu.HBM)


def place_of(partner, experts):
    k = lax.axis_index("ex") ^ partner
    spot = jnp.int32(0)
    for at, name in enumerate(far_first(experts)):
        spot = spot + jnp.where(k == name, at * MOST, 0)
    return pl.ds(pl.multiple_of(spot, 8), MOST)


def tour(count):
    return list(range(count))


def steps(count):
    return list(range(1, count)) + [0]


def ahead(step, count):
    me, names = lax.axis_index("ex"), tour(count)
    found = jnp.int32(0)
    for at, name in enumerate(names):
        found = found + jnp.where(me == name, names[(at + step) % count], 0)
    return found


def shift(value, axis, step):
    count = lax.axis_size(axis)
    names = tour(count)
    return lax.ppermute(
        value, axis, [(name, names[(at + step) % count]) for at, name in enumerate(names)]
    )


def swap(value, axis, bit):
    count = lax.axis_size(axis)
    return lax.ppermute(value, axis, [(i, i ^ bit) for i in range(count)])


def exchange(pieces, axis):
    order = far_first(len(pieces))
    return [swap(piece, axis, k) if k else piece for piece, k in zip(pieces, order)]


def local(inputs, grad_output, routes, gate_probs, gate_up, down_proj):
    experts = lax.axis_size("ex")
    ways = lax.axis_size("ey")
    tokens, width = inputs.shape
    hidden = gate_up.shape[2]
    half = hidden // 2
    capacity = 5 * tokens * experts * routes.shape[1] // (4 * EXPERTS)
    rows = experts * MOST
    weight_bytes = hidden * width * 2
    weight_flops = 2 * capacity * hidden * width
    sds = jax.ShapeDtypeStruct
    piece = [sds((MOST, width), BF)] * experts
    dma = lambda count: pltpu.SemaphoreType.DMA((count,))

    order = far_first(experts)
    pick, prob, grads, *send_in, own_in = call(
        functools.partial(pick_inputs, experts),
        [
            sds((rows, tokens), BF),
            sds((rows, 1), F32),
            pltpu.VMEM((tokens, width), BF),
        ]
        + piece,
        (far(routes.T), far(gate_probs.T), far(inputs), far(grad_output)),
        [HBM] * 4,
        [
            pltpu.VMEM(routes.shape[::-1], jnp.int32),
            pltpu.VMEM(routes.shape[::-1], BF),
            pltpu.VMEM((tokens, width), BF),
            dma(4),
        ],
        flops=2 * rows * tokens * width,
        traffic=4 * tokens * width,
    )
    near, *send_grad = call(
        functools.partial(pick_grads, experts),
        [sds((2 * MOST, width), BF)] + piece[1:],
        (pick, prob, grads, send_in[-1]),
        [VMEM] * 4,
        flops=2 * rows * tokens * width,
        traffic=2 * tokens * width,
    )
    near = swap(near, "ex", 1)
    got_in = [swap(part, "ex", k) for part, k in zip(send_in[:-1], order)] + [near, own_in]
    got_in[0] = call(
        early_rows,
        piece[0],
        (got_in[0],),
        [VMEM],
        flops=int(C0COST * weight_flops),
        traffic=weight_bytes,
    )
    held_other, held_mine, *send_grad = call(
        functools.partial(stage, experts - 1),
        [pltpu.VMEM((3, half, width), BF)] * 2 + piece[1:],
        (far(gate_up), far(down_proj), *send_grad),
        [HBM] * 2 + [VMEM] * (experts - 1),
        [dma(6)],
        flops=WCOST * weight_flops,
        traffic=WCOST * weight_bytes,
    )
    got_grad = [swap(part, "ex", k) for part, k in zip(send_grad[:-1], order)][::-1]
    got_grad = got_grad + [near, send_grad[-1]]
    pair_other, place, rows_in = call(
        functools.partial(other_pair, experts, capacity),
        [sds((2, capacity, half), BF), sds((rows, capacity), BF), sds((capacity, width), BF)],
        (*got_in, held_other),
        [VMEM] * (experts + 1),
        flops=2 * weight_flops,
        traffic=weight_bytes,
    )
    pair_mine = call(
        mine_pair,
        sds((2, capacity, half), BF),
        (rows_in, held_mine),
        [VMEM] * 2,
        flops=C2COST * weight_flops,
        traffic=C2COST * weight_bytes,
    )

    def total(held, sent):
        bit = 2
        while bit * 2 < ways:
            held = held + swap(sent, "ey", bit).astype(F32)
            sent = held.astype(BF)
            bit *= 2
        return held, swap(sent, "ey", bit)

    pair, pair_sent = call(
        pair_sum,
        [sds((2, capacity, half), F32), sds((2, capacity, half), BF)],
        (pair_mine, swap(pair_other, "ey", 1)),
        [VMEM] * 2,
        traffic=10 * capacity * hidden,
    )
    pair, pair_far = total(pair, pair_sent)
    def act_of(own, held, outs, tied, cost):
        return call(
            functools.partial(act_part, experts, own),
            outs + [sds((capacity, half), BF)],
            (*got_grad, place, held, *tied),
            [VMEM] * (experts + 2) + [ANY] * len(tied),
            flops=cost * weight_flops,
            traffic=cost * weight_bytes,
        )

    (act_other,) = act_of(False, held_other, [], [pair_sent], D1COST)
    rows_grad, act_mine = act_of(True, held_mine, [sds((capacity, width), BF)], [], D2COST)
    act = act_mine.astype(F32) + swap(act_other, "ey", 1).astype(F32)
    act, act_far = total(act, act.astype(BF))
    mine_act, by_gate, by_up = call(
        gates,
        [sds((capacity, half), BF)] + [sds((capacity, half), F32)] * 2,
        (pair, pair_far),
        [VMEM] * 2,
        traffic=18 * capacity * half,
        flops=GFLOP * weight_flops,
    )
    other_act = swap(mine_act, "ey", 1)
    mine = call(
        grads_of,
        sds((2, capacity, half), BF),
        (act, act_far, by_gate, by_up, other_act),
        [VMEM] * 4 + [ANY],
        traffic=18 * capacity * half,
    )
    other = swap(mine, "ey", 1)
    own = call(
        own_rows,
        sds((capacity, width), F32),
        (mine, held_mine),
        [VMEM] * 2,
        flops=weight_flops,
        traffic=weight_bytes,
    )
    back = call(
        functools.partial(other_rows, experts),
        piece,
        (own, other, place, held_other),
        [VMEM] * 4,
        [pltpu.VMEM((rows, width), F32)],
        flops=weight_flops,
        traffic=weight_bytes,
    )
    home = [shift(part, "ex", step) if step else part for part, step in zip(back, steps(experts))]
    pair_grad, down_grad = call(
        weight_grads,
        [sds((1, 2, hidden, width), BF), sds((1, hidden, width), BF)],
        (mine_act, other_act, mine, other, rows_in, rows_grad),
        [VMEM] * 6,
        [pltpu.VMEM((24, half // 4, width), BF), dma(24)],
        limit=24,
        flops=3 * weight_flops,
        traffic=3 * weight_bytes,
        out_specs=[ANY, ANY],
    )
    grad_inputs = call(
        functools.partial(combine, experts),
        sds((tokens, width), BF),
        (pick, *home),
        [VMEM] * (experts + 1),
        [pltpu.VMEM((rows, width), F32), pltpu.VMEM((2, tokens // 2, width), BF), dma(2)],
        flops=2 * rows * tokens * width,
        traffic=4 * tokens * width,
        out_specs=ANY,
    )
    return (grad_inputs, pair_grad, down_grad)


def solution(mesh):
    return jax.shard_map(
        local,
        mesh=mesh,
        in_specs=(
            P(("groups", "ex"), "ey"),
            P(("groups", "ex"), "ey"),
            P(("groups", "ex"), None),
            P(("groups", "ex"), None),
            P("ex", None, None, "ey"),
            P("ex", None, "ey"),
        ),
        out_specs=(
            P(("groups", "ex"), "ey"),
            P("ex", "groups", None, "ey"),
            P("ex", "groups", "ey"),
        ),
        check_vma=False,
    )
```
